32 devices in a mesh: ep: 8 (over z, y), tp: 4 (over x, core).
Axes of the slice: x: 2, y: 2, z: 4, core: 2. Of those that a mesh axis runs over, the one named last changes fastest.
Arguments:
- tokens: bfloat16 [4096, 2048], P('ep', 'tp'), may hold values from -6 to 6
- out_grad: bfloat16 [4096, 2048], P('ep', 'tp'), may hold values from -6 to 6
- first_gain: float32 [2048], replicated, may hold values from 0.5 to 1.5
- query_weight: bfloat16 [2048, 2048], P(None, 'tp'), may hold values from -0.125 to 0.125
- key_weight: bfloat16 [2048, 2048], P(None, 'tp'), may hold values from -0.125 to 0.125
- value_weight: bfloat16 [2048, 2048], P(None, 'tp'), may hold values from -0.125 to 0.125
- query_bias: float32 [2048], P('tp'), may hold values from -0.6 to 0.6
- key_bias: float32 [2048], P('tp'), may hold values from -0.6 to 0.6
- value_bias: float32 [2048], P('tp'), may hold values from -0.6 to 0.6
- output_weight: bfloat16 [2048, 2048], P('tp'), may hold values from -1.5 to 1.5
- second_gain: float32 [2048], replicated, may hold values from 0.5 to 1.5
- router_weight: bfloat16 [2048, 8], replicated, may hold values from -0.0625 to 0.0625
- shared_gate_weight: bfloat16 [2048, 5632], P(None, 'tp'), may hold values from -0.125 to 0.125
- shared_up_weight: bfloat16 [2048, 5632], P(None, 'tp'), may hold values from -0.125 to 0.125
- shared_down_weight: bfloat16 [5632, 2048], P('tp'), may hold values from -0.078125 to 0.078125
- switch_vector: bfloat16 [2048], replicated, may hold values from -0.125 to 0.125
- expert_gate_weight: bfloat16 [8, 2048, 1408], P('ep', None, 'tp'), may hold values from -0.125 to 0.125
- expert_up_weight: bfloat16 [8, 2048, 1408], P('ep', None, 'tp'), may hold values from -0.125 to 0.125
- expert_down_weight: bfloat16 [8, 1408, 2048], P('ep', 'tp'), may hold values from -0.625 to 0.625
- expert_ids: int32 [4096, 4], P('ep'), may hold values from 0 to 7, all different within a row
- pair_order: int32 [8, 2048], P('ep'), may hold values from 0 to 2047, each once within a row
Outputs:
- mixed: bfloat16 [4096, 2048], P('ep', 'tp')
- tokens_grad: bfloat16 [4096, 2048], P('ep', 'tp')
- first_gain_grad: float32 [2048], P('ep')
- query_weight_grad: float32 [2048, 2048], P('ep', 'tp')
- key_weight_grad: float32 [2048, 2048], P('ep', 'tp')
- value_weight_grad: float32 [2048, 2048], P('ep', 'tp')
- query_bias_grad: float32 [16, 128], P('tp', 'ep')
- key_bias_grad: float32 [16, 128], P('tp', 'ep')
- value_bias_grad: float32 [16, 128], P('tp', 'ep')
- output_weight_grad: float32 [2048, 2048], P('tp', 'ep')
- second_gain_grad: float32 [2048], P('ep')
- router_weight_grad: float32 [2048, 8], P('ep')
- shared_gate_grad: float32 [2048, 5632], P('ep', 'tp')
- shared_up_grad: float32 [2048, 5632], P('ep', 'tp')
- shared_down_grad: float32 [5632, 2048], P('tp', 'ep')
- switch_vector_grad: float32 [2048], P('ep')
- expert_gate_grad: float32 [8, 2048, 1408], P('ep', None, 'tp')
- expert_up_grad: float32 [8, 2048, 1408], P('ep', None, 'tp')
- expert_down_grad: float32 [8, 1408, 2048], P('ep', 'tp')
The draws below stay inside these ranges and needn't reach their ends.
Inputs may be any that keep to these rules, and one draw needn't show every extreme that they name: `expert_ids`: each row names 4 different experts; every expert is named by some row. `pair_order`: each row holds every pair number t * 4 + k of its group of rows once.
All inputs are finite; a program needn't handle non-finite values.
Results may differ from the reference program's by a relative error of at most 0.024.
Values may be sent and summed in bfloat16 or wider, within the bound.
A program may use at most 320 MiB of HBM per device.

```python
import math
import jax
import jax.numpy as jnp
from jax import lax

D = 2048
HEADS = 16
HD = 128
EFF = 1408
SFF = 5632
TOP = 4
BLOCK = 256
TOK_DEV = 512
SEQ_LEN = 1024
SEQS = 4
TOKENS = 4096
EXPERTS = 8
CAP = 288
N_EP = 8


def levels(key, dims, shards, least, high):
    level = 1.0
    for axis_at, shards_of in shards:
        heights = jax.random.uniform(jax.random.fold_in(jax.random.fold_in(key, 6), axis_at), (shards_of,), jnp.float32, least / len(shards), high / len(shards))
        level = level * jnp.repeat(jnp.exp(heights), dims[axis_at] // shards_of).reshape((-1,) + (1,) * (len(dims) - 1 - axis_at))
    return level


def picks_of(key, rows, count, top, lift):
    order = jax.random.permutation(jax.random.fold_in(key, 1), count)
    favour = order
    for power in range(3):
        favour = favour * favour // count
    favour = favour * lift // count
    chance = jax.random.randint(jax.random.fold_in(key, 2), (rows, count), 0, 4096) + favour
    sure = jax.random.permutation(jax.random.fold_in(key, 3), rows)[jnp.arange(count) % rows]
    chance = jnp.where(jnp.arange(rows)[:, None] == sure[None, :], 1 << 14, chance)
    priority = chance * count + jnp.arange(count)
    return lax.top_k(priority.astype(jnp.int32), top)[1].astype(jnp.int32)


def centred(key, shape, width, most, cuts=(), kind=jnp.bfloat16):
    values = jax.random.normal(key, shape, jnp.float32) * width
    if len(cuts) > 0:
        values = levels(key, shape, cuts, -0.22, 0.18) * values
    return jnp.clip(values, min=-most, max=most).astype(kind)


def setup_inputs(seed: int = 0) -> dict:
    streams_of = jax.random.split(jax.random.key(seed), 22)
    return {
        "tokens": centred(streams_of[0], (TOKENS, D), 1.0, 6.0, ((0, 8), (1, 4))),
        "out_grad": centred(streams_of[1], (TOKENS, D), 1.0, 6.0, ((0, 8), (1, 4))),
        "first_gain": jnp.clip(1.0 + 0.1 * jax.random.normal(streams_of[2], (D,), jnp.float32), 0.5, 1.5),
        "query_weight": centred(streams_of[3], (D, HEADS * HD), D ** -0.5, 0.125, ((1, 4),)),
        "key_weight": centred(streams_of[4], (D, HEADS * HD), D ** -0.5, 0.125, ((1, 4),)),
        "value_weight": centred(streams_of[5], (D, HEADS * HD), D ** -0.5, 0.125, ((1, 4),)),
        "query_bias": centred(streams_of[6], (HEADS * HD,), 0.1, 0.6, ((0, 4),), jnp.float32),
        "key_bias": centred(streams_of[7], (HEADS * HD,), 0.1, 0.6, ((0, 4),), jnp.float32),
        "value_bias": centred(streams_of[8], (HEADS * HD,), 0.1, 0.6, ((0, 4),), jnp.float32),
        "output_weight": centred(streams_of[9], (HEADS * HD, D), (max(16, 2 * HEADS * HD // SEQ_LEN)) ** -0.5, 1.5, ((0, 4),)),
        "second_gain": jnp.clip(1.0 + 0.1 * jax.random.normal(streams_of[10], (D,), jnp.float32), 0.5, 1.5),
        "router_weight": centred(streams_of[11], (D, EXPERTS), (4 * D) ** -0.5, 0.0625),
        "shared_gate_weight": centred(streams_of[12], (D, SFF), D ** -0.5, 0.125, ((1, 4),)),
        "shared_up_weight": centred(streams_of[13], (D, SFF), D ** -0.5, 0.125, ((1, 4),)),
        "shared_down_weight": centred(streams_of[14], (SFF, D), SFF ** -0.5, 0.078125, ((0, 4),)),
        "switch_vector": centred(streams_of[15], (D,), D ** -0.5, 0.125),
        "expert_gate_weight": centred(streams_of[16], (EXPERTS, D, EFF), D ** -0.5, 0.125, ((0, 8), (2, 4))),
        "expert_up_weight": centred(streams_of[17], (EXPERTS, D, EFF), D ** -0.5, 0.125, ((0, 8), (2, 4))),
        "expert_down_weight": centred(streams_of[18], (EXPERTS, EFF, D), (max(1, 4 * EFF // (EXPERTS * EXPERTS))) ** -0.5, 0.625, ((0, 8), (1, 4))),
        "expert_ids": picks_of(streams_of[19], TOKENS, EXPERTS, TOP, 4096),
        "pair_order": jax.vmap(lambda own: jax.random.permutation(own, TOK_DEV * TOP))(jax.random.split(streams_of[20], N_EP)).reshape((N_EP, TOK_DEV * TOP)).astype(jnp.int32),
    }


@jax.custom_vjp
def low(v):
    return lax.optimization_barrier(v.astype(jnp.bfloat16)).astype(jnp.float32)

@jax.custom_vjp
def low_back(v):
    return v

def low_keep(v):
    return (low(v), None)

def low_pass(kept, grad):
    return (grad,)

def back_keep(v):
    return (v, None)

def back_low(kept, grad):
    return (low(grad),)
low.defvjp(low_keep, low_pass)
low_back.defvjp(back_keep, back_low)
highest = lax.Precision.HIGHEST
rope_theta = 1000000.0
norm_eps = 1e-06
masked_score = -1e+30

def matmul_high(left_side, right_side):
    return jnp.dot(left_side, right_side, precision=highest)

def row_norm(values, gain_vec):
    inv_rms = lax.rsqrt(lax.optimization_barrier(jnp.mean(values * values, axis=-1, keepdims=True)) + norm_eps)
    return values * inv_rms * gain_vec

def softmax_rows(scores):
    row_max = lax.optimization_barrier(jnp.max(scores, axis=-1, keepdims=True))
    powers = jnp.exp(scores - row_max)
    return powers / lax.optimization_barrier(jnp.sum(powers, axis=-1, keepdims=True))

def swish(values):
    return values * jax.nn.sigmoid(values)

def rope_tables(row_count, head_dim):
    positions = jnp.arange(row_count, dtype=jnp.float32)
    frequency = jnp.exp(jnp.arange(head_dim // 2, dtype=jnp.float32) * (-2.0 * math.log(rope_theta) / head_dim))
    angles = positions[:, None] * frequency[None, :]
    return (jnp.cos(angles)[:, None, :], jnp.sin(angles)[:, None, :])

def rotate(values, cosine, sine_part):
    half_dim = values.shape[-1] // 2
    first_half = values[..., :half_dim]
    second_half = values[..., half_dim:]
    return jnp.concatenate([first_half * cosine - second_half * sine_part, second_half * cosine + first_half * sine_part], axis=-1)

def attend_sequence(normed, query_weight, key_weight, value_weight, query_bias, key_bias, value_bias, output_weight):
    row_count = normed.shape[0]
    cosine, sine_part = rope_tables(row_count, HD)
    query_lin = low_back(matmul_high(normed, query_weight) + query_bias)
    key_lin = low_back(matmul_high(normed, key_weight) + key_bias)
    value_lin = matmul_high(normed, value_weight) + value_bias
    queries = low(rotate(query_lin.reshape(row_count, HEADS, HD), cosine, sine_part))
    keys_rot = low(rotate(key_lin.reshape(row_count, HEADS, HD), cosine, sine_part))
    values_all = low_back(low(value_lin.reshape(row_count, HEADS, HD)))
    scores = jnp.einsum('qhd,khd->hqk', queries, keys_rot, precision=highest) * HD ** (-0.5)
    blocks = jnp.arange(row_count) // BLOCK
    allowed = blocks[None, :] <= blocks[:, None]
    scores = low_back(jnp.where(allowed[None], scores, masked_score))
    attn_probs = softmax_rows(scores)
    context = jnp.einsum('hqk,khd->qhd', low(attn_probs), values_all, precision=highest)
    context = low_back(low(context.reshape(row_count, HEADS * HD)))
    return low_back(matmul_high(context, output_weight))

def shared_sequence(normed, gate_weight, up_weight, down_weight):
    gate_lin = low_back(matmul_high(normed, gate_weight))
    up_lin = low_back(matmul_high(normed, up_weight))
    hidden = low(swish(gate_lin) * up_lin)
    return low_back(matmul_high(hidden, down_weight))

def expert_block(rows_in, gate_weight, up_weight, down_weight):
    rows_in = low_back(rows_in)
    gate_lin = low_back(matmul_high(rows_in, gate_weight))
    up_lin = low_back(matmul_high(rows_in, up_weight))
    hidden = low(swish(gate_lin) * up_lin)
    return low_back(low(matmul_high(hidden, down_weight)))

def routing_tables(expert_ids, pair_order):
    pair_total = TOK_DEV * TOP
    group_count = N_EP
    flat_ids = expert_ids.reshape(group_count, pair_total)
    in_turn = jnp.take_along_axis(flat_ids, pair_order, axis=1)
    onehot = (in_turn[:, :, None] == jnp.arange(EXPERTS, dtype=jnp.int32)[None, None, :]).astype(jnp.int32)
    earlier = jnp.cumsum(onehot, axis=1) - onehot
    turn_slot = lax.optimization_barrier(jnp.sum(earlier * onehot, axis=2))
    group_rows = jnp.arange(group_count, dtype=jnp.int32)[:, None]
    slot_index = jnp.zeros((group_count, pair_total), jnp.int32).at[group_rows, pair_order].set(turn_slot)
    kept_pair = slot_index < CAP
    rows_all = N_EP * CAP
    target = jnp.where(kept_pair, flat_ids * rows_all + group_rows * CAP + slot_index, EXPERTS * rows_all).reshape(-1)
    pair_index = jnp.arange(group_count * pair_total, dtype=jnp.int32)
    slot_pair = jnp.full((EXPERTS * rows_all + 1,), group_count * pair_total, jnp.int32).at[target].set(pair_index)[:-1]
    slot_token = jnp.where(slot_pair < group_count * pair_total, slot_pair // TOP, TOKENS).astype(jnp.int32)
    return (slot_pair, slot_token)

def forward(tokens, first_gain, query_weight, key_weight, value_weight, query_bias, key_bias, value_bias, output_weight, second_gain, router_weight, shared_gate_weight, shared_up_weight, shared_down_weight, switch_vector, expert_gate_weight, expert_up_weight, expert_down_weight, slot_pair, slot_token, expert_ids):
    seq_view = tokens.reshape(SEQS, SEQ_LEN, D)
    normed = low(row_norm(seq_view, first_gain))

    def attend_one(normed_seq):
        return attend_sequence(normed_seq, query_weight, key_weight, value_weight, query_bias, key_bias, value_bias, output_weight)
    attended = lax.map(jax.checkpoint(attend_one), normed)
    hidden_one = seq_view + attended
    normed_two = low(row_norm(hidden_one, second_gain))

    def shared_one(normed_seq):
        return shared_sequence(normed_seq, shared_gate_weight, shared_up_weight, shared_down_weight)
    shared_out = lax.map(jax.checkpoint(shared_one), normed_two).reshape(TOKENS, D)
    flat_two = normed_two.reshape(TOKENS, D)
    logits = low_back(matmul_high(flat_two, router_weight))
    router_probs = softmax_rows(logits)
    gate_values = jnp.take_along_axis(router_probs, expert_ids, axis=1)
    switch = jax.nn.sigmoid(matmul_high(flat_two, switch_vector))
    padded = jnp.concatenate([flat_two, jnp.zeros((1, D), flat_two.dtype)], axis=0)
    gate_pad = jnp.concatenate([gate_values.reshape(-1), jnp.zeros((1,), gate_values.dtype)])
    slot_gate = gate_pad[slot_pair].reshape(EXPERTS, N_EP * CAP)
    slot_table = slot_token.reshape(EXPERTS, N_EP * CAP)

    def expert_one(expert_items):
        gate_weight, up_weight, down_weight, table_row, gate_row = expert_items
        return gate_row[:, None] * expert_block(padded[table_row], gate_weight, up_weight, down_weight)
    expert_out = lax.map(jax.checkpoint(expert_one), (expert_gate_weight, expert_up_weight, expert_down_weight, slot_table, slot_gate))
    routed = jnp.zeros((TOKENS + 1, D), flat_two.dtype).at[slot_token].add(expert_out.reshape(-1, D))[:TOKENS]
    return hidden_one.reshape(TOKENS, D) + switch[:, None] * shared_out + routed

def reference(tokens, out_grad, first_gain, query_weight, key_weight, value_weight, query_bias, key_bias, value_bias, output_weight, second_gain, router_weight, shared_gate_weight, shared_up_weight, shared_down_weight, switch_vector, expert_gate_weight, expert_up_weight, expert_down_weight, expert_ids, pair_order):
    slot_pair, slot_token = routing_tables(expert_ids, pair_order)
    float_args = (tokens, first_gain, query_weight, key_weight, value_weight, query_bias, key_bias, value_bias, output_weight, second_gain, router_weight, shared_gate_weight, shared_up_weight, shared_down_weight, switch_vector, expert_gate_weight, expert_up_weight, expert_down_weight)
    float_args = tuple((argument.astype(jnp.float32) for argument in float_args))

    def wrapped(*layer_args):
        return forward(*layer_args, slot_pair, slot_token, expert_ids)
    layer_out, pullback = jax.vjp(wrapped, *float_args)
    gradients = pullback(out_grad.astype(jnp.float32))
    return (layer_out.astype(jnp.bfloat16), gradients[0].astype(jnp.bfloat16), gradients[1], gradients[2], gradients[3], gradients[4], gradients[5].reshape(HEADS, HD), gradients[6].reshape(HEADS, HD), gradients[7].reshape(HEADS, HD), gradients[8], gradients[9], gradients[10], gradients[11], gradients[12], gradients[13], gradients[14], gradients[15], gradients[16], gradients[17])
```

```python
import math

import jax
import jax.numpy as jnp
from jax import lax
from jax.experimental import pallas as pl
from jax.experimental.pallas import tpu as pltpu
from jax.sharding import PartitionSpec as P

HD = 128
BLOCK = 256
SPAN = 2


rope_theta = 1000000.0
norm_eps = 1e-06
masked_score = -1e30


def passed_along(value, axis, steps):
    count = lax.axis_size(axis)
    leading, last = (max(0, -steps), min(count, count - steps))
    return lax.ppermute(value, axis, [(source, source + steps) for source in range(leading, last)])


def rope_tables(row_count, head_dim, first_position):
    positions = jnp.arange(row_count, dtype=jnp.float32) + first_position.astype(jnp.float32)
    frequency = jnp.exp(
        jnp.arange(head_dim // 2, dtype=jnp.float32) * (-2.0 * math.log(rope_theta) / head_dim)
    )
    angles = positions[:, None] * frequency[None, :]
    return (jnp.cos(angles)[:, None, :], jnp.sin(angles)[:, None, :])


def rotate(values, cosine, sine_part):
    half_dim = values.shape[-1] // 2
    first_half = values[..., :half_dim]
    second_half = values[..., half_dim:]
    return jnp.concatenate(
        [
            first_half * cosine - second_half * sine_part,
            second_half * cosine + first_half * sine_part,
        ],
        axis=-1,
    )


def inner_rows(left_side, right_side):
    return lax.dot_general(
        left_side, right_side, (((0,), (0,)), ((), ())), preferred_element_type=jnp.float32
    )


def times_transpose(left_side, right_side):
    return lax.dot_general(
        left_side, right_side, (((1,), (1,)), ((), ())), preferred_element_type=jnp.float32
    )


def row_stats(values):
    inv_rms = lax.rsqrt(jnp.mean(values * values, axis=-1, keepdims=True) + norm_eps)
    return (values * inv_rms, inv_rms)


def norm_back(grad_rows, unit_rows, inv_rms, gain_vec):
    scaled = grad_rows * gain_vec
    return inv_rms * (scaled - unit_rows * jnp.mean(scaled * unit_rows, axis=-1, keepdims=True))


def softmax_rows(scores):
    row_max = jnp.max(scores, axis=-1, keepdims=True)
    powers = jnp.exp(scores - row_max)
    return powers / jnp.sum(powers, axis=-1, keepdims=True)


def to_experts(block_rows, local_count):
    sources, span_rows, col_count = block_rows.shape
    slot_count = span_rows // local_count
    shaped = block_rows.reshape(sources, local_count, slot_count, col_count)
    return shaped.swapaxes(0, 1).reshape(local_count, sources * slot_count, col_count)


def to_sources(block_rows, sources):
    local_count, rows_all, col_count = block_rows.shape
    slot_count = rows_all // sources
    shaped = block_rows.reshape(local_count, sources, slot_count, col_count)
    return shaped.swapaxes(0, 1).reshape(sources, local_count * slot_count, col_count)


def deliver(block_rows):
    arrived = lax.all_to_all(block_rows, "ep", split_axis=0, concat_axis=0, tiled=True)
    return arrived


def collect(block_rows):
    return lax.all_to_all(block_rows, "ep", split_axis=0, concat_axis=0, tiled=True)


def slot_plan(
    tokens,
    out_grad,
    first_gain,
    query_weight,
    key_weight,
    value_weight,
    query_bias,
    key_bias,
    value_bias,
    output_weight,
    second_gain,
    router_weight,
    shared_gate_weight,
    shared_up_weight,
    shared_down_weight,
    switch_vector,
    expert_gate_weight,
    expert_up_weight,
    expert_down_weight,
    expert_ids,
    pair_order,
):
    whole_in, whole_grad = (
        lax.all_gather(tokens, "tp", axis=1, tiled=True),
        lax.all_gather(out_grad, "tp", axis=1, tiled=True),
    )
    tok_count = whole_in.shape[0]
    model_dim = whole_in.shape[1]
    col_width = tokens.shape[1]
    col_start = lax.axis_index("tp") * col_width
    sources = lax.axis_size("ep")
    place_in_seq = lax.axis_index("ep") % SPAN
    has_earlier = place_in_seq > 0
    local_experts = expert_gate_weight.shape[0]
    expert_total = router_weight.shape[1]
    top_count = expert_ids.shape[1]
    pair_count = tok_count * top_count
    capacity = 9 * pair_count // (8 * expert_total)
    head_count = query_weight.shape[1] // HD
    score_scale = HD ** (-0.5)
    inputs_full = whole_in.astype(jnp.float32)
    unit_one, inv_one = row_stats(inputs_full)
    normed_one = (unit_one * first_gain).astype(jnp.bfloat16)
    query_lin = jnp.dot(normed_one, query_weight, preferred_element_type=jnp.float32) + query_bias
    key_lin = jnp.dot(normed_one, key_weight, preferred_element_type=jnp.float32) + key_bias
    value_lin = jnp.dot(normed_one, value_weight, preferred_element_type=jnp.float32) + value_bias
    cosine, sine_part = rope_tables(tok_count, HD, place_in_seq * tok_count)
    queries = rotate(query_lin.reshape(tok_count, head_count, HD), cosine, sine_part).astype(
        jnp.bfloat16
    )
    keys_rot = rotate(key_lin.reshape(tok_count, head_count, HD), cosine, sine_part).astype(
        jnp.bfloat16
    )
    values_all = value_lin.reshape(tok_count, head_count, HD).astype(jnp.bfloat16)
    earlier_keys, earlier_values = passed_along((keys_rot, values_all), "ep", 1)
    keys_both = jnp.concatenate([earlier_keys, keys_rot], axis=0)
    values_both = jnp.concatenate([earlier_values, values_all], axis=0)
    blocks = jnp.arange(tok_count) // BLOCK
    local_allowed = blocks[None, :] <= blocks[:, None]
    remote_allowed = jnp.broadcast_to(has_earlier, (tok_count, tok_count))
    allowed = jnp.concatenate([remote_allowed, local_allowed], axis=1)[None]

    def attention_scores():
        scored = (
            jnp.einsum("qhd,khd->hqk", queries, keys_both, preferred_element_type=jnp.float32)
            * score_scale
        )
        return jnp.where(allowed, scored, masked_score)

    scores = attention_scores()
    row_max = jnp.max(scores, axis=-1, keepdims=True)
    powers = jnp.exp(scores - row_max)
    totals = jnp.sum(powers, axis=-1, keepdims=True)
    log_total = row_max + jnp.log(totals)
    probs_low = (powers / totals).astype(jnp.bfloat16)
    context = jnp.einsum("hqk,khd->qhd", probs_low, values_both, preferred_element_type=jnp.float32)
    context = context.reshape(tok_count, head_count * HD).astype(jnp.bfloat16)
    attn_part = jnp.dot(context, output_weight, preferred_element_type=jnp.float32)
    attended = lax.psum(attn_part, "tp")
    hidden_one = inputs_full + attended
    unit_two, inv_two = row_stats(hidden_one)
    normed_two = (unit_two * second_gain).astype(jnp.bfloat16)
    logits = jnp.dot(normed_two, router_weight, preferred_element_type=jnp.float32)
    router_probs = softmax_rows(logits)
    gate_values = jnp.take_along_axis(router_probs, expert_ids, axis=1)
    switch = jax.nn.sigmoid(jnp.dot(normed_two, switch_vector, preferred_element_type=jnp.float32))
    flat_ids = expert_ids.reshape(-1)
    turn_order = pair_order.reshape(-1)
    in_turn = flat_ids[turn_order]
    onehot = (in_turn[:, None] == jnp.arange(expert_total, dtype=jnp.int32)[None, :]).astype(
        jnp.int32
    )
    earlier = jnp.cumsum(onehot, axis=0) - onehot
    turn_slot = jnp.sum(earlier * onehot, axis=1)
    slot_index = jnp.zeros((pair_count,), jnp.int32).at[turn_order].set(turn_slot)
    kept_pair = slot_index < capacity
    slot_rows = expert_total * capacity
    target = jnp.where(kept_pair, flat_ids * capacity + slot_index, slot_rows)
    pair_token = jnp.arange(pair_count, dtype=jnp.int32) // top_count
    slot_token = (
        jnp.full((slot_rows + 1,), tok_count, jnp.int32).at[target].set(pair_token)[:slot_rows]
    )
    slot_gate = (
        jnp.zeros((slot_rows + 1,), jnp.float32).at[target].set(gate_values.reshape(-1))[:slot_rows]
    )
    padded_two = jnp.concatenate([normed_two, jnp.zeros((1, model_dim), jnp.bfloat16)], axis=0)
    send_rows = padded_two[slot_token].reshape(sources, local_experts * capacity, model_dim)
    expert_rows = to_experts(deliver(send_rows), local_experts)
    gate_lin = jnp.einsum(
        "erd,edf->erf", expert_rows, expert_gate_weight, preferred_element_type=jnp.float32
    )
    up_lin = jnp.einsum(
        "erd,edf->erf", expert_rows, expert_up_weight, preferred_element_type=jnp.float32
    )
    gate_sig = jax.nn.sigmoid(gate_lin)
    gate_act = gate_lin * gate_sig
    expert_hidden = (gate_act * up_lin).astype(jnp.bfloat16)
    expert_part = jnp.einsum(
        "erf,efd->erd", expert_hidden, expert_down_weight, preferred_element_type=jnp.float32
    )
    shared_gate_lin = jnp.dot(normed_two, shared_gate_weight, preferred_element_type=jnp.float32)
    shared_up_lin = jnp.dot(normed_two, shared_up_weight, preferred_element_type=jnp.float32)
    shared_sig = jax.nn.sigmoid(shared_gate_lin)
    shared_act = shared_gate_lin * shared_sig
    shared_hidden = (shared_act * shared_up_lin).astype(jnp.bfloat16)
    shared_part = jnp.dot(shared_hidden, shared_down_weight, preferred_element_type=jnp.float32)
    expert_cols, shared_cols = (
        lax.psum_scatter(expert_part.reshape(-1, model_dim), "tp", scatter_dimension=1, tiled=True),
        lax.psum_scatter(shared_part, "tp", scatter_dimension=1, tiled=True),
    )
    returned = collect(
        to_sources(expert_cols.astype(jnp.bfloat16).reshape(local_experts, -1, col_width), sources)
    )
    back_flat = jnp.concatenate(
        [returned.reshape(slot_rows, col_width), jnp.zeros((1, col_width), jnp.bfloat16)], axis=0
    )
    pair_out = back_flat[target].astype(jnp.float32).reshape(tok_count, top_count, col_width)
    routed = jnp.sum(gate_values[:, :, None] * pair_out, axis=1)
    hidden_cols = lax.dynamic_slice_in_dim(hidden_one, col_start, col_width, 1)
    layer_out = (hidden_cols + switch[:, None] * shared_cols + routed).astype(jnp.bfloat16)
    grad_full = whole_grad.astype(jnp.float32)
    grad_cols = out_grad.astype(jnp.float32)
    gate_part = jnp.sum(pair_out * grad_cols[:, None, :], axis=-1)
    switch_part = jnp.sum(grad_cols * shared_cols, axis=-1)
    gate_grad, switch_grad = lax.psum((gate_part, switch_part), "tp")
    padded_grad = jnp.concatenate([whole_grad, jnp.zeros((1, model_dim), jnp.bfloat16)], axis=0)
    send_grads = (slot_gate[:, None] * padded_grad[slot_token].astype(jnp.float32)).astype(
        jnp.bfloat16
    )
    expert_grads = to_experts(
        deliver(send_grads.reshape(sources, local_experts * capacity, model_dim)), local_experts
    )
    hidden_grad = jnp.einsum(
        "erd,efd->erf", expert_grads, expert_down_weight, preferred_element_type=jnp.float32
    )
    gate_lin_grad = (hidden_grad * up_lin * gate_sig * (1.0 + gate_lin * (1.0 - gate_sig))).astype(
        jnp.bfloat16
    )
    up_lin_grad = (hidden_grad * gate_act).astype(jnp.bfloat16)
    expert_down_grad = jnp.einsum(
        "erf,erd->efd", expert_hidden, expert_grads, preferred_element_type=jnp.float32
    )
    expert_gate_grad = jnp.einsum(
        "erd,erf->edf", expert_rows, gate_lin_grad, preferred_element_type=jnp.float32
    )
    expert_up_grad = jnp.einsum(
        "erd,erf->edf", expert_rows, up_lin_grad, preferred_element_type=jnp.float32
    )
    rows_grad = jnp.einsum(
        "erf,edf->erd", gate_lin_grad, expert_gate_weight, preferred_element_type=jnp.float32
    )
    rows_grad = rows_grad + jnp.einsum(
        "erf,edf->erd", up_lin_grad, expert_up_weight, preferred_element_type=jnp.float32
    )
    rows_grad_cols = lax.psum_scatter(
        rows_grad.reshape(-1, model_dim), "tp", scatter_dimension=1, tiled=True
    )
    returned_grad = collect(
        to_sources(
            rows_grad_cols.astype(jnp.bfloat16).reshape(local_experts, -1, col_width), sources
        )
    )
    back_grad = jnp.concatenate(
        [returned_grad.reshape(slot_rows, col_width), jnp.zeros((1, col_width), jnp.bfloat16)],
        axis=0,
    )
    routed_grad = jnp.sum(
        back_grad[target].astype(jnp.float32).reshape(tok_count, top_count, col_width), axis=1
    )
    shared_out_grad = (switch[:, None] * grad_full).astype(jnp.bfloat16)
    shared_hidden_grad = times_transpose(shared_out_grad, shared_down_weight)
    shared_gate_lin_grad = (
        shared_hidden_grad
        * shared_up_lin
        * shared_sig
        * (1.0 + shared_gate_lin * (1.0 - shared_sig))
    ).astype(jnp.bfloat16)
    shared_up_lin_grad = (shared_hidden_grad * shared_act).astype(jnp.bfloat16)
    shared_down_grad = inner_rows(shared_hidden, shared_out_grad)
    shared_gate_grad = inner_rows(normed_two, shared_gate_lin_grad)
    shared_up_grad = inner_rows(normed_two, shared_up_lin_grad)
    normed_grad = times_transpose(shared_gate_lin_grad, shared_gate_weight) + times_transpose(
        shared_up_lin_grad, shared_up_weight
    )
    normed_grad = normed_grad + lax.dynamic_update_slice_in_dim(
        jnp.zeros_like(normed_grad), routed_grad, col_start, 1
    )
    normed_grad = lax.psum(normed_grad, "tp")
    picked = (
        expert_ids[:, :, None] == jnp.arange(expert_total, dtype=jnp.int32)[None, None, :]
    ).astype(jnp.float32)
    probs_grad = jnp.sum(picked * gate_grad[:, :, None], axis=1)
    logit_grad = (
        router_probs * (probs_grad - jnp.sum(router_probs * probs_grad, axis=-1, keepdims=True))
    ).astype(jnp.bfloat16)
    router_grad = inner_rows(normed_two, logit_grad)
    switch_lin_grad = switch_grad * switch * (1.0 - switch)
    switch_vector_grad = jnp.dot(switch_lin_grad, normed_two, preferred_element_type=jnp.float32)
    normed_grad = normed_grad + times_transpose(logit_grad, router_weight)
    normed_grad = (
        normed_grad + switch_lin_grad[:, None] * switch_vector.astype(jnp.float32)[None, :]
    )
    second_gain_grad = jnp.sum(normed_grad * unit_two, axis=0)
    hidden_grad_one = grad_full + norm_back(normed_grad, unit_two, inv_two, second_gain)
    attended_grad = hidden_grad_one.astype(jnp.bfloat16)
    output_grad = inner_rows(context, attended_grad)
    context_grad = (
        times_transpose(attended_grad, output_weight)
        .astype(jnp.bfloat16)
        .reshape(tok_count, head_count, HD)
    )
    scores = attention_scores()
    attn_probs = jnp.exp(scores - log_total)
    probs_again = attn_probs.astype(jnp.bfloat16)
    probs_grad_att = jnp.einsum(
        "qhd,khd->hqk", context_grad, values_both, preferred_element_type=jnp.float32
    )
    values_both_grad = jnp.einsum(
        "hqk,qhd->khd", probs_again, context_grad, preferred_element_type=jnp.float32
    )
    scores_grad = (
        attn_probs * (probs_grad_att - jnp.sum(attn_probs * probs_grad_att, axis=-1, keepdims=True))
    ).astype(jnp.bfloat16)
    queries_grad = (
        jnp.einsum("hqk,khd->qhd", scores_grad, keys_both, preferred_element_type=jnp.float32)
        * score_scale
    )
    keys_both_grad = (
        jnp.einsum("hqk,qhd->khd", scores_grad, queries, preferred_element_type=jnp.float32)
        * score_scale
    )
    later_keys_grad, later_values_grad = passed_along(
        (keys_both_grad[:tok_count], values_both_grad[:tok_count]), "ep", -1
    )
    keep_later = jnp.where(has_earlier, 0.0, 1.0).astype(jnp.float32)
    keys_grad = keys_both_grad[tok_count:] + keep_later * later_keys_grad
    values_grad = values_both_grad[tok_count:] + keep_later * later_values_grad
    value_lin_grad = values_grad.reshape(tok_count, head_count * HD).astype(jnp.bfloat16)
    query_lin_grad = (
        rotate(queries_grad, cosine, -sine_part)
        .reshape(tok_count, head_count * HD)
        .astype(jnp.bfloat16)
    )
    key_lin_grad = (
        rotate(keys_grad, cosine, -sine_part)
        .reshape(tok_count, head_count * HD)
        .astype(jnp.bfloat16)
    )
    query_grad = inner_rows(normed_one, query_lin_grad)
    key_grad = inner_rows(normed_one, key_lin_grad)
    value_grad = inner_rows(normed_one, value_lin_grad)
    query_bias_grad = jnp.sum(query_lin_grad.astype(jnp.float32), axis=0).reshape(head_count, HD)
    key_bias_grad = jnp.sum(key_lin_grad.astype(jnp.float32), axis=0).reshape(head_count, HD)
    value_bias_grad = jnp.sum(value_lin_grad.astype(jnp.float32), axis=0).reshape(head_count, HD)
    normed_one_grad = times_transpose(query_lin_grad, query_weight) + times_transpose(
        key_lin_grad, key_weight
    )
    normed_one_grad = normed_one_grad + times_transpose(value_lin_grad, value_weight)
    normed_one_grad = lax.psum(normed_one_grad.astype(jnp.bfloat16), "tp").astype(jnp.float32)
    first_gain_grad = jnp.sum(normed_one_grad * unit_one, axis=0)
    input_grad = hidden_grad_one + norm_back(normed_one_grad, unit_one, inv_one, first_gain)
    tokens_grad = lax.dynamic_slice_in_dim(input_grad, col_start, col_width, 1).astype(jnp.bfloat16)
    reduced = (
        lax.psum_scatter(
            first_gain_grad.astype(jnp.bfloat16), "ep", scatter_dimension=0, tiled=True
        ).astype(jnp.float32),
        lax.psum_scatter(
            query_grad.astype(jnp.bfloat16), "ep", scatter_dimension=0, tiled=True
        ).astype(jnp.float32),
        lax.psum_scatter(
            key_grad.astype(jnp.bfloat16), "ep", scatter_dimension=0, tiled=True
        ).astype(jnp.float32),
        lax.psum_scatter(
            value_grad.astype(jnp.bfloat16), "ep", scatter_dimension=0, tiled=True
        ).astype(jnp.float32),
        lax.psum_scatter(
            query_bias_grad.astype(jnp.bfloat16), "ep", scatter_dimension=1, tiled=True
        ).astype(jnp.float32),
        lax.psum_scatter(
            key_bias_grad.astype(jnp.bfloat16), "ep", scatter_dimension=1, tiled=True
        ).astype(jnp.float32),
        lax.psum_scatter(
            value_bias_grad.astype(jnp.bfloat16), "ep", scatter_dimension=1, tiled=True
        ).astype(jnp.float32),
        lax.psum_scatter(
            output_grad.astype(jnp.bfloat16), "ep", scatter_dimension=1, tiled=True
        ).astype(jnp.float32),
        lax.psum_scatter(
            second_gain_grad.astype(jnp.bfloat16), "ep", scatter_dimension=0, tiled=True
        ).astype(jnp.float32),
        lax.psum_scatter(
            router_grad.astype(jnp.bfloat16), "ep", scatter_dimension=0, tiled=True
        ).astype(jnp.float32),
        lax.psum_scatter(
            shared_gate_grad.astype(jnp.bfloat16), "ep", scatter_dimension=0, tiled=True
        ).astype(jnp.float32),
        lax.psum_scatter(
            shared_up_grad.astype(jnp.bfloat16), "ep", scatter_dimension=0, tiled=True
        ).astype(jnp.float32),
        lax.psum_scatter(
            shared_down_grad.astype(jnp.bfloat16), "ep", scatter_dimension=1, tiled=True
        ).astype(jnp.float32),
        lax.psum_scatter(
            switch_vector_grad.astype(jnp.bfloat16), "ep", scatter_dimension=0, tiled=True
        ).astype(jnp.float32),
    )
    return (
        layer_out,
        tokens_grad,
        reduced[0],
        reduced[1],
        reduced[2],
        reduced[3],
        reduced[4],
        reduced[5],
        reduced[6],
        reduced[7],
        reduced[8],
        reduced[9],
        reduced[10],
        reduced[11],
        reduced[12],
        reduced[13],
        expert_gate_grad,
        expert_up_grad,
        expert_down_grad,
    )


MESH = pl.DeviceIdType.MESH
Z_ORDER = (0, 3, 1, 2)


def place():
    ep, tp = lax.axis_index("ep"), lax.axis_index("tp")
    return ep, tp, ep // 2, lax.rem(ep, 2), tp // 2, lax.rem(tp, 2)


def greet(always, along_z=False):
    barrier = pltpu.get_barrier_semaphore()
    for device in always:
        pl.semaphore_signal(barrier, inc=1, device_id=device, device_id_type=MESH)
    count = len(always)
    if along_z:
        ep, tp, z, _, _, _ = place()

        @pl.when(z < 3)
        def _():
            pl.semaphore_signal(barrier, inc=1, device_id=(ep + 2, tp), device_id_type=MESH)

        @pl.when(z > 0)
        def _():
            pl.semaphore_signal(barrier, inc=1, device_id=(ep - 2, tp), device_id_type=MESH)

        count = count + lax.min(z, 1) + lax.min(3 - z, 1)
    pl.semaphore_wait(barrier, count)


def remote(source, target, send_sem, recv_sem, device):
    return pltpu.make_async_remote_copy(
        src_ref=source,
        dst_ref=target,
        send_sem=send_sem,
        recv_sem=recv_sem,
        device_id=device,
        device_id_type=MESH,
    )


def add_blocks(target, sources, rows):
    step = 64

    def body(i, carry):
        span = pl.ds(pl.multiple_of(i * step, step), step)
        total = target[span, :].astype(jnp.float32)
        for source in sources:
            total = total + source[span, :].astype(jnp.float32)
        target[span, :] = total.astype(target.dtype)
        return carry

    lax.fori_loop(0, rows // step, body, 0)


def gather_tp_kernel(x_ref, o_ref, send_sem, recv_sem, own_sem):
    ep, tp, _, _, x, core = place()
    cols = x_ref.shape[1]
    sibling = (ep, tp + 1 - 2 * core)
    across = (ep, tp + 2 - 4 * x)
    greet([sibling, across])
    mine = o_ref.at[:, pl.ds(pl.multiple_of(tp * cols, cols), cols)]
    theirs = o_ref.at[:, pl.ds(pl.multiple_of((tp + 2 - 4 * x) * cols, cols), cols)]
    out_x = remote(x_ref, mine, send_sem.at[0], recv_sem.at[0], across)
    out_s = remote(x_ref, mine, send_sem.at[1], recv_sem.at[1], sibling)
    own = pltpu.make_async_copy(x_ref, mine, own_sem)
    out_x.start()
    out_s.start()
    own.start()
    remote(x_ref, theirs, send_sem.at[0], recv_sem.at[0], across).wait_recv()
    passing = remote(theirs, theirs, send_sem.at[2], recv_sem.at[2], sibling)
    passing.start()
    out_s.wait_recv()
    passing.wait_recv()
    own.wait()
    out_x.wait_send()
    out_s.wait_send()
    passing.wait_send()


def gather_tp(value, cid):
    rows, cols = value.shape
    return pl.pallas_call(
        gather_tp_kernel,
        out_shape=jax.ShapeDtypeStruct((rows, 4 * cols), value.dtype),
        in_specs=[pl.BlockSpec(memory_space=pl.ANY)],
        out_specs=pl.BlockSpec(memory_space=pl.ANY),
        scratch_shapes=[
            pltpu.SemaphoreType.DMA((3,)),
            pltpu.SemaphoreType.DMA((3,)),
            pltpu.SemaphoreType.DMA,
        ],
        compiler_params=pltpu.CompilerParams(collective_id=cid, has_side_effects=True),
        name="gather_tp",
    )(value)


def scatter_tp_kernel(p_ref, o_ref, mine, from_sib, from_x, own_sem, send_sem, recv_sem):
    ep, tp, _, _, x, core = place()
    rows, cols = o_ref.shape
    sibling = (ep, tp + 1 - 2 * core)
    across = (ep, tp + 2 - 4 * x)
    greet([sibling, across])

    def part(x_at, core_at):
        return p_ref.at[:, pl.ds(pl.multiple_of((x_at * 2 + core_at) * cols, cols), cols)]

    sends, owns = [], []
    for i, x_at in enumerate((1 - x, x)):
        owns.append(pltpu.make_async_copy(part(x_at, core), mine.at[i], own_sem.at[i]))
        sends.append(
            remote(part(x_at, 1 - core), from_sib.at[i], send_sem.at[i], recv_sem.at[i], sibling)
        )
        sends[-1].start()
        owns[-1].start()
    owns[0].wait()
    sends[0].wait_recv()
    add_blocks(mine.at[0], [from_sib.at[0]], rows)
    out_x = remote(mine.at[0], from_x, send_sem.at[2], recv_sem.at[2], across)
    out_x.start()
    owns[1].wait()
    sends[1].wait_recv()
    out_x.wait_recv()
    o_ref[...] = jnp.zeros_like(o_ref)
    add_blocks(o_ref, [mine.at[1], from_sib.at[1], from_x], rows)
    out_x.wait_send()
    sends[0].wait_send()
    sends[1].wait_send()


def scatter_tp(value, cid):
    rows, cols = value.shape[0], value.shape[1] // 4
    return pl.pallas_call(
        scatter_tp_kernel,
        out_shape=jax.ShapeDtypeStruct((rows, cols), jnp.float32),
        in_specs=[pl.BlockSpec(memory_space=pl.ANY)],
        out_specs=pl.BlockSpec(memory_space=pltpu.VMEM),
        scratch_shapes=[
            pltpu.VMEM((2, rows, cols), value.dtype),
            pltpu.VMEM((2, rows, cols), value.dtype),
            pltpu.VMEM((rows, cols), value.dtype),
            pltpu.SemaphoreType.DMA((2,)),
            pltpu.SemaphoreType.DMA((3,)),
            pltpu.SemaphoreType.DMA((3,)),
        ],
        compiler_params=pltpu.CompilerParams(
            collective_id=cid, has_side_effects=True, vmem_limit_bytes=32 * 2**20
        ),
        name="scatter_tp",
    )(value)


def lane_peers():
    ep, tp, z, y, x, core = place()
    to_y, to_x = 1 - 2 * y, 1 - 2 * x
    peer_a = (ep + (1 - core) * to_y, tp + core * 2 * to_x)
    peer_b = (ep + core * to_y, tp + (1 - core) * 2 * to_x)
    sibling = (ep, tp + 1 - 2 * core)
    above, below = (ep + 2, tp), (ep - 2, tp)
    return peer_a, peer_b, sibling, above, below


def lane_spot(z_at, da, db, core_at):
    _, _, _, y, x, _ = place()
    y_at = y + (1 - 2 * y) * ((1 - core_at) * da + core_at * db)
    x_at = x + (1 - 2 * x) * (core_at * da + (1 - core_at) * db)
    return z_at * 2 + y_at, x_at * 2 + core_at


def gather_all_kernel(x_ref, o_ref, up_sem, down_sem, a_sem, b_sem, s_sem, recv_sem, sib_sem, own_sem):
    ep, tp, z, y, x, core = place()
    rows, cols = x_ref.shape
    peer_a, peer_b, sibling, above, below = lane_peers()
    greet([peer_a, peer_b, sibling], True)

    def spot(z_at, da, db):
        group, quarter = lane_spot(z_at, da, db, core)
        return o_ref.at[
            pl.ds(pl.multiple_of(group * rows, rows), rows),
            pl.ds(pl.multiple_of(quarter * cols, cols), cols),
        ]

    def at(z_at, da, db):
        return z_at * 4 + da * 2 + db

    def arrived(z_at, da, db):
        block = spot(z_at, da, db)
        remote(block, block, s_sem.at[at(z_at, da, db)], recv_sem.at[at(z_at, da, db)], sibling).wait_recv()

    def up(z_at, source):
        return remote(source, spot(z_at, 0, 0), up_sem.at[z_at], recv_sem.at[at(z_at, 0, 0)], above)

    def down(z_at, source):
        return remote(source, spot(z_at, 0, 0), down_sem.at[z_at], recv_sem.at[at(z_at, 0, 0)], below)

    def over_a(z_at, source):
        return remote(source, spot(z_at, 0, 0), a_sem.at[z_at], recv_sem.at[at(z_at, 1, 0)], peer_a)

    def over_b(z_at, da, source):
        return remote(
            source, spot(z_at, da, 0), b_sem.at[z_at * 2 + da], recv_sem.at[at(z_at, da, 1)], peer_b
        )

    def to_sibling(z_at, da, db, source):
        n = at(z_at, da, db)
        return remote(source, spot(z_at, da, db), s_sem.at[n], sib_sem.at[n], sibling)

    own = pltpu.make_async_copy(x_ref, spot(z, 0, 0), own_sem)
    over_b(z, 0, x_ref).start()
    over_a(z, x_ref).start()

    @pl.when(z < 3)
    def _():
        up(z, x_ref).start()

    @pl.when(z > 0)
    def _():
        down(z, x_ref).start()

    to_sibling(z, 0, 0, x_ref).start()
    own.start()

    def from_a(z_at):
        arrived(z_at, 1, 0)
        block = spot(z_at, 1, 0)
        over_b(z_at, 1, block).start()
        to_sibling(z_at, 1, 0, block).start()

    def from_z(z_at, onward):
        arrived(z_at, 0, 0)
        block = spot(z_at, 0, 0)
        onward(block)
        over_a(z_at, block).start()
        over_b(z_at, 0, block).start()
        to_sibling(z_at, 0, 0, block).start()

    def from_below(z_at):
        def onward(block):
            @pl.when(z < 3)
            def _():
                up(z_at, block).start()

        from_z(z_at, onward)

    def from_above(z_at):
        def onward(block):
            @pl.when(z > 0)
            def _():
                down(z_at, block).start()

        from_z(z_at, onward)

    for d in range(1, 4):

        @pl.when(z >= d)
        def _(d=d):
            from_below(z - d)

        @pl.when(z + d <= 3)
        def _(d=d):
            from_above(z + d)

        if d == 1:
            from_a(z)
        else:

            @pl.when(z >= d - 1)
            def _(d=d):
                from_a(z - d + 1)

            @pl.when(z + d - 1 <= 3)
            def _(d=d):
                from_a(z + d - 1)

    @pl.when(z >= 3)
    def _():
        from_a(z - 3)

    @pl.when(z + 3 <= 3)
    def _():
        from_a(z + 3)

    def from_b(z_at, da):
        arrived(z_at, da, 1)
        to_sibling(z_at, da, 1, spot(z_at, da, 1)).start()

    for da in range(2):
        from_b(z, da)
    for d in range(1, 4):
        for da in range(2):

            @pl.when(z >= d)
            def _(d=d, da=da):
                from_b(z - d, da)

            @pl.when(z + d <= 3)
            def _(d=d, da=da):
                from_b(z + d, da)

    def finish_sibling(i, carry):
        block = spot(0, 0, 0)
        copy = remote(block, block, s_sem.at[i], sib_sem.at[i], sibling)
        copy.wait_recv()
        copy.wait_send()
        return carry

    lax.fori_loop(0, 16, finish_sibling, 0)

    def finish_links(i, carry):
        over_a(i, x_ref).wait_send()
        over_b(i, 0, x_ref).wait_send()
        over_b(i, 1, x_ref).wait_send()

        @pl.when((z < 3) & (i <= z))
        def _():
            up(i, x_ref).wait_send()

        @pl.when((z > 0) & (i >= z))
        def _():
            down(i, x_ref).wait_send()

        return carry

    lax.fori_loop(0, 4, finish_links, 0)
    own.wait()


def gather_all(value, cid):
    rows, cols = value.shape
    return pl.pallas_call(
        gather_all_kernel,
        out_shape=jax.ShapeDtypeStruct((8 * rows, 4 * cols), value.dtype),
        in_specs=[pl.BlockSpec(memory_space=pl.ANY)],
        out_specs=pl.BlockSpec(memory_space=pl.ANY),
        scratch_shapes=[
            pltpu.SemaphoreType.DMA((4,)),
            pltpu.SemaphoreType.DMA((4,)),
            pltpu.SemaphoreType.DMA((4,)),
            pltpu.SemaphoreType.DMA((8,)),
            pltpu.SemaphoreType.DMA((16,)),
            pltpu.SemaphoreType.DMA((16,)),
            pltpu.SemaphoreType.DMA((16,)),
            pltpu.SemaphoreType.DMA,
        ],
        compiler_params=pltpu.CompilerParams(collective_id=cid, has_side_effects=True),
        name="gather_all",
    )(value)


def z_chain(blocks, totals, from_below, from_above, up_send, up_recv, down_send, down_recv, rows, final):
    ep, tp, z, _, _, _ = place()
    above, below = (ep + 2, tp), (ep - 2, tp)

    def up(z_at):
        return remote(totals(z_at), from_below.at[z_at], up_send.at[z_at], up_recv.at[z_at], above)

    def down(z_at):
        return remote(totals(z_at), from_above.at[z_at], down_send.at[z_at], down_recv.at[z_at], below)

    for z_at in Z_ORDER:
        blocks(z_at)

        @pl.when(z_at > z)
        def _(z_at=z_at):
            @pl.when(z > 0)
            def _():
                up(z_at).wait_recv()
                add_blocks(totals(z_at), [from_below.at[z_at]], rows)

            up(z_at).start()

        @pl.when(z_at < z)
        def _(z_at=z_at):
            @pl.when(z < 3)
            def _():
                down(z_at).wait_recv()
                add_blocks(totals(z_at), [from_above.at[z_at]], rows)

            down(z_at).start()

    for z_at in range(4):

        @pl.when(z_at == z)
        def _(z_at=z_at):
            @pl.when(z > 0)
            def _():
                up(z_at).wait_recv()

            @pl.when(z < 3)
            def _():
                down(z_at).wait_recv()

            @pl.when(z == 0)
            def _():
                final(z_at, [from_above.at[z_at]])

            @pl.when(z == 3)
            def _():
                final(z_at, [from_below.at[z_at]])

            @pl.when((z > 0) & (z < 3))
            def _():
                final(z_at, [from_below.at[z_at], from_above.at[z_at]])

    for z_at in range(4):

        @pl.when(z_at > z)
        def _(z_at=z_at):
            up(z_at).wait_send()

        @pl.when(z_at < z)
        def _(z_at=z_at):
            down(z_at).wait_send()


def scatter_all_kernel(
    p_ref,
    o_ref,
    mine,
    from_sib,
    from_b,
    from_a,
    from_below,
    from_above,
    own_sem,
    s_send,
    s_recv,
    b_send,
    b_recv,
    a_send,
    a_recv,
    up_send,
    up_recv,
    down_send,
    down_recv,
):
    ep, tp, z, y, x, core = place()
    rows, cols = o_ref.shape
    peer_a, peer_b, sibling, above, below = lane_peers()
    greet([peer_a, peer_b, sibling], True)

    def part(z_at, da, db, core_at):
        group, quarter = lane_spot(z_at, da, db, core_at)
        return p_ref.at[
            pl.ds(pl.multiple_of(group * rows, rows), rows),
            pl.ds(pl.multiple_of(quarter * cols, cols), cols),
        ]

    def at(z_at, da, db):
        return z_at * 4 + da * 2 + db

    def own(z_at, da, db):
        n = at(z_at, da, db)
        return pltpu.make_async_copy(part(z_at, da, db, core), mine.at[n], own_sem.at[n])

    def to_sibling(z_at, da, db):
        n = at(z_at, da, db)
        return remote(
            part(z_at, da, db, 1 - core), from_sib.at[n], s_send.at[n], s_recv.at[n], sibling
        )

    for da, db in ((1, 1), (0, 1), (1, 0), (0, 0)):
        for z_at in Z_ORDER:
            to_sibling(z_at, da, db).start()
            own(z_at, da, db).start()

    def here(z_at, da, db):
        own(z_at, da, db).wait()
        to_sibling(z_at, da, db).wait_recv()
        return mine.at[at(z_at, da, db)], from_sib.at[at(z_at, da, db)]

    def over_b(z_at, da):
        n = z_at * 2 + da
        return remote(mine.at[at(z_at, da, 1)], from_b.at[n], b_send.at[n], b_recv.at[n], peer_b)

    def over_a(z_at):
        return remote(mine.at[at(z_at, 1, 0)], from_a.at[z_at], a_send.at[z_at], a_recv.at[z_at], peer_a)

    for da in (1, 0):
        for z_at in Z_ORDER:
            own_part, sib_part = here(z_at, da, 1)
            add_blocks(own_part, [sib_part], rows)
            over_b(z_at, da).start()
    for z_at in Z_ORDER:
        own_part, sib_part = here(z_at, 1, 0)
        over_b(z_at, 1).wait_recv()
        add_blocks(own_part, [sib_part, from_b.at[z_at * 2 + 1]], rows)
        over_a(z_at).start()

    def blocks(z_at):
        own_part, sib_part = here(z_at, 0, 0)
        over_b(z_at, 0).wait_recv()
        over_a(z_at).wait_recv()
        add_blocks(own_part, [sib_part, from_b.at[z_at * 2], from_a.at[z_at]], rows)

    def final(z_at, others):
        o_ref[...] = jnp.zeros_like(o_ref)
        add_blocks(o_ref, [mine.at[at(z_at, 0, 0)], *others], rows)

    z_chain(
        blocks,
        lambda z_at: mine.at[at(z_at, 0, 0)],
        from_below,
        from_above,
        up_send,
        up_recv,
        down_send,
        down_recv,
        rows,
        final,
    )
    for z_at in range(4):
        over_a(z_at).wait_send()
        for da in range(2):
            over_b(z_at, da).wait_send()
            for db in range(2):
                to_sibling(z_at, da, db).wait_send()


def scatter_all(value, cid):
    rows, cols = value.shape[0] // 8, value.shape[1] // 4
    dma = pltpu.SemaphoreType.DMA

    def held(count):
        return pltpu.VMEM((count, rows, cols), value.dtype)

    return pl.pallas_call(
        scatter_all_kernel,
        out_shape=jax.ShapeDtypeStruct((rows, cols), jnp.float32),
        in_specs=[pl.BlockSpec(memory_space=pl.ANY)],
        out_specs=pl.BlockSpec(memory_space=pltpu.VMEM),
        scratch_shapes=[held(16), held(16), held(8), held(4), held(4), held(4)]
        + [dma((16,)), dma((16,)), dma((16,)), dma((8,)), dma((8,))]
        + [dma((4,))] * 6,
        compiler_params=pltpu.CompilerParams(
            collective_id=cid, has_side_effects=True, vmem_limit_bytes=48 * 2**20
        ),
        name="scatter_all",
    )(value)


def scatter_ep_kernel(
    p_ref, o_ref, mine, from_y, from_below, from_above, own_sem, y_send, y_recv, up_send, up_recv, down_send, down_recv
):
    ep, tp, z, y, _, _ = place()
    rows, cols = o_ref.shape
    across = (ep + 1 - 2 * y, tp)
    above, below = (ep + 2, tp), (ep - 2, tp)
    greet([across], True)

    def part(z_at, y_at):
        return p_ref.at[pl.ds(pl.multiple_of((z_at * 2 + y_at) * rows, rows), rows), :]

    def own(z_at):
        return pltpu.make_async_copy(part(z_at, y), mine.at[z_at], own_sem.at[z_at])

    def over_y(z_at):
        return remote(part(z_at, 1 - y), from_y.at[z_at], y_send.at[z_at], y_recv.at[z_at], across)

    for z_at in Z_ORDER:
        over_y(z_at).start()
        own(z_at).start()

    def blocks(z_at):
        own(z_at).wait()
        over_y(z_at).wait_recv()
        add_blocks(mine.at[z_at], [from_y.at[z_at]], rows)

    def final(z_at, others):
        o_ref[...] = jnp.zeros_like(o_ref)
        add_blocks(o_ref, [mine.at[z_at], *others], rows)

    z_chain(
        blocks,
        lambda z_at: mine.at[z_at],
        from_below,
        from_above,
        up_send,
        up_recv,
        down_send,
        down_recv,
        rows,
        final,
    )
    for z_at in range(4):
        over_y(z_at).wait_send()


def scatter_ep(value, cid):
    rows, cols = value.shape[0] // 8, value.shape[1]
    dma = pltpu.SemaphoreType.DMA

    def held():
        return pltpu.VMEM((4, rows, cols), value.dtype)

    return pl.pallas_call(
        scatter_ep_kernel,
        out_shape=jax.ShapeDtypeStruct((rows, cols), jnp.float32),
        in_specs=[pl.BlockSpec(memory_space=pl.ANY)],
        out_specs=pl.BlockSpec(memory_space=pltpu.VMEM),
        scratch_shapes=[held(), held(), held(), held()] + [dma((4,))] * 7,
        compiler_params=pltpu.CompilerParams(
            collective_id=cid, has_side_effects=True, vmem_limit_bytes=40 * 2**20
        ),
        name="scatter_ep",
    )(value)


def tp_total(value):
    return lax.psum(value, "tp")


def kept_choice(expert_ids, pair_order, expert_total, capacity):
    tok_count, top_count = expert_ids.shape
    pair_count = tok_count * top_count
    order = pair_order.reshape(-1)
    pairs = jnp.arange(pair_count, dtype=jnp.int32)
    turn = jnp.sum(jnp.where(order[None, :] == pairs[:, None], pairs[None, :], 0), axis=1)
    turn = turn.reshape(tok_count, top_count)
    picked = expert_ids[:, :, None] == jnp.arange(expert_total, dtype=jnp.int32)[None, None, :]
    turn_of = jnp.sum(jnp.where(picked, turn[:, :, None], 0), axis=1)
    named = jnp.any(picked, axis=1)
    turn_of = jnp.where(named, turn_of, pair_count)
    slot = jnp.sum((turn_of[None, :, :] < turn_of[:, None, :]).astype(jnp.int32), axis=1)
    return (named & (slot < capacity)).astype(jnp.float32)


def dense_plan(
    tokens,
    out_grad,
    first_gain,
    query_weight,
    key_weight,
    value_weight,
    query_bias,
    key_bias,
    value_bias,
    output_weight,
    second_gain,
    router_weight,
    shared_gate_weight,
    shared_up_weight,
    shared_down_weight,
    switch_vector,
    expert_gate_weight,
    expert_up_weight,
    expert_down_weight,
    expert_ids,
    pair_order,
):
    ep, tp = lax.axis_index("ep"), lax.axis_index("tp")
    tok_count, col_width = tokens.shape
    model_dim = query_weight.shape[0]
    sources = lax.axis_size("ep")
    place_in_seq = ep % SPAN
    has_earlier = place_in_seq > 0
    expert_total = router_weight.shape[1]
    capacity = 9 * tok_count * expert_ids.shape[1] // (8 * expert_total)
    head_count = query_weight.shape[1] // HD
    score_scale = HD ** (-0.5)
    expert_width = expert_gate_weight.shape[2]
    shared_width = shared_gate_weight.shape[1] // sources
    width = expert_width + shared_width

    def own_cols(vector):
        return lax.dynamic_slice_in_dim(vector, tp * col_width, col_width, vector.ndim - 1)

    grads_all = lax.all_gather(
        lax.all_gather(out_grad, "ep", axis=0, tiled=True), "tp", axis=1, tiled=True
    )
    kept_own = kept_choice(expert_ids, pair_order, expert_total, capacity)
    kept_all = lax.all_gather(kept_own, "ep", axis=0, tiled=True)

    inputs_full = gather_tp(tokens, 0).astype(jnp.float32)
    unit_one, inv_one = row_stats(inputs_full)
    normed_one = (unit_one * first_gain).astype(jnp.bfloat16)
    query_lin = jnp.dot(normed_one, query_weight, preferred_element_type=jnp.float32) + query_bias
    key_lin = jnp.dot(normed_one, key_weight, preferred_element_type=jnp.float32) + key_bias
    value_lin = jnp.dot(normed_one, value_weight, preferred_element_type=jnp.float32) + value_bias
    cosine, sine_part = rope_tables(tok_count, HD, place_in_seq * tok_count)
    queries = rotate(query_lin.reshape(tok_count, head_count, HD), cosine, sine_part).astype(
        jnp.bfloat16
    )
    keys_rot = rotate(key_lin.reshape(tok_count, head_count, HD), cosine, sine_part).astype(
        jnp.bfloat16
    )
    values_all = value_lin.reshape(tok_count, head_count, HD).astype(jnp.bfloat16)
    earlier_keys, earlier_values = passed_along((keys_rot, values_all), "ep", 1)
    keys_both = jnp.concatenate([earlier_keys, keys_rot], axis=0)
    values_both = jnp.concatenate([earlier_values, values_all], axis=0)
    blocks = jnp.arange(tok_count) // BLOCK
    local_allowed = blocks[None, :] <= blocks[:, None]
    remote_allowed = jnp.broadcast_to(has_earlier, (tok_count, tok_count))
    allowed = jnp.concatenate([remote_allowed, local_allowed], axis=1)[None]

    def attention_scores():
        scored = (
            jnp.einsum("qhd,khd->hqk", queries, keys_both, preferred_element_type=jnp.float32)
            * score_scale
        )
        return jnp.where(allowed, scored, masked_score)

    scores = attention_scores()
    row_max = jnp.max(scores, axis=-1, keepdims=True)
    powers = jnp.exp(scores - row_max)
    totals = jnp.sum(powers, axis=-1, keepdims=True)
    log_total = row_max + jnp.log(totals)
    probs_low = (powers / totals).astype(jnp.bfloat16)
    context = jnp.einsum("hqk,khd->qhd", probs_low, values_both, preferred_element_type=jnp.float32)
    context = context.reshape(tok_count, head_count * HD).astype(jnp.bfloat16)
    attn_part = jnp.dot(context, output_weight, preferred_element_type=jnp.float32)
    attended = scatter_tp(attn_part.astype(jnp.bfloat16), 1)

    hidden_cols = tokens.astype(jnp.float32) + attended
    squares = tp_total(jnp.sum(hidden_cols * hidden_cols, axis=-1, keepdims=True))
    inv_two = lax.rsqrt(squares / model_dim + norm_eps)
    unit_two = hidden_cols * inv_two
    second_cols = own_cols(second_gain)
    normed_cols = (unit_two * second_cols).astype(jnp.bfloat16)
    normed_all = gather_all(normed_cols, 2)

    def hidden_rows(expert_part, shared_part):
        cut = lax.dynamic_slice_in_dim(shared_part, ep * shared_width, shared_width, 1)
        return jnp.concatenate([expert_part[0].T, cut.T], axis=0)

    gate_rows = hidden_rows(expert_gate_weight, shared_gate_weight)
    up_rows = hidden_rows(expert_up_weight, shared_up_weight)
    down_rows = jnp.concatenate(
        [
            expert_down_weight[0],
            lax.dynamic_slice_in_dim(shared_down_weight, ep * shared_width, shared_width, 0),
        ],
        axis=0,
    )
    both_rows = jnp.concatenate([gate_rows, up_rows], axis=0)
    rows_in = jnp.concatenate([both_rows, router_weight.T, switch_vector[None, :]], axis=0)
    lin_all = times_transpose(normed_all, rows_in)
    gate_lin = lin_all[:, :width]
    up_lin = lin_all[:, width : 2 * width]
    logits = lin_all[:, 2 * width : 2 * width + expert_total]
    router_probs = softmax_rows(logits)
    gates_all = jnp.sum(
        jnp.where(jnp.arange(expert_total)[None, :] == ep, router_probs * kept_all, 0.0),
        axis=1,
        keepdims=True,
    )
    switch_all = jax.nn.sigmoid(lin_all[:, 2 * width + expert_total :])
    is_expert = jnp.arange(width)[None, :] < expert_width
    scale = jnp.where(is_expert, gates_all, switch_all)
    hidden_grad = times_transpose(grads_all, down_rows)
    gate_sig = jax.nn.sigmoid(gate_lin)
    gate_act = gate_lin * gate_sig
    hidden = gate_act * up_lin
    agreement = hidden * hidden_grad
    gate_part = jnp.sum(jnp.where(is_expert, agreement, 0.0), axis=1)
    switch_part = jnp.sum(jnp.where(is_expert, 0.0, agreement), axis=1)
    scaled_hidden = (hidden * scale).astype(jnp.bfloat16)
    scaled_grad = hidden_grad * scale
    gate_lin_grad = (scaled_grad * up_lin * gate_sig * (1.0 + gate_lin * (1.0 - gate_sig))).astype(
        jnp.bfloat16
    )
    up_lin_grad = (scaled_grad * gate_act).astype(jnp.bfloat16)
    both_grad = jnp.concatenate([gate_lin_grad, up_lin_grad], axis=1)
    normed_grad_part = jnp.dot(both_grad, both_rows, preferred_element_type=jnp.float32)
    normed_grad = scatter_all(normed_grad_part.astype(jnp.bfloat16), 3)
    out_part = jnp.dot(scaled_hidden, down_rows, preferred_element_type=jnp.float32)
    ffn_cols = scatter_all(out_part.astype(jnp.bfloat16), 3)
    layer_out = (hidden_cols + ffn_cols).astype(jnp.bfloat16)
    down_grad = inner_rows(scaled_hidden, grads_all)
    both_rows_grad = inner_rows(both_grad, normed_all)
    expert_down_grad = down_grad[None, :expert_width]
    expert_gate_grad = both_rows_grad[:expert_width].T[None]
    expert_up_grad = both_rows_grad[width : width + expert_width].T[None]
    shared_parts = jnp.stack(
        [
            both_rows_grad[expert_width:width],
            both_rows_grad[width + expert_width :],
            down_grad[expert_width:],
        ]
    ).astype(jnp.bfloat16)
    shared_parts = shared_parts.reshape(3, shared_width, sources, -1).transpose(2, 0, 1, 3)
    shared_parts = lax.all_to_all(shared_parts, "ep", split_axis=0, concat_axis=0, tiled=True)
    shared_parts = shared_parts.transpose(1, 0, 2, 3).reshape(3, sources * shared_width, -1)
    shared_parts = shared_parts.astype(jnp.float32)
    shared_gate_grad = shared_parts[0].T
    shared_up_grad = shared_parts[1].T
    shared_down_grad = shared_parts[2]

    scalar_parts = jnp.stack([gate_part, switch_part]).reshape(2, sources, tok_count).swapaxes(0, 1)
    scalar_parts = lax.all_to_all(scalar_parts, "ep", split_axis=0, concat_axis=0, tiled=True)
    scalar_sums = tp_total(
        jnp.concatenate([scalar_parts[:, 0], jnp.sum(scalar_parts[:, 1], axis=0)[None]], axis=0)
    )
    probs_grad = scalar_sums[:sources].T * kept_own
    switch_grad = scalar_sums[sources]
    own_rows = lax.dynamic_slice_in_dim(lin_all, ep * tok_count, tok_count, 0)
    probs_own = softmax_rows(own_rows[:, 2 * width : 2 * width + expert_total])
    switch = jax.nn.sigmoid(own_rows[:, 2 * width + expert_total])
    logit_grad = (
        probs_own * (probs_grad - jnp.sum(probs_own * probs_grad, axis=-1, keepdims=True))
    ).astype(jnp.bfloat16)
    router_grad = inner_rows(normed_cols, logit_grad)
    switch_lin_grad = switch_grad * switch * (1.0 - switch)
    switch_vector_grad = jnp.dot(switch_lin_grad, normed_cols, preferred_element_type=jnp.float32)
    router_cols = lax.dynamic_slice_in_dim(router_weight, tp * col_width, col_width, 0)
    normed_grad = normed_grad + times_transpose(logit_grad, router_cols)
    normed_grad = (
        normed_grad
        + switch_lin_grad[:, None] * own_cols(switch_vector).astype(jnp.float32)[None, :]
    )
    second_gain_grad = jnp.sum(normed_grad * unit_two, axis=0)
    scaled_two = normed_grad * second_cols
    mean_two = tp_total(jnp.sum(scaled_two * unit_two, axis=-1, keepdims=True)) / model_dim
    hidden_grad_cols = out_grad.astype(jnp.float32) + inv_two * (scaled_two - unit_two * mean_two)

    attended_grad = gather_tp(hidden_grad_cols.astype(jnp.bfloat16), 0)
    output_grad = inner_rows(attended_grad, context)
    output_grad = lax.psum_scatter(
        output_grad.astype(jnp.bfloat16), "ep", scatter_dimension=0, tiled=True
    )
    output_grad = output_grad.astype(jnp.float32).T
    context_grad = (
        times_transpose(attended_grad, output_weight)
        .astype(jnp.bfloat16)
        .reshape(tok_count, head_count, HD)
    )
    scores = attention_scores()
    attn_probs = jnp.exp(scores - log_total)
    probs_again = attn_probs.astype(jnp.bfloat16)
    probs_grad_att = jnp.einsum(
        "qhd,khd->hqk", context_grad, values_both, preferred_element_type=jnp.float32
    )
    values_both_grad = jnp.einsum(
        "hqk,qhd->khd", probs_again, context_grad, preferred_element_type=jnp.float32
    )
    scores_grad = (
        attn_probs * (probs_grad_att - jnp.sum(attn_probs * probs_grad_att, axis=-1, keepdims=True))
    ).astype(jnp.bfloat16)
    queries_grad = (
        jnp.einsum("hqk,khd->qhd", scores_grad, keys_both, preferred_element_type=jnp.float32)
        * score_scale
    )
    keys_both_grad = (
        jnp.einsum("hqk,qhd->khd", scores_grad, queries, preferred_element_type=jnp.float32)
        * score_scale
    )
    later_keys_grad, later_values_grad = passed_along(
        (
            keys_both_grad[:tok_count].astype(jnp.bfloat16),
            values_both_grad[:tok_count].astype(jnp.bfloat16),
        ),
        "ep",
        -1,
    )
    keep_later = jnp.where(has_earlier, 0.0, 1.0).astype(jnp.float32)
    keys_grad = keys_both_grad[tok_count:] + keep_later * later_keys_grad
    values_grad = values_both_grad[tok_count:] + keep_later * later_values_grad
    value_lin_grad = values_grad.reshape(tok_count, head_count * HD).astype(jnp.bfloat16)
    query_lin_grad = (
        rotate(queries_grad, cosine, -sine_part)
        .reshape(tok_count, head_count * HD)
        .astype(jnp.bfloat16)
    )
    key_lin_grad = (
        rotate(keys_grad, cosine, -sine_part)
        .reshape(tok_count, head_count * HD)
        .astype(jnp.bfloat16)
    )
    lin_grads = jnp.concatenate([query_lin_grad, key_lin_grad, value_lin_grad], axis=1)
    weight_grads = scatter_ep(inner_rows(normed_one, lin_grads).astype(jnp.bfloat16), 5)
    lin_width = head_count * HD
    normed_one_grad = times_transpose(query_lin_grad, query_weight) + times_transpose(
        key_lin_grad, key_weight
    )
    normed_one_grad = normed_one_grad + times_transpose(value_lin_grad, value_weight)
    normed_one_cols = scatter_tp(normed_one_grad.astype(jnp.bfloat16), 1)
    unit_cols = tokens.astype(jnp.float32) * inv_one
    first_cols = own_cols(first_gain)
    first_gain_grad = jnp.sum(normed_one_cols * unit_cols, axis=0)
    scaled_one = normed_one_cols * first_cols
    mean_one = tp_total(jnp.sum(scaled_one * unit_cols, axis=-1, keepdims=True)) / model_dim
    tokens_grad = (hidden_grad_cols + inv_one * (scaled_one - unit_cols * mean_one)).astype(
        jnp.bfloat16
    )
    bias_grad = jnp.sum(lin_grads.astype(jnp.float32), axis=0)

    by_cols = jnp.concatenate(
        [first_gain_grad[None], second_gain_grad[None], switch_vector_grad[None], router_grad.T],
        axis=0,
    )
    small = lax.psum(jnp.concatenate([by_cols, bias_grad.reshape(3, -1)], axis=0), "ep")
    spread = lax.all_gather(small[: 3 + expert_total], "tp", axis=1, tiled=True)
    share = model_dim // sources
    spread = lax.dynamic_slice_in_dim(spread, ep * share, share, 1)
    bias_width = HD // sources
    bias_sums = lax.dynamic_slice_in_dim(
        small[3 + expert_total :].reshape(3, head_count, HD), ep * bias_width, bias_width, 2
    )
    return (
        layer_out,
        tokens_grad,
        spread[0],
        weight_grads[:, :lin_width],
        weight_grads[:, lin_width : 2 * lin_width],
        weight_grads[:, 2 * lin_width :],
        bias_sums[0],
        bias_sums[1],
        bias_sums[2],
        output_grad,
        spread[1],
        spread[3:].T,
        shared_gate_grad,
        shared_up_grad,
        shared_down_grad,
        spread[2],
        expert_gate_grad,
        expert_up_grad,
        expert_down_grad,
    )


def solution(mesh):
    plan = dense_plan if dict(mesh.shape) == {"ep": 8, "tp": 4} else slot_plan
    return jax.shard_map(
        plan,
        mesh=mesh,
        in_specs=(
            P("ep", "tp"),
            P("ep", "tp"),
            P(),
            P(None, "tp"),
            P(None, "tp"),
            P(None, "tp"),
            P("tp"),
            P("tp"),
            P("tp"),
            P("tp", None),
            P(),
            P(),
            P(None, "tp"),
            P(None, "tp"),
            P("tp", None),
            P(),
            P("ep", None, "tp"),
            P("ep", None, "tp"),
            P("ep", "tp", None),
            P("ep", None),
            P("ep", None),
        ),
        out_specs=(
            P("ep", "tp"),
            P("ep", "tp"),
            P("ep"),
            P("ep", "tp"),
            P("ep", "tp"),
            P("ep", "tp"),
            P("tp", "ep"),
            P("tp", "ep"),
            P("tp", "ep"),
            P("tp", "ep"),
            P("ep"),
            P("ep", None),
            P("ep", "tp"),
            P("ep", "tp"),
            P("tp", "ep"),
            P("ep"),
            P("ep", None, "tp"),
            P("ep", None, "tp"),
            P("ep", "tp", None),
        ),
        check_vma=False,
    )
```

```python
import functools
import math

import jax
import jax.numpy as jnp
from jax import lax
from jax.experimental import pallas as pl
from jax.experimental.pallas import tpu as pltpu
from jax.sharding import PartitionSpec as P

HD = 128
BLOCK = 256
SPAN = 2


rope_theta = 1000000.0
norm_eps = 1e-06
masked_score = -1e30


def passed_along(value, axis, steps):
    count = lax.axis_size(axis)
    leading, last = (max(0, -steps), min(count, count - steps))
    return lax.ppermute(value, axis, [(source, source + steps) for source in range(leading, last)])


def rope_tables(row_count, head_dim, first_position):
    positions = jnp.arange(row_count, dtype=jnp.float32) + first_position.astype(jnp.float32)
    frequency = jnp.exp(
        jnp.arange(head_dim // 2, dtype=jnp.float32) * (-2.0 * math.log(rope_theta) / head_dim)
    )
    angles = positions[:, None] * frequency[None, :]
    return (jnp.cos(angles)[:, None, :], jnp.sin(angles)[:, None, :])


def rotate(values, cosine, sine_part):
    half_dim = values.shape[-1] // 2
    first_half = values[..., :half_dim]
    second_half = values[..., half_dim:]
    return jnp.concatenate(
        [
            first_half * cosine - second_half * sine_part,
            second_half * cosine + first_half * sine_part,
        ],
        axis=-1,
    )


def inner_rows(left_side, right_side):
    return lax.dot_general(
        left_side, right_side, (((0,), (0,)), ((), ())), preferred_element_type=jnp.float32
    )


def times_transpose(left_side, right_side):
    return lax.dot_general(
        left_side, right_side, (((1,), (1,)), ((), ())), preferred_element_type=jnp.float32
    )


def row_stats(values):
    inv_rms = lax.rsqrt(jnp.mean(values * values, axis=-1, keepdims=True) + norm_eps)
    return (values * inv_rms, inv_rms)


def norm_back(grad_rows, unit_rows, inv_rms, gain_vec):
    scaled = grad_rows * gain_vec
    return inv_rms * (scaled - unit_rows * jnp.mean(scaled * unit_rows, axis=-1, keepdims=True))


def softmax_rows(scores):
    row_max = jnp.max(scores, axis=-1, keepdims=True)
    powers = jnp.exp(scores - row_max)
    return powers / jnp.sum(powers, axis=-1, keepdims=True)


def to_experts(block_rows, local_count):
    sources, span_rows, col_count = block_rows.shape
    slot_count = span_rows // local_count
    shaped = block_rows.reshape(sources, local_count, slot_count, col_count)
    return shaped.swapaxes(0, 1).reshape(local_count, sources * slot_count, col_count)


def to_sources(block_rows, sources):
    local_count, rows_all, col_count = block_rows.shape
    slot_count = rows_all // sources
    shaped = block_rows.reshape(local_count, sources, slot_count, col_count)
    return shaped.swapaxes(0, 1).reshape(sources, local_count * slot_count, col_count)


def deliver(block_rows):
    arrived = lax.all_to_all(block_rows, "ep", split_axis=0, concat_axis=0, tiled=True)
    return arrived


def collect(block_rows):
    return lax.all_to_all(block_rows, "ep", split_axis=0, concat_axis=0, tiled=True)


def slot_plan(
    tokens,
    out_grad,
    first_gain,
    query_weight,
    key_weight,
    value_weight,
    query_bias,
    key_bias,
    value_bias,
    output_weight,
    second_gain,
    router_weight,
    shared_gate_weight,
    shared_up_weight,
    shared_down_weight,
    switch_vector,
    expert_gate_weight,
    expert_up_weight,
    expert_down_weight,
    expert_ids,
    pair_order,
):
    whole_in, whole_grad = (
        lax.all_gather(tokens, "tp", axis=1, tiled=True),
        lax.all_gather(out_grad, "tp", axis=1, tiled=True),
    )
    tok_count = whole_in.shape[0]
    model_dim = whole_in.shape[1]
    col_width = tokens.shape[1]
    col_start = lax.axis_index("tp") * col_width
    sources = lax.axis_size("ep")
    place_in_seq = lax.axis_index("ep") % SPAN
    has_earlier = place_in_seq > 0
    local_experts = expert_gate_weight.shape[0]
    expert_total = router_weight.shape[1]
    top_count = expert_ids.shape[1]
    pair_count = tok_count * top_count
    capacity = 9 * pair_count // (8 * expert_total)
    head_count = query_weight.shape[1] // HD
    score_scale = HD ** (-0.5)
    inputs_full = whole_in.astype(jnp.float32)
    unit_one, inv_one = row_stats(inputs_full)
    normed_one = (unit_one * first_gain).astype(jnp.bfloat16)
    query_lin = jnp.dot(normed_one, query_weight, preferred_element_type=jnp.float32) + query_bias
    key_lin = jnp.dot(normed_one, key_weight, preferred_element_type=jnp.float32) + key_bias
    value_lin = jnp.dot(normed_one, value_weight, preferred_element_type=jnp.float32) + value_bias
    cosine, sine_part = rope_tables(tok_count, HD, place_in_seq * tok_count)
    queries = rotate(query_lin.reshape(tok_count, head_count, HD), cosine, sine_part).astype(
        jnp.bfloat16
    )
    keys_rot = rotate(key_lin.reshape(tok_count, head_count, HD), cosine, sine_part).astype(
        jnp.bfloat16
    )
    values_all = value_lin.reshape(tok_count, head_count, HD).astype(jnp.bfloat16)
    earlier_keys, earlier_values = passed_along((keys_rot, values_all), "ep", 1)
    keys_both = jnp.concatenate([earlier_keys, keys_rot], axis=0)
    values_both = jnp.concatenate([earlier_values, values_all], axis=0)
    blocks = jnp.arange(tok_count) // BLOCK
    local_allowed = blocks[None, :] <= blocks[:, None]
    remote_allowed = jnp.broadcast_to(has_earlier, (tok_count, tok_count))
    allowed = jnp.concatenate([remote_allowed, local_allowed], axis=1)[None]

    def attention_scores():
        scored = (
            jnp.einsum("qhd,khd->hqk", queries, keys_both, preferred_element_type=jnp.float32)
            * score_scale
        )
        return jnp.where(allowed, scored, masked_score)

    scores = attention_scores()
    row_max = jnp.max(scores, axis=-1, keepdims=True)
    powers = jnp.exp(scores - row_max)
    totals = jnp.sum(powers, axis=-1, keepdims=True)
    log_total = row_max + jnp.log(totals)
    probs_low = (powers / totals).astype(jnp.bfloat16)
    context = jnp.einsum("hqk,khd->qhd", probs_low, values_both, preferred_element_type=jnp.float32)
    context = context.reshape(tok_count, head_count * HD).astype(jnp.bfloat16)
    attn_part = jnp.dot(context, output_weight, preferred_element_type=jnp.float32)
    attended = lax.psum(attn_part, "tp")
    hidden_one = inputs_full + attended
    unit_two, inv_two = row_stats(hidden_one)
    normed_two = (unit_two * second_gain).astype(jnp.bfloat16)
    logits = jnp.dot(normed_two, router_weight, preferred_element_type=jnp.float32)
    router_probs = softmax_rows(logits)
    gate_values = jnp.take_along_axis(router_probs, expert_ids, axis=1)
    switch = jax.nn.sigmoid(jnp.dot(normed_two, switch_vector, preferred_element_type=jnp.float32))
    flat_ids = expert_ids.reshape(-1)
    turn_order = pair_order.reshape(-1)
    in_turn = flat_ids[turn_order]
    onehot = (in_turn[:, None] == jnp.arange(expert_total, dtype=jnp.int32)[None, :]).astype(
        jnp.int32
    )
    earlier = jnp.cumsum(onehot, axis=0) - onehot
    turn_slot = jnp.sum(earlier * onehot, axis=1)
    slot_index = jnp.zeros((pair_count,), jnp.int32).at[turn_order].set(turn_slot)
    kept_pair = slot_index < capacity
    slot_rows = expert_total * capacity
    target = jnp.where(kept_pair, flat_ids * capacity + slot_index, slot_rows)
    pair_token = jnp.arange(pair_count, dtype=jnp.int32) // top_count
    slot_token = (
        jnp.full((slot_rows + 1,), tok_count, jnp.int32).at[target].set(pair_token)[:slot_rows]
    )
    slot_gate = (
        jnp.zeros((slot_rows + 1,), jnp.float32).at[target].set(gate_values.reshape(-1))[:slot_rows]
    )
    padded_two = jnp.concatenate([normed_two, jnp.zeros((1, model_dim), jnp.bfloat16)], axis=0)
    send_rows = padded_two[slot_token].reshape(sources, local_experts * capacity, model_dim)
    expert_rows = to_experts(deliver(send_rows), local_experts)
    gate_lin = jnp.einsum(
        "erd,edf->erf", expert_rows, expert_gate_weight, preferred_element_type=jnp.float32
    )
    up_lin = jnp.einsum(
        "erd,edf->erf", expert_rows, expert_up_weight, preferred_element_type=jnp.float32
    )
    gate_sig = jax.nn.sigmoid(gate_lin)
    gate_act = gate_lin * gate_sig
    expert_hidden = (gate_act * up_lin).astype(jnp.bfloat16)
    expert_part = jnp.einsum(
        "erf,efd->erd", expert_hidden, expert_down_weight, preferred_element_type=jnp.float32
    )
    shared_gate_lin = jnp.dot(normed_two, shared_gate_weight, preferred_element_type=jnp.float32)
    shared_up_lin = jnp.dot(normed_two, shared_up_weight, preferred_element_type=jnp.float32)
    shared_sig = jax.nn.sigmoid(shared_gate_lin)
    shared_act = shared_gate_lin * shared_sig
    shared_hidden = (shared_act * shared_up_lin).astype(jnp.bfloat16)
    shared_part = jnp.dot(shared_hidden, shared_down_weight, preferred_element_type=jnp.float32)
    expert_cols, shared_cols = (
        lax.psum_scatter(expert_part.reshape(-1, model_dim), "tp", scatter_dimension=1, tiled=True),
        lax.psum_scatter(shared_part, "tp", scatter_dimension=1, tiled=True),
    )
    returned = collect(
        to_sources(expert_cols.astype(jnp.bfloat16).reshape(local_experts, -1, col_width), sources)
    )
    back_flat = jnp.concatenate(
        [returned.reshape(slot_rows, col_width), jnp.zeros((1, col_width), jnp.bfloat16)], axis=0
    )
    pair_out = back_flat[target].astype(jnp.float32).reshape(tok_count, top_count, col_width)
    routed = jnp.sum(gate_values[:, :, None] * pair_out, axis=1)
    hidden_cols = lax.dynamic_slice_in_dim(hidden_one, col_start, col_width, 1)
    layer_out = (hidden_cols + switch[:, None] * shared_cols + routed).astype(jnp.bfloat16)
    grad_full = whole_grad.astype(jnp.float32)
    grad_cols = out_grad.astype(jnp.float32)
    gate_part = jnp.sum(pair_out * grad_cols[:, None, :], axis=-1)
    switch_part = jnp.sum(grad_cols * shared_cols, axis=-1)
    gate_grad, switch_grad = lax.psum((gate_part, switch_part), "tp")
    padded_grad = jnp.concatenate([whole_grad, jnp.zeros((1, model_dim), jnp.bfloat16)], axis=0)
    send_grads = (slot_gate[:, None] * padded_grad[slot_token].astype(jnp.float32)).astype(
        jnp.bfloat16
    )
    expert_grads = to_experts(
        deliver(send_grads.reshape(sources, local_experts * capacity, model_dim)), local_experts
    )
    hidden_grad = jnp.einsum(
        "erd,efd->erf", expert_grads, expert_down_weight, preferred_element_type=jnp.float32
    )
    gate_lin_grad = (hidden_grad * up_lin * gate_sig * (1.0 + gate_lin * (1.0 - gate_sig))).astype(
        jnp.bfloat16
    )
    up_lin_grad = (hidden_grad * gate_act).astype(jnp.bfloat16)
    expert_down_grad = jnp.einsum(
        "erf,erd->efd", expert_hidden, expert_grads, preferred_element_type=jnp.float32
    )
    expert_gate_grad = jnp.einsum(
        "erd,erf->edf", expert_rows, gate_lin_grad, preferred_element_type=jnp.float32
    )
    expert_up_grad = jnp.einsum(
        "erd,erf->edf", expert_rows, up_lin_grad, preferred_element_type=jnp.float32
    )
    rows_grad = jnp.einsum(
        "erf,edf->erd", gate_lin_grad, expert_gate_weight, preferred_element_type=jnp.float32
    )
    rows_grad = rows_grad + jnp.einsum(
        "erf,edf->erd", up_lin_grad, expert_up_weight, preferred_element_type=jnp.float32
    )
    rows_grad_cols = lax.psum_scatter(
        rows_grad.reshape(-1, model_dim), "tp", scatter_dimension=1, tiled=True
    )
    returned_grad = collect(
        to_sources(
            rows_grad_cols.astype(jnp.bfloat16).reshape(local_experts, -1, col_width), sources
        )
    )
    back_grad = jnp.concatenate(
        [returned_grad.reshape(slot_rows, col_width), jnp.zeros((1, col_width), jnp.bfloat16)],
        axis=0,
    )
    routed_grad = jnp.sum(
        back_grad[target].astype(jnp.float32).reshape(tok_count, top_count, col_width), axis=1
    )
    shared_out_grad = (switch[:, None] * grad_full).astype(jnp.bfloat16)
    shared_hidden_grad = times_transpose(shared_out_grad, shared_down_weight)
    shared_gate_lin_grad = (
        shared_hidden_grad
        * shared_up_lin
        * shared_sig
        * (1.0 + shared_gate_lin * (1.0 - shared_sig))
    ).astype(jnp.bfloat16)
    shared_up_lin_grad = (shared_hidden_grad * shared_act).astype(jnp.bfloat16)
    shared_down_grad = inner_rows(shared_hidden, shared_out_grad)
    shared_gate_grad = inner_rows(normed_two, shared_gate_lin_grad)
    shared_up_grad = inner_rows(normed_two, shared_up_lin_grad)
    normed_grad = times_transpose(shared_gate_lin_grad, shared_gate_weight) + times_transpose(
        shared_up_lin_grad, shared_up_weight
    )
    normed_grad = normed_grad + lax.dynamic_update_slice_in_dim(
        jnp.zeros_like(normed_grad), routed_grad, col_start, 1
    )
    normed_grad = lax.psum(normed_grad, "tp")
    picked = (
        expert_ids[:, :, None] == jnp.arange(expert_total, dtype=jnp.int32)[None, None, :]
    ).astype(jnp.float32)
    probs_grad = jnp.sum(picked * gate_grad[:, :, None], axis=1)
    logit_grad = (
        router_probs * (probs_grad - jnp.sum(router_probs * probs_grad, axis=-1, keepdims=True))
    ).astype(jnp.bfloat16)
    router_grad = inner_rows(normed_two, logit_grad)
    switch_lin_grad = switch_grad * switch * (1.0 - switch)
    switch_vector_grad = jnp.dot(switch_lin_grad, normed_two, preferred_element_type=jnp.float32)
    normed_grad = normed_grad + times_transpose(logit_grad, router_weight)
    normed_grad = (
        normed_grad + switch_lin_grad[:, None] * switch_vector.astype(jnp.float32)[None, :]
    )
    second_gain_grad = jnp.sum(normed_grad * unit_two, axis=0)
    hidden_grad_one = grad_full + norm_back(normed_grad, unit_two, inv_two, second_gain)
    attended_grad = hidden_grad_one.astype(jnp.bfloat16)
    output_grad = inner_rows(context, attended_grad)
    context_grad = (
        times_transpose(attended_grad, output_weight)
        .astype(jnp.bfloat16)
        .reshape(tok_count, head_count, HD)
    )
    scores = attention_scores()
    attn_probs = jnp.exp(scores - log_total)
    probs_again = attn_probs.astype(jnp.bfloat16)
    probs_grad_att = jnp.einsum(
        "qhd,khd->hqk", context_grad, values_both, preferred_element_type=jnp.float32
    )
    values_both_grad = jnp.einsum(
        "hqk,qhd->khd", probs_again, context_grad, preferred_element_type=jnp.float32
    )
    scores_grad = (
        attn_probs * (probs_grad_att - jnp.sum(attn_probs * probs_grad_att, axis=-1, keepdims=True))
    ).astype(jnp.bfloat16)
    queries_grad = (
        jnp.einsum("hqk,khd->qhd", scores_grad, keys_both, preferred_element_type=jnp.float32)
        * score_scale
    )
    keys_both_grad = (
        jnp.einsum("hqk,qhd->khd", scores_grad, queries, preferred_element_type=jnp.float32)
        * score_scale
    )
    later_keys_grad, later_values_grad = passed_along(
        (keys_both_grad[:tok_count], values_both_grad[:tok_count]), "ep", -1
    )
    keep_later = jnp.where(has_earlier, 0.0, 1.0).astype(jnp.float32)
    keys_grad = keys_both_grad[tok_count:] + keep_later * later_keys_grad
    values_grad = values_both_grad[tok_count:] + keep_later * later_values_grad
    value_lin_grad = values_grad.reshape(tok_count, head_count * HD).astype(jnp.bfloat16)
    query_lin_grad = (
        rotate(queries_grad, cosine, -sine_part)
        .reshape(tok_count, head_count * HD)
        .astype(jnp.bfloat16)
    )
    key_lin_grad = (
        rotate(keys_grad, cosine, -sine_part)
        .reshape(tok_count, head_count * HD)
        .astype(jnp.bfloat16)
    )
    query_grad = inner_rows(normed_one, query_lin_grad)
    key_grad = inner_rows(normed_one, key_lin_grad)
    value_grad = inner_rows(normed_one, value_lin_grad)
    query_bias_grad = jnp.sum(query_lin_grad.astype(jnp.float32), axis=0).reshape(head_count, HD)
    key_bias_grad = jnp.sum(key_lin_grad.astype(jnp.float32), axis=0).reshape(head_count, HD)
    value_bias_grad = jnp.sum(value_lin_grad.astype(jnp.float32), axis=0).reshape(head_count, HD)
    normed_one_grad = times_transpose(query_lin_grad, query_weight) + times_transpose(
        key_lin_grad, key_weight
    )
    normed_one_grad = normed_one_grad + times_transpose(value_lin_grad, value_weight)
    normed_one_grad = lax.psum(normed_one_grad.astype(jnp.bfloat16), "tp").astype(jnp.float32)
    first_gain_grad = jnp.sum(normed_one_grad * unit_one, axis=0)
    input_grad = hidden_grad_one + norm_back(normed_one_grad, unit_one, inv_one, first_gain)
    tokens_grad = lax.dynamic_slice_in_dim(input_grad, col_start, col_width, 1).astype(jnp.bfloat16)
    reduced = (
        lax.psum_scatter(
            first_gain_grad.astype(jnp.bfloat16), "ep", scatter_dimension=0, tiled=True
        ).astype(jnp.float32),
        lax.psum_scatter(
            query_grad.astype(jnp.bfloat16), "ep", scatter_dimension=0, tiled=True
        ).astype(jnp.float32),
        lax.psum_scatter(
            key_grad.astype(jnp.bfloat16), "ep", scatter_dimension=0, tiled=True
        ).astype(jnp.float32),
        lax.psum_scatter(
            value_grad.astype(jnp.bfloat16), "ep", scatter_dimension=0, tiled=True
        ).astype(jnp.float32),
        lax.psum_scatter(
            query_bias_grad.astype(jnp.bfloat16), "ep", scatter_dimension=1, tiled=True
        ).astype(jnp.float32),
        lax.psum_scatter(
            key_bias_grad.astype(jnp.bfloat16), "ep", scatter_dimension=1, tiled=True
        ).astype(jnp.float32),
        lax.psum_scatter(
            value_bias_grad.astype(jnp.bfloat16), "ep", scatter_dimension=1, tiled=True
        ).astype(jnp.float32),
        lax.psum_scatter(
            output_grad.astype(jnp.bfloat16), "ep", scatter_dimension=1, tiled=True
        ).astype(jnp.float32),
        lax.psum_scatter(
            second_gain_grad.astype(jnp.bfloat16), "ep", scatter_dimension=0, tiled=True
        ).astype(jnp.float32),
        lax.psum_scatter(
            router_grad.astype(jnp.bfloat16), "ep", scatter_dimension=0, tiled=True
        ).astype(jnp.float32),
        lax.psum_scatter(
            shared_gate_grad.astype(jnp.bfloat16), "ep", scatter_dimension=0, tiled=True
        ).astype(jnp.float32),
        lax.psum_scatter(
            shared_up_grad.astype(jnp.bfloat16), "ep", scatter_dimension=0, tiled=True
        ).astype(jnp.float32),
        lax.psum_scatter(
            shared_down_grad.astype(jnp.bfloat16), "ep", scatter_dimension=1, tiled=True
        ).astype(jnp.float32),
        lax.psum_scatter(
            switch_vector_grad.astype(jnp.bfloat16), "ep", scatter_dimension=0, tiled=True
        ).astype(jnp.float32),
    )
    return (
        layer_out,
        tokens_grad,
        reduced[0],
        reduced[1],
        reduced[2],
        reduced[3],
        reduced[4],
        reduced[5],
        reduced[6],
        reduced[7],
        reduced[8],
        reduced[9],
        reduced[10],
        reduced[11],
        reduced[12],
        reduced[13],
        expert_gate_grad,
        expert_up_grad,
        expert_down_grad,
    )


MESH = pl.DeviceIdType.MESH
Z_ORDER = (0, 3, 1, 2)


def place():
    ep, tp = lax.axis_index("ep"), lax.axis_index("tp")
    return ep, tp, ep // 2, lax.rem(ep, 2), tp // 2, lax.rem(tp, 2)


def greet(always, along_z=False):
    barrier = pltpu.get_barrier_semaphore()
    for device in always:
        pl.semaphore_signal(barrier, inc=1, device_id=device, device_id_type=MESH)
    count = len(always)
    if along_z:
        ep, tp, z, _, _, _ = place()

        @pl.when(z < 3)
        def _():
            pl.semaphore_signal(barrier, inc=1, device_id=(ep + 2, tp), device_id_type=MESH)

        @pl.when(z > 0)
        def _():
            pl.semaphore_signal(barrier, inc=1, device_id=(ep - 2, tp), device_id_type=MESH)

        count = count + lax.min(z, 1) + lax.min(3 - z, 1)
    pl.semaphore_wait(barrier, count)


def remote(source, target, send_sem, recv_sem, device):
    return pltpu.make_async_remote_copy(
        src_ref=source,
        dst_ref=target,
        send_sem=send_sem,
        recv_sem=recv_sem,
        device_id=device,
        device_id_type=MESH,
    )


def add_blocks(target, sources, rows):
    step = next(size for size in (64, 48, 16) if rows % size == 0)

    def body(i, carry):
        span = pl.ds(pl.multiple_of(i * step, 16), step)
        total = target[span, :].astype(jnp.float32)
        for source in sources:
            total = total + source[span, :].astype(jnp.float32)
        target[span, :] = total.astype(target.dtype)
        return carry

    lax.fori_loop(0, rows // step, body, 0)


def gather_tp_kernel(x_ref, o_ref, send_sem, recv_sem, own_sem):
    ep, tp, _, _, x, core = place()
    cols = x_ref.shape[1]
    sibling = (ep, tp + 1 - 2 * core)
    across = (ep, tp + 2 - 4 * x)
    greet([sibling, across])
    mine = o_ref.at[:, pl.ds(pl.multiple_of(tp * cols, cols), cols)]
    theirs = o_ref.at[:, pl.ds(pl.multiple_of((tp + 2 - 4 * x) * cols, cols), cols)]
    out_x = remote(x_ref, mine, send_sem.at[0], recv_sem.at[0], across)
    out_s = remote(x_ref, mine, send_sem.at[1], recv_sem.at[1], sibling)
    own = pltpu.make_async_copy(x_ref, mine, own_sem)
    out_x.start()
    out_s.start()
    own.start()
    remote(x_ref, theirs, send_sem.at[0], recv_sem.at[0], across).wait_recv()
    passing = remote(theirs, theirs, send_sem.at[2], recv_sem.at[2], sibling)
    passing.start()
    out_s.wait_recv()
    passing.wait_recv()
    own.wait()
    out_x.wait_send()
    out_s.wait_send()
    passing.wait_send()


def gather_tp(value, cid):
    rows, cols = value.shape
    return pl.pallas_call(
        gather_tp_kernel,
        out_shape=jax.ShapeDtypeStruct((rows, 4 * cols), value.dtype),
        in_specs=[pl.BlockSpec(memory_space=pl.ANY)],
        out_specs=pl.BlockSpec(memory_space=pl.ANY),
        scratch_shapes=[
            pltpu.SemaphoreType.DMA((3,)),
            pltpu.SemaphoreType.DMA((3,)),
            pltpu.SemaphoreType.DMA,
        ],
        compiler_params=pltpu.CompilerParams(collective_id=cid, has_side_effects=True),
        name="gather_tp",
    )(value)


def scatter_tp_kernel(p_ref, o_ref, mine, from_sib, from_x, own_sem, send_sem, recv_sem):
    ep, tp, _, _, x, core = place()
    rows, cols = o_ref.shape
    sibling = (ep, tp + 1 - 2 * core)
    across = (ep, tp + 2 - 4 * x)
    greet([sibling, across])

    def part(x_at, core_at):
        return p_ref.at[:, pl.ds(pl.multiple_of((x_at * 2 + core_at) * cols, cols), cols)]

    sends, owns = [], []
    for i, x_at in enumerate((1 - x, x)):
        owns.append(pltpu.make_async_copy(part(x_at, core), mine.at[i], own_sem.at[i]))
        sends.append(
            remote(part(x_at, 1 - core), from_sib.at[i], send_sem.at[i], recv_sem.at[i], sibling)
        )
        sends[-1].start()
        owns[-1].start()
    owns[0].wait()
    sends[0].wait_recv()
    add_blocks(mine.at[0], [from_sib.at[0]], rows)
    out_x = remote(mine.at[0], from_x, send_sem.at[2], recv_sem.at[2], across)
    out_x.start()
    owns[1].wait()
    sends[1].wait_recv()
    out_x.wait_recv()
    o_ref[...] = jnp.zeros_like(o_ref)
    add_blocks(o_ref, [mine.at[1], from_sib.at[1], from_x], rows)
    out_x.wait_send()
    sends[0].wait_send()
    sends[1].wait_send()


def scatter_tp(value, cid):
    rows, cols = value.shape[0], value.shape[1] // 4
    return pl.pallas_call(
        scatter_tp_kernel,
        out_shape=jax.ShapeDtypeStruct((rows, cols), jnp.float32),
        in_specs=[pl.BlockSpec(memory_space=pl.ANY)],
        out_specs=pl.BlockSpec(memory_space=pltpu.VMEM),
        scratch_shapes=[
            pltpu.VMEM((2, rows, cols), value.dtype),
            pltpu.VMEM((2, rows, cols), value.dtype),
            pltpu.VMEM((rows, cols), value.dtype),
            pltpu.SemaphoreType.DMA((2,)),
            pltpu.SemaphoreType.DMA((3,)),
            pltpu.SemaphoreType.DMA((3,)),
        ],
        compiler_params=pltpu.CompilerParams(
            collective_id=cid, has_side_effects=True, vmem_limit_bytes=32 * 2**20
        ),
        name="scatter_tp",
    )(value)


def lane_peers():
    ep, tp, z, y, x, core = place()
    to_y, to_x = 1 - 2 * y, 1 - 2 * x
    peer_a = (ep + (1 - core) * to_y, tp + core * 2 * to_x)
    peer_b = (ep + core * to_y, tp + (1 - core) * 2 * to_x)
    sibling = (ep, tp + 1 - 2 * core)
    above, below = (ep + 2, tp), (ep - 2, tp)
    return peer_a, peer_b, sibling, above, below


def lane_spot(z_at, da, db, core_at):
    _, _, _, y, x, _ = place()
    y_at = y + (1 - 2 * y) * ((1 - core_at) * da + core_at * db)
    x_at = x + (1 - 2 * x) * (core_at * da + (1 - core_at) * db)
    return z_at * 2 + y_at, x_at * 2 + core_at


def gather_all_kernel(x_ref, o_ref, up_sem, down_sem, a_sem, b_sem, s_sem, recv_sem, sib_sem, own_sem):
    ep, tp, z, y, x, core = place()
    rows, cols = x_ref.shape
    peer_a, peer_b, sibling, above, below = lane_peers()
    greet([peer_a, peer_b, sibling], True)

    def spot(z_at, da, db):
        group, quarter = lane_spot(z_at, da, db, core)
        return o_ref.at[
            pl.ds(pl.multiple_of(group * rows, rows), rows),
            pl.ds(pl.multiple_of(quarter * cols, cols), cols),
        ]

    def at(z_at, da, db):
        return z_at * 4 + da * 2 + db

    def arrived(z_at, da, db):
        block = spot(z_at, da, db)
        remote(block, block, s_sem.at[at(z_at, da, db)], recv_sem.at[at(z_at, da, db)], sibling).wait_recv()

    def up(z_at, source):
        return remote(source, spot(z_at, 0, 0), up_sem.at[z_at], recv_sem.at[at(z_at, 0, 0)], above)

    def down(z_at, source):
        return remote(source, spot(z_at, 0, 0), down_sem.at[z_at], recv_sem.at[at(z_at, 0, 0)], below)

    def over_a(z_at, source):
        return remote(source, spot(z_at, 0, 0), a_sem.at[z_at], recv_sem.at[at(z_at, 1, 0)], peer_a)

    def over_b(z_at, da, source):
        return remote(
            source, spot(z_at, da, 0), b_sem.at[z_at * 2 + da], recv_sem.at[at(z_at, da, 1)], peer_b
        )

    def to_sibling(z_at, da, db, source):
        n = at(z_at, da, db)
        return remote(source, spot(z_at, da, db), s_sem.at[n], sib_sem.at[n], sibling)

    own = pltpu.make_async_copy(x_ref, spot(z, 0, 0), own_sem)
    over_b(z, 0, x_ref).start()
    over_a(z, x_ref).start()

    @pl.when(z < 3)
    def _():
        up(z, x_ref).start()

    @pl.when(z > 0)
    def _():
        down(z, x_ref).start()

    to_sibling(z, 0, 0, x_ref).start()
    own.start()

    def from_a(z_at):
        arrived(z_at, 1, 0)
        block = spot(z_at, 1, 0)
        over_b(z_at, 1, block).start()
        to_sibling(z_at, 1, 0, block).start()

    def from_z(z_at, onward):
        arrived(z_at, 0, 0)
        block = spot(z_at, 0, 0)
        onward(block)
        over_a(z_at, block).start()
        over_b(z_at, 0, block).start()
        to_sibling(z_at, 0, 0, block).start()

    def from_below(z_at):
        def onward(block):
            @pl.when(z < 3)
            def _():
                up(z_at, block).start()

        from_z(z_at, onward)

    def from_above(z_at):
        def onward(block):
            @pl.when(z > 0)
            def _():
                down(z_at, block).start()

        from_z(z_at, onward)

    for d in range(1, 4):

        @pl.when(z >= d)
        def _(d=d):
            from_below(z - d)

        @pl.when(z + d <= 3)
        def _(d=d):
            from_above(z + d)

        if d == 1:
            from_a(z)
        else:

            @pl.when(z >= d - 1)
            def _(d=d):
                from_a(z - d + 1)

            @pl.when(z + d - 1 <= 3)
            def _(d=d):
                from_a(z + d - 1)

    @pl.when(z >= 3)
    def _():
        from_a(z - 3)

    @pl.when(z + 3 <= 3)
    def _():
        from_a(z + 3)

    def from_b(z_at, da):
        arrived(z_at, da, 1)
        to_sibling(z_at, da, 1, spot(z_at, da, 1)).start()

    for da in range(2):
        from_b(z, da)
    for d in range(1, 4):
        for da in range(2):

            @pl.when(z >= d)
            def _(d=d, da=da):
                from_b(z - d, da)

            @pl.when(z + d <= 3)
            def _(d=d, da=da):
                from_b(z + d, da)

    def finish_sibling(i, carry):
        block = spot(0, 0, 0)
        copy = remote(block, block, s_sem.at[i], sib_sem.at[i], sibling)
        copy.wait_recv()
        copy.wait_send()
        return carry

    lax.fori_loop(0, 16, finish_sibling, 0)

    def finish_links(i, carry):
        over_a(i, x_ref).wait_send()
        over_b(i, 0, x_ref).wait_send()
        over_b(i, 1, x_ref).wait_send()

        @pl.when((z < 3) & (i <= z))
        def _():
            up(i, x_ref).wait_send()

        @pl.when((z > 0) & (i >= z))
        def _():
            down(i, x_ref).wait_send()

        return carry

    lax.fori_loop(0, 4, finish_links, 0)
    own.wait()


def gather_all(value, cid):
    rows, cols = value.shape
    return pl.pallas_call(
        gather_all_kernel,
        out_shape=jax.ShapeDtypeStruct((8 * rows, 4 * cols), value.dtype),
        in_specs=[pl.BlockSpec(memory_space=pl.ANY)],
        out_specs=pl.BlockSpec(memory_space=pl.ANY),
        scratch_shapes=[
            pltpu.SemaphoreType.DMA((4,)),
            pltpu.SemaphoreType.DMA((4,)),
            pltpu.SemaphoreType.DMA((4,)),
            pltpu.SemaphoreType.DMA((8,)),
            pltpu.SemaphoreType.DMA((16,)),
            pltpu.SemaphoreType.DMA((16,)),
            pltpu.SemaphoreType.DMA((16,)),
            pltpu.SemaphoreType.DMA,
        ],
        compiler_params=pltpu.CompilerParams(collective_id=cid, has_side_effects=True),
        name="gather_all",
    )(value)


def z_chain(blocks, totals, from_below, from_above, up_send, up_recv, down_send, down_recv, rows, final):
    ep, tp, z, _, _, _ = place()
    above, below = (ep + 2, tp), (ep - 2, tp)

    def up(z_at):
        return remote(totals(z_at), from_below.at[z_at], up_send.at[z_at], up_recv.at[z_at], above)

    def down(z_at):
        return remote(totals(z_at), from_above.at[z_at], down_send.at[z_at], down_recv.at[z_at], below)

    for z_at in Z_ORDER:
        blocks(z_at)

        @pl.when(z_at > z)
        def _(z_at=z_at):
            @pl.when(z > 0)
            def _():
                up(z_at).wait_recv()
                add_blocks(totals(z_at), [from_below.at[z_at]], rows)

            up(z_at).start()

        @pl.when(z_at < z)
        def _(z_at=z_at):
            @pl.when(z < 3)
            def _():
                down(z_at).wait_recv()
                add_blocks(totals(z_at), [from_above.at[z_at]], rows)

            down(z_at).start()

    for z_at in range(4):

        @pl.when(z_at == z)
        def _(z_at=z_at):
            @pl.when(z > 0)
            def _():
                up(z_at).wait_recv()

            @pl.when(z < 3)
            def _():
                down(z_at).wait_recv()

            @pl.when(z == 0)
            def _():
                final(z_at, [from_above.at[z_at]])

            @pl.when(z == 3)
            def _():
                final(z_at, [from_below.at[z_at]])

            @pl.when((z > 0) & (z < 3))
            def _():
                final(z_at, [from_below.at[z_at], from_above.at[z_at]])

    for z_at in range(4):

        @pl.when(z_at > z)
        def _(z_at=z_at):
            up(z_at).wait_send()

        @pl.when(z_at < z)
        def _(z_at=z_at):
            down(z_at).wait_send()


def scatter_all_kernel(
    p_ref,
    o_ref,
    mine,
    from_sib,
    from_b,
    from_a,
    from_below,
    from_above,
    own_sem,
    s_send,
    s_recv,
    b_send,
    b_recv,
    a_send,
    a_recv,
    up_send,
    up_recv,
    down_send,
    down_recv,
):
    ep, tp, z, y, x, core = place()
    rows, cols = o_ref.shape
    peer_a, peer_b, sibling, above, below = lane_peers()
    greet([peer_a, peer_b, sibling], True)

    def part(z_at, da, db, core_at):
        group, quarter = lane_spot(z_at, da, db, core_at)
        return p_ref.at[
            pl.ds(pl.multiple_of(group * rows, rows), rows),
            pl.ds(pl.multiple_of(quarter * cols, cols), cols),
        ]

    def at(z_at, da, db):
        return z_at * 4 + da * 2 + db

    def own(z_at, da, db):
        n = at(z_at, da, db)
        return pltpu.make_async_copy(part(z_at, da, db, core), mine.at[n], own_sem.at[n])

    def to_sibling(z_at, da, db):
        n = at(z_at, da, db)
        return remote(
            part(z_at, da, db, 1 - core), from_sib.at[n], s_send.at[n], s_recv.at[n], sibling
        )

    for da, db in ((1, 1), (0, 1), (1, 0), (0, 0)):
        for z_at in Z_ORDER:
            to_sibling(z_at, da, db).start()
            own(z_at, da, db).start()

    def here(z_at, da, db):
        own(z_at, da, db).wait()
        to_sibling(z_at, da, db).wait_recv()
        return mine.at[at(z_at, da, db)], from_sib.at[at(z_at, da, db)]

    def over_b(z_at, da):
        n = z_at * 2 + da
        return remote(mine.at[at(z_at, da, 1)], from_b.at[n], b_send.at[n], b_recv.at[n], peer_b)

    def over_a(z_at):
        return remote(mine.at[at(z_at, 1, 0)], from_a.at[z_at], a_send.at[z_at], a_recv.at[z_at], peer_a)

    for da in (1, 0):
        for z_at in Z_ORDER:
            own_part, sib_part = here(z_at, da, 1)
            add_blocks(own_part, [sib_part], rows)
            over_b(z_at, da).start()
    for z_at in Z_ORDER:
        own_part, sib_part = here(z_at, 1, 0)
        over_b(z_at, 1).wait_recv()
        add_blocks(own_part, [sib_part, from_b.at[z_at * 2 + 1]], rows)
        over_a(z_at).start()

    def blocks(z_at):
        own_part, sib_part = here(z_at, 0, 0)
        over_b(z_at, 0).wait_recv()
        over_a(z_at).wait_recv()
        add_blocks(own_part, [sib_part, from_b.at[z_at * 2], from_a.at[z_at]], rows)

    def final(z_at, others):
        o_ref[...] = jnp.zeros_like(o_ref)
        add_blocks(o_ref, [mine.at[at(z_at, 0, 0)], *others], rows)

    z_chain(
        blocks,
        lambda z_at: mine.at[at(z_at, 0, 0)],
        from_below,
        from_above,
        up_send,
        up_recv,
        down_send,
        down_recv,
        rows,
        final,
    )
    for z_at in range(4):
        over_a(z_at).wait_send()
        for da in range(2):
            over_b(z_at, da).wait_send()
            for db in range(2):
                to_sibling(z_at, da, db).wait_send()


def scatter_all(value, cid):
    rows, cols = value.shape[0] // 8, value.shape[1] // 4
    dma = pltpu.SemaphoreType.DMA

    def held(count):
        return pltpu.VMEM((count, rows, cols), value.dtype)

    return pl.pallas_call(
        scatter_all_kernel,
        out_shape=jax.ShapeDtypeStruct((rows, cols), jnp.float32),
        in_specs=[pl.BlockSpec(memory_space=pl.ANY)],
        out_specs=pl.BlockSpec(memory_space=pltpu.VMEM),
        scratch_shapes=[held(16), held(16), held(8), held(4), held(4), held(4)]
        + [dma((16,)), dma((16,)), dma((16,)), dma((8,)), dma((8,))]
        + [dma((4,))] * 6,
        compiler_params=pltpu.CompilerParams(
            collective_id=cid, has_side_effects=True, vmem_limit_bytes=48 * 2**20
        ),
        name="scatter_all",
    )(value)


def scatter_ep_kernel(
    p_ref, e_ref, o_ref, mine, from_y, from_below, from_above, own_sem, y_send, y_recv, up_send, up_recv, down_send, down_recv
):
    ep, tp, z, y, _, _ = place()
    rows, extra = p_ref.shape[0] // 8, e_ref.shape[0]
    tall = rows + extra
    across = (ep + 1 - 2 * y, tp)
    greet([across], True)

    def part(z_at, y_at):
        return p_ref.at[pl.ds(pl.multiple_of((z_at * 2 + y_at) * rows, rows), rows), :]

    def own(z_at):
        return (
            pltpu.make_async_copy(part(z_at, y), mine.at[z_at, pl.ds(0, rows)], own_sem.at[z_at]),
            pltpu.make_async_copy(e_ref, mine.at[z_at, pl.ds(rows, extra)], own_sem.at[4 + z_at]),
        )

    def over_y(z_at):
        return (
            remote(
                part(z_at, 1 - y),
                from_y.at[z_at, pl.ds(0, rows)],
                y_send.at[z_at],
                y_recv.at[z_at],
                across,
            ),
            remote(
                e_ref,
                from_y.at[z_at, pl.ds(rows, extra)],
                y_send.at[4 + z_at],
                y_recv.at[4 + z_at],
                across,
            ),
        )

    for z_at in Z_ORDER:
        for copy in over_y(z_at) + own(z_at):
            copy.start()

    def blocks(z_at):
        for copy in own(z_at):
            copy.wait()
        for copy in over_y(z_at):
            copy.wait_recv()
        add_blocks(mine.at[z_at], [from_y.at[z_at]], tall)

    def final(z_at, others):
        o_ref[...] = jnp.zeros_like(o_ref)
        add_blocks(o_ref, [mine.at[z_at], *others], tall)

    z_chain(
        blocks,
        lambda z_at: mine.at[z_at],
        from_below,
        from_above,
        up_send,
        up_recv,
        down_send,
        down_recv,
        tall,
        final,
    )
    for z_at in range(4):
        for copy in over_y(z_at):
            copy.wait_send()


def scatter_ep(value, extra, cid):
    rows, cols = value.shape[0] // 8, value.shape[1]
    tall = rows + extra.shape[0]
    dma = pltpu.SemaphoreType.DMA

    def held():
        return pltpu.VMEM((4, tall, cols), value.dtype)

    return pl.pallas_call(
        scatter_ep_kernel,
        out_shape=jax.ShapeDtypeStruct((tall, cols), jnp.float32),
        in_specs=[pl.BlockSpec(memory_space=pl.ANY)] * 2,
        out_specs=pl.BlockSpec(memory_space=pltpu.VMEM),
        scratch_shapes=[held(), held(), held(), held()] + [dma((8,))] * 3 + [dma((4,))] * 4,
        compiler_params=pltpu.CompilerParams(
            collective_id=cid, has_side_effects=True, vmem_limit_bytes=40 * 2**20
        ),
        name="scatter_ep",
    )(value, extra)


def experts_kernel(
    expert_width,
    shared_width,
    expert_total,
    x_ref,
    g_ref,
    kept_ref,
    expert_gate_ref,
    shared_gate_ref,
    extra_ref,
    expert_up_ref,
    shared_up_ref,
    expert_down_ref,
    shared_down_ref,
    all_ref,
    hidden_ref,
    both_ref,
    out_ref,
    grad_ref,
    logit_ref,
    in_ref,
    down_ref,
    scalars,
    kept_held,
    x_held,
    g_held,
    lin,
    hidden_grad,
    hidden_held,
    both_held,
    out_held,
    kept_cols,
    staged,
    mine,
    from_sib,
    from_b,
    from_a,
    from_below,
    from_above,
    up_sem,
    down_sem,
    a_sem,
    b_sem,
    s_sem,
    recv_sem,
    sib_sem,
    own_sem,
    load_sem,
    store_sem,
    weight_sem,
    kept_send,
    kept_recv,
    rs_send,
    rs_recv,
    rb_send,
    rb_recv,
    ra_send,
    ra_recv,
    ru_send,
    ru_recv,
    rd_send,
    rd_recv,
):
    ep, tp, z, y, x, core = place()
    rows, cols = x_ref.shape
    width = down_ref.shape[0]
    peer_a, peer_b, sibling, above, below = lane_peers()
    sources = kept_held.shape[0]
    others = [(lax.rem(ep + i, sources), tp) for i in range(1, sources)]
    x_peer = (ep, tp + 2 - 4 * x)
    greet([x_peer, sibling] + others)

    def spot(z_at, da, db):
        group, quarter = lane_spot(z_at, da, db, core)
        return all_ref.at[
            pl.ds(pl.multiple_of(group * rows, rows), rows),
            pl.ds(pl.multiple_of(quarter * cols, cols), cols),
        ]

    def at(z_at, da, db):
        return z_at * 4 + da * 2 + db

    turns = (
        z,
        1 + lax.rem(z, 2),
        jnp.where(z == 0, 2, jnp.where(z == 1, 0, jnp.where(z == 2, 3, 1))),
        3 * (1 - z // 2),
    )
    edge = (z == 0) | (z == 3)

    def arrived(z_at, da, db):
        block, n = spot(z_at, da, db), at(z_at, da, db)
        remote(block, block, s_sem.at[n], recv_sem.at[n], sibling).wait_recv()
        return block

    def up(z_at, source):
        return remote(source, spot(z_at, 0, 0), up_sem.at[z_at], recv_sem.at[at(z_at, 0, 0)], above)

    def down(z_at, source):
        return remote(source, spot(z_at, 0, 0), down_sem.at[z_at], recv_sem.at[at(z_at, 0, 0)], below)

    def over_a(z_at, source):
        return remote(source, spot(z_at, 0, 0), a_sem.at[z_at], recv_sem.at[at(z_at, 1, 0)], peer_a)

    def over_b(z_at, da, source):
        return remote(
            source, spot(z_at, da, 0), b_sem.at[z_at * 2 + da], recv_sem.at[at(z_at, da, 1)], peer_b
        )

    def to_sibling(z_at, da, db, source):
        n = at(z_at, da, db)
        return remote(source, spot(z_at, da, db), s_sem.at[n], sib_sem.at[n], sibling)

    def pass_z(k):
        z_at = turns[k]
        block = arrived(z_at, 0, 0)

        @pl.when((z_at > z) & (z > 0))
        def _():
            down(z_at, block).start()

        @pl.when((z_at < z) & (z < 3))
        def _():
            up(z_at, block).start()

        over_a(z_at, block).start()
        over_b(z_at, 0, block).start()
        to_sibling(z_at, 0, 0, block).start()

    def pass_a(k):
        block = arrived(turns[k], 1, 0)
        over_b(turns[k], 1, block).start()
        to_sibling(turns[k], 1, 0, block).start()

    def pass_b(k, da):
        block = arrived(turns[k], da, 1)
        to_sibling(turns[k], da, 1, block).start()

    def sibling_blocks(k, dy):
        for dx in range(2):
            da, db = core * dy + (1 - core) * dx, core * dx + (1 - core) * dy
            n = at(turns[k], da, db)
            block = spot(0, 0, 0)
            remote(block, block, s_sem.at[n], sib_sem.at[n], sibling).wait_recv()

    def group_rows(k, dy):
        group = turns[k] * 2 + y + (1 - 2 * y) * dy
        return group, pl.ds(pl.multiple_of(group * rows, rows), rows)

    def load_x(k, dy):
        _, span = group_rows(k, dy)
        return pltpu.make_async_copy(all_ref.at[span, :], x_held.at[dy], load_sem.at[dy])

    def load_g(k, dy):
        _, span = group_rows(k, dy)
        return pltpu.make_async_copy(g_ref.at[span, :], g_held.at[dy], load_sem.at[2 + dy])

    def project(k, dy):
        def body(i, carry):
            cut = pl.ds(pl.multiple_of(i * width, width), width)
            lin[:, cut] = times_transpose(x_held[dy], in_ref[cut, :])
            return carry

        lax.fori_loop(0, 2, body, 0)

    def project_grad(k, dy):
        hidden_grad[...] = times_transpose(g_held[dy], down_ref[...])

    def stores(k, dy):
        _, span = group_rows(k, dy)
        return (
            pltpu.make_async_copy(hidden_held.at[dy], hidden_ref.at[span, :], store_sem.at[dy]),
            pltpu.make_async_copy(both_held.at[dy], both_ref.at[span, :], store_sem.at[2 + dy]),
            pltpu.make_async_copy(out_held.at[dy], out_ref.at[span, :], store_sem.at[4 + dy]),
        )

    step = 64
    tile_start = width - 128
    logit_at = expert_width + shared_width - tile_start

    def activate(k, dy):
        group, _ = group_rows(k, dy)
        lane = lax.broadcasted_iota(jnp.int32, (1, width), 1)
        near = lax.broadcasted_iota(jnp.int32, (1, 128), 1)
        is_logit = (near >= logit_at) & (near < logit_at + expert_total)
        kept_cols[:, :16] = kept_held[group].astype(jnp.float32).T

        def body(i, carry):
            span = pl.ds(pl.multiple_of(i * step, step), step)
            gate_lin, up_lin = lin[span, :width], lin[span, width:]
            grad = hidden_grad[span, :]
            tail = lin[span, tile_start:width]
            if k == 0 and dy == 0:
                logit_ref[span, :] = tail
            most = jnp.max(jnp.where(is_logit, tail, -1e30), axis=1, keepdims=True)
            powers = jnp.where(is_logit, jnp.exp(jnp.minimum(tail - most, 0.0)), 0.0)
            kept = jnp.sum(jnp.where(near == ep, kept_cols[span, :], 0.0), axis=1, keepdims=True)
            gate = jnp.sum(jnp.where(near == logit_at + ep, powers, 0.0), axis=1, keepdims=True)
            gate = gate / jnp.sum(powers, axis=1, keepdims=True) * kept
            switch = jax.nn.sigmoid(
                jnp.sum(
                    jnp.where(near == logit_at + expert_total, tail, 0.0), axis=1, keepdims=True
                )
            )
            scale = jnp.where(lane < expert_width, gate, switch)
            sig = jax.nn.sigmoid(gate_lin)
            act = gate_lin * sig
            hidden = act * up_lin
            agreement = hidden * grad
            gate_part = jnp.sum(jnp.where(lane < expert_width, agreement, 0.0), axis=1, keepdims=True)
            switch_part = jnp.sum(
                jnp.where(lane < expert_width, 0.0, agreement), axis=1, keepdims=True
            )
            scaled = grad * scale
            hidden_held[dy, span, :] = (hidden * scale).astype(jnp.bfloat16)
            both_held[dy, span, :width] = (
                scaled * up_lin * sig * (1.0 + gate_lin * (1.0 - sig))
            ).astype(jnp.bfloat16)
            both_held[dy, span, width:] = (scaled * act).astype(jnp.bfloat16)
            scalars[span, :] = jnp.where(
                near == ep, gate_part, jnp.where(near == expert_total, switch_part, 0.0)
            )
            return carry

        lax.fori_loop(0, rows // step, body, 0)

    def out_rows(k, dy):
        def body(i, carry):
            cut = pl.ds(pl.multiple_of(i * cols, cols), cols)
            out_held[dy, :, cut] = jnp.dot(
                hidden_held[dy], down_ref[:, cut], preferred_element_type=jnp.float32
            ).astype(jnp.bfloat16)
            return carry

        lax.fori_loop(0, 4, body, 0)

    tall = mine.shape[1]

    def lane_at(k, dx, dy, core_at):
        da, db = (1 - core_at) * dy + core_at * dx, (1 - core_at) * dx + core_at * dy
        return at(turns[k], da, db)

    def rs_sibling(k, dx, dy):
        n = lane_at(k, dx, dy, 1 - core)
        return remote(
            staged.at[dy * 2 + dx], from_sib.at[n], rs_send.at[n], rs_recv.at[n], sibling
        )

    def grad_rows(k, dy):
        sums = scalars[...].T[:16, :].astype(jnp.bfloat16)

        def body(dx, carry):
            x_at = x + (1 - 2 * x) * dx
            theirs = pl.ds(pl.multiple_of((x_at * 2 + 1 - core) * cols, cols), cols)
            ours = pl.ds(pl.multiple_of((x_at * 2 + core) * cols, cols), cols)
            staged[dy * 2 + dx, :rows, :] = jnp.dot(
                both_held[dy], in_ref[:, theirs], preferred_element_type=jnp.float32
            ).astype(jnp.bfloat16)
            staged[dy * 2 + dx, rows:, :] = sums
            rs_sibling(k, dx, dy).start()
            ours_at = lane_at(k, dx, dy, core)
            mine[ours_at, :rows, :] = jnp.dot(
                both_held[dy], in_ref[:, ours], preferred_element_type=jnp.float32
            ).astype(jnp.bfloat16)
            mine[ours_at, rows:, :] = sums
            return carry

        lax.fori_loop(0, 2, body, 0)

    def staged_free(k, dy):
        for dx in range(2):
            rs_sibling(k, dx, dy).wait_send()

    def rs_over_b(k, da):
        n = turns[k] * 2 + da
        return remote(
            mine.at[at(turns[k], da, 1)], from_b.at[n], rb_send.at[n], rb_recv.at[n], peer_b
        )

    def rs_over_a(k):
        z_at = turns[k]
        return remote(
            mine.at[at(z_at, 1, 0)], from_a.at[z_at], ra_send.at[z_at], ra_recv.at[z_at], peer_a
        )

    def rs_up(z_at):
        return remote(
            mine.at[at(z_at, 0, 0)], from_below.at[z_at], ru_send.at[z_at], ru_recv.at[z_at], above
        )

    def rs_down(z_at):
        return remote(
            mine.at[at(z_at, 0, 0)], from_above.at[z_at], rd_send.at[z_at], rd_recv.at[z_at], below
        )

    def reduce_sibling(k, dy):
        for dx in range(2):
            n = lane_at(k, dx, dy, core)
            remote(staged.at[0], from_sib.at[n], rs_send.at[n], rs_recv.at[n], sibling).wait_recv()
            add_blocks(mine.at[n], [from_sib.at[n]], tall)

        @pl.when(core == 0)
        def _():
            rs_over_b(k, dy).start()

        if dy == 1:

            @pl.when(core == 1)
            def _():
                rs_over_b(k, 0).start()
                rs_over_b(k, 1).start()

    def reduce_b(k):
        rs_over_b(k, 1).wait_recv()
        add_blocks(mine.at[at(turns[k], 1, 0)], [from_b.at[turns[k] * 2 + 1]], tall)
        rs_over_a(k).start()

    def reduce_a(k):
        z_at = turns[k]
        rs_over_b(k, 0).wait_recv()
        rs_over_a(k).wait_recv()
        add_blocks(mine.at[at(z_at, 0, 0)], [from_b.at[z_at * 2], from_a.at[z_at]], tall)
        if k > 0:

            @pl.when(z == 0)
            def _():
                rs_up(z_at).start()

            @pl.when(z == 3)
            def _():
                rs_down(z_at).start()

    def chain(z_at):
        @pl.when(z_at > z)
        def _():
            rs_up(z_at).wait_recv()
            add_blocks(mine.at[at(z_at, 0, 0)], [from_below.at[z_at]], tall)
            rs_up(z_at).start()

        @pl.when(z_at < z)
        def _():
            rs_down(z_at).wait_recv()
            add_blocks(mine.at[at(z_at, 0, 0)], [from_above.at[z_at]], tall)
            rs_down(z_at).start()

    own = pltpu.make_async_copy(x_ref, spot(z, 0, 0), own_sem)
    over_b(z, 0, x_ref).start()
    over_a(z, x_ref).start()

    @pl.when(z < 3)
    def _():
        up(z, x_ref).start()

    @pl.when(z > 0)
    def _():
        down(z, x_ref).start()

    to_sibling(z, 0, 0, x_ref).start()
    own.start()
    load_g(0, 0).start()

    def kept_to(i):
        return remote(
            kept_ref, kept_held.at[ep], kept_send.at[i - 1], kept_recv.at[i - 1], others[i - 1]
        )

    for i in range(1, sources):
        kept_to(i).start()
    own_kept = pltpu.make_async_copy(kept_ref, kept_held.at[ep], weight_sem.at[7])
    own_kept.start()
    pieces = [
        (expert_gate_ref, in_ref, 0),
        (shared_gate_ref, in_ref, expert_width),
        (extra_ref, in_ref, expert_width + shared_width),
        (expert_up_ref, in_ref, width),
        (shared_up_ref, in_ref, width + expert_width),
        (expert_down_ref, down_ref, 0),
    ]
    weight_copies = [
        pltpu.make_async_copy(piece, target.at[pl.ds(at_row, piece.shape[0]), :], weight_sem.at[i])
        for i, (piece, target, at_row) in enumerate(pieces)
    ]
    weight_copies.append(
        pltpu.make_async_copy(
            shared_down_ref.at[pl.ds(pl.multiple_of(ep * shared_width, 16), shared_width), :],
            down_ref.at[pl.ds(expert_width, shared_width), :],
            weight_sem.at[6],
        )
    )
    for copy in weight_copies:
        copy.start()
    filled = expert_width + shared_width
    for target, first, last_row in (
        (in_ref, filled + 16, width),
        (in_ref, width + filled, 2 * width),
        (down_ref, filled, width),
    ):
        target[first:last_row, :] = jnp.zeros((last_row - first, target.shape[1]), target.dtype)
    for copy in weight_copies:
        copy.wait()
    own_kept.wait()
    for i in range(1, sources):
        kept_to(i).wait_recv()
    own.wait()

    def ready(k, dy):
        if dy == 0:
            pass_a(k)
            pass_b(k, 0)
        else:
            pass_b(k, 1)
        sibling_blocks(k, dy)
        load_x(k, dy).start()

    order = [(k, dy) for k in range(4) for dy in range(2)]
    ready(0, 0)
    for s, (k, dy) in enumerate(order):
        following = order[s + 1] if s < 7 else None
        load_x(k, dy).wait()
        load_g(k, dy).wait()
        if following is not None:
            load_g(*following).start()
        project(k, dy)
        if s == 0:
            pass_z(1)
        if s >= 1:
            reduce_sibling(*order[s - 1])
        project_grad(k, dy)
        if s == 0:
            pass_z(2)
        if s == 1:
            pass_z(3)
        if dy == 1 and k >= 1:
            reduce_b(k - 1)
        if s >= 2:
            for copy in stores(*order[s - 2]):
                copy.wait()
        activate(k, dy)
        if following is not None:
            ready(*following)
        if dy == 0 and k >= 2:
            reduce_a(k - 2)
        if s >= 2:
            staged_free(*order[s - 2])
        grad_rows(k, dy)
        out_rows(k, dy)
        for copy in stores(k, dy):
            copy.start()
    reduce_sibling(3, 1)
    reduce_a(2)
    reduce_b(3)
    for s in (6, 7):
        for copy in stores(*order[s]):
            copy.wait()
    reduce_a(3)

    @pl.when(z == 1)
    def _():
        for z_at in (2, 3, 0):
            chain(z_at)

    @pl.when(z == 2)
    def _():
        for z_at in (1, 0, 3):
            chain(z_at)

    last = mine.at[at(z, 0, 0)]

    @pl.when(z > 0)
    def _():
        rs_up(z).wait_recv()

    @pl.when(z < 3)
    def _():
        rs_down(z).wait_recv()

    grad_ref[...] = jnp.zeros_like(grad_ref)

    @pl.when(z == 0)
    def _():
        add_blocks(grad_ref, [last, from_above.at[0]], tall)

    @pl.when(z == 3)
    def _():
        add_blocks(grad_ref, [last, from_below.at[3]], tall)

    @pl.when((z > 0) & (z < 3))
    def _():
        add_blocks(grad_ref, [last, from_below.at[z], from_above.at[z]], tall)

    for i in range(1, sources):
        kept_to(i).wait_send()
    staged_free(3, 0)
    staged_free(3, 1)

    def finish(i, carry):
        over_a(i, x_ref).wait_send()
        over_b(i, 0, x_ref).wait_send()
        over_b(i, 1, x_ref).wait_send()
        remote(mine.at[0], from_a.at[0], ra_send.at[i], ra_recv.at[i], peer_a).wait_send()
        for da in range(2):
            n = i * 2 + da
            remote(mine.at[0], from_b.at[0], rb_send.at[n], rb_recv.at[n], peer_b).wait_send()
        for n in range(4):
            block = spot(0, 0, 0)
            remote(block, block, s_sem.at[i * 4 + n], sib_sem.at[i * 4 + n], sibling).wait_send()

        @pl.when((z < 3) & (i <= z))
        def _():
            up(i, x_ref).wait_send()

        @pl.when((z > 0) & (i >= z))
        def _():
            down(i, x_ref).wait_send()

        @pl.when(i > z)
        def _():
            rs_up(i).wait_send()

        @pl.when(i < z)
        def _():
            rs_down(i).wait_send()

        return carry

    lax.fori_loop(0, 4, finish, 0)


def experts(x_cols, grads_all, kept_rows, weights, expert_total, cid):
    rows, cols = x_cols.shape
    total, model_dim = grads_all.shape
    expert_width, shared_width = weights[0].shape[0], weights[1].shape[0]
    width = -(-(expert_width + shared_width + expert_total + 1) // 128) * 128
    low, dma = jnp.bfloat16, pltpu.SemaphoreType.DMA
    vmem, hbm = pl.BlockSpec(memory_space=pltpu.VMEM), pl.BlockSpec(memory_space=pl.ANY)

    def held(count):
        return pltpu.VMEM((count, rows + 16, cols), low)

    return pl.pallas_call(
        functools.partial(experts_kernel, expert_width, shared_width, expert_total),
        out_shape=[
            jax.ShapeDtypeStruct((total, model_dim), low),
            jax.ShapeDtypeStruct((total, width), low),
            jax.ShapeDtypeStruct((total, 2 * width), low),
            jax.ShapeDtypeStruct((total, model_dim), low),
            jax.ShapeDtypeStruct((rows + 16, cols), jnp.float32),
            jax.ShapeDtypeStruct((rows, 128), jnp.float32),
        ],
        in_specs=[hbm] * 10,
        out_specs=[hbm, hbm, hbm, hbm, vmem, vmem],
        scratch_shapes=[
            pltpu.VMEM((2 * width, model_dim), low),
            pltpu.VMEM((width, model_dim), low),
            pltpu.VMEM((rows, 128), jnp.float32),
            pltpu.VMEM((total // rows, 16, rows), low),
            pltpu.VMEM((2, rows, model_dim), low),
            pltpu.VMEM((2, rows, model_dim), low),
            pltpu.VMEM((rows, 2 * width), jnp.float32),
            pltpu.VMEM((rows, width), jnp.float32),
            pltpu.VMEM((2, rows, width), low),
            pltpu.VMEM((2, rows, 2 * width), low),
            pltpu.VMEM((2, rows, model_dim), low),
            pltpu.VMEM((rows, 128), jnp.float32),
            held(4),
            held(16),
            held(16),
            held(8),
            held(4),
            held(4),
            held(4),
        ]
        + [dma((4,)), dma((4,)), dma((4,)), dma((8,)), dma((16,)), dma((16,)), dma((16,)), dma]
        + [dma((4,)), dma((6,)), dma((8,)), dma((7,)), dma((7,))]
        + [dma((16,)), dma((16,)), dma((8,)), dma((8,))]
        + [dma((4,))] * 6,
        compiler_params=pltpu.CompilerParams(
            collective_id=cid, has_side_effects=True, vmem_limit_bytes=63 * 2**20
        ),
        name="experts",
    )(x_cols, grads_all, kept_rows, *weights)


def tp_total(value):
    return lax.psum(value, "tp")


def kept_choice(expert_ids, pair_order, expert_total, capacity):
    tok_count, top_count = expert_ids.shape
    pair_count = tok_count * top_count
    order = pair_order.reshape(-1)
    pairs = jnp.arange(pair_count, dtype=jnp.int32)
    turn = jnp.sum(jnp.where(order[None, :] == pairs[:, None], pairs[None, :], 0), axis=1)
    turn = turn.reshape(tok_count, top_count)
    picked = expert_ids[:, :, None] == jnp.arange(expert_total, dtype=jnp.int32)[None, None, :]
    turn_of = jnp.sum(jnp.where(picked, turn[:, :, None], 0), axis=1)
    named = jnp.any(picked, axis=1)
    turn_of = jnp.where(named, turn_of, pair_count)
    slot = jnp.sum((turn_of[None, :, :] < turn_of[:, None, :]).astype(jnp.int32), axis=1)
    return (named & (slot < capacity)).astype(jnp.float32)


def dense_plan(
    tokens,
    out_grad,
    first_gain,
    query_weight,
    key_weight,
    value_weight,
    query_bias,
    key_bias,
    value_bias,
    output_weight,
    second_gain,
    router_weight,
    shared_gate_weight,
    shared_up_weight,
    shared_down_weight,
    switch_vector,
    expert_gate_weight,
    expert_up_weight,
    expert_down_weight,
    expert_ids,
    pair_order,
):
    ep, tp = lax.axis_index("ep"), lax.axis_index("tp")
    tok_count, col_width = tokens.shape
    model_dim = query_weight.shape[0]
    sources = lax.axis_size("ep")
    place_in_seq = ep % SPAN
    has_earlier = place_in_seq > 0
    expert_total = router_weight.shape[1]
    capacity = 9 * tok_count * expert_ids.shape[1] // (8 * expert_total)
    head_count = query_weight.shape[1] // HD
    score_scale = HD ** (-0.5)
    expert_width = expert_gate_weight.shape[2]
    shared_width = shared_gate_weight.shape[1] // sources
    width = expert_width + shared_width

    def own_cols(vector):
        return lax.dynamic_slice_in_dim(vector, tp * col_width, col_width, vector.ndim - 1)

    kept_own = kept_choice(expert_ids, pair_order, expert_total, capacity)
    grads_all = gather_all(out_grad, 2)

    inputs_full = gather_tp(tokens, 0).astype(jnp.float32)
    unit_one, inv_one = row_stats(inputs_full)
    normed_one = (unit_one * first_gain).astype(jnp.bfloat16)
    query_lin = jnp.dot(normed_one, query_weight, preferred_element_type=jnp.float32) + query_bias
    key_lin = jnp.dot(normed_one, key_weight, preferred_element_type=jnp.float32) + key_bias
    value_lin = jnp.dot(normed_one, value_weight, preferred_element_type=jnp.float32) + value_bias
    cosine, sine_part = rope_tables(tok_count, HD, place_in_seq * tok_count)
    queries = rotate(query_lin.reshape(tok_count, head_count, HD), cosine, sine_part).astype(
        jnp.bfloat16
    )
    keys_rot = rotate(key_lin.reshape(tok_count, head_count, HD), cosine, sine_part).astype(
        jnp.bfloat16
    )
    values_all = value_lin.reshape(tok_count, head_count, HD).astype(jnp.bfloat16)
    earlier_keys, earlier_values = passed_along((keys_rot, values_all), "ep", 1)
    keys_both = jnp.concatenate([earlier_keys, keys_rot], axis=0)
    values_both = jnp.concatenate([earlier_values, values_all], axis=0)
    blocks = jnp.arange(tok_count) // BLOCK
    local_allowed = blocks[None, :] <= blocks[:, None]
    remote_allowed = jnp.broadcast_to(has_earlier, (tok_count, tok_count))
    allowed = jnp.concatenate([remote_allowed, local_allowed], axis=1)[None]

    def attention_scores():
        scored = (
            jnp.einsum("qhd,khd->hqk", queries, keys_both, preferred_element_type=jnp.float32)
            * score_scale
        )
        return jnp.where(allowed, scored, masked_score)

    scores = attention_scores()
    row_max = jnp.max(scores, axis=-1, keepdims=True)
    powers = jnp.exp(scores - row_max)
    totals = jnp.sum(powers, axis=-1, keepdims=True)
    log_total = row_max + jnp.log(totals)
    probs_low = (powers / totals).astype(jnp.bfloat16)
    context = jnp.einsum("hqk,khd->qhd", probs_low, values_both, preferred_element_type=jnp.float32)
    context = context.reshape(tok_count, head_count * HD).astype(jnp.bfloat16)
    attn_part = jnp.dot(context, output_weight, preferred_element_type=jnp.float32)
    attended = scatter_tp(attn_part.astype(jnp.bfloat16), 1)

    hidden_cols = tokens.astype(jnp.float32) + attended
    squares = tp_total(jnp.sum(hidden_cols * hidden_cols, axis=-1, keepdims=True))
    inv_two = lax.rsqrt(squares / model_dim + norm_eps)
    unit_two = hidden_cols * inv_two
    second_cols = own_cols(second_gain)
    normed_cols = (unit_two * second_cols).astype(jnp.bfloat16)

    def shared_rows(weight):
        return lax.dynamic_slice_in_dim(weight, ep * shared_width, shared_width, 1).T

    extra_rows = jnp.concatenate([router_weight.T, switch_vector[None, :]], axis=0)
    extra_rows = jnp.pad(extra_rows, ((0, 16 - extra_rows.shape[0]), (0, 0)))
    kept_rows = jnp.pad(kept_own.T, ((0, 16 - expert_total), (0, 0))).astype(jnp.bfloat16)
    normed_all, hidden_all, both_all, out_part, reduced, logit_tile = experts(
        normed_cols,
        grads_all,
        kept_rows,
        [
            expert_gate_weight[0].T,
            shared_rows(shared_gate_weight),
            extra_rows,
            expert_up_weight[0].T,
            shared_rows(shared_up_weight),
            expert_down_weight[0],
            shared_down_weight,
        ],
        expert_total,
        4,
    )
    padded = hidden_all.shape[1]
    ffn_cols = lax.psum_scatter(
        lax.psum_scatter(out_part, "tp", scatter_dimension=1, tiled=True),
        "ep",
        scatter_dimension=0,
        tiled=True,
    )
    layer_out = (hidden_cols + ffn_cols.astype(jnp.float32)).astype(jnp.bfloat16)
    down_grad = inner_rows(hidden_all[:, :width], grads_all)
    gate_rows_grad = inner_rows(both_all[:, :width], normed_all)
    up_rows_grad = inner_rows(both_all[:, padded : padded + width], normed_all)
    expert_down_grad = down_grad[None, :expert_width]
    expert_gate_grad = gate_rows_grad[:expert_width].T[None]
    expert_up_grad = up_rows_grad[:expert_width].T[None]
    shared_parts = jnp.stack(
        [
            gate_rows_grad[expert_width:],
            up_rows_grad[expert_width:],
            down_grad[expert_width:],
        ]
    ).astype(jnp.bfloat16)
    shared_parts = shared_parts.reshape(3, shared_width, sources, -1).transpose(2, 0, 1, 3)
    shared_parts = lax.all_to_all(shared_parts, "ep", split_axis=0, concat_axis=0, tiled=True)
    shared_parts = shared_parts.transpose(1, 0, 2, 3).reshape(3, sources * shared_width, -1)
    shared_parts = shared_parts.astype(jnp.float32)
    shared_gate_grad = shared_parts[0].T
    shared_up_grad = shared_parts[1].T
    shared_down_grad = shared_parts[2]

    normed_grad = reduced[:tok_count]
    probs_grad = reduced[tok_count : tok_count + expert_total].T * kept_own
    switch_grad = reduced[tok_count + expert_total]
    logit_at = width - (padded - 128)
    probs_own = softmax_rows(logit_tile[:, logit_at : logit_at + expert_total])
    switch = jax.nn.sigmoid(logit_tile[:, logit_at + expert_total])
    logit_grad = (
        probs_own * (probs_grad - jnp.sum(probs_own * probs_grad, axis=-1, keepdims=True))
    ).astype(jnp.bfloat16)
    router_grad = inner_rows(normed_cols, logit_grad)
    switch_lin_grad = switch_grad * switch * (1.0 - switch)
    switch_vector_grad = jnp.dot(switch_lin_grad, normed_cols, preferred_element_type=jnp.float32)
    router_cols = lax.dynamic_slice_in_dim(router_weight, tp * col_width, col_width, 0)
    normed_grad = normed_grad + times_transpose(logit_grad, router_cols)
    normed_grad = (
        normed_grad
        + switch_lin_grad[:, None] * own_cols(switch_vector).astype(jnp.float32)[None, :]
    )
    second_gain_grad = jnp.sum(normed_grad * unit_two, axis=0)
    scaled_two = normed_grad * second_cols
    mean_two = tp_total(jnp.sum(scaled_two * unit_two, axis=-1, keepdims=True)) / model_dim
    hidden_grad_cols = out_grad.astype(jnp.float32) + inv_two * (scaled_two - unit_two * mean_two)

    attended_grad = gather_tp(hidden_grad_cols.astype(jnp.bfloat16), 0)
    output_grad = inner_rows(attended_grad, context)
    output_grad = lax.psum_scatter(
        output_grad.astype(jnp.bfloat16), "ep", scatter_dimension=0, tiled=True
    )
    output_grad = output_grad.astype(jnp.float32).T
    context_grad = (
        times_transpose(attended_grad, output_weight)
        .astype(jnp.bfloat16)
        .reshape(tok_count, head_count, HD)
    )
    scores = attention_scores()
    attn_probs = jnp.exp(scores - log_total)
    probs_again = attn_probs.astype(jnp.bfloat16)
    probs_grad_att = jnp.einsum(
        "qhd,khd->hqk", context_grad, values_both, preferred_element_type=jnp.float32
    )
    values_both_grad = jnp.einsum(
        "hqk,qhd->khd", probs_again, context_grad, preferred_element_type=jnp.float32
    )
    scores_grad = (
        attn_probs * (probs_grad_att - jnp.sum(attn_probs * probs_grad_att, axis=-1, keepdims=True))
    ).astype(jnp.bfloat16)
    queries_grad = (
        jnp.einsum("hqk,khd->qhd", scores_grad, keys_both, preferred_element_type=jnp.float32)
        * score_scale
    )
    keys_both_grad = (
        jnp.einsum("hqk,qhd->khd", scores_grad, queries, preferred_element_type=jnp.float32)
        * score_scale
    )
    later_keys_grad, later_values_grad = passed_along(
        (
            keys_both_grad[:tok_count].astype(jnp.bfloat16),
            values_both_grad[:tok_count].astype(jnp.bfloat16),
        ),
        "ep",
        -1,
    )
    keep_later = jnp.where(has_earlier, 0.0, 1.0).astype(jnp.float32)
    keys_grad = keys_both_grad[tok_count:] + keep_later * later_keys_grad
    values_grad = values_both_grad[tok_count:] + keep_later * later_values_grad
    value_lin_grad = values_grad.reshape(tok_count, head_count * HD).astype(jnp.bfloat16)
    query_lin_grad = (
        rotate(queries_grad, cosine, -sine_part)
        .reshape(tok_count, head_count * HD)
        .astype(jnp.bfloat16)
    )
    key_lin_grad = (
        rotate(keys_grad, cosine, -sine_part)
        .reshape(tok_count, head_count * HD)
        .astype(jnp.bfloat16)
    )
    lin_grads = jnp.concatenate([query_lin_grad, key_lin_grad, value_lin_grad], axis=1)
    lin_width = head_count * HD
    normed_one_grad = times_transpose(query_lin_grad, query_weight) + times_transpose(
        key_lin_grad, key_weight
    )
    normed_one_grad = normed_one_grad + times_transpose(value_lin_grad, value_weight)
    normed_one_cols = scatter_tp(normed_one_grad.astype(jnp.bfloat16), 1)
    unit_cols = tokens.astype(jnp.float32) * inv_one
    first_cols = own_cols(first_gain)
    first_gain_grad = jnp.sum(normed_one_cols * unit_cols, axis=0)
    scaled_one = normed_one_cols * first_cols
    mean_one = tp_total(jnp.sum(scaled_one * unit_cols, axis=-1, keepdims=True)) / model_dim
    tokens_grad = (hidden_grad_cols + inv_one * (scaled_one - unit_cols * mean_one)).astype(
        jnp.bfloat16
    )

    small = jnp.concatenate(
        [first_gain_grad[None], second_gain_grad[None], switch_vector_grad[None], router_grad.T],
        axis=0,
    )
    small_rows = small.shape[0]
    small = jnp.concatenate([jnp.sum(lin_grads.astype(jnp.float32), axis=0), small.reshape(-1)])
    small = jnp.pad(small, (0, 16 * 3 * lin_width - small.shape[0])).reshape(16, 3 * lin_width)
    weight_grads = scatter_ep(
        inner_rows(normed_one, lin_grads).astype(jnp.bfloat16), small.astype(jnp.bfloat16), 5
    )
    share = model_dim // sources
    small = weight_grads[share:].reshape(-1)
    weight_grads = weight_grads[:share]
    bias_width = HD // sources
    bias_sums = lax.dynamic_slice_in_dim(
        small[: 3 * lin_width].reshape(3, head_count, HD), ep * bias_width, bias_width, 2
    )
    small = small[3 * lin_width : 3 * lin_width + small_rows * col_width]
    spread = lax.all_gather(small.reshape(small_rows, col_width), "tp", axis=1, tiled=True)
    spread = lax.dynamic_slice_in_dim(spread, ep * share, share, 1)
    return (
        layer_out,
        tokens_grad,
        spread[0],
        weight_grads[:, :lin_width],
        weight_grads[:, lin_width : 2 * lin_width],
        weight_grads[:, 2 * lin_width :],
        bias_sums[0],
        bias_sums[1],
        bias_sums[2],
        output_grad,
        spread[1],
        spread[3:].T,
        shared_gate_grad,
        shared_up_grad,
        shared_down_grad,
        spread[2],
        expert_gate_grad,
        expert_up_grad,
        expert_down_grad,
    )


def solution(mesh):
    plan = dense_plan if dict(mesh.shape) == {"ep": 8, "tp": 4} else slot_plan
    return jax.shard_map(
        plan,
        mesh=mesh,
        in_specs=(
            P("ep", "tp"),
            P("ep", "tp"),
            P(),
            P(None, "tp"),
            P(None, "tp"),
            P(None, "tp"),
            P("tp"),
            P("tp"),
            P("tp"),
            P("tp", None),
            P(),
            P(),
            P(None, "tp"),
            P(None, "tp"),
            P("tp", None),
            P(),
            P("ep", None, "tp"),
            P("ep", None, "tp"),
            P("ep", "tp", None),
            P("ep", None),
            P("ep", None),
        ),
        out_specs=(
            P("ep", "tp"),
            P("ep", "tp"),
            P("ep"),
            P("ep", "tp"),
            P("ep", "tp"),
            P("ep", "tp"),
            P("tp", "ep"),
            P("tp", "ep"),
            P("tp", "ep"),
            P("tp", "ep"),
            P("ep"),
            P("ep", None),
            P("ep", "tp"),
            P("ep", "tp"),
            P("tp", "ep"),
            P("ep"),
            P("ep", None, "tp"),
            P("ep", None, "tp"),
            P("ep", "tp", None),
        ),
        check_vma=False,
    )
```

```python
import functools
import math

import jax
import jax.numpy as jnp
from jax import lax
from jax.experimental import pallas as pl
from jax.experimental.pallas import tpu as pltpu
from jax.sharding import PartitionSpec as P

HD = 128
BLOCK = 256
SPAN = 2


rope_theta = 1000000.0
norm_eps = 1e-06
masked_score = -1e30


def passed_along(value, axis, steps):
    count = lax.axis_size(axis)
    leading, last = (max(0, -steps), min(count, count - steps))
    return lax.ppermute(value, axis, [(source, source + steps) for source in range(leading, last)])


def rope_tables(row_count, head_dim, first_position):
    positions = jnp.arange(row_count, dtype=jnp.float32) + first_position.astype(jnp.float32)
    frequency = jnp.exp(
        jnp.arange(head_dim // 2, dtype=jnp.float32) * (-2.0 * math.log(rope_theta) / head_dim)
    )
    angles = positions[:, None] * frequency[None, :]
    return (jnp.cos(angles)[:, None, :], jnp.sin(angles)[:, None, :])


def rotate(values, cosine, sine_part):
    half_dim = values.shape[-1] // 2
    first_half = values[..., :half_dim]
    second_half = values[..., half_dim:]
    return jnp.concatenate(
        [
            first_half * cosine - second_half * sine_part,
            second_half * cosine + first_half * sine_part,
        ],
        axis=-1,
    )


def inner_rows(left_side, right_side):
    return lax.dot_general(
        left_side, right_side, (((0,), (0,)), ((), ())), preferred_element_type=jnp.float32
    )


def times_transpose(left_side, right_side):
    return lax.dot_general(
        left_side, right_side, (((1,), (1,)), ((), ())), preferred_element_type=jnp.float32
    )


def row_stats(values):
    inv_rms = lax.rsqrt(jnp.mean(values * values, axis=-1, keepdims=True) + norm_eps)
    return (values * inv_rms, inv_rms)


def norm_back(grad_rows, unit_rows, inv_rms, gain_vec):
    scaled = grad_rows * gain_vec
    return inv_rms * (scaled - unit_rows * jnp.mean(scaled * unit_rows, axis=-1, keepdims=True))


def softmax_rows(scores):
    row_max = jnp.max(scores, axis=-1, keepdims=True)
    powers = jnp.exp(scores - row_max)
    return powers / jnp.sum(powers, axis=-1, keepdims=True)


def to_experts(block_rows, local_count):
    sources, span_rows, col_count = block_rows.shape
    slot_count = span_rows // local_count
    shaped = block_rows.reshape(sources, local_count, slot_count, col_count)
    return shaped.swapaxes(0, 1).reshape(local_count, sources * slot_count, col_count)


def to_sources(block_rows, sources):
    local_count, rows_all, col_count = block_rows.shape
    slot_count = rows_all // sources
    shaped = block_rows.reshape(local_count, sources, slot_count, col_count)
    return shaped.swapaxes(0, 1).reshape(sources, local_count * slot_count, col_count)


def deliver(block_rows):
    arrived = lax.all_to_all(block_rows, "ep", split_axis=0, concat_axis=0, tiled=True)
    return arrived


def collect(block_rows):
    return lax.all_to_all(block_rows, "ep", split_axis=0, concat_axis=0, tiled=True)


def slot_plan(
    tokens,
    out_grad,
    first_gain,
    query_weight,
    key_weight,
    value_weight,
    query_bias,
    key_bias,
    value_bias,
    output_weight,
    second_gain,
    router_weight,
    shared_gate_weight,
    shared_up_weight,
    shared_down_weight,
    switch_vector,
    expert_gate_weight,
    expert_up_weight,
    expert_down_weight,
    expert_ids,
    pair_order,
):
    whole_in, whole_grad = (
        lax.all_gather(tokens, "tp", axis=1, tiled=True),
        lax.all_gather(out_grad, "tp", axis=1, tiled=True),
    )
    tok_count = whole_in.shape[0]
    model_dim = whole_in.shape[1]
    col_width = tokens.shape[1]
    col_start = lax.axis_index("tp") * col_width
    sources = lax.axis_size("ep")
    place_in_seq = lax.axis_index("ep") % SPAN
    has_earlier = place_in_seq > 0
    local_experts = expert_gate_weight.shape[0]
    expert_total = router_weight.shape[1]
    top_count = expert_ids.shape[1]
    pair_count = tok_count * top_count
    capacity = 9 * pair_count // (8 * expert_total)
    head_count = query_weight.shape[1] // HD
    score_scale = HD ** (-0.5)
    inputs_full = whole_in.astype(jnp.float32)
    unit_one, inv_one = row_stats(inputs_full)
    normed_one = (unit_one * first_gain).astype(jnp.bfloat16)
    query_lin = jnp.dot(normed_one, query_weight, preferred_element_type=jnp.float32) + query_bias
    key_lin = jnp.dot(normed_one, key_weight, preferred_element_type=jnp.float32) + key_bias
    value_lin = jnp.dot(normed_one, value_weight, preferred_element_type=jnp.float32) + value_bias
    cosine, sine_part = rope_tables(tok_count, HD, place_in_seq * tok_count)
    queries = rotate(query_lin.reshape(tok_count, head_count, HD), cosine, sine_part).astype(
        jnp.bfloat16
    )
    keys_rot = rotate(key_lin.reshape(tok_count, head_count, HD), cosine, sine_part).astype(
        jnp.bfloat16
    )
    values_all = value_lin.reshape(tok_count, head_count, HD).astype(jnp.bfloat16)
    earlier_keys, earlier_values = passed_along((keys_rot, values_all), "ep", 1)
    keys_both = jnp.concatenate([earlier_keys, keys_rot], axis=0)
    values_both = jnp.concatenate([earlier_values, values_all], axis=0)
    blocks = jnp.arange(tok_count) // BLOCK
    local_allowed = blocks[None, :] <= blocks[:, None]
    remote_allowed = jnp.broadcast_to(has_earlier, (tok_count, tok_count))
    allowed = jnp.concatenate([remote_allowed, local_allowed], axis=1)[None]

    def attention_scores():
        scored = (
            jnp.einsum("qhd,khd->hqk", queries, keys_both, preferred_element_type=jnp.float32)
            * score_scale
        )
        return jnp.where(allowed, scored, masked_score)

    scores = attention_scores()
    row_max = jnp.max(scores, axis=-1, keepdims=True)
    powers = jnp.exp(scores - row_max)
    totals = jnp.sum(powers, axis=-1, keepdims=True)
    log_total = row_max + jnp.log(totals)
    probs_low = (powers / totals).astype(jnp.bfloat16)
    context = jnp.einsum("hqk,khd->qhd", probs_low, values_both, preferred_element_type=jnp.float32)
    context = context.reshape(tok_count, head_count * HD).astype(jnp.bfloat16)
    attn_part = jnp.dot(context, output_weight, preferred_element_type=jnp.float32)
    attended = lax.psum(attn_part, "tp")
    hidden_one = inputs_full + attended
    unit_two, inv_two = row_stats(hidden_one)
    normed_two = (unit_two * second_gain).astype(jnp.bfloat16)
    logits = jnp.dot(normed_two, router_weight, preferred_element_type=jnp.float32)
    router_probs = softmax_rows(logits)
    gate_values = jnp.take_along_axis(router_probs, expert_ids, axis=1)
    switch = jax.nn.sigmoid(jnp.dot(normed_two, switch_vector, preferred_element_type=jnp.float32))
    flat_ids = expert_ids.reshape(-1)
    turn_order = pair_order.reshape(-1)
    in_turn = flat_ids[turn_order]
    onehot = (in_turn[:, None] == jnp.arange(expert_total, dtype=jnp.int32)[None, :]).astype(
        jnp.int32
    )
    earlier = jnp.cumsum(onehot, axis=0) - onehot
    turn_slot = jnp.sum(earlier * onehot, axis=1)
    slot_index = jnp.zeros((pair_count,), jnp.int32).at[turn_order].set(turn_slot)
    kept_pair = slot_index < capacity
    slot_rows = expert_total * capacity
    target = jnp.where(kept_pair, flat_ids * capacity + slot_index, slot_rows)
    pair_token = jnp.arange(pair_count, dtype=jnp.int32) // top_count
    slot_token = (
        jnp.full((slot_rows + 1,), tok_count, jnp.int32).at[target].set(pair_token)[:slot_rows]
    )
    slot_gate = (
        jnp.zeros((slot_rows + 1,), jnp.float32).at[target].set(gate_values.reshape(-1))[:slot_rows]
    )
    padded_two = jnp.concatenate([normed_two, jnp.zeros((1, model_dim), jnp.bfloat16)], axis=0)
    send_rows = padded_two[slot_token].reshape(sources, local_experts * capacity, model_dim)
    expert_rows = to_experts(deliver(send_rows), local_experts)
    gate_lin = jnp.einsum(
        "erd,edf->erf", expert_rows, expert_gate_weight, preferred_element_type=jnp.float32
    )
    up_lin = jnp.einsum(
        "erd,edf->erf", expert_rows, expert_up_weight, preferred_element_type=jnp.float32
    )
    gate_sig = jax.nn.sigmoid(gate_lin)
    gate_act = gate_lin * gate_sig
    expert_hidden = (gate_act * up_lin).astype(jnp.bfloat16)
    expert_part = jnp.einsum(
        "erf,efd->erd", expert_hidden, expert_down_weight, preferred_element_type=jnp.float32
    )
    shared_gate_lin = jnp.dot(normed_two, shared_gate_weight, preferred_element_type=jnp.float32)
    shared_up_lin = jnp.dot(normed_two, shared_up_weight, preferred_element_type=jnp.float32)
    shared_sig = jax.nn.sigmoid(shared_gate_lin)
    shared_act = shared_gate_lin * shared_sig
    shared_hidden = (shared_act * shared_up_lin).astype(jnp.bfloat16)
    shared_part = jnp.dot(shared_hidden, shared_down_weight, preferred_element_type=jnp.float32)
    expert_cols, shared_cols = (
        lax.psum_scatter(expert_part.reshape(-1, model_dim), "tp", scatter_dimension=1, tiled=True),
        lax.psum_scatter(shared_part, "tp", scatter_dimension=1, tiled=True),
    )
    returned = collect(
        to_sources(expert_cols.astype(jnp.bfloat16).reshape(local_experts, -1, col_width), sources)
    )
    back_flat = jnp.concatenate(
        [returned.reshape(slot_rows, col_width), jnp.zeros((1, col_width), jnp.bfloat16)], axis=0
    )
    pair_out = back_flat[target].astype(jnp.float32).reshape(tok_count, top_count, col_width)
    routed = jnp.sum(gate_values[:, :, None] * pair_out, axis=1)
    hidden_cols = lax.dynamic_slice_in_dim(hidden_one, col_start, col_width, 1)
    layer_out = (hidden_cols + switch[:, None] * shared_cols + routed).astype(jnp.bfloat16)
    grad_full = whole_grad.astype(jnp.float32)
    grad_cols = out_grad.astype(jnp.float32)
    gate_part = jnp.sum(pair_out * grad_cols[:, None, :], axis=-1)
    switch_part = jnp.sum(grad_cols * shared_cols, axis=-1)
    gate_grad, switch_grad = lax.psum((gate_part, switch_part), "tp")
    padded_grad = jnp.concatenate([whole_grad, jnp.zeros((1, model_dim), jnp.bfloat16)], axis=0)
    send_grads = (slot_gate[:, None] * padded_grad[slot_token].astype(jnp.float32)).astype(
        jnp.bfloat16
    )
    expert_grads = to_experts(
        deliver(send_grads.reshape(sources, local_experts * capacity, model_dim)), local_experts
    )
    hidden_grad = jnp.einsum(
        "erd,efd->erf", expert_grads, expert_down_weight, preferred_element_type=jnp.float32
    )
    gate_lin_grad = (hidden_grad * up_lin * gate_sig * (1.0 + gate_lin * (1.0 - gate_sig))).astype(
        jnp.bfloat16
    )
    up_lin_grad = (hidden_grad * gate_act).astype(jnp.bfloat16)
    expert_down_grad = jnp.einsum(
        "erf,erd->efd", expert_hidden, expert_grads, preferred_element_type=jnp.float32
    )
    expert_gate_grad = jnp.einsum(
        "erd,erf->edf", expert_rows, gate_lin_grad, preferred_element_type=jnp.float32
    )
    expert_up_grad = jnp.einsum(
        "erd,erf->edf", expert_rows, up_lin_grad, preferred_element_type=jnp.float32
    )
    rows_grad = jnp.einsum(
        "erf,edf->erd", gate_lin_grad, expert_gate_weight, preferred_element_type=jnp.float32
    )
    rows_grad = rows_grad + jnp.einsum(
        "erf,edf->erd", up_lin_grad, expert_up_weight, preferred_element_type=jnp.float32
    )
    rows_grad_cols = lax.psum_scatter(
        rows_grad.reshape(-1, model_dim), "tp", scatter_dimension=1, tiled=True
    )
    returned_grad = collect(
        to_sources(
            rows_grad_cols.astype(jnp.bfloat16).reshape(local_experts, -1, col_width), sources
        )
    )
    back_grad = jnp.concatenate(
        [returned_grad.reshape(slot_rows, col_width), jnp.zeros((1, col_width), jnp.bfloat16)],
        axis=0,
    )
    routed_grad = jnp.sum(
        back_grad[target].astype(jnp.float32).reshape(tok_count, top_count, col_width), axis=1
    )
    shared_out_grad = (switch[:, None] * grad_full).astype(jnp.bfloat16)
    shared_hidden_grad = times_transpose(shared_out_grad, shared_down_weight)
    shared_gate_lin_grad = (
        shared_hidden_grad
        * shared_up_lin
        * shared_sig
        * (1.0 + shared_gate_lin * (1.0 - shared_sig))
    ).astype(jnp.bfloat16)
    shared_up_lin_grad = (shared_hidden_grad * shared_act).astype(jnp.bfloat16)
    shared_down_grad = inner_rows(shared_hidden, shared_out_grad)
    shared_gate_grad = inner_rows(normed_two, shared_gate_lin_grad)
    shared_up_grad = inner_rows(normed_two, shared_up_lin_grad)
    normed_grad = times_transpose(shared_gate_lin_grad, shared_gate_weight) + times_transpose(
        shared_up_lin_grad, shared_up_weight
    )
    normed_grad = normed_grad + lax.dynamic_update_slice_in_dim(
        jnp.zeros_like(normed_grad), routed_grad, col_start, 1
    )
    normed_grad = lax.psum(normed_grad, "tp")
    picked = (
        expert_ids[:, :, None] == jnp.arange(expert_total, dtype=jnp.int32)[None, None, :]
    ).astype(jnp.float32)
    probs_grad = jnp.sum(picked * gate_grad[:, :, None], axis=1)
    logit_grad = (
        router_probs * (probs_grad - jnp.sum(router_probs * probs_grad, axis=-1, keepdims=True))
    ).astype(jnp.bfloat16)
    router_grad = inner_rows(normed_two, logit_grad)
    switch_lin_grad = switch_grad * switch * (1.0 - switch)
    switch_vector_grad = jnp.dot(switch_lin_grad, normed_two, preferred_element_type=jnp.float32)
    normed_grad = normed_grad + times_transpose(logit_grad, router_weight)
    normed_grad = (
        normed_grad + switch_lin_grad[:, None] * switch_vector.astype(jnp.float32)[None, :]
    )
    second_gain_grad = jnp.sum(normed_grad * unit_two, axis=0)
    hidden_grad_one = grad_full + norm_back(normed_grad, unit_two, inv_two, second_gain)
    attended_grad = hidden_grad_one.astype(jnp.bfloat16)
    output_grad = inner_rows(context, attended_grad)
    context_grad = (
        times_transpose(attended_grad, output_weight)
        .astype(jnp.bfloat16)
        .reshape(tok_count, head_count, HD)
    )
    scores = attention_scores()
    attn_probs = jnp.exp(scores - log_total)
    probs_again = attn_probs.astype(jnp.bfloat16)
    probs_grad_att = jnp.einsum(
        "qhd,khd->hqk", context_grad, values_both, preferred_element_type=jnp.float32
    )
    values_both_grad = jnp.einsum(
        "hqk,qhd->khd", probs_again, context_grad, preferred_element_type=jnp.float32
    )
    scores_grad = (
        attn_probs * (probs_grad_att - jnp.sum(attn_probs * probs_grad_att, axis=-1, keepdims=True))
    ).astype(jnp.bfloat16)
    queries_grad = (
        jnp.einsum("hqk,khd->qhd", scores_grad, keys_both, preferred_element_type=jnp.float32)
        * score_scale
    )
    keys_both_grad = (
        jnp.einsum("hqk,qhd->khd", scores_grad, queries, preferred_element_type=jnp.float32)
        * score_scale
    )
    later_keys_grad, later_values_grad = passed_along(
        (keys_both_grad[:tok_count], values_both_grad[:tok_count]), "ep", -1
    )
    keep_later = jnp.where(has_earlier, 0.0, 1.0).astype(jnp.float32)
    keys_grad = keys_both_grad[tok_count:] + keep_later * later_keys_grad
    values_grad = values_both_grad[tok_count:] + keep_later * later_values_grad
    value_lin_grad = values_grad.reshape(tok_count, head_count * HD).astype(jnp.bfloat16)
    query_lin_grad = (
        rotate(queries_grad, cosine, -sine_part)
        .reshape(tok_count, head_count * HD)
        .astype(jnp.bfloat16)
    )
    key_lin_grad = (
        rotate(keys_grad, cosine, -sine_part)
        .reshape(tok_count, head_count * HD)
        .astype(jnp.bfloat16)
    )
    query_grad = inner_rows(normed_one, query_lin_grad)
    key_grad = inner_rows(normed_one, key_lin_grad)
    value_grad = inner_rows(normed_one, value_lin_grad)
    query_bias_grad = jnp.sum(query_lin_grad.astype(jnp.float32), axis=0).reshape(head_count, HD)
    key_bias_grad = jnp.sum(key_lin_grad.astype(jnp.float32), axis=0).reshape(head_count, HD)
    value_bias_grad = jnp.sum(value_lin_grad.astype(jnp.float32), axis=0).reshape(head_count, HD)
    normed_one_grad = times_transpose(query_lin_grad, query_weight) + times_transpose(
        key_lin_grad, key_weight
    )
    normed_one_grad = normed_one_grad + times_transpose(value_lin_grad, value_weight)
    normed_one_grad = lax.psum(normed_one_grad.astype(jnp.bfloat16), "tp").astype(jnp.float32)
    first_gain_grad = jnp.sum(normed_one_grad * unit_one, axis=0)
    input_grad = hidden_grad_one + norm_back(normed_one_grad, unit_one, inv_one, first_gain)
    tokens_grad = lax.dynamic_slice_in_dim(input_grad, col_start, col_width, 1).astype(jnp.bfloat16)
    reduced = (
        lax.psum_scatter(
            first_gain_grad.astype(jnp.bfloat16), "ep", scatter_dimension=0, tiled=True
        ).astype(jnp.float32),
        lax.psum_scatter(
            query_grad.astype(jnp.bfloat16), "ep", scatter_dimension=0, tiled=True
        ).astype(jnp.float32),
        lax.psum_scatter(
            key_grad.astype(jnp.bfloat16), "ep", scatter_dimension=0, tiled=True
        ).astype(jnp.float32),
        lax.psum_scatter(
            value_grad.astype(jnp.bfloat16), "ep", scatter_dimension=0, tiled=True
        ).astype(jnp.float32),
        lax.psum_scatter(
            query_bias_grad.astype(jnp.bfloat16), "ep", scatter_dimension=1, tiled=True
        ).astype(jnp.float32),
        lax.psum_scatter(
            key_bias_grad.astype(jnp.bfloat16), "ep", scatter_dimension=1, tiled=True
        ).astype(jnp.float32),
        lax.psum_scatter(
            value_bias_grad.astype(jnp.bfloat16), "ep", scatter_dimension=1, tiled=True
        ).astype(jnp.float32),
        lax.psum_scatter(
            output_grad.astype(jnp.bfloat16), "ep", scatter_dimension=1, tiled=True
        ).astype(jnp.float32),
        lax.psum_scatter(
            second_gain_grad.astype(jnp.bfloat16), "ep", scatter_dimension=0, tiled=True
        ).astype(jnp.float32),
        lax.psum_scatter(
            router_grad.astype(jnp.bfloat16), "ep", scatter_dimension=0, tiled=True
        ).astype(jnp.float32),
        lax.psum_scatter(
            shared_gate_grad.astype(jnp.bfloat16), "ep", scatter_dimension=0, tiled=True
        ).astype(jnp.float32),
        lax.psum_scatter(
            shared_up_grad.astype(jnp.bfloat16), "ep", scatter_dimension=0, tiled=True
        ).astype(jnp.float32),
        lax.psum_scatter(
            shared_down_grad.astype(jnp.bfloat16), "ep", scatter_dimension=1, tiled=True
        ).astype(jnp.float32),
        lax.psum_scatter(
            switch_vector_grad.astype(jnp.bfloat16), "ep", scatter_dimension=0, tiled=True
        ).astype(jnp.float32),
    )
    return (
        layer_out,
        tokens_grad,
        reduced[0],
        reduced[1],
        reduced[2],
        reduced[3],
        reduced[4],
        reduced[5],
        reduced[6],
        reduced[7],
        reduced[8],
        reduced[9],
        reduced[10],
        reduced[11],
        reduced[12],
        reduced[13],
        expert_gate_grad,
        expert_up_grad,
        expert_down_grad,
    )


MESH = pl.DeviceIdType.MESH
Z_ORDER = (0, 3, 1, 2)


def place():
    ep, tp = lax.axis_index("ep"), lax.axis_index("tp")
    return ep, tp, ep // 2, lax.rem(ep, 2), tp // 2, lax.rem(tp, 2)


def greet(always, along_z=False):
    barrier = pltpu.get_barrier_semaphore()
    for device in always:
        pl.semaphore_signal(barrier, inc=1, device_id=device, device_id_type=MESH)
    count = len(always)
    if along_z:
        ep, tp, z, _, _, _ = place()

        @pl.when(z < 3)
        def _():
            pl.semaphore_signal(barrier, inc=1, device_id=(ep + 2, tp), device_id_type=MESH)

        @pl.when(z > 0)
        def _():
            pl.semaphore_signal(barrier, inc=1, device_id=(ep - 2, tp), device_id_type=MESH)

        count = count + lax.min(z, 1) + lax.min(3 - z, 1)
    pl.semaphore_wait(barrier, count)


def remote(source, target, send_sem, recv_sem, device):
    return pltpu.make_async_remote_copy(
        src_ref=source,
        dst_ref=target,
        send_sem=send_sem,
        recv_sem=recv_sem,
        device_id=device,
        device_id_type=MESH,
    )


def add_blocks(target, sources, rows):
    step = next(size for size in (80, 64, 48, 16) if rows % size == 0)

    def body(i, carry):
        span = pl.ds(pl.multiple_of(i * step, 16), step)
        total = target[span, :]
        for source in sources:
            total = total + source[span, :].astype(target.dtype)
        target[span, :] = total
        return carry

    lax.fori_loop(0, rows // step, body, 0)


def gather_tp_kernel(x_ref, o_ref, send_sem, recv_sem, own_sem):
    ep, tp, _, _, x, core = place()
    cols = x_ref.shape[1]
    sibling = (ep, tp + 1 - 2 * core)
    across = (ep, tp + 2 - 4 * x)
    greet([sibling, across])
    mine = o_ref.at[:, pl.ds(pl.multiple_of(tp * cols, cols), cols)]
    theirs = o_ref.at[:, pl.ds(pl.multiple_of((tp + 2 - 4 * x) * cols, cols), cols)]
    out_x = remote(x_ref, mine, send_sem.at[0], recv_sem.at[0], across)
    out_s = remote(x_ref, mine, send_sem.at[1], recv_sem.at[1], sibling)
    own = pltpu.make_async_copy(x_ref, mine, own_sem)
    out_x.start()
    out_s.start()
    own.start()
    remote(x_ref, theirs, send_sem.at[0], recv_sem.at[0], across).wait_recv()
    passing = remote(theirs, theirs, send_sem.at[2], recv_sem.at[2], sibling)
    passing.start()
    out_s.wait_recv()
    passing.wait_recv()
    own.wait()
    out_x.wait_send()
    out_s.wait_send()
    passing.wait_send()


def gather_tp(value, cid):
    rows, cols = value.shape
    return pl.pallas_call(
        gather_tp_kernel,
        out_shape=jax.ShapeDtypeStruct((rows, 4 * cols), value.dtype),
        in_specs=[pl.BlockSpec(memory_space=pl.ANY)],
        out_specs=pl.BlockSpec(memory_space=pl.ANY),
        scratch_shapes=[
            pltpu.SemaphoreType.DMA((3,)),
            pltpu.SemaphoreType.DMA((3,)),
            pltpu.SemaphoreType.DMA,
        ],
        compiler_params=pltpu.CompilerParams(collective_id=cid, has_side_effects=True),
        name="gather_tp",
    )(value)


def scatter_tp_kernel(p_ref, o_ref, mine, from_sib, from_x, own_sem, send_sem, recv_sem):
    ep, tp, _, _, x, core = place()
    rows, cols = o_ref.shape
    sibling = (ep, tp + 1 - 2 * core)
    across = (ep, tp + 2 - 4 * x)
    greet([sibling, across])

    def part(x_at, core_at):
        return p_ref.at[:, pl.ds(pl.multiple_of((x_at * 2 + core_at) * cols, cols), cols)]

    sends, owns = [], []
    for i, x_at in enumerate((1 - x, x)):
        owns.append(pltpu.make_async_copy(part(x_at, core), mine.at[i], own_sem.at[i]))
        sends.append(
            remote(part(x_at, 1 - core), from_sib.at[i], send_sem.at[i], recv_sem.at[i], sibling)
        )
        sends[-1].start()
        owns[-1].start()
    owns[0].wait()
    sends[0].wait_recv()
    add_blocks(mine.at[0], [from_sib.at[0]], rows)
    out_x = remote(mine.at[0], from_x, send_sem.at[2], recv_sem.at[2], across)
    out_x.start()
    owns[1].wait()
    sends[1].wait_recv()
    out_x.wait_recv()
    o_ref[...] = jnp.zeros_like(o_ref)
    add_blocks(o_ref, [mine.at[1], from_sib.at[1], from_x], rows)
    out_x.wait_send()
    sends[0].wait_send()
    sends[1].wait_send()


def scatter_tp(value, cid):
    rows, cols = value.shape[0], value.shape[1] // 4
    return pl.pallas_call(
        scatter_tp_kernel,
        out_shape=jax.ShapeDtypeStruct((rows, cols), jnp.float32),
        in_specs=[pl.BlockSpec(memory_space=pl.ANY)],
        out_specs=pl.BlockSpec(memory_space=pltpu.VMEM),
        scratch_shapes=[
            pltpu.VMEM((2, rows, cols), value.dtype),
            pltpu.VMEM((2, rows, cols), value.dtype),
            pltpu.VMEM((rows, cols), value.dtype),
            pltpu.SemaphoreType.DMA((2,)),
            pltpu.SemaphoreType.DMA((3,)),
            pltpu.SemaphoreType.DMA((3,)),
        ],
        compiler_params=pltpu.CompilerParams(
            collective_id=cid, has_side_effects=True, vmem_limit_bytes=32 * 2**20
        ),
        name="scatter_tp",
    )(value)


def lane_peers():
    ep, tp, z, y, x, core = place()
    to_y, to_x = 1 - 2 * y, 1 - 2 * x
    peer_a = (ep + (1 - core) * to_y, tp + core * 2 * to_x)
    peer_b = (ep + core * to_y, tp + (1 - core) * 2 * to_x)
    sibling = (ep, tp + 1 - 2 * core)
    above, below = (ep + 2, tp), (ep - 2, tp)
    return peer_a, peer_b, sibling, above, below


def lane_spot(z_at, da, db, core_at):
    _, _, _, y, x, _ = place()
    y_at = y + (1 - 2 * y) * ((1 - core_at) * da + core_at * db)
    x_at = x + (1 - 2 * x) * (core_at * da + (1 - core_at) * db)
    return z_at * 2 + y_at, x_at * 2 + core_at


def gather_all_kernel(x_ref, o_ref, up_sem, down_sem, a_sem, b_sem, s_sem, recv_sem, sib_sem, own_sem):
    ep, tp, z, y, x, core = place()
    rows, cols = x_ref.shape
    peer_a, peer_b, sibling, above, below = lane_peers()
    greet([peer_a, peer_b, sibling], True)

    def spot(z_at, da, db):
        group, quarter = lane_spot(z_at, da, db, core)
        return o_ref.at[
            pl.ds(pl.multiple_of(group * rows, rows), rows),
            pl.ds(pl.multiple_of(quarter * cols, cols), cols),
        ]

    def at(z_at, da, db):
        return z_at * 4 + da * 2 + db

    def arrived(z_at, da, db):
        block = spot(z_at, da, db)
        remote(block, block, s_sem.at[at(z_at, da, db)], recv_sem.at[at(z_at, da, db)], sibling).wait_recv()

    def up(z_at, source):
        return remote(source, spot(z_at, 0, 0), up_sem.at[z_at], recv_sem.at[at(z_at, 0, 0)], above)

    def down(z_at, source):
        return remote(source, spot(z_at, 0, 0), down_sem.at[z_at], recv_sem.at[at(z_at, 0, 0)], below)

    def over_a(z_at, source):
        return remote(source, spot(z_at, 0, 0), a_sem.at[z_at], recv_sem.at[at(z_at, 1, 0)], peer_a)

    def over_b(z_at, da, source):
        return remote(
            source, spot(z_at, da, 0), b_sem.at[z_at * 2 + da], recv_sem.at[at(z_at, da, 1)], peer_b
        )

    def to_sibling(z_at, da, db, source):
        n = at(z_at, da, db)
        return remote(source, spot(z_at, da, db), s_sem.at[n], sib_sem.at[n], sibling)

    own = pltpu.make_async_copy(x_ref, spot(z, 0, 0), own_sem)
    over_b(z, 0, x_ref).start()
    over_a(z, x_ref).start()

    @pl.when(z < 3)
    def _():
        up(z, x_ref).start()

    @pl.when(z > 0)
    def _():
        down(z, x_ref).start()

    to_sibling(z, 0, 0, x_ref).start()
    own.start()

    def from_a(z_at):
        arrived(z_at, 1, 0)
        block = spot(z_at, 1, 0)
        over_b(z_at, 1, block).start()
        to_sibling(z_at, 1, 0, block).start()

    def from_z(z_at, onward):
        arrived(z_at, 0, 0)
        block = spot(z_at, 0, 0)
        onward(block)
        over_a(z_at, block).start()
        over_b(z_at, 0, block).start()
        to_sibling(z_at, 0, 0, block).start()

    def from_below(z_at):
        def onward(block):
            @pl.when(z < 3)
            def _():
                up(z_at, block).start()

        from_z(z_at, onward)

    def from_above(z_at):
        def onward(block):
            @pl.when(z > 0)
            def _():
                down(z_at, block).start()

        from_z(z_at, onward)

    for d in range(1, 4):

        @pl.when(z >= d)
        def _(d=d):
            from_below(z - d)

        @pl.when(z + d <= 3)
        def _(d=d):
            from_above(z + d)

        if d == 1:
            from_a(z)
        else:

            @pl.when(z >= d - 1)
            def _(d=d):
                from_a(z - d + 1)

            @pl.when(z + d - 1 <= 3)
            def _(d=d):
                from_a(z + d - 1)

    @pl.when(z >= 3)
    def _():
        from_a(z - 3)

    @pl.when(z + 3 <= 3)
    def _():
        from_a(z + 3)

    def from_b(z_at, da):
        arrived(z_at, da, 1)
        to_sibling(z_at, da, 1, spot(z_at, da, 1)).start()

    for da in range(2):
        from_b(z, da)
    for d in range(1, 4):
        for da in range(2):

            @pl.when(z >= d)
            def _(d=d, da=da):
                from_b(z - d, da)

            @pl.when(z + d <= 3)
            def _(d=d, da=da):
                from_b(z + d, da)

    def finish_sibling(i, carry):
        block = spot(0, 0, 0)
        copy = remote(block, block, s_sem.at[i], sib_sem.at[i], sibling)
        copy.wait_recv()
        copy.wait_send()
        return carry

    lax.fori_loop(0, 16, finish_sibling, 0)

    def finish_links(i, carry):
        over_a(i, x_ref).wait_send()
        over_b(i, 0, x_ref).wait_send()
        over_b(i, 1, x_ref).wait_send()

        @pl.when((z < 3) & (i <= z))
        def _():
            up(i, x_ref).wait_send()

        @pl.when((z > 0) & (i >= z))
        def _():
            down(i, x_ref).wait_send()

        return carry

    lax.fori_loop(0, 4, finish_links, 0)
    own.wait()


def gather_all(value, cid):
    rows, cols = value.shape
    return pl.pallas_call(
        gather_all_kernel,
        out_shape=jax.ShapeDtypeStruct((8 * rows, 4 * cols), value.dtype),
        in_specs=[pl.BlockSpec(memory_space=pl.ANY)],
        out_specs=pl.BlockSpec(memory_space=pl.ANY),
        scratch_shapes=[
            pltpu.SemaphoreType.DMA((4,)),
            pltpu.SemaphoreType.DMA((4,)),
            pltpu.SemaphoreType.DMA((4,)),
            pltpu.SemaphoreType.DMA((8,)),
            pltpu.SemaphoreType.DMA((16,)),
            pltpu.SemaphoreType.DMA((16,)),
            pltpu.SemaphoreType.DMA((16,)),
            pltpu.SemaphoreType.DMA,
        ],
        compiler_params=pltpu.CompilerParams(collective_id=cid, has_side_effects=True),
        name="gather_all",
    )(value)


def z_chain(blocks, totals, from_below, from_above, up_send, up_recv, down_send, down_recv, rows, final):
    ep, tp, z, _, _, _ = place()
    above, below = (ep + 2, tp), (ep - 2, tp)

    def up(z_at):
        return remote(totals(z_at), from_below.at[z_at], up_send.at[z_at], up_recv.at[z_at], above)

    def down(z_at):
        return remote(totals(z_at), from_above.at[z_at], down_send.at[z_at], down_recv.at[z_at], below)

    for z_at in Z_ORDER:
        blocks(z_at)

        @pl.when(z_at > z)
        def _(z_at=z_at):
            @pl.when(z > 0)
            def _():
                up(z_at).wait_recv()
                add_blocks(totals(z_at), [from_below.at[z_at]], rows)

            up(z_at).start()

        @pl.when(z_at < z)
        def _(z_at=z_at):
            @pl.when(z < 3)
            def _():
                down(z_at).wait_recv()
                add_blocks(totals(z_at), [from_above.at[z_at]], rows)

            down(z_at).start()

    for z_at in range(4):

        @pl.when(z_at == z)
        def _(z_at=z_at):
            @pl.when(z > 0)
            def _():
                up(z_at).wait_recv()

            @pl.when(z < 3)
            def _():
                down(z_at).wait_recv()

            @pl.when(z == 0)
            def _():
                final(z_at, [from_above.at[z_at]])

            @pl.when(z == 3)
            def _():
                final(z_at, [from_below.at[z_at]])

            @pl.when((z > 0) & (z < 3))
            def _():
                final(z_at, [from_below.at[z_at], from_above.at[z_at]])

    for z_at in range(4):

        @pl.when(z_at > z)
        def _(z_at=z_at):
            up(z_at).wait_send()

        @pl.when(z_at < z)
        def _(z_at=z_at):
            down(z_at).wait_send()


def scatter_all_kernel(
    p_ref,
    o_ref,
    mine,
    from_sib,
    from_b,
    from_a,
    from_below,
    from_above,
    own_sem,
    s_send,
    s_recv,
    b_send,
    b_recv,
    a_send,
    a_recv,
    up_send,
    up_recv,
    down_send,
    down_recv,
):
    ep, tp, z, y, x, core = place()
    rows, cols = o_ref.shape
    peer_a, peer_b, sibling, above, below = lane_peers()
    greet([peer_a, peer_b, sibling], True)

    def part(z_at, da, db, core_at):
        group, quarter = lane_spot(z_at, da, db, core_at)
        return p_ref.at[
            pl.ds(pl.multiple_of(group * rows, rows), rows),
            pl.ds(pl.multiple_of(quarter * cols, cols), cols),
        ]

    def at(z_at, da, db):
        return z_at * 4 + da * 2 + db

    def own(z_at, da, db):
        n = at(z_at, da, db)
        return pltpu.make_async_copy(part(z_at, da, db, core), mine.at[n], own_sem.at[n])

    def to_sibling(z_at, da, db):
        n = at(z_at, da, db)
        return remote(
            part(z_at, da, db, 1 - core), from_sib.at[n], s_send.at[n], s_recv.at[n], sibling
        )

    for da, db in ((1, 1), (0, 1), (1, 0), (0, 0)):
        for z_at in Z_ORDER:
            to_sibling(z_at, da, db).start()
            own(z_at, da, db).start()

    def here(z_at, da, db):
        own(z_at, da, db).wait()
        to_sibling(z_at, da, db).wait_recv()
        return mine.at[at(z_at, da, db)], from_sib.at[at(z_at, da, db)]

    def over_b(z_at, da):
        n = z_at * 2 + da
        return remote(mine.at[at(z_at, da, 1)], from_b.at[n], b_send.at[n], b_recv.at[n], peer_b)

    def over_a(z_at):
        return remote(mine.at[at(z_at, 1, 0)], from_a.at[z_at], a_send.at[z_at], a_recv.at[z_at], peer_a)

    for da in (1, 0):
        for z_at in Z_ORDER:
            own_part, sib_part = here(z_at, da, 1)
            add_blocks(own_part, [sib_part], rows)
            over_b(z_at, da).start()
    for z_at in Z_ORDER:
        own_part, sib_part = here(z_at, 1, 0)
        over_b(z_at, 1).wait_recv()
        add_blocks(own_part, [sib_part, from_b.at[z_at * 2 + 1]], rows)
        over_a(z_at).start()

    def blocks(z_at):
        own_part, sib_part = here(z_at, 0, 0)
        over_b(z_at, 0).wait_recv()
        over_a(z_at).wait_recv()
        add_blocks(own_part, [sib_part, from_b.at[z_at * 2], from_a.at[z_at]], rows)

    def final(z_at, others):
        o_ref[...] = jnp.zeros_like(o_ref)
        add_blocks(o_ref, [mine.at[at(z_at, 0, 0)], *others], rows)

    z_chain(
        blocks,
        lambda z_at: mine.at[at(z_at, 0, 0)],
        from_below,
        from_above,
        up_send,
        up_recv,
        down_send,
        down_recv,
        rows,
        final,
    )
    for z_at in range(4):
        over_a(z_at).wait_send()
        for da in range(2):
            over_b(z_at, da).wait_send()
            for db in range(2):
                to_sibling(z_at, da, db).wait_send()


def scatter_all(value, cid):
    rows, cols = value.shape[0] // 8, value.shape[1] // 4
    dma = pltpu.SemaphoreType.DMA

    def held(count):
        return pltpu.VMEM((count, rows, cols), value.dtype)

    return pl.pallas_call(
        scatter_all_kernel,
        out_shape=jax.ShapeDtypeStruct((rows, cols), jnp.float32),
        in_specs=[pl.BlockSpec(memory_space=pl.ANY)],
        out_specs=pl.BlockSpec(memory_space=pltpu.VMEM),
        scratch_shapes=[held(16), held(16), held(8), held(4), held(4), held(4)]
        + [dma((16,)), dma((16,)), dma((16,)), dma((8,)), dma((8,))]
        + [dma((4,))] * 6,
        compiler_params=pltpu.CompilerParams(
            collective_id=cid, has_side_effects=True, vmem_limit_bytes=48 * 2**20
        ),
        name="scatter_all",
    )(value)


def scatter_ep_kernel(
    p_ref, e_ref, o_ref, mine, from_y, from_below, from_above, own_sem, y_send, y_recv, up_send, up_recv, down_send, down_recv
):
    ep, tp, z, y, _, _ = place()
    rows, extra = p_ref.shape[0] // 8, e_ref.shape[0]
    tall = rows + extra
    across = (ep + 1 - 2 * y, tp)
    greet([across], True)

    def part(z_at, y_at):
        return p_ref.at[pl.ds(pl.multiple_of((z_at * 2 + y_at) * rows, rows), rows), :]

    def own(z_at):
        return (
            pltpu.make_async_copy(part(z_at, y), mine.at[z_at, pl.ds(0, rows)], own_sem.at[z_at]),
            pltpu.make_async_copy(e_ref, mine.at[z_at, pl.ds(rows, extra)], own_sem.at[4 + z_at]),
        )

    def over_y(z_at):
        return (
            remote(
                part(z_at, 1 - y),
                from_y.at[z_at, pl.ds(0, rows)],
                y_send.at[z_at],
                y_recv.at[z_at],
                across,
            ),
            remote(
                e_ref,
                from_y.at[z_at, pl.ds(rows, extra)],
                y_send.at[4 + z_at],
                y_recv.at[4 + z_at],
                across,
            ),
        )

    for z_at in Z_ORDER:
        for copy in over_y(z_at) + own(z_at):
            copy.start()

    def blocks(z_at):
        for copy in own(z_at):
            copy.wait()
        for copy in over_y(z_at):
            copy.wait_recv()
        add_blocks(mine.at[z_at], [from_y.at[z_at]], tall)

    def final(z_at, others):
        o_ref[...] = jnp.zeros_like(o_ref)
        add_blocks(o_ref, [mine.at[z_at], *others], tall)

    z_chain(
        blocks,
        lambda z_at: mine.at[z_at],
        from_below,
        from_above,
        up_send,
        up_recv,
        down_send,
        down_recv,
        tall,
        final,
    )
    for z_at in range(4):
        for copy in over_y(z_at):
            copy.wait_send()


def scatter_ep(value, extra, cid):
    rows, cols = value.shape[0] // 8, value.shape[1]
    tall = rows + extra.shape[0]
    dma = pltpu.SemaphoreType.DMA

    def held():
        return pltpu.VMEM((4, tall, cols), value.dtype)

    return pl.pallas_call(
        scatter_ep_kernel,
        out_shape=jax.ShapeDtypeStruct((tall, cols), jnp.float32),
        in_specs=[pl.BlockSpec(memory_space=pl.ANY)] * 2,
        out_specs=pl.BlockSpec(memory_space=pltpu.VMEM),
        scratch_shapes=[held(), held(), held(), held()] + [dma((8,))] * 3 + [dma((4,))] * 4,
        compiler_params=pltpu.CompilerParams(
            collective_id=cid, has_side_effects=True, vmem_limit_bytes=40 * 2**20
        ),
        name="scatter_ep",
    )(value, extra)


def experts_kernel(
    expert_width,
    shared_width,
    expert_total,
    x_ref,
    g_ref,
    kept_ref,
    expert_gate_ref,
    shared_gate_ref,
    extra_ref,
    expert_up_ref,
    shared_up_ref,
    expert_down_ref,
    shared_down_ref,
    grad_ref,
    ffn_ref,
    logit_ref,
    expert_grads_ref,
    shared_grads_ref,
    all_ref,
    from_sib,
    from_b,
    from_a,
    from_below,
    from_above,
    in_ref,
    down_ref,
    scalars,
    kept_held,
    x_held,
    g_held,
    lin,
    hidden_grad,
    hidden_all,
    both_all,
    kept_cols,
    staged,
    mine,
    landed,
    x_tile,
    g_tile,
    tile_out,
    shared_out,
    up_sem,
    down_sem,
    a_sem,
    b_sem,
    s_sem,
    recv_sem,
    sib_sem,
    own_sem,
    load_sem,
    fetch_sem,
    store_sem,
    weight_sem,
    kept_send,
    kept_recv,
    rs_send,
    rs_recv,
    rb_send,
    rb_recv,
    ra_send,
    ra_recv,
    ru_send,
    ru_recv,
    rd_send,
    rd_recv,
):
    ep, tp, z, y, x, core = place()
    rows, cols = x_ref.shape
    width = down_ref.shape[0]
    filled = expert_width + shared_width
    tall = mine.shape[1]
    out_at = rows + 16
    cuts = ((0, out_at), (out_at, tall - out_at))
    peer_a, peer_b, sibling, above, below = lane_peers()
    sources = kept_held.shape[0]
    others = [(lax.rem(ep + i, sources), tp) for i in range(1, sources)]
    greet([(ep, tp + 2 - 4 * x), sibling] + others)

    def spot(z_at, da, db):
        group, quarter = lane_spot(z_at, da, db, core)
        return all_ref.at[
            pl.ds(pl.multiple_of(group * rows, rows), rows),
            pl.ds(pl.multiple_of(quarter * cols, cols), cols),
        ]

    def at(z_at, da, db):
        return z_at * 4 + da * 2 + db

    def choose(*values):
        return jnp.where(
            z == 0, values[0], jnp.where(z == 1, values[1], jnp.where(z == 2, values[2], values[3]))
        )

    coming = (z, choose(1, 0, 3, 2), choose(2, 2, 1, 1), choose(3, 3, 0, 0))
    turns = (z, choose(2, 0, 3, 1), choose(3, 3, 0, 0), choose(1, 2, 1, 2))

    def arrived(z_at, da, db):
        block, n = spot(z_at, da, db), at(z_at, da, db)
        remote(block, block, s_sem.at[n], recv_sem.at[n], sibling).wait_recv()
        return block

    def up(z_at, source):
        return remote(source, spot(z_at, 0, 0), up_sem.at[z_at], recv_sem.at[at(z_at, 0, 0)], above)

    def down(z_at, source):
        return remote(source, spot(z_at, 0, 0), down_sem.at[z_at], recv_sem.at[at(z_at, 0, 0)], below)

    def over_a(z_at, source):
        return remote(source, spot(z_at, 0, 0), a_sem.at[z_at], recv_sem.at[at(z_at, 1, 0)], peer_a)

    def over_b(z_at, da, source):
        return remote(
            source, spot(z_at, da, 0), b_sem.at[z_at * 2 + da], recv_sem.at[at(z_at, da, 1)], peer_b
        )

    def to_sibling(z_at, da, db, source):
        n = at(z_at, da, db)
        return remote(source, spot(z_at, da, db), s_sem.at[n], sib_sem.at[n], sibling)

    def pass_z(z_at):
        block = arrived(z_at, 0, 0)

        @pl.when((z_at > z) & (z > 0))
        def _():
            down(z_at, block).start()

        @pl.when((z_at < z) & (z < 3))
        def _():
            up(z_at, block).start()

        over_a(z_at, block).start()
        over_b(z_at, 0, block).start()
        to_sibling(z_at, 0, 0, block).start()

    def pass_a(z_at):
        block = arrived(z_at, 1, 0)
        over_b(z_at, 1, block).start()
        to_sibling(z_at, 1, 0, block).start()

    def pass_b(z_at, da):
        block = arrived(z_at, da, 1)
        to_sibling(z_at, da, 1, block).start()

    def sibling_blocks(k, dy):
        for dx in range(2):
            da, db = core * dy + (1 - core) * dx, core * dx + (1 - core) * dy
            n = at(turns[k], da, db)
            block = spot(0, 0, 0)
            remote(block, block, s_sem.at[n], sib_sem.at[n], sibling).wait_recv()

    def group_rows(k, dy):
        group = turns[k] * 2 + y + (1 - 2 * y) * dy
        return group, pl.ds(pl.multiple_of(group * rows, rows), rows)

    def load_x(k, dy):
        _, span = group_rows(k, dy)
        return pltpu.make_async_copy(all_ref.at[span, :], x_held, load_sem.at[0])

    def load_g(k, dy):
        _, span = group_rows(k, dy)
        return pltpu.make_async_copy(g_ref.at[span, :], g_held, load_sem.at[1])

    def project():
        def body(i, carry):
            cut = pl.ds(pl.multiple_of(i * width, width), width)
            lin[:, cut] = times_transpose(x_held[...], in_ref[cut, :])
            return carry

        lax.fori_loop(0, 2, body, 0)

    def project_grad():
        hidden_grad[...] = times_transpose(g_held[...], down_ref[...])

    step = 64
    tile_start = width - 128
    logit_at = filled - tile_start

    def activate(k, dy):
        group, _ = group_rows(k, dy)
        lane = lax.broadcasted_iota(jnp.int32, (1, width), 1)
        near = lax.broadcasted_iota(jnp.int32, (1, 128), 1)
        is_logit = (near >= logit_at) & (near < logit_at + expert_total)
        kept_cols[:, :16] = kept_held[group].astype(jnp.float32).T

        def body(i, carry):
            span = pl.ds(pl.multiple_of(i * step, step), step)
            whole = pl.ds(pl.multiple_of(group * rows + i * step, step), step)
            gate_lin, up_lin = lin[span, :width], lin[span, width:]
            grad = hidden_grad[span, :]
            tail = lin[span, tile_start:width]
            if k == 0 and dy == 0:
                logit_ref[span, :] = tail
            most = jnp.max(jnp.where(is_logit, tail, -1e30), axis=1, keepdims=True)
            powers = jnp.where(is_logit, jnp.exp(jnp.minimum(tail - most, 0.0)), 0.0)
            kept = jnp.sum(jnp.where(near == ep, kept_cols[span, :], 0.0), axis=1, keepdims=True)
            gate = jnp.sum(jnp.where(near == logit_at + ep, powers, 0.0), axis=1, keepdims=True)
            gate = gate / jnp.sum(powers, axis=1, keepdims=True) * kept
            switch = jax.nn.sigmoid(
                jnp.sum(
                    jnp.where(near == logit_at + expert_total, tail, 0.0), axis=1, keepdims=True
                )
            )
            scale = jnp.where(lane < expert_width, gate, switch)
            sig = jax.nn.sigmoid(gate_lin)
            act = gate_lin * sig
            hidden = act * up_lin
            agreement = hidden * grad
            gate_part = jnp.sum(jnp.where(lane < expert_width, agreement, 0.0), axis=1, keepdims=True)
            switch_part = jnp.sum(
                jnp.where(lane < expert_width, 0.0, agreement), axis=1, keepdims=True
            )
            scaled = grad * scale
            hidden_all[whole, :] = (hidden * scale).astype(jnp.bfloat16)
            both_all[whole, :width] = (
                scaled * up_lin * sig * (1.0 + gate_lin * (1.0 - sig))
            ).astype(jnp.bfloat16)
            both_all[whole, width:] = (scaled * act).astype(jnp.bfloat16)
            scalars[span, :] = jnp.where(
                near == ep, gate_part, jnp.where(near == expert_total, switch_part, 0.0)
            )
            return carry

        lax.fori_loop(0, rows // step, body, 0)

    def hold(k, da, db):
        slot = 2 if k == 0 else k % 2
        return db * (7 + slot * 2 + da) + (1 - db) * (da * (4 + slot) + (1 - da) * k)

    def lane_offsets(dx, dy, core_at):
        return (1 - core_at) * dy + core_at * dx, (1 - core_at) * dx + core_at * dy

    def rs_sibling(k, dx, dy):
        n = at(turns[k], *lane_offsets(dx, dy, 1 - core))
        return remote(staged.at[dx], from_sib.at[n], rs_send.at[n], rs_recv.at[n], sibling)

    def block_rows(k, dy):
        sums = scalars[...].T[:16, :].astype(jnp.bfloat16)
        _, span = group_rows(k, dy)

        def fill(target, cut):
            target[:rows, :] = jnp.dot(
                both_all[span, :], in_ref[:, cut], preferred_element_type=jnp.float32
            ).astype(jnp.bfloat16)
            target[rows:out_at, :] = sums
            target[out_at:, :] = jnp.dot(
                hidden_all[span, :], down_ref[:, cut], preferred_element_type=jnp.float32
            ).astype(jnp.bfloat16)

        def body(dx, carry):
            x_at = x + (1 - 2 * x) * dx
            fill(staged.at[dx], pl.ds(pl.multiple_of((x_at * 2 + 1 - core) * cols, cols), cols))
            rs_sibling(k, dx, dy).start()
            fill(
                mine.at[hold(k, *lane_offsets(dx, dy, core))],
                pl.ds(pl.multiple_of((x_at * 2 + core) * cols, cols), cols),
            )
            return carry

        lax.fori_loop(0, 2, body, 0)

    def staged_free(k, dy):
        for dx in range(2):
            rs_sibling(k, dx, dy).wait_send()

    def rs_over_b(k, da):
        n = turns[k] * 2 + da
        return remote(mine.at[hold(k, da, 1)], from_b.at[n], rb_send.at[n], rb_recv.at[n], peer_b)

    def rs_over_a(k):
        z_at = turns[k]
        return remote(
            mine.at[hold(k, 1, 0)], from_a.at[z_at], ra_send.at[z_at], ra_recv.at[z_at], peer_a
        )

    def rs_up(k, z_at, half):
        first, count = cuts[half]
        n = z_at * 2 + half
        span = pl.ds(first, count)
        return remote(
            mine.at[k, span], from_below.at[z_at, span], ru_send.at[n], ru_recv.at[n], above
        )

    def rs_down(k, z_at, half):
        first, count = cuts[half]
        n = z_at * 2 + half
        span = pl.ds(first, count)
        return remote(
            mine.at[k, span], from_above.at[z_at, span], rd_send.at[n], rd_recv.at[n], below
        )

    def fetch(source, i):
        return pltpu.make_async_copy(source, landed.at[i], fetch_sem.at[i])

    def fetch_part(source, half, i):
        span = pl.ds(*cuts[half])
        return pltpu.make_async_copy(source.at[span], landed.at[i, span], fetch_sem.at[i])

    def reduce_sibling(k, dy):
        spots = []
        for dx in range(2):
            n = at(turns[k], *lane_offsets(dx, dy, core))
            remote(staged.at[0], from_sib.at[n], rs_send.at[n], rs_recv.at[n], sibling).wait_recv()
            fetch(from_sib.at[n], dx).start()
            spots.append(n)
        for dx in range(2):
            fetch(from_sib.at[spots[dx]], dx).wait()
            add_blocks(mine.at[hold(k, *lane_offsets(dx, dy, core))], [landed.at[dx]], tall)

        @pl.when(core == 0)
        def _():
            rs_over_b(k, dy).start()

        if dy == 1:

            @pl.when(core == 1)
            def _():
                rs_over_b(k, 0).start()
                rs_over_b(k, 1).start()

    def reduce_b(k):
        rs_over_b(k, 1).wait_recv()
        source = from_b.at[turns[k] * 2 + 1]
        fetch(source, 0).start()
        fetch(source, 0).wait()
        add_blocks(mine.at[hold(k, 1, 0)], [landed.at[0]], tall)
        rs_over_a(k).start()

    def reduce_a(k):
        z_at = turns[k]
        rs_over_b(k, 0).wait_recv()
        fetch(from_b.at[z_at * 2], 0).start()
        rs_over_a(k).wait_recv()
        fetch(from_a.at[z_at], 1).start()
        fetch(from_b.at[z_at * 2], 0).wait()
        fetch(from_a.at[z_at], 1).wait()
        add_blocks(mine.at[k], [landed.at[0], landed.at[1]], tall)
        if k > 0:
            for half in range(2):

                @pl.when(z == 0)
                def _(half=half):
                    rs_up(k, z_at, half).start()

                @pl.when(z == 3)
                def _(half=half):
                    rs_down(k, z_at, half).start()

    def chain(k):
        z_at = turns[k]
        first, count = cuts[0]
        for half, (first, count) in enumerate(cuts):
            span = pl.ds(first, count)

            @pl.when((z > 0) & (z < 3) & (z_at > z))
            def _(half=half, span=span, count=count):
                rs_up(k, z_at, half).wait_recv()
                fetch_part(from_below.at[z_at], half, half).start()
                fetch_part(from_below.at[z_at], half, half).wait()
                add_blocks(mine.at[k, span], [landed.at[half, span]], count)
                rs_up(k, z_at, half).start()

            @pl.when((z > 0) & (z < 3) & (z_at < z))
            def _(half=half, span=span, count=count):
                rs_down(k, z_at, half).wait_recv()
                fetch_part(from_above.at[z_at], half, half).start()
                fetch_part(from_above.at[z_at], half, half).wait()
                add_blocks(mine.at[k, span], [landed.at[half, span]], count)
                rs_down(k, z_at, half).start()

    tile = x_tile.shape[1]

    def load_tile(source, target, t, sem):
        cut = pl.ds(pl.multiple_of(t * tile, tile), tile)
        return pltpu.make_async_copy(source.at[:, cut], target, load_sem.at[sem])

    def tile_stores(t, kind):
        cut = pl.ds(pl.multiple_of(t * tile, tile), tile)
        return (
            pltpu.make_async_copy(
                tile_out.at[kind, pl.ds(0, expert_width)],
                expert_grads_ref.at[kind, :, cut],
                store_sem.at[kind],
            ),
            pltpu.make_async_copy(
                shared_out.at[kind], shared_grads_ref.at[t, kind], store_sem.at[3 + kind]
            ),
        )

    def weight_tile(t, kind):
        @pl.when(t > 0)
        def _():
            for copy in tile_stores(t - 1, kind):
                copy.wait()

        if kind == 0:
            left, right = hidden_all[:, :filled], g_tile[...]
        else:
            left, right = both_all[:, (kind - 1) * width : (kind - 1) * width + filled], x_tile[...]
        result = inner_rows(left, right)
        tile_out[kind] = result
        shared_out[kind] = result[expert_width:, :].astype(jnp.bfloat16)
        for copy in tile_stores(t, kind):
            copy.start()

    own = pltpu.make_async_copy(x_ref, spot(z, 0, 0), own_sem)
    over_b(z, 0, x_ref).start()
    over_a(z, x_ref).start()

    @pl.when(z < 3)
    def _():
        up(z, x_ref).start()

    @pl.when(z > 0)
    def _():
        down(z, x_ref).start()

    to_sibling(z, 0, 0, x_ref).start()
    own.start()
    load_g(0, 0).start()

    def kept_to(i):
        return remote(
            kept_ref, kept_held.at[ep], kept_send.at[i - 1], kept_recv.at[i - 1], others[i - 1]
        )

    for i in range(1, sources):
        kept_to(i).start()
    own_kept = pltpu.make_async_copy(kept_ref, kept_held.at[ep], weight_sem.at[7])
    own_kept.start()
    pieces = [
        (expert_down_ref, down_ref, 0),
        (
            shared_down_ref.at[pl.ds(pl.multiple_of(ep * shared_width, 16), shared_width), :],
            down_ref,
            expert_width,
        ),
        (expert_gate_ref, in_ref, 0),
        (shared_gate_ref, in_ref, expert_width),
        (extra_ref, in_ref, filled),
        (expert_up_ref, in_ref, width),
        (shared_up_ref, in_ref, width + expert_width),
    ]
    weight_copies = [
        pltpu.make_async_copy(piece, target.at[pl.ds(at_row, piece.shape[0]), :], weight_sem.at[i])
        for i, (piece, target, at_row) in enumerate(pieces)
    ]
    for copy in weight_copies:
        copy.start()
    for target, first, last_row in (
        (in_ref, filled + 16, width),
        (in_ref, width + filled, 2 * width),
        (down_ref, filled, width),
    ):
        target[first:last_row, :] = jnp.zeros((last_row - first, target.shape[1]), target.dtype)
    for copy in weight_copies:
        copy.wait()
    load_g(0, 0).wait()
    project_grad()
    own_kept.wait()
    for i in range(1, sources):
        kept_to(i).wait_recv()
    own.wait()

    def ready(k, dy):
        if k > 0:
            pass_b(turns[k], dy)
        sibling_blocks(k, dy)
        load_x(k, dy).start()

    order = [(0, 0)] + [(k, dy) for k in range(1, 4) for dy in range(2)] + [(0, 1)]
    pass_a(z)
    pass_b(z, 0)
    ready(0, 0)
    for s, (k, dy) in enumerate(order):
        following = order[s + 1] if s < 7 else None
        load_x(k, dy).wait()
        project()
        if s == 0:
            pass_z(coming[1])
        if s >= 1:
            load_g(k, dy).wait()
            project_grad()
        if following is not None:
            load_g(*following).start()
        if s == 0:
            pass_z(coming[2])
            pass_b(z, 1)
            pass_a(coming[1])
        if s == 1:
            pass_z(coming[3])
        if s >= 1:
            reduce_sibling(*order[s - 1])
        if s in (4, 6):
            reduce_b(s // 2 - 1)
        activate(k, dy)
        if s == 0:
            pass_a(coming[2])
        if s == 2:
            pass_a(coming[3])
        if following is not None:
            ready(*following)
        if s in (5, 7):
            reduce_a((s - 3) // 2)
        if s >= 1:
            staged_free(*order[s - 1])
        if s == 5:
            for da in range(2):
                rs_over_b(1, da).wait_send()
            rs_over_a(1).wait_send()
        block_rows(k, dy)

    load_tile(g_ref, g_tile, 0, 2).start()
    load_tile(all_ref, x_tile, 0, 3).start()
    tiles = shared_grads_ref.shape[0]
    services = {
        (0, 1): lambda: reduce_sibling(0, 1),
        (0, 2): lambda: chain(2),
        (1, 1): lambda: reduce_b(3),
        (1, 2): lambda: reduce_b(0),
        (2, 0): lambda: chain(1),
        (3, 0): lambda: reduce_a(3),
        (4, 0): lambda: chain(3),
        (5, 1): lambda: reduce_a(0),
    }

    def tile_step(t, carry):
        for kind in range(3):
            if kind == 0:
                load_tile(g_ref, g_tile, t, 2).wait()
            if kind == 1:
                load_tile(all_ref, x_tile, t, 3).wait()
            weight_tile(t, kind)

            @pl.when(t + 1 < tiles)
            def _(kind=kind):
                if kind == 0:
                    load_tile(g_ref, g_tile, t + 1, 2).start()
                if kind == 2:
                    load_tile(all_ref, x_tile, t + 1, 3).start()

            for (at_tile, at_kind), service in services.items():
                if at_kind == kind:
                    pl.when(t == at_tile)(service)
        return carry

    lax.fori_loop(0, tiles, tile_step, 0)
    for kind in range(3):
        for copy in tile_stores(tiles - 1, kind):
            copy.wait()

    for half in range(2):

        @pl.when(z > 0)
        def _(half=half):
            rs_up(0, z, half).wait_recv()
            fetch_part(from_below.at[z], half, 0).start()
            fetch_part(from_below.at[z], half, 0).wait()

        @pl.when(z < 3)
        def _(half=half):
            rs_down(0, z, half).wait_recv()
            fetch_part(from_above.at[z], half, 1).start()
            fetch_part(from_above.at[z], half, 1).wait()

    def total(parts):
        def body(i, carry):
            for target, first in ((grad_ref, 0), (ffn_ref, out_at)):
                span = pl.ds(pl.multiple_of(i * 16, 16), 16)
                source = pl.ds(pl.multiple_of(first + i * 16, 16), 16)
                value = mine[0, source, :].astype(jnp.float32)
                for part in parts:
                    value = value + landed[part, source, :].astype(jnp.float32)
                target[span, :] = value
            return carry

        lax.fori_loop(0, rows // 16, body, 0)
        value = mine[0, rows:out_at, :].astype(jnp.float32)
        for part in parts:
            value = value + landed[part, rows:out_at, :].astype(jnp.float32)
        grad_ref[rows:, :] = value

    @pl.when(z == 0)
    def _():
        total([1])

    @pl.when(z == 3)
    def _():
        total([0])

    @pl.when((z > 0) & (z < 3))
    def _():
        total([0, 1])

    for i in range(1, sources):
        kept_to(i).wait_send()
    staged_free(0, 1)
    for k in (0, 2, 3):
        rs_over_a(k).wait_send()
        for da in range(2):
            rs_over_b(k, da).wait_send()

    def finish(i, carry):
        over_a(i, x_ref).wait_send()
        over_b(i, 0, x_ref).wait_send()
        over_b(i, 1, x_ref).wait_send()
        for n in range(4):
            block = spot(0, 0, 0)
            remote(block, block, s_sem.at[i * 4 + n], sib_sem.at[i * 4 + n], sibling).wait_send()

        @pl.when((z < 3) & (i <= z))
        def _():
            up(i, x_ref).wait_send()

        @pl.when((z > 0) & (i >= z))
        def _():
            down(i, x_ref).wait_send()

        for half in range(2):

            @pl.when(i > z)
            def _(half=half):
                rs_up(0, i, half).wait_send()

            @pl.when(i < z)
            def _(half=half):
                rs_down(0, i, half).wait_send()

        return carry

    lax.fori_loop(0, 4, finish, 0)


def experts(x_cols, grads_all, kept_rows, weights, expert_total, cid):
    rows, cols = x_cols.shape
    total, model_dim = grads_all.shape
    sources = total // rows
    expert_width, shared_width = weights[0].shape[0], weights[1].shape[0]
    filled = expert_width + shared_width
    width = -(-(filled + expert_total + 1) // 128) * 128
    tall = 2 * rows + 16
    tile = model_dim // sources
    low, dma = jnp.bfloat16, pltpu.SemaphoreType.DMA
    vmem, hbm = pl.BlockSpec(memory_space=pltpu.VMEM), pl.BlockSpec(memory_space=pl.ANY)

    def landing(count):
        return jax.ShapeDtypeStruct((count, tall, cols), low)

    return pl.pallas_call(
        functools.partial(experts_kernel, expert_width, shared_width, expert_total),
        out_shape=[
            jax.ShapeDtypeStruct((rows + 16, cols), jnp.float32),
            jax.ShapeDtypeStruct((rows, cols), jnp.float32),
            jax.ShapeDtypeStruct((rows, 128), jnp.float32),
            jax.ShapeDtypeStruct((3, expert_width, model_dim), jnp.float32),
            jax.ShapeDtypeStruct((sources, 3, shared_width, tile), low),
            jax.ShapeDtypeStruct((total, model_dim), low),
            landing(16),
            landing(8),
            landing(4),
            landing(4),
            landing(4),
        ],
        in_specs=[hbm] * 10,
        out_specs=[vmem, vmem, vmem] + [hbm] * 8,
        scratch_shapes=[
            pltpu.VMEM((2 * width, model_dim), low),
            pltpu.VMEM((width, model_dim), low),
            pltpu.VMEM((rows, 128), jnp.float32),
            pltpu.VMEM((sources, 16, rows), low),
            pltpu.VMEM((rows, model_dim), low),
            pltpu.VMEM((rows, model_dim), low),
            pltpu.VMEM((rows, 2 * width), jnp.float32),
            pltpu.VMEM((rows, width), jnp.float32),
            pltpu.VMEM((total, width), low),
            pltpu.VMEM((total, 2 * width), low),
            pltpu.VMEM((rows, 128), jnp.float32),
            pltpu.VMEM((2, tall, cols), low),
            pltpu.VMEM((13, tall, cols), low),
            pltpu.VMEM((2, tall, cols), low),
            pltpu.VMEM((total, tile), low),
            pltpu.VMEM((total, tile), low),
            pltpu.VMEM((3, filled, tile), jnp.float32),
            pltpu.VMEM((3, shared_width, tile), low),
        ]
        + [dma((4,)), dma((4,)), dma((4,)), dma((8,)), dma((16,)), dma((16,)), dma((16,)), dma]
        + [dma((4,)), dma((2,)), dma((6,)), dma((8,)), dma((7,)), dma((7,))]
        + [dma((16,)), dma((16,)), dma((8,)), dma((8,)), dma((4,)), dma((4,))]
        + [dma((8,))] * 4,
        compiler_params=pltpu.CompilerParams(
            collective_id=cid, has_side_effects=True, vmem_limit_bytes=63 * 2**20
        ),
        name="experts",
    )(x_cols, grads_all, kept_rows, *weights)


def row_of(columns):
    part = columns[:, :128]
    for i in range(1, columns.shape[1] // 128):
        part = part + columns[:, i * 128 : (i + 1) * 128]
    total = jnp.sum(part.T, axis=0, keepdims=True)
    return jnp.broadcast_to(total, (8, total.shape[1]))


def unwind_kernel(
    dn2_ref,
    unit_ref,
    inv_ref,
    second_ref,
    grad_ref,
    tokens_ref,
    inv_one_ref,
    first_ref,
    small_ref,
    q_ref,
    k_ref,
    v_ref,
    ke_ref,
    ve_ref,
    context_ref,
    log_ref,
    cos_ref,
    sin_ref,
    n1_hbm,
    wq_hbm,
    wk_hbm,
    wv_hbm,
    wo_hbm,
    tokens_grad_ref,
    weight_grads_ref,
    sums_ref,
    n1,
    wq,
    wk,
    wv,
    wo,
    grad_all,
    grad_own,
    hidden_grad,
    dc,
    dq,
    dk,
    dv,
    lin_grads,
    dke,
    dve,
    later_k,
    later_v,
    staged,
    mine,
    from_y,
    from_below,
    from_above,
    tp_staged,
    tp_mine,
    tp_sib,
    tp_x,
    dn1,
    row_mine,
    row_sib,
    row_x,
    smalls,
    load_sem,
    g_send,
    g_recv,
    row_send,
    row_recv,
    kv_send,
    kv_recv,
    y_send,
    y_recv,
    up_send,
    up_recv,
    down_send,
    down_recv,
    tp_send,
    tp_recv,
    small_send,
    small_recv,
):
    ep, tp, z, y, x, core = place()
    rows, cols = unit_ref.shape
    model_dim = n1.shape[1]
    heads = cols // HD
    block = mine.shape[1]
    low, full = jnp.bfloat16, jnp.float32
    score_scale = HD ** (-0.5)
    sibling, across = (ep, tp + 1 - 2 * core), (ep, tp + 2 - 4 * x)
    beside = (ep + 1 - 2 * y, tp)
    above, below = (ep + 2, tp), (ep - 2, tp)
    sources = smalls.shape[0]
    others = [(lax.rem(ep + i, sources), tp) for i in range(1, sources)]
    loads = [
        pltpu.make_async_copy(source, target, load_sem.at[i])
        for i, (source, target) in enumerate(
            ((wo_hbm, wo), (n1_hbm, n1), (wq_hbm, wq), (wk_hbm, wk), (wv_hbm, wv))
        )
    ]
    for copy in loads:
        copy.start()
    greet([across, sibling] + others)

    step = 64

    def by_rows(body):
        def one(i, carry):
            body(pl.ds(pl.multiple_of(i * step, step), step))
            return carry

        lax.fori_loop(0, rows // step, one, 0)

    def row_exchange(i, values):
        row_mine[2 * i] = values
        first = remote(
            row_mine.at[2 * i], row_sib.at[i], row_send.at[2 * i], row_recv.at[2 * i], sibling
        )
        first.start()
        first.wait_recv()
        row_mine[2 * i + 1] = row_mine[2 * i] + row_sib[i]
        second = remote(
            row_mine.at[2 * i + 1],
            row_x.at[i],
            row_send.at[2 * i + 1],
            row_recv.at[2 * i + 1],
            across,
        )
        second.start()
        second.wait_recv()
        first.wait_send()
        second.wait_send()
        return (row_mine[2 * i + 1] + row_x[i]).T[:, :1]

    dn1[...] = dn2_ref[...] * second_ref[:1, :] * unit_ref[...]
    mean = row_exchange(0, row_of(dn1[...])) * (1.0 / model_dim)
    dn1[:, :128] = jnp.broadcast_to(mean, (rows, 128))

    def norm_two(span):
        scaled = dn2_ref[span, :] * second_ref[:1, :]
        value = grad_ref[span, :].astype(full) + inv_ref[span, :1] * (
            scaled - unit_ref[span, :] * dn1[span, :1]
        )
        hidden_grad[span, :] = value
        grad_own[span, :] = value.astype(low)

    by_rows(norm_two)

    def quarter(at):
        return grad_all.at[:, pl.ds(pl.multiple_of(at * cols, cols), cols)]

    g_x = remote(grad_own, quarter(tp), g_send.at[0], g_recv.at[0], across)
    g_s = remote(grad_own, quarter(tp), g_send.at[1], g_recv.at[1], sibling)
    g_x.start()
    g_s.start()
    own_cut = pl.ds(pl.multiple_of(tp * cols, cols), cols)
    grad_all[:, own_cut] = grad_own[...]
    g_x.wait_recv()
    theirs = quarter(tp + 2 - 4 * x)
    g_f = remote(theirs, theirs, g_send.at[2], g_recv.at[2], sibling)
    g_f.start()
    g_s.wait_recv()
    g_f.wait_recv()
    loads[0].wait()
    dc[...] = times_transpose(grad_all[...], wo[...]).astype(low)

    def over_y(kind, z_at):
        n = kind * 4 + z_at
        return remote(staged.at[n], from_y.at[n], y_send.at[n], y_recv.at[n], beside)

    def weight_blocks(kind, left, right):
        def other(i, carry):
            z_at = lax.rem(i * 3, 4)
            cut = pl.ds(pl.multiple_of((z_at * 2 + 1 - y) * block, block), block)
            staged[kind * 4 + z_at] = inner_rows(left[:, cut], right[...]).astype(low)
            over_y(kind, z_at).start()
            return carry

        def ours(i, carry):
            z_at = lax.rem(i * 3, 4)
            cut = pl.ds(pl.multiple_of((z_at * 2 + y) * block, block), block)
            mine[kind * 4 + z_at] = inner_rows(left[:, cut], right[...]).astype(low)
            return carry

        lax.fori_loop(0, 4, other, 0)
        lax.fori_loop(0, 4, ours, 0)

    def up(kind, z_at):
        n = kind * 4 + z_at
        return remote(mine.at[n], from_below.at[n], up_send.at[n], up_recv.at[n], above)

    def down(kind, z_at):
        n = kind * 4 + z_at
        return remote(mine.at[n], from_above.at[n], down_send.at[n], down_recv.at[n], below)

    def y_stage(kind):
        def one(i, carry):
            z_at = lax.rem(i * 3, 4)
            n = kind * 4 + z_at
            over_y(kind, z_at).wait_recv()
            add_blocks(mine.at[n], [from_y.at[n]], block)

            @pl.when((z == 0) & (z_at > 0))
            def _():
                up(kind, z_at).start()

            @pl.when((z == 3) & (z_at < 3))
            def _():
                down(kind, z_at).start()

            return carry

        lax.fori_loop(0, 4, one, 0)

    def chain(kind):
        def rise(z_at):
            n = kind * 4 + z_at
            up(kind, z_at).wait_recv()
            add_blocks(mine.at[n], [from_below.at[n]], block)
            up(kind, z_at).start()

        def fall(z_at):
            n = kind * 4 + z_at
            down(kind, z_at).wait_recv()
            add_blocks(mine.at[n], [from_above.at[n]], block)
            down(kind, z_at).start()

        @pl.when(z == 1)
        def _():
            rise(3)
            rise(2)
            fall(0)

        @pl.when(z == 2)
        def _():
            fall(0)
            fall(1)
            rise(3)

    def final(kind):
        n = kind * 4 + z

        @pl.when(z > 0)
        def _():
            up(kind, z).wait_recv()

        @pl.when(z < 3)
        def _():
            down(kind, z).wait_recv()

        def one(i, carry):
            span = pl.ds(pl.multiple_of(i * 32, 32), 32)
            value = mine[n, span, :].astype(full)
            low_part = from_below[n, span, :].astype(full)
            high_part = from_above[n, span, :].astype(full)
            value = value + jnp.where(z > 0, low_part, 0.0) + jnp.where(z < 3, high_part, 0.0)
            weight_grads_ref[kind, span, :] = value
            return carry

        lax.fori_loop(0, block // 32, one, 0)

    weight_blocks(0, grad_all, context_ref)

    half = rows // 2

    def terms(h, qb, key_count, keys, values):
        cut = pl.ds(pl.multiple_of(h * HD, HD), HD)
        span = pl.ds(qb * half, half)
        lane = lax.broadcasted_iota(jnp.int32, (1, 128), 1)
        log_total = jnp.sum(jnp.where(lane == h, log_ref[span, :], 0.0), axis=1, keepdims=True)
        queries, grads = q_ref[span, cut], dc[span, cut]
        delta = jnp.sum(
            grads.astype(full) * context_ref[span, cut].astype(full), axis=1, keepdims=True
        )
        key_part, value_part = keys[:key_count, cut], values[:key_count, cut]
        probs = jnp.exp(times_transpose(queries, key_part) * score_scale - log_total)
        scores_grad = (probs * (times_transpose(grads, value_part) - delta)).astype(low)
        return (
            jnp.dot(scores_grad, key_part, preferred_element_type=full),
            inner_rows(scores_grad, queries),
            inner_rows(probs.astype(low), grads),
        )

    def spans(h, qb):
        return pl.ds(qb * half, half), pl.ds(pl.multiple_of(h * HD, HD), HD)

    later = (
        remote(dke, later_k, kv_send.at[0], kv_recv.at[0], beside),
        remote(dve, later_v, kv_send.at[1], kv_recv.at[1], beside),
    )

    @pl.when(y == 1)
    def _():
        def head(h, carry):
            cut = pl.ds(pl.multiple_of(h * HD, HD), HD)
            first = terms(h, 0, rows, ke_ref, ve_ref)
            dq[spans(h, 0)[0], cut] = first[0]
            dk[:, cut] = first[1]
            dv[:, cut] = first[2]
            second = terms(h, 1, rows, ke_ref, ve_ref)
            dq[spans(h, 1)[0], cut] = second[0]
            dke[:, cut] = ((dk[:, cut] + second[1]) * score_scale).astype(low)
            dve[:, cut] = (dv[:, cut] + second[2]).astype(low)
            return carry

        lax.fori_loop(0, heads, head, 0)
        for copy in later:
            copy.start()

    @pl.when(y == 0)
    def _():
        dq[...] = jnp.zeros_like(dq)

    y_stage(0)

    def head(h, carry):
        cut = pl.ds(pl.multiple_of(h * HD, HD), HD)
        second = terms(h, 1, rows, k_ref, v_ref)
        dq[half:, cut] = dq[half:, cut] + second[0]
        dk[:, cut] = second[1] * score_scale
        dv[:, cut] = second[2]
        first = terms(h, 0, half, k_ref, v_ref)
        dq[:half, cut] = dq[:half, cut] + first[0]
        dk[:half, cut] = dk[:half, cut] + first[1] * score_scale
        dv[:half, cut] = dv[:half, cut] + first[2]
        return carry

    lax.fori_loop(0, heads, head, 0)

    def rotate_back(source, target, scale):
        def one(h, carry):
            cut = pl.ds(pl.multiple_of(h * HD, HD), HD)
            value = source[:, cut] * scale
            turned = value * cos_ref[...] - pltpu.roll(value, HD // 2, 1) * sin_ref[...]
            lin_grads[target, :, cut] = turned.astype(low)
            return carry

        lax.fori_loop(0, heads, one, 0)

    rotate_back(dq, 0, score_scale)
    loads[1].wait()
    weight_blocks(1, n1, lin_grads.at[0])
    chain(0)

    @pl.when(y == 0)
    def _():
        for copy in later:
            copy.wait_recv()

        def add(span):
            dk[span, :] = dk[span, :] + later_k[span, :].astype(full)
            dv[span, :] = dv[span, :] + later_v[span, :].astype(full)

        by_rows(add)

    rotate_back(dk, 1, 1.0)
    lin_grads[2] = dv[...].astype(low)
    weight_blocks(2, n1, lin_grads.at[1])
    weight_blocks(3, n1, lin_grads.at[2])
    y_stage(1)
    for copy in loads[2:]:
        copy.wait()

    def dn1_part(at, target):
        cut = pl.ds(pl.multiple_of(at * cols, cols), cols)
        total = times_transpose(lin_grads[0], wq[cut, :])
        total = total + times_transpose(lin_grads[1], wk[cut, :])
        total = total + times_transpose(lin_grads[2], wv[cut, :])
        target[...] = total.astype(low)

    def to_sibling(i):
        return remote(tp_staged.at[i], tp_sib.at[i], tp_send.at[i], tp_recv.at[i], sibling)

    def part_of(i):
        x_at = 1 - x + (2 * x - 1) * i
        dn1_part(x_at * 2 + 1 - core, tp_staged.at[i])
        to_sibling(i).start()
        dn1_part(x_at * 2 + core, tp_mine.at[i])

    out_x = remote(tp_mine.at[0], tp_x, tp_send.at[2], tp_recv.at[2], across)
    part_of(0)
    to_sibling(0).wait_recv()
    add_blocks(tp_mine.at[0], [tp_sib.at[0]], rows)
    out_x.start()
    part_of(1)
    chain(1)
    to_sibling(1).wait_recv()
    out_x.wait_recv()

    def sum_parts(span):
        dn1[span, :] = (
            tp_mine[1, span, :].astype(full)
            + tp_sib[1, span, :].astype(full)
            + tp_x[span, :].astype(full)
        )

    by_rows(sum_parts)

    def unit_one(span):
        return tokens_ref[span, :].astype(full) * inv_one_ref[span, :1]

    def products(span):
        dq[span, :] = dn1[span, :] * unit_one(span)

    by_rows(products)
    gain_grad = jnp.sum(dq[...], axis=0, keepdims=True)
    dq[...] = dq[...] * first_ref[:1, :]
    total = row_exchange(1, row_of(dq[...]))
    dk[:, :128] = jnp.broadcast_to(total * (1.0 / model_dim), (rows, 128))

    def norm_one(span):
        scaled = dn1[span, :] * first_ref[:1, :]
        value = hidden_grad[span, :] + inv_one_ref[span, :1] * (
            scaled - unit_one(span) * dk[span, :1]
        )
        tokens_grad_ref[span, :] = value.astype(low)

    by_rows(norm_one)

    own = smalls.at[ep]
    own[...] = small_ref[...]
    own[0:1, :] = gain_grad
    for i in range(3):
        own[i + 1 : i + 2, :] = jnp.sum(lin_grads[i].astype(full), axis=0, keepdims=True)

    def small_to(i):
        return remote(own, own, small_send.at[i - 1], small_recv.at[i - 1], others[i - 1])

    for i in range(1, sources):
        small_to(i).start()
    y_stage(2)
    final(0)
    chain(2)
    y_stage(3)
    final(1)
    chain(3)
    for i in range(1, sources):
        small_to(i).wait_recv()
    total = smalls[0]
    for i in range(1, sources):
        total = total + smalls[i]
    sums_ref[...] = total
    final(2)
    final(3)

    for copy in (g_x, g_s, g_f, out_x, to_sibling(0), to_sibling(1)):
        copy.wait_send()

    @pl.when(y == 1)
    def _():
        for copy in later:
            copy.wait_send()

    for i in range(1, sources):
        small_to(i).wait_send()

    def finish(n, carry):
        remote(staged.at[0], from_y.at[0], y_send.at[n], y_recv.at[n], beside).wait_send()
        z_at = lax.rem(n, 4)

        @pl.when(z_at > z)
        def _():
            remote(mine.at[0], from_below.at[0], up_send.at[n], up_recv.at[n], above).wait_send()

        @pl.when(z_at < z)
        def _():
            remote(mine.at[0], from_above.at[0], down_send.at[n], down_recv.at[n], below).wait_send()

        return carry

    lax.fori_loop(0, 16, finish, 0)


def unwind(vmem_args, hbm_args, cid):
    rows, cols = vmem_args[0].shape
    model_dim = hbm_args[0].shape[1]
    sources = 8
    block = model_dim // sources
    low, full, dma = jnp.bfloat16, jnp.float32, pltpu.SemaphoreType.DMA
    vmem, hbm = pl.BlockSpec(memory_space=pltpu.VMEM), pl.BlockSpec(memory_space=pl.ANY)

    def buffers(*shape, dtype=low):
        return pltpu.VMEM(shape, dtype)

    return pl.pallas_call(
        unwind_kernel,
        out_shape=[
            jax.ShapeDtypeStruct((rows, cols), low),
            jax.ShapeDtypeStruct((4, block, cols), full),
            jax.ShapeDtypeStruct((16, cols), full),
        ],
        in_specs=[vmem] * len(vmem_args) + [hbm] * len(hbm_args),
        out_specs=[vmem] * 3,
        scratch_shapes=[buffers(*arg.shape) for arg in hbm_args]
        + [
            buffers(rows, model_dim),
            buffers(rows, cols),
            buffers(rows, cols, dtype=full),
            buffers(rows, cols),
            buffers(rows, cols, dtype=full),
            buffers(rows, cols, dtype=full),
            buffers(rows, cols, dtype=full),
            buffers(3, rows, cols),
            buffers(rows, cols),
            buffers(rows, cols),
            buffers(rows, cols),
            buffers(rows, cols),
        ]
        + [buffers(16, block, cols)] * 5
        + [
            buffers(2, rows, cols),
            buffers(2, rows, cols),
            buffers(2, rows, cols),
            buffers(rows, cols),
            buffers(rows, cols, dtype=full),
            buffers(4, 8, rows, dtype=full),
            buffers(2, 8, rows, dtype=full),
            buffers(2, 8, rows, dtype=full),
            buffers(sources, 16, cols, dtype=full),
        ]
        + [dma((5,)), dma((3,)), dma((3,)), dma((4,)), dma((4,)), dma((2,)), dma((2,))]
        + [dma((16,))] * 6
        + [dma((3,)), dma((3,)), dma((7,)), dma((7,))],
        compiler_params=pltpu.CompilerParams(
            collective_id=cid, has_side_effects=True, vmem_limit_bytes=60 * 2**20
        ),
        name="unwind",
    )(*vmem_args, *hbm_args)


def tp_total(value):
    return lax.psum(value, "tp")


def kept_choice(expert_ids, pair_order, expert_total, capacity):
    tok_count, top_count = expert_ids.shape
    pair_count = tok_count * top_count
    order = pair_order.reshape(-1)
    pairs = jnp.arange(pair_count, dtype=jnp.int32)
    turn = jnp.sum(jnp.where(order[None, :] == pairs[:, None], pairs[None, :], 0), axis=1)
    turn = turn.reshape(tok_count, top_count)
    picked = expert_ids[:, :, None] == jnp.arange(expert_total, dtype=jnp.int32)[None, None, :]
    turn_of = jnp.sum(jnp.where(picked, turn[:, :, None], 0), axis=1)
    named = jnp.any(picked, axis=1)
    turn_of = jnp.where(named, turn_of, pair_count)
    slot = jnp.sum((turn_of[None, :, :] < turn_of[:, None, :]).astype(jnp.int32), axis=1)
    return (named & (slot < capacity)).astype(jnp.float32)


def dense_plan(
    tokens,
    out_grad,
    first_gain,
    query_weight,
    key_weight,
    value_weight,
    query_bias,
    key_bias,
    value_bias,
    output_weight,
    second_gain,
    router_weight,
    shared_gate_weight,
    shared_up_weight,
    shared_down_weight,
    switch_vector,
    expert_gate_weight,
    expert_up_weight,
    expert_down_weight,
    expert_ids,
    pair_order,
):
    ep, tp = lax.axis_index("ep"), lax.axis_index("tp")
    tok_count, col_width = tokens.shape
    model_dim = query_weight.shape[0]
    sources = lax.axis_size("ep")
    place_in_seq = ep % SPAN
    has_earlier = place_in_seq > 0
    expert_total = router_weight.shape[1]
    capacity = 9 * tok_count * expert_ids.shape[1] // (8 * expert_total)
    head_count = query_weight.shape[1] // HD
    score_scale = HD ** (-0.5)
    expert_width = expert_gate_weight.shape[2]
    shared_width = shared_gate_weight.shape[1] // sources
    width = expert_width + shared_width

    def own_cols(vector):
        return lax.dynamic_slice_in_dim(vector, tp * col_width, col_width, vector.ndim - 1)

    kept_own = kept_choice(expert_ids, pair_order, expert_total, capacity)
    grads_all = gather_all(out_grad, 2)

    inputs_full = gather_tp(tokens, 0).astype(jnp.float32)
    unit_one, inv_one = row_stats(inputs_full)
    normed_one = (unit_one * first_gain).astype(jnp.bfloat16)
    query_lin = jnp.dot(normed_one, query_weight, preferred_element_type=jnp.float32) + query_bias
    key_lin = jnp.dot(normed_one, key_weight, preferred_element_type=jnp.float32) + key_bias
    value_lin = jnp.dot(normed_one, value_weight, preferred_element_type=jnp.float32) + value_bias
    cosine, sine_part = rope_tables(tok_count, HD, place_in_seq * tok_count)
    queries = rotate(query_lin.reshape(tok_count, head_count, HD), cosine, sine_part).astype(
        jnp.bfloat16
    )
    keys_rot = rotate(key_lin.reshape(tok_count, head_count, HD), cosine, sine_part).astype(
        jnp.bfloat16
    )
    values_all = value_lin.reshape(tok_count, head_count, HD).astype(jnp.bfloat16)
    earlier_keys, earlier_values = passed_along((keys_rot, values_all), "ep", 1)
    keys_both = jnp.concatenate([earlier_keys, keys_rot], axis=0)
    values_both = jnp.concatenate([earlier_values, values_all], axis=0)
    blocks = jnp.arange(tok_count) // BLOCK
    local_allowed = blocks[None, :] <= blocks[:, None]
    remote_allowed = jnp.broadcast_to(has_earlier, (tok_count, tok_count))
    allowed = jnp.concatenate([remote_allowed, local_allowed], axis=1)[None]

    def attention_scores():
        scored = (
            jnp.einsum("qhd,khd->hqk", queries, keys_both, preferred_element_type=jnp.float32)
            * score_scale
        )
        return jnp.where(allowed, scored, masked_score)

    scores = attention_scores()
    row_max = jnp.max(scores, axis=-1, keepdims=True)
    powers = jnp.exp(scores - row_max)
    totals = jnp.sum(powers, axis=-1, keepdims=True)
    log_total = row_max + jnp.log(totals)
    probs_low = (powers / totals).astype(jnp.bfloat16)
    context = jnp.einsum("hqk,khd->qhd", probs_low, values_both, preferred_element_type=jnp.float32)
    context = context.reshape(tok_count, head_count * HD).astype(jnp.bfloat16)
    attn_part = jnp.dot(context, output_weight, preferred_element_type=jnp.float32)
    attended = scatter_tp(attn_part.astype(jnp.bfloat16), 1)

    hidden_cols = tokens.astype(jnp.float32) + attended
    squares = tp_total(jnp.sum(hidden_cols * hidden_cols, axis=-1, keepdims=True))
    inv_two = lax.rsqrt(squares / model_dim + norm_eps)
    unit_two = hidden_cols * inv_two
    second_cols = own_cols(second_gain)
    normed_cols = (unit_two * second_cols).astype(jnp.bfloat16)

    def shared_rows(weight):
        return lax.dynamic_slice_in_dim(weight, ep * shared_width, shared_width, 1).T

    extra_rows = jnp.concatenate([router_weight.T, switch_vector[None, :]], axis=0)
    extra_rows = jnp.pad(extra_rows, ((0, 16 - extra_rows.shape[0]), (0, 0)))
    kept_rows = jnp.pad(kept_own.T, ((0, 16 - expert_total), (0, 0))).astype(jnp.bfloat16)
    reduced, ffn_cols, logit_tile, expert_grads, shared_parts, *_ = experts(
        normed_cols,
        grads_all,
        kept_rows,
        [
            expert_gate_weight[0].T,
            shared_rows(shared_gate_weight),
            extra_rows,
            expert_up_weight[0].T,
            shared_rows(shared_up_weight),
            expert_down_weight[0],
            shared_down_weight,
        ],
        expert_total,
        4,
    )
    layer_out = (hidden_cols + ffn_cols).astype(jnp.bfloat16)
    shared_parts = lax.all_to_all(shared_parts, "ep", split_axis=0, concat_axis=0, tiled=True)
    shared_parts = shared_parts.transpose(1, 0, 2, 3).reshape(3, sources * shared_width, -1)
    shared_parts = shared_parts.astype(jnp.float32)
    shared_gate_grad = shared_parts[1].T
    shared_up_grad = shared_parts[2].T
    shared_down_grad = shared_parts[0]

    normed_grad = reduced[:tok_count]
    probs_grad = reduced[tok_count : tok_count + expert_total].T * kept_own
    switch_grad = reduced[tok_count + expert_total]
    logit_at = width % 128
    probs_own = softmax_rows(logit_tile[:, logit_at : logit_at + expert_total])
    switch = jax.nn.sigmoid(logit_tile[:, logit_at + expert_total])
    logit_grad = (
        probs_own * (probs_grad - jnp.sum(probs_own * probs_grad, axis=-1, keepdims=True))
    ).astype(jnp.bfloat16)
    router_grad = inner_rows(normed_cols, logit_grad)
    switch_lin_grad = switch_grad * switch * (1.0 - switch)
    switch_vector_grad = jnp.dot(switch_lin_grad, normed_cols, preferred_element_type=jnp.float32)
    router_cols = lax.dynamic_slice_in_dim(router_weight, tp * col_width, col_width, 0)
    normed_grad = normed_grad + times_transpose(logit_grad, router_cols)
    normed_grad = (
        normed_grad
        + switch_lin_grad[:, None] * own_cols(switch_vector).astype(jnp.float32)[None, :]
    )
    second_gain_grad = jnp.sum(normed_grad * unit_two, axis=0)

    def wide(column):
        return jnp.broadcast_to(column, (tok_count, 128))

    def tall(vector):
        return jnp.broadcast_to(vector[None, :], (8, vector.shape[0]))

    def flat(heads_apart):
        return heads_apart.reshape(tok_count, head_count * HD)

    small = jnp.concatenate(
        [second_gain_grad[None], switch_vector_grad[None], router_grad.T], axis=0
    )
    small_rows = small.shape[0]
    small = jnp.pad(small, ((4, 12 - small_rows), (0, 0)))
    log_rows = jnp.pad(log_total[:, :, 0].T, ((0, 0), (0, 128 - head_count)))
    cos_wide = jnp.concatenate([cosine[:, 0], cosine[:, 0]], axis=1)
    sin_wide = jnp.concatenate([-sine_part[:, 0], sine_part[:, 0]], axis=1)
    tokens_grad, weight_grads, sums = unwind(
        [
            normed_grad,
            unit_two,
            wide(inv_two),
            tall(second_cols),
            out_grad,
            tokens,
            wide(inv_one),
            tall(own_cols(first_gain)),
            small,
            flat(queries),
            flat(keys_rot),
            flat(values_all),
            flat(earlier_keys),
            flat(earlier_values),
            context,
            log_rows,
            cos_wide,
            sin_wide,
        ],
        [normed_one, query_weight, key_weight, value_weight, output_weight],
        5,
    )
    share = model_dim // sources
    bias_width = HD // sources
    bias_sums = lax.dynamic_slice_in_dim(
        sums[1:4].reshape(3, head_count, HD), ep * bias_width, bias_width, 2
    )
    spread = jnp.concatenate([sums[:1], sums[4 : 4 + small_rows]], axis=0)
    spread = lax.all_gather(spread, "tp", axis=1, tiled=True)
    spread = lax.dynamic_slice_in_dim(spread, ep * share, share, 1)
    return (
        layer_out,
        tokens_grad,
        spread[0],
        weight_grads[1],
        weight_grads[2],
        weight_grads[3],
        bias_sums[0],
        bias_sums[1],
        bias_sums[2],
        weight_grads[0].T,
        spread[1],
        spread[3:].T,
        shared_gate_grad,
        shared_up_grad,
        shared_down_grad,
        spread[2],
        expert_grads[1].T[None],
        expert_grads[2].T[None],
        expert_grads[0][None],
    )


def solution(mesh):
    plan = dense_plan if dict(mesh.shape) == {"ep": 8, "tp": 4} else slot_plan
    return jax.shard_map(
        plan,
        mesh=mesh,
        in_specs=(
            P("ep", "tp"),
            P("ep", "tp"),
            P(),
            P(None, "tp"),
            P(None, "tp"),
            P(None, "tp"),
            P("tp"),
            P("tp"),
            P("tp"),
            P("tp", None),
            P(),
            P(),
            P(None, "tp"),
            P(None, "tp"),
            P("tp", None),
            P(),
            P("ep", None, "tp"),
            P("ep", None, "tp"),
            P("ep", "tp", None),
            P("ep", None),
            P("ep", None),
        ),
        out_specs=(
            P("ep", "tp"),
            P("ep", "tp"),
            P("ep"),
            P("ep", "tp"),
            P("ep", "tp"),
            P("ep", "tp"),
            P("tp", "ep"),
            P("tp", "ep"),
            P("tp", "ep"),
            P("tp", "ep"),
            P("ep"),
            P("ep", None),
            P("ep", "tp"),
            P("ep", "tp"),
            P("tp", "ep"),
            P("ep"),
            P("ep", None, "tp"),
            P("ep", None, "tp"),
            P("ep", "tp", None),
        ),
        check_vma=False,
    )
```

```python
import functools
import math

import jax
import jax.numpy as jnp
from jax import lax
from jax.experimental import pallas as pl
from jax.experimental.pallas import tpu as pltpu
from jax.sharding import PartitionSpec as P

HD = 128
BLOCK = 256
SPAN = 2


rope_theta = 1000000.0
norm_eps = 1e-06
masked_score = -1e30


def passed_along(value, axis, steps):
    count = lax.axis_size(axis)
    leading, last = (max(0, -steps), min(count, count - steps))
    return lax.ppermute(value, axis, [(source, source + steps) for source in range(leading, last)])


def rope_tables(row_count, head_dim, first_position):
    positions = jnp.arange(row_count, dtype=jnp.float32) + first_position.astype(jnp.float32)
    frequency = jnp.exp(
        jnp.arange(head_dim // 2, dtype=jnp.float32) * (-2.0 * math.log(rope_theta) / head_dim)
    )
    angles = positions[:, None] * frequency[None, :]
    return (jnp.cos(angles)[:, None, :], jnp.sin(angles)[:, None, :])


def rotate(values, cosine, sine_part):
    half_dim = values.shape[-1] // 2
    first_half = values[..., :half_dim]
    second_half = values[..., half_dim:]
    return jnp.concatenate(
        [
            first_half * cosine - second_half * sine_part,
            second_half * cosine + first_half * sine_part,
        ],
        axis=-1,
    )


def inner_rows(left_side, right_side):
    return lax.dot_general(
        left_side, right_side, (((0,), (0,)), ((), ())), preferred_element_type=jnp.float32
    )


def times_transpose(left_side, right_side):
    return lax.dot_general(
        left_side, right_side, (((1,), (1,)), ((), ())), preferred_element_type=jnp.float32
    )


def row_stats(values):
    inv_rms = lax.rsqrt(jnp.mean(values * values, axis=-1, keepdims=True) + norm_eps)
    return (values * inv_rms, inv_rms)


def norm_back(grad_rows, unit_rows, inv_rms, gain_vec):
    scaled = grad_rows * gain_vec
    return inv_rms * (scaled - unit_rows * jnp.mean(scaled * unit_rows, axis=-1, keepdims=True))


def softmax_rows(scores):
    row_max = jnp.max(scores, axis=-1, keepdims=True)
    powers = jnp.exp(scores - row_max)
    return powers / jnp.sum(powers, axis=-1, keepdims=True)


def to_experts(block_rows, local_count):
    sources, span_rows, col_count = block_rows.shape
    slot_count = span_rows // local_count
    shaped = block_rows.reshape(sources, local_count, slot_count, col_count)
    return shaped.swapaxes(0, 1).reshape(local_count, sources * slot_count, col_count)


def to_sources(block_rows, sources):
    local_count, rows_all, col_count = block_rows.shape
    slot_count = rows_all // sources
    shaped = block_rows.reshape(local_count, sources, slot_count, col_count)
    return shaped.swapaxes(0, 1).reshape(sources, local_count * slot_count, col_count)


def deliver(block_rows):
    arrived = lax.all_to_all(block_rows, "ep", split_axis=0, concat_axis=0, tiled=True)
    return arrived


def collect(block_rows):
    return lax.all_to_all(block_rows, "ep", split_axis=0, concat_axis=0, tiled=True)


def slot_plan(
    tokens,
    out_grad,
    first_gain,
    query_weight,
    key_weight,
    value_weight,
    query_bias,
    key_bias,
    value_bias,
    output_weight,
    second_gain,
    router_weight,
    shared_gate_weight,
    shared_up_weight,
    shared_down_weight,
    switch_vector,
    expert_gate_weight,
    expert_up_weight,
    expert_down_weight,
    expert_ids,
    pair_order,
):
    whole_in, whole_grad = (
        lax.all_gather(tokens, "tp", axis=1, tiled=True),
        lax.all_gather(out_grad, "tp", axis=1, tiled=True),
    )
    tok_count = whole_in.shape[0]
    model_dim = whole_in.shape[1]
    col_width = tokens.shape[1]
    col_start = lax.axis_index("tp") * col_width
    sources = lax.axis_size("ep")
    place_in_seq = lax.axis_index("ep") % SPAN
    has_earlier = place_in_seq > 0
    local_experts = expert_gate_weight.shape[0]
    expert_total = router_weight.shape[1]
    top_count = expert_ids.shape[1]
    pair_count = tok_count * top_count
    capacity = 9 * pair_count // (8 * expert_total)
    head_count = query_weight.shape[1] // HD
    score_scale = HD ** (-0.5)
    inputs_full = whole_in.astype(jnp.float32)
    unit_one, inv_one = row_stats(inputs_full)
    normed_one = (unit_one * first_gain).astype(jnp.bfloat16)
    query_lin = jnp.dot(normed_one, query_weight, preferred_element_type=jnp.float32) + query_bias
    key_lin = jnp.dot(normed_one, key_weight, preferred_element_type=jnp.float32) + key_bias
    value_lin = jnp.dot(normed_one, value_weight, preferred_element_type=jnp.float32) + value_bias
    cosine, sine_part = rope_tables(tok_count, HD, place_in_seq * tok_count)
    queries = rotate(query_lin.reshape(tok_count, head_count, HD), cosine, sine_part).astype(
        jnp.bfloat16
    )
    keys_rot = rotate(key_lin.reshape(tok_count, head_count, HD), cosine, sine_part).astype(
        jnp.bfloat16
    )
    values_all = value_lin.reshape(tok_count, head_count, HD).astype(jnp.bfloat16)
    earlier_keys, earlier_values = passed_along((keys_rot, values_all), "ep", 1)
    keys_both = jnp.concatenate([earlier_keys, keys_rot], axis=0)
    values_both = jnp.concatenate([earlier_values, values_all], axis=0)
    blocks = jnp.arange(tok_count) // BLOCK
    local_allowed = blocks[None, :] <= blocks[:, None]
    remote_allowed = jnp.broadcast_to(has_earlier, (tok_count, tok_count))
    allowed = jnp.concatenate([remote_allowed, local_allowed], axis=1)[None]

    def attention_scores():
        scored = (
            jnp.einsum("qhd,khd->hqk", queries, keys_both, preferred_element_type=jnp.float32)
            * score_scale
        )
        return jnp.where(allowed, scored, masked_score)

    scores = attention_scores()
    row_max = jnp.max(scores, axis=-1, keepdims=True)
    powers = jnp.exp(scores - row_max)
    totals = jnp.sum(powers, axis=-1, keepdims=True)
    log_total = row_max + jnp.log(totals)
    probs_low = (powers / totals).astype(jnp.bfloat16)
    context = jnp.einsum("hqk,khd->qhd", probs_low, values_both, preferred_element_type=jnp.float32)
    context = context.reshape(tok_count, head_count * HD).astype(jnp.bfloat16)
    attn_part = jnp.dot(context, output_weight, preferred_element_type=jnp.float32)
    attended = lax.psum(attn_part, "tp")
    hidden_one = inputs_full + attended
    unit_two, inv_two = row_stats(hidden_one)
    normed_two = (unit_two * second_gain).astype(jnp.bfloat16)
    logits = jnp.dot(normed_two, router_weight, preferred_element_type=jnp.float32)
    router_probs = softmax_rows(logits)
    gate_values = jnp.take_along_axis(router_probs, expert_ids, axis=1)
    switch = jax.nn.sigmoid(jnp.dot(normed_two, switch_vector, preferred_element_type=jnp.float32))
    flat_ids = expert_ids.reshape(-1)
    turn_order = pair_order.reshape(-1)
    in_turn = flat_ids[turn_order]
    onehot = (in_turn[:, None] == jnp.arange(expert_total, dtype=jnp.int32)[None, :]).astype(
        jnp.int32
    )
    earlier = jnp.cumsum(onehot, axis=0) - onehot
    turn_slot = jnp.sum(earlier * onehot, axis=1)
    slot_index = jnp.zeros((pair_count,), jnp.int32).at[turn_order].set(turn_slot)
    kept_pair = slot_index < capacity
    slot_rows = expert_total * capacity
    target = jnp.where(kept_pair, flat_ids * capacity + slot_index, slot_rows)
    pair_token = jnp.arange(pair_count, dtype=jnp.int32) // top_count
    slot_token = (
        jnp.full((slot_rows + 1,), tok_count, jnp.int32).at[target].set(pair_token)[:slot_rows]
    )
    slot_gate = (
        jnp.zeros((slot_rows + 1,), jnp.float32).at[target].set(gate_values.reshape(-1))[:slot_rows]
    )
    padded_two = jnp.concatenate([normed_two, jnp.zeros((1, model_dim), jnp.bfloat16)], axis=0)
    send_rows = padded_two[slot_token].reshape(sources, local_experts * capacity, model_dim)
    expert_rows = to_experts(deliver(send_rows), local_experts)
    gate_lin = jnp.einsum(
        "erd,edf->erf", expert_rows, expert_gate_weight, preferred_element_type=jnp.float32
    )
    up_lin = jnp.einsum(
        "erd,edf->erf", expert_rows, expert_up_weight, preferred_element_type=jnp.float32
    )
    gate_sig = jax.nn.sigmoid(gate_lin)
    gate_act = gate_lin * gate_sig
    expert_hidden = (gate_act * up_lin).astype(jnp.bfloat16)
    expert_part = jnp.einsum(
        "erf,efd->erd", expert_hidden, expert_down_weight, preferred_element_type=jnp.float32
    )
    shared_gate_lin = jnp.dot(normed_two, shared_gate_weight, preferred_element_type=jnp.float32)
    shared_up_lin = jnp.dot(normed_two, shared_up_weight, preferred_element_type=jnp.float32)
    shared_sig = jax.nn.sigmoid(shared_gate_lin)
    shared_act = shared_gate_lin * shared_sig
    shared_hidden = (shared_act * shared_up_lin).astype(jnp.bfloat16)
    shared_part = jnp.dot(shared_hidden, shared_down_weight, preferred_element_type=jnp.float32)
    expert_cols, shared_cols = (
        lax.psum_scatter(expert_part.reshape(-1, model_dim), "tp", scatter_dimension=1, tiled=True),
        lax.psum_scatter(shared_part, "tp", scatter_dimension=1, tiled=True),
    )
    returned = collect(
        to_sources(expert_cols.astype(jnp.bfloat16).reshape(local_experts, -1, col_width), sources)
    )
    back_flat = jnp.concatenate(
        [returned.reshape(slot_rows, col_width), jnp.zeros((1, col_width), jnp.bfloat16)], axis=0
    )
    pair_out = back_flat[target].astype(jnp.float32).reshape(tok_count, top_count, col_width)
    routed = jnp.sum(gate_values[:, :, None] * pair_out, axis=1)
    hidden_cols = lax.dynamic_slice_in_dim(hidden_one, col_start, col_width, 1)
    layer_out = (hidden_cols + switch[:, None] * shared_cols + routed).astype(jnp.bfloat16)
    grad_full = whole_grad.astype(jnp.float32)
    grad_cols = out_grad.astype(jnp.float32)
    gate_part = jnp.sum(pair_out * grad_cols[:, None, :], axis=-1)
    switch_part = jnp.sum(grad_cols * shared_cols, axis=-1)
    gate_grad, switch_grad = lax.psum((gate_part, switch_part), "tp")
    padded_grad = jnp.concatenate([whole_grad, jnp.zeros((1, model_dim), jnp.bfloat16)], axis=0)
    send_grads = (slot_gate[:, None] * padded_grad[slot_token].astype(jnp.float32)).astype(
        jnp.bfloat16
    )
    expert_grads = to_experts(
        deliver(send_grads.reshape(sources, local_experts * capacity, model_dim)), local_experts
    )
    hidden_grad = jnp.einsum(
        "erd,efd->erf", expert_grads, expert_down_weight, preferred_element_type=jnp.float32
    )
    gate_lin_grad = (hidden_grad * up_lin * gate_sig * (1.0 + gate_lin * (1.0 - gate_sig))).astype(
        jnp.bfloat16
    )
    up_lin_grad = (hidden_grad * gate_act).astype(jnp.bfloat16)
    expert_down_grad = jnp.einsum(
        "erf,erd->efd", expert_hidden, expert_grads, preferred_element_type=jnp.float32
    )
    expert_gate_grad = jnp.einsum(
        "erd,erf->edf", expert_rows, gate_lin_grad, preferred_element_type=jnp.float32
    )
    expert_up_grad = jnp.einsum(
        "erd,erf->edf", expert_rows, up_lin_grad, preferred_element_type=jnp.float32
    )
    rows_grad = jnp.einsum(
        "erf,edf->erd", gate_lin_grad, expert_gate_weight, preferred_element_type=jnp.float32
    )
    rows_grad = rows_grad + jnp.einsum(
        "erf,edf->erd", up_lin_grad, expert_up_weight, preferred_element_type=jnp.float32
    )
    rows_grad_cols = lax.psum_scatter(
        rows_grad.reshape(-1, model_dim), "tp", scatter_dimension=1, tiled=True
    )
    returned_grad = collect(
        to_sources(
            rows_grad_cols.astype(jnp.bfloat16).reshape(local_experts, -1, col_width), sources
        )
    )
    back_grad = jnp.concatenate(
        [returned_grad.reshape(slot_rows, col_width), jnp.zeros((1, col_width), jnp.bfloat16)],
        axis=0,
    )
    routed_grad = jnp.sum(
        back_grad[target].astype(jnp.float32).reshape(tok_count, top_count, col_width), axis=1
    )
    shared_out_grad = (switch[:, None] * grad_full).astype(jnp.bfloat16)
    shared_hidden_grad = times_transpose(shared_out_grad, shared_down_weight)
    shared_gate_lin_grad = (
        shared_hidden_grad
        * shared_up_lin
        * shared_sig
        * (1.0 + shared_gate_lin * (1.0 - shared_sig))
    ).astype(jnp.bfloat16)
    shared_up_lin_grad = (shared_hidden_grad * shared_act).astype(jnp.bfloat16)
    shared_down_grad = inner_rows(shared_hidden, shared_out_grad)
    shared_gate_grad = inner_rows(normed_two, shared_gate_lin_grad)
    shared_up_grad = inner_rows(normed_two, shared_up_lin_grad)
    normed_grad = times_transpose(shared_gate_lin_grad, shared_gate_weight) + times_transpose(
        shared_up_lin_grad, shared_up_weight
    )
    normed_grad = normed_grad + lax.dynamic_update_slice_in_dim(
        jnp.zeros_like(normed_grad), routed_grad, col_start, 1
    )
    normed_grad = lax.psum(normed_grad, "tp")
    picked = (
        expert_ids[:, :, None] == jnp.arange(expert_total, dtype=jnp.int32)[None, None, :]
    ).astype(jnp.float32)
    probs_grad = jnp.sum(picked * gate_grad[:, :, None], axis=1)
    logit_grad = (
        router_probs * (probs_grad - jnp.sum(router_probs * probs_grad, axis=-1, keepdims=True))
    ).astype(jnp.bfloat16)
    router_grad = inner_rows(normed_two, logit_grad)
    switch_lin_grad = switch_grad * switch * (1.0 - switch)
    switch_vector_grad = jnp.dot(switch_lin_grad, normed_two, preferred_element_type=jnp.float32)
    normed_grad = normed_grad + times_transpose(logit_grad, router_weight)
    normed_grad = (
        normed_grad + switch_lin_grad[:, None] * switch_vector.astype(jnp.float32)[None, :]
    )
    second_gain_grad = jnp.sum(normed_grad * unit_two, axis=0)
    hidden_grad_one = grad_full + norm_back(normed_grad, unit_two, inv_two, second_gain)
    attended_grad = hidden_grad_one.astype(jnp.bfloat16)
    output_grad = inner_rows(context, attended_grad)
    context_grad = (
        times_transpose(attended_grad, output_weight)
        .astype(jnp.bfloat16)
        .reshape(tok_count, head_count, HD)
    )
    scores = attention_scores()
    attn_probs = jnp.exp(scores - log_total)
    probs_again = attn_probs.astype(jnp.bfloat16)
    probs_grad_att = jnp.einsum(
        "qhd,khd->hqk", context_grad, values_both, preferred_element_type=jnp.float32
    )
    values_both_grad = jnp.einsum(
        "hqk,qhd->khd", probs_again, context_grad, preferred_element_type=jnp.float32
    )
    scores_grad = (
        attn_probs * (probs_grad_att - jnp.sum(attn_probs * probs_grad_att, axis=-1, keepdims=True))
    ).astype(jnp.bfloat16)
    queries_grad = (
        jnp.einsum("hqk,khd->qhd", scores_grad, keys_both, preferred_element_type=jnp.float32)
        * score_scale
    )
    keys_both_grad = (
        jnp.einsum("hqk,qhd->khd", scores_grad, queries, preferred_element_type=jnp.float32)
        * score_scale
    )
    later_keys_grad, later_values_grad = passed_along(
        (keys_both_grad[:tok_count], values_both_grad[:tok_count]), "ep", -1
    )
    keep_later = jnp.where(has_earlier, 0.0, 1.0).astype(jnp.float32)
    keys_grad = keys_both_grad[tok_count:] + keep_later * later_keys_grad
    values_grad = values_both_grad[tok_count:] + keep_later * later_values_grad
    value_lin_grad = values_grad.reshape(tok_count, head_count * HD).astype(jnp.bfloat16)
    query_lin_grad = (
        rotate(queries_grad, cosine, -sine_part)
        .reshape(tok_count, head_count * HD)
        .astype(jnp.bfloat16)
    )
    key_lin_grad = (
        rotate(keys_grad, cosine, -sine_part)
        .reshape(tok_count, head_count * HD)
        .astype(jnp.bfloat16)
    )
    query_grad = inner_rows(normed_one, query_lin_grad)
    key_grad = inner_rows(normed_one, key_lin_grad)
    value_grad = inner_rows(normed_one, value_lin_grad)
    query_bias_grad = jnp.sum(query_lin_grad.astype(jnp.float32), axis=0).reshape(head_count, HD)
    key_bias_grad = jnp.sum(key_lin_grad.astype(jnp.float32), axis=0).reshape(head_count, HD)
    value_bias_grad = jnp.sum(value_lin_grad.astype(jnp.float32), axis=0).reshape(head_count, HD)
    normed_one_grad = times_transpose(query_lin_grad, query_weight) + times_transpose(
        key_lin_grad, key_weight
    )
    normed_one_grad = normed_one_grad + times_transpose(value_lin_grad, value_weight)
    normed_one_grad = lax.psum(normed_one_grad.astype(jnp.bfloat16), "tp").astype(jnp.float32)
    first_gain_grad = jnp.sum(normed_one_grad * unit_one, axis=0)
    input_grad = hidden_grad_one + norm_back(normed_one_grad, unit_one, inv_one, first_gain)
    tokens_grad = lax.dynamic_slice_in_dim(input_grad, col_start, col_width, 1).astype(jnp.bfloat16)
    reduced = (
        lax.psum_scatter(
            first_gain_grad.astype(jnp.bfloat16), "ep", scatter_dimension=0, tiled=True
        ).astype(jnp.float32),
        lax.psum_scatter(
            query_grad.astype(jnp.bfloat16), "ep", scatter_dimension=0, tiled=True
        ).astype(jnp.float32),
        lax.psum_scatter(
            key_grad.astype(jnp.bfloat16), "ep", scatter_dimension=0, tiled=True
        ).astype(jnp.float32),
        lax.psum_scatter(
            value_grad.astype(jnp.bfloat16), "ep", scatter_dimension=0, tiled=True
        ).astype(jnp.float32),
        lax.psum_scatter(
            query_bias_grad.astype(jnp.bfloat16), "ep", scatter_dimension=1, tiled=True
        ).astype(jnp.float32),
        lax.psum_scatter(
            key_bias_grad.astype(jnp.bfloat16), "ep", scatter_dimension=1, tiled=True
        ).astype(jnp.float32),
        lax.psum_scatter(
            value_bias_grad.astype(jnp.bfloat16), "ep", scatter_dimension=1, tiled=True
        ).astype(jnp.float32),
        lax.psum_scatter(
            output_grad.astype(jnp.bfloat16), "ep", scatter_dimension=1, tiled=True
        ).astype(jnp.float32),
        lax.psum_scatter(
            second_gain_grad.astype(jnp.bfloat16), "ep", scatter_dimension=0, tiled=True
        ).astype(jnp.float32),
        lax.psum_scatter(
            router_grad.astype(jnp.bfloat16), "ep", scatter_dimension=0, tiled=True
        ).astype(jnp.float32),
        lax.psum_scatter(
            shared_gate_grad.astype(jnp.bfloat16), "ep", scatter_dimension=0, tiled=True
        ).astype(jnp.float32),
        lax.psum_scatter(
            shared_up_grad.astype(jnp.bfloat16), "ep", scatter_dimension=0, tiled=True
        ).astype(jnp.float32),
        lax.psum_scatter(
            shared_down_grad.astype(jnp.bfloat16), "ep", scatter_dimension=1, tiled=True
        ).astype(jnp.float32),
        lax.psum_scatter(
            switch_vector_grad.astype(jnp.bfloat16), "ep", scatter_dimension=0, tiled=True
        ).astype(jnp.float32),
    )
    return (
        layer_out,
        tokens_grad,
        reduced[0],
        reduced[1],
        reduced[2],
        reduced[3],
        reduced[4],
        reduced[5],
        reduced[6],
        reduced[7],
        reduced[8],
        reduced[9],
        reduced[10],
        reduced[11],
        reduced[12],
        reduced[13],
        expert_gate_grad,
        expert_up_grad,
        expert_down_grad,
    )


MESH = pl.DeviceIdType.MESH
Z_ORDER = (0, 3, 1, 2)


def place():
    ep, tp = lax.axis_index("ep"), lax.axis_index("tp")
    return ep, tp, ep // 2, lax.rem(ep, 2), tp // 2, lax.rem(tp, 2)


def greet(always, along_z=False):
    barrier = pltpu.get_barrier_semaphore()
    for device in always:
        pl.semaphore_signal(barrier, inc=1, device_id=device, device_id_type=MESH)
    count = len(always)
    if along_z:
        ep, tp, z, _, _, _ = place()

        @pl.when(z < 3)
        def _():
            pl.semaphore_signal(barrier, inc=1, device_id=(ep + 2, tp), device_id_type=MESH)

        @pl.when(z > 0)
        def _():
            pl.semaphore_signal(barrier, inc=1, device_id=(ep - 2, tp), device_id_type=MESH)

        count = count + lax.min(z, 1) + lax.min(3 - z, 1)
    pl.semaphore_wait(barrier, count)


def remote(source, target, send_sem, recv_sem, device):
    return pltpu.make_async_remote_copy(
        src_ref=source,
        dst_ref=target,
        send_sem=send_sem,
        recv_sem=recv_sem,
        device_id=device,
        device_id_type=MESH,
    )


def add_blocks(target, sources, rows):
    step = next(size for size in (80, 64, 48, 16) if rows % size == 0)

    def body(i, carry):
        span = pl.ds(pl.multiple_of(i * step, 16), step)
        total = target[span, :]
        for source in sources:
            total = total + source[span, :].astype(target.dtype)
        target[span, :] = total
        return carry

    lax.fori_loop(0, rows // step, body, 0)


def gather_tp_kernel(x_ref, o_ref, send_sem, recv_sem, own_sem):
    ep, tp, _, _, x, core = place()
    cols = x_ref.shape[1]
    sibling = (ep, tp + 1 - 2 * core)
    across = (ep, tp + 2 - 4 * x)
    greet([sibling, across])
    mine = o_ref.at[:, pl.ds(pl.multiple_of(tp * cols, cols), cols)]
    theirs = o_ref.at[:, pl.ds(pl.multiple_of((tp + 2 - 4 * x) * cols, cols), cols)]
    out_x = remote(x_ref, mine, send_sem.at[0], recv_sem.at[0], across)
    out_s = remote(x_ref, mine, send_sem.at[1], recv_sem.at[1], sibling)
    own = pltpu.make_async_copy(x_ref, mine, own_sem)
    out_x.start()
    out_s.start()
    own.start()
    remote(x_ref, theirs, send_sem.at[0], recv_sem.at[0], across).wait_recv()
    passing = remote(theirs, theirs, send_sem.at[2], recv_sem.at[2], sibling)
    passing.start()
    out_s.wait_recv()
    passing.wait_recv()
    own.wait()
    out_x.wait_send()
    out_s.wait_send()
    passing.wait_send()


def gather_tp(value, cid):
    rows, cols = value.shape
    return pl.pallas_call(
        gather_tp_kernel,
        out_shape=jax.ShapeDtypeStruct((rows, 4 * cols), value.dtype),
        in_specs=[pl.BlockSpec(memory_space=pl.ANY)],
        out_specs=pl.BlockSpec(memory_space=pl.ANY),
        scratch_shapes=[
            pltpu.SemaphoreType.DMA((3,)),
            pltpu.SemaphoreType.DMA((3,)),
            pltpu.SemaphoreType.DMA,
        ],
        compiler_params=pltpu.CompilerParams(collective_id=cid, has_side_effects=True),
        name="gather_tp",
    )(value)


def scatter_tp_kernel(p_ref, o_ref, mine, from_sib, from_x, own_sem, send_sem, recv_sem):
    ep, tp, _, _, x, core = place()
    rows, cols = o_ref.shape
    sibling = (ep, tp + 1 - 2 * core)
    across = (ep, tp + 2 - 4 * x)
    greet([sibling, across])

    def part(x_at, core_at):
        return p_ref.at[:, pl.ds(pl.multiple_of((x_at * 2 + core_at) * cols, cols), cols)]

    sends, owns = [], []
    for i, x_at in enumerate((1 - x, x)):
        owns.append(pltpu.make_async_copy(part(x_at, core), mine.at[i], own_sem.at[i]))
        sends.append(
            remote(part(x_at, 1 - core), from_sib.at[i], send_sem.at[i], recv_sem.at[i], sibling)
        )
        sends[-1].start()
        owns[-1].start()
    owns[0].wait()
    sends[0].wait_recv()
    add_blocks(mine.at[0], [from_sib.at[0]], rows)
    out_x = remote(mine.at[0], from_x, send_sem.at[2], recv_sem.at[2], across)
    out_x.start()
    owns[1].wait()
    sends[1].wait_recv()
    out_x.wait_recv()
    o_ref[...] = jnp.zeros_like(o_ref)
    add_blocks(o_ref, [mine.at[1], from_sib.at[1], from_x], rows)
    out_x.wait_send()
    sends[0].wait_send()
    sends[1].wait_send()


def scatter_tp(value, cid):
    rows, cols = value.shape[0], value.shape[1] // 4
    return pl.pallas_call(
        scatter_tp_kernel,
        out_shape=jax.ShapeDtypeStruct((rows, cols), jnp.float32),
        in_specs=[pl.BlockSpec(memory_space=pl.ANY)],
        out_specs=pl.BlockSpec(memory_space=pltpu.VMEM),
        scratch_shapes=[
            pltpu.VMEM((2, rows, cols), value.dtype),
            pltpu.VMEM((2, rows, cols), value.dtype),
            pltpu.VMEM((rows, cols), value.dtype),
            pltpu.SemaphoreType.DMA((2,)),
            pltpu.SemaphoreType.DMA((3,)),
            pltpu.SemaphoreType.DMA((3,)),
        ],
        compiler_params=pltpu.CompilerParams(
            collective_id=cid, has_side_effects=True, vmem_limit_bytes=32 * 2**20
        ),
        name="scatter_tp",
    )(value)


def lane_peers():
    ep, tp, z, y, x, core = place()
    to_y, to_x = 1 - 2 * y, 1 - 2 * x
    peer_a = (ep + (1 - core) * to_y, tp + core * 2 * to_x)
    peer_b = (ep + core * to_y, tp + (1 - core) * 2 * to_x)
    sibling = (ep, tp + 1 - 2 * core)
    above, below = (ep + 2, tp), (ep - 2, tp)
    return peer_a, peer_b, sibling, above, below


def lane_spot(z_at, da, db, core_at):
    _, _, _, y, x, _ = place()
    y_at = y + (1 - 2 * y) * ((1 - core_at) * da + core_at * db)
    x_at = x + (1 - 2 * x) * (core_at * da + (1 - core_at) * db)
    return z_at * 2 + y_at, x_at * 2 + core_at


def gather_all_kernel(x_ref, o_ref, up_sem, down_sem, a_sem, b_sem, s_sem, recv_sem, sib_sem, own_sem):
    ep, tp, z, y, x, core = place()
    rows, cols = x_ref.shape
    peer_a, peer_b, sibling, above, below = lane_peers()
    greet([peer_a, peer_b, sibling], True)

    def spot(z_at, da, db):
        group, quarter = lane_spot(z_at, da, db, core)
        return o_ref.at[
            pl.ds(pl.multiple_of(group * rows, rows), rows),
            pl.ds(pl.multiple_of(quarter * cols, cols), cols),
        ]

    def at(z_at, da, db):
        return z_at * 4 + da * 2 + db

    def arrived(z_at, da, db):
        block = spot(z_at, da, db)
        remote(block, block, s_sem.at[at(z_at, da, db)], recv_sem.at[at(z_at, da, db)], sibling).wait_recv()

    def up(z_at, source):
        return remote(source, spot(z_at, 0, 0), up_sem.at[z_at], recv_sem.at[at(z_at, 0, 0)], above)

    def down(z_at, source):
        return remote(source, spot(z_at, 0, 0), down_sem.at[z_at], recv_sem.at[at(z_at, 0, 0)], below)

    def over_a(z_at, source):
        return remote(source, spot(z_at, 0, 0), a_sem.at[z_at], recv_sem.at[at(z_at, 1, 0)], peer_a)

    def over_b(z_at, da, source):
        return remote(
            source, spot(z_at, da, 0), b_sem.at[z_at * 2 + da], recv_sem.at[at(z_at, da, 1)], peer_b
        )

    def to_sibling(z_at, da, db, source):
        n = at(z_at, da, db)
        return remote(source, spot(z_at, da, db), s_sem.at[n], sib_sem.at[n], sibling)

    own = pltpu.make_async_copy(x_ref, spot(z, 0, 0), own_sem)
    over_b(z, 0, x_ref).start()
    over_a(z, x_ref).start()

    @pl.when(z < 3)
    def _():
        up(z, x_ref).start()

    @pl.when(z > 0)
    def _():
        down(z, x_ref).start()

    to_sibling(z, 0, 0, x_ref).start()
    own.start()

    def from_a(z_at):
        arrived(z_at, 1, 0)
        block = spot(z_at, 1, 0)
        over_b(z_at, 1, block).start()
        to_sibling(z_at, 1, 0, block).start()

    def from_z(z_at, onward):
        arrived(z_at, 0, 0)
        block = spot(z_at, 0, 0)
        onward(block)
        over_a(z_at, block).start()
        over_b(z_at, 0, block).start()
        to_sibling(z_at, 0, 0, block).start()

    def from_below(z_at):
        def onward(block):
            @pl.when(z < 3)
            def _():
                up(z_at, block).start()

        from_z(z_at, onward)

    def from_above(z_at):
        def onward(block):
            @pl.when(z > 0)
            def _():
                down(z_at, block).start()

        from_z(z_at, onward)

    for d in range(1, 4):

        @pl.when(z >= d)
        def _(d=d):
            from_below(z - d)

        @pl.when(z + d <= 3)
        def _(d=d):
            from_above(z + d)

        if d == 1:
            from_a(z)
        else:

            @pl.when(z >= d - 1)
            def _(d=d):
                from_a(z - d + 1)

            @pl.when(z + d - 1 <= 3)
            def _(d=d):
                from_a(z + d - 1)

    @pl.when(z >= 3)
    def _():
        from_a(z - 3)

    @pl.when(z + 3 <= 3)
    def _():
        from_a(z + 3)

    def from_b(z_at, da):
        arrived(z_at, da, 1)
        to_sibling(z_at, da, 1, spot(z_at, da, 1)).start()

    for da in range(2):
        from_b(z, da)
    for d in range(1, 4):
        for da in range(2):

            @pl.when(z >= d)
            def _(d=d, da=da):
                from_b(z - d, da)

            @pl.when(z + d <= 3)
            def _(d=d, da=da):
                from_b(z + d, da)

    def finish_sibling(i, carry):
        block = spot(0, 0, 0)
        copy = remote(block, block, s_sem.at[i], sib_sem.at[i], sibling)
        copy.wait_recv()
        copy.wait_send()
        return carry

    lax.fori_loop(0, 16, finish_sibling, 0)

    def finish_links(i, carry):
        over_a(i, x_ref).wait_send()
        over_b(i, 0, x_ref).wait_send()
        over_b(i, 1, x_ref).wait_send()

        @pl.when((z < 3) & (i <= z))
        def _():
            up(i, x_ref).wait_send()

        @pl.when((z > 0) & (i >= z))
        def _():
            down(i, x_ref).wait_send()

        return carry

    lax.fori_loop(0, 4, finish_links, 0)
    own.wait()


def gather_all(value, cid):
    rows, cols = value.shape
    return pl.pallas_call(
        gather_all_kernel,
        out_shape=jax.ShapeDtypeStruct((8 * rows, 4 * cols), value.dtype),
        in_specs=[pl.BlockSpec(memory_space=pl.ANY)],
        out_specs=pl.BlockSpec(memory_space=pl.ANY),
        scratch_shapes=[
            pltpu.SemaphoreType.DMA((4,)),
            pltpu.SemaphoreType.DMA((4,)),
            pltpu.SemaphoreType.DMA((4,)),
            pltpu.SemaphoreType.DMA((8,)),
            pltpu.SemaphoreType.DMA((16,)),
            pltpu.SemaphoreType.DMA((16,)),
            pltpu.SemaphoreType.DMA((16,)),
            pltpu.SemaphoreType.DMA,
        ],
        compiler_params=pltpu.CompilerParams(collective_id=cid, has_side_effects=True),
        name="gather_all",
    )(value)


def z_chain(blocks, totals, from_below, from_above, up_send, up_recv, down_send, down_recv, rows, final):
    ep, tp, z, _, _, _ = place()
    above, below = (ep + 2, tp), (ep - 2, tp)

    def up(z_at):
        return remote(totals(z_at), from_below.at[z_at], up_send.at[z_at], up_recv.at[z_at], above)

    def down(z_at):
        return remote(totals(z_at), from_above.at[z_at], down_send.at[z_at], down_recv.at[z_at], below)

    for z_at in Z_ORDER:
        blocks(z_at)

        @pl.when(z_at > z)
        def _(z_at=z_at):
            @pl.when(z > 0)
            def _():
                up(z_at).wait_recv()
                add_blocks(totals(z_at), [from_below.at[z_at]], rows)

            up(z_at).start()

        @pl.when(z_at < z)
        def _(z_at=z_at):
            @pl.when(z < 3)
            def _():
                down(z_at).wait_recv()
                add_blocks(totals(z_at), [from_above.at[z_at]], rows)

            down(z_at).start()

    for z_at in range(4):

        @pl.when(z_at == z)
        def _(z_at=z_at):
            @pl.when(z > 0)
            def _():
                up(z_at).wait_recv()

            @pl.when(z < 3)
            def _():
                down(z_at).wait_recv()

            @pl.when(z == 0)
            def _():
                final(z_at, [from_above.at[z_at]])

            @pl.when(z == 3)
            def _():
                final(z_at, [from_below.at[z_at]])

            @pl.when((z > 0) & (z < 3))
            def _():
                final(z_at, [from_below.at[z_at], from_above.at[z_at]])

    for z_at in range(4):

        @pl.when(z_at > z)
        def _(z_at=z_at):
            up(z_at).wait_send()

        @pl.when(z_at < z)
        def _(z_at=z_at):
            down(z_at).wait_send()


def scatter_all_kernel(
    p_ref,
    o_ref,
    mine,
    from_sib,
    from_b,
    from_a,
    from_below,
    from_above,
    own_sem,
    s_send,
    s_recv,
    b_send,
    b_recv,
    a_send,
    a_recv,
    up_send,
    up_recv,
    down_send,
    down_recv,
):
    ep, tp, z, y, x, core = place()
    rows, cols = o_ref.shape
    peer_a, peer_b, sibling, above, below = lane_peers()
    greet([peer_a, peer_b, sibling], True)

    def part(z_at, da, db, core_at):
        group, quarter = lane_spot(z_at, da, db, core_at)
        return p_ref.at[
            pl.ds(pl.multiple_of(group * rows, rows), rows),
            pl.ds(pl.multiple_of(quarter * cols, cols), cols),
        ]

    def at(z_at, da, db):
        return z_at * 4 + da * 2 + db

    def own(z_at, da, db):
        n = at(z_at, da, db)
        return pltpu.make_async_copy(part(z_at, da, db, core), mine.at[n], own_sem.at[n])

    def to_sibling(z_at, da, db):
        n = at(z_at, da, db)
        return remote(
            part(z_at, da, db, 1 - core), from_sib.at[n], s_send.at[n], s_recv.at[n], sibling
        )

    for da, db in ((1, 1), (0, 1), (1, 0), (0, 0)):
        for z_at in Z_ORDER:
            to_sibling(z_at, da, db).start()
            own(z_at, da, db).start()

    def here(z_at, da, db):
        own(z_at, da, db).wait()
        to_sibling(z_at, da, db).wait_recv()
        return mine.at[at(z_at, da, db)], from_sib.at[at(z_at, da, db)]

    def over_b(z_at, da):
        n = z_at * 2 + da
        return remote(mine.at[at(z_at, da, 1)], from_b.at[n], b_send.at[n], b_recv.at[n], peer_b)

    def over_a(z_at):
        return remote(mine.at[at(z_at, 1, 0)], from_a.at[z_at], a_send.at[z_at], a_recv.at[z_at], peer_a)

    for da in (1, 0):
        for z_at in Z_ORDER:
            own_part, sib_part = here(z_at, da, 1)
            add_blocks(own_part, [sib_part], rows)
            over_b(z_at, da).start()
    for z_at in Z_ORDER:
        own_part, sib_part = here(z_at, 1, 0)
        over_b(z_at, 1).wait_recv()
        add_blocks(own_part, [sib_part, from_b.at[z_at * 2 + 1]], rows)
        over_a(z_at).start()

    def blocks(z_at):
        own_part, sib_part = here(z_at, 0, 0)
        over_b(z_at, 0).wait_recv()
        over_a(z_at).wait_recv()
        add_blocks(own_part, [sib_part, from_b.at[z_at * 2], from_a.at[z_at]], rows)

    def final(z_at, others):
        o_ref[...] = jnp.zeros_like(o_ref)
        add_blocks(o_ref, [mine.at[at(z_at, 0, 0)], *others], rows)

    z_chain(
        blocks,
        lambda z_at: mine.at[at(z_at, 0, 0)],
        from_below,
        from_above,
        up_send,
        up_recv,
        down_send,
        down_recv,
        rows,
        final,
    )
    for z_at in range(4):
        over_a(z_at).wait_send()
        for da in range(2):
            over_b(z_at, da).wait_send()
            for db in range(2):
                to_sibling(z_at, da, db).wait_send()


def scatter_all(value, cid):
    rows, cols = value.shape[0] // 8, value.shape[1] // 4
    dma = pltpu.SemaphoreType.DMA

    def held(count):
        return pltpu.VMEM((count, rows, cols), value.dtype)

    return pl.pallas_call(
        scatter_all_kernel,
        out_shape=jax.ShapeDtypeStruct((rows, cols), jnp.float32),
        in_specs=[pl.BlockSpec(memory_space=pl.ANY)],
        out_specs=pl.BlockSpec(memory_space=pltpu.VMEM),
        scratch_shapes=[held(16), held(16), held(8), held(4), held(4), held(4)]
        + [dma((16,)), dma((16,)), dma((16,)), dma((8,)), dma((8,))]
        + [dma((4,))] * 6,
        compiler_params=pltpu.CompilerParams(
            collective_id=cid, has_side_effects=True, vmem_limit_bytes=48 * 2**20
        ),
        name="scatter_all",
    )(value)


def scatter_ep_kernel(
    p_ref, e_ref, o_ref, mine, from_y, from_below, from_above, own_sem, y_send, y_recv, up_send, up_recv, down_send, down_recv
):
    ep, tp, z, y, _, _ = place()
    rows, extra = p_ref.shape[0] // 8, e_ref.shape[0]
    tall = rows + extra
    across = (ep + 1 - 2 * y, tp)
    greet([across], True)

    def part(z_at, y_at):
        return p_ref.at[pl.ds(pl.multiple_of((z_at * 2 + y_at) * rows, rows), rows), :]

    def own(z_at):
        return (
            pltpu.make_async_copy(part(z_at, y), mine.at[z_at, pl.ds(0, rows)], own_sem.at[z_at]),
            pltpu.make_async_copy(e_ref, mine.at[z_at, pl.ds(rows, extra)], own_sem.at[4 + z_at]),
        )

    def over_y(z_at):
        return (
            remote(
                part(z_at, 1 - y),
                from_y.at[z_at, pl.ds(0, rows)],
                y_send.at[z_at],
                y_recv.at[z_at],
                across,
            ),
            remote(
                e_ref,
                from_y.at[z_at, pl.ds(rows, extra)],
                y_send.at[4 + z_at],
                y_recv.at[4 + z_at],
                across,
            ),
        )

    for z_at in Z_ORDER:
        for copy in over_y(z_at) + own(z_at):
            copy.start()

    def blocks(z_at):
        for copy in own(z_at):
            copy.wait()
        for copy in over_y(z_at):
            copy.wait_recv()
        add_blocks(mine.at[z_at], [from_y.at[z_at]], tall)

    def final(z_at, others):
        o_ref[...] = jnp.zeros_like(o_ref)
        add_blocks(o_ref, [mine.at[z_at], *others], tall)

    z_chain(
        blocks,
        lambda z_at: mine.at[z_at],
        from_below,
        from_above,
        up_send,
        up_recv,
        down_send,
        down_recv,
        tall,
        final,
    )
    for z_at in range(4):
        for copy in over_y(z_at):
            copy.wait_send()


def scatter_ep(value, extra, cid):
    rows, cols = value.shape[0] // 8, value.shape[1]
    tall = rows + extra.shape[0]
    dma = pltpu.SemaphoreType.DMA

    def held():
        return pltpu.VMEM((4, tall, cols), value.dtype)

    return pl.pallas_call(
        scatter_ep_kernel,
        out_shape=jax.ShapeDtypeStruct((tall, cols), jnp.float32),
        in_specs=[pl.BlockSpec(memory_space=pl.ANY)] * 2,
        out_specs=pl.BlockSpec(memory_space=pltpu.VMEM),
        scratch_shapes=[held(), held(), held(), held()] + [dma((8,))] * 3 + [dma((4,))] * 4,
        compiler_params=pltpu.CompilerParams(
            collective_id=cid, has_side_effects=True, vmem_limit_bytes=40 * 2**20
        ),
        name="scatter_ep",
    )(value, extra)


def experts_kernel(
    expert_width,
    shared_width,
    expert_total,
    x_ref,
    g_ref,
    kept_ref,
    expert_gate_ref,
    shared_gate_ref,
    extra_ref,
    expert_up_ref,
    shared_up_ref,
    expert_down_ref,
    shared_down_ref,
    grad_ref,
    ffn_ref,
    logit_ref,
    expert_grads_ref,
    shared_grads_ref,
    all_ref,
    from_sib,
    from_b,
    from_a,
    from_below,
    from_above,
    in_ref,
    down_ref,
    scalars,
    kept_held,
    x_held,
    g_held,
    lin,
    hidden_grad,
    hidden_all,
    both_all,
    kept_cols,
    staged,
    mine,
    landed,
    x_tile,
    g_tile,
    tile_out,
    shared_out,
    up_sem,
    down_sem,
    a_sem,
    b_sem,
    s_sem,
    recv_sem,
    sib_sem,
    own_sem,
    load_sem,
    fetch_sem,
    store_sem,
    weight_sem,
    kept_send,
    kept_recv,
    rs_send,
    rs_recv,
    rb_send,
    rb_recv,
    ra_send,
    ra_recv,
    ru_send,
    ru_recv,
    rd_send,
    rd_recv,
):
    ep, tp, z, y, x, core = place()
    rows, cols = x_ref.shape
    width = down_ref.shape[0]
    filled = expert_width + shared_width
    tall = mine.shape[1]
    out_at = rows + 16
    cuts = ((0, out_at), (out_at, tall - out_at))
    peer_a, peer_b, sibling, above, below = lane_peers()
    sources = kept_held.shape[0]
    others = [(lax.rem(ep + i, sources), tp) for i in range(1, sources)]
    greet([(ep, tp + 2 - 4 * x), sibling] + others)

    def spot(z_at, da, db):
        group, quarter = lane_spot(z_at, da, db, core)
        return all_ref.at[
            pl.ds(pl.multiple_of(group * rows, rows), rows),
            pl.ds(pl.multiple_of(quarter * cols, cols), cols),
        ]

    def at(z_at, da, db):
        return z_at * 4 + da * 2 + db

    def choose(*values):
        return jnp.where(
            z == 0, values[0], jnp.where(z == 1, values[1], jnp.where(z == 2, values[2], values[3]))
        )

    coming = (z, choose(1, 0, 3, 2), choose(2, 2, 1, 1), choose(3, 3, 0, 0))
    turns = (z, choose(2, 0, 3, 1), choose(3, 3, 0, 0), choose(1, 2, 1, 2))

    def arrived(z_at, da, db):
        block, n = spot(z_at, da, db), at(z_at, da, db)
        remote(block, block, s_sem.at[n], recv_sem.at[n], sibling).wait_recv()
        return block

    def up(z_at, source):
        return remote(source, spot(z_at, 0, 0), up_sem.at[z_at], recv_sem.at[at(z_at, 0, 0)], above)

    def down(z_at, source):
        return remote(source, spot(z_at, 0, 0), down_sem.at[z_at], recv_sem.at[at(z_at, 0, 0)], below)

    def over_a(z_at, source):
        return remote(source, spot(z_at, 0, 0), a_sem.at[z_at], recv_sem.at[at(z_at, 1, 0)], peer_a)

    def over_b(z_at, da, source):
        return remote(
            source, spot(z_at, da, 0), b_sem.at[z_at * 2 + da], recv_sem.at[at(z_at, da, 1)], peer_b
        )

    def to_sibling(z_at, da, db, source):
        n = at(z_at, da, db)
        return remote(source, spot(z_at, da, db), s_sem.at[n], sib_sem.at[n], sibling)

    def pass_z(z_at):
        block = arrived(z_at, 0, 0)

        @pl.when((z_at > z) & (z > 0))
        def _():
            down(z_at, block).start()

        @pl.when((z_at < z) & (z < 3))
        def _():
            up(z_at, block).start()

        over_a(z_at, block).start()
        over_b(z_at, 0, block).start()
        to_sibling(z_at, 0, 0, block).start()

    def pass_a(z_at):
        block = arrived(z_at, 1, 0)
        over_b(z_at, 1, block).start()
        to_sibling(z_at, 1, 0, block).start()

    def pass_b(z_at, da):
        block = arrived(z_at, da, 1)
        to_sibling(z_at, da, 1, block).start()

    def sibling_blocks(k, dy):
        for dx in range(2):
            da, db = core * dy + (1 - core) * dx, core * dx + (1 - core) * dy
            n = at(turns[k], da, db)
            block = spot(0, 0, 0)
            remote(block, block, s_sem.at[n], sib_sem.at[n], sibling).wait_recv()

    def group_rows(k, dy):
        group = turns[k] * 2 + y + (1 - 2 * y) * dy
        return group, pl.ds(pl.multiple_of(group * rows, rows), rows)

    def load_x(k, dy):
        _, span = group_rows(k, dy)
        return pltpu.make_async_copy(all_ref.at[span, :], x_held, load_sem.at[0])

    def load_g(k, dy):
        _, span = group_rows(k, dy)
        return pltpu.make_async_copy(g_ref.at[span, :], g_held, load_sem.at[1])

    def project():
        def body(i, carry):
            cut = pl.ds(pl.multiple_of(i * width, width), width)
            lin[:, cut] = times_transpose(x_held[...], in_ref[cut, :])
            return carry

        lax.fori_loop(0, 2, body, 0)

    def project_grad():
        hidden_grad[...] = times_transpose(g_held[...], down_ref[...])

    step = 64
    tile_start = width - 128
    logit_at = filled - tile_start

    def activate(k, dy):
        group, _ = group_rows(k, dy)
        lane = lax.broadcasted_iota(jnp.int32, (1, width), 1)
        near = lax.broadcasted_iota(jnp.int32, (1, 128), 1)
        is_logit = (near >= logit_at) & (near < logit_at + expert_total)
        kept_cols[:, :16] = kept_held[group].astype(jnp.float32).T

        def body(i, carry):
            span = pl.ds(pl.multiple_of(i * step, step), step)
            whole = pl.ds(pl.multiple_of(group * rows + i * step, step), step)
            gate_lin, up_lin = lin[span, :width], lin[span, width:]
            grad = hidden_grad[span, :]
            tail = lin[span, tile_start:width]
            if k == 0 and dy == 0:
                logit_ref[span, :] = tail
            most = jnp.max(jnp.where(is_logit, tail, -1e30), axis=1, keepdims=True)
            powers = jnp.where(is_logit, jnp.exp(jnp.minimum(tail - most, 0.0)), 0.0)
            kept = jnp.sum(jnp.where(near == ep, kept_cols[span, :], 0.0), axis=1, keepdims=True)
            gate = jnp.sum(jnp.where(near == logit_at + ep, powers, 0.0), axis=1, keepdims=True)
            gate = gate / jnp.sum(powers, axis=1, keepdims=True) * kept
            switch = jax.nn.sigmoid(
                jnp.sum(
                    jnp.where(near == logit_at + expert_total, tail, 0.0), axis=1, keepdims=True
                )
            )
            scale = jnp.where(lane < expert_width, gate, switch)
            sig = jax.nn.sigmoid(gate_lin)
            act = gate_lin * sig
            hidden = act * up_lin
            agreement = hidden * grad
            gate_part = jnp.sum(jnp.where(lane < expert_width, agreement, 0.0), axis=1, keepdims=True)
            switch_part = jnp.sum(
                jnp.where(lane < expert_width, 0.0, agreement), axis=1, keepdims=True
            )
            scaled = grad * scale
            hidden_all[whole, :] = (hidden * scale).astype(jnp.bfloat16)
            both_all[whole, :width] = (
                scaled * up_lin * sig * (1.0 + gate_lin * (1.0 - sig))
            ).astype(jnp.bfloat16)
            both_all[whole, width:] = (scaled * act).astype(jnp.bfloat16)
            scalars[span, :] = jnp.where(
                near == ep, gate_part, jnp.where(near == expert_total, switch_part, 0.0)
            )
            return carry

        lax.fori_loop(0, rows // step, body, 0)

    def hold(k, da, db):
        slot = 2 if k == 0 else k % 2
        return db * (7 + slot * 2 + da) + (1 - db) * (da * (4 + slot) + (1 - da) * k)

    def lane_offsets(dx, dy, core_at):
        return (1 - core_at) * dy + core_at * dx, (1 - core_at) * dx + core_at * dy

    def rs_sibling(k, dx, dy):
        n = at(turns[k], *lane_offsets(dx, dy, 1 - core))
        return remote(staged.at[dx], from_sib.at[n], rs_send.at[n], rs_recv.at[n], sibling)

    def block_rows(k, dy):
        sums = scalars[...].T[:16, :].astype(jnp.bfloat16)
        _, span = group_rows(k, dy)

        def fill(target, cut):
            target[:rows, :] = jnp.dot(
                both_all[span, :], in_ref[:, cut], preferred_element_type=jnp.float32
            ).astype(jnp.bfloat16)
            target[rows:out_at, :] = sums
            target[out_at:, :] = jnp.dot(
                hidden_all[span, :], down_ref[:, cut], preferred_element_type=jnp.float32
            ).astype(jnp.bfloat16)

        def body(dx, carry):
            x_at = x + (1 - 2 * x) * dx
            fill(staged.at[dx], pl.ds(pl.multiple_of((x_at * 2 + 1 - core) * cols, cols), cols))
            rs_sibling(k, dx, dy).start()
            fill(
                mine.at[hold(k, *lane_offsets(dx, dy, core))],
                pl.ds(pl.multiple_of((x_at * 2 + core) * cols, cols), cols),
            )
            return carry

        lax.fori_loop(0, 2, body, 0)

    def staged_free(k, dy):
        for dx in range(2):
            rs_sibling(k, dx, dy).wait_send()

    def rs_over_b(k, da):
        n = turns[k] * 2 + da
        return remote(mine.at[hold(k, da, 1)], from_b.at[n], rb_send.at[n], rb_recv.at[n], peer_b)

    def rs_over_a(k):
        z_at = turns[k]
        return remote(
            mine.at[hold(k, 1, 0)], from_a.at[z_at], ra_send.at[z_at], ra_recv.at[z_at], peer_a
        )

    def rs_up(k, z_at, half):
        first, count = cuts[half]
        n = z_at * 2 + half
        span = pl.ds(first, count)
        return remote(
            mine.at[k, span], from_below.at[z_at, span], ru_send.at[n], ru_recv.at[n], above
        )

    def rs_down(k, z_at, half):
        first, count = cuts[half]
        n = z_at * 2 + half
        span = pl.ds(first, count)
        return remote(
            mine.at[k, span], from_above.at[z_at, span], rd_send.at[n], rd_recv.at[n], below
        )

    def fetch(source, i):
        return pltpu.make_async_copy(source, landed.at[i], fetch_sem.at[i])

    def fetch_part(source, half, i):
        span = pl.ds(*cuts[half])
        return pltpu.make_async_copy(source.at[span], landed.at[i, span], fetch_sem.at[i])

    def reduce_sibling(k, dy):
        spots = []
        for dx in range(2):
            n = at(turns[k], *lane_offsets(dx, dy, core))
            remote(staged.at[0], from_sib.at[n], rs_send.at[n], rs_recv.at[n], sibling).wait_recv()
            fetch(from_sib.at[n], dx).start()
            spots.append(n)
        for dx in range(2):
            fetch(from_sib.at[spots[dx]], dx).wait()
            add_blocks(mine.at[hold(k, *lane_offsets(dx, dy, core))], [landed.at[dx]], tall)

        @pl.when(core == 0)
        def _():
            rs_over_b(k, dy).start()

        if dy == 1:

            @pl.when(core == 1)
            def _():
                rs_over_b(k, 0).start()
                rs_over_b(k, 1).start()

    def reduce_b(k):
        rs_over_b(k, 1).wait_recv()
        source = from_b.at[turns[k] * 2 + 1]
        fetch(source, 0).start()
        fetch(source, 0).wait()
        add_blocks(mine.at[hold(k, 1, 0)], [landed.at[0]], tall)
        rs_over_a(k).start()

    def reduce_a(k):
        z_at = turns[k]
        rs_over_b(k, 0).wait_recv()
        fetch(from_b.at[z_at * 2], 0).start()
        rs_over_a(k).wait_recv()
        fetch(from_a.at[z_at], 1).start()
        fetch(from_b.at[z_at * 2], 0).wait()
        fetch(from_a.at[z_at], 1).wait()
        add_blocks(mine.at[k], [landed.at[0], landed.at[1]], tall)
        if k > 0:
            for half in range(2):

                @pl.when(z == 0)
                def _(half=half):
                    rs_up(k, z_at, half).start()

                @pl.when(z == 3)
                def _(half=half):
                    rs_down(k, z_at, half).start()

    def chain(k):
        z_at = turns[k]
        first, count = cuts[0]
        for half, (first, count) in enumerate(cuts):
            span = pl.ds(first, count)

            @pl.when((z > 0) & (z < 3) & (z_at > z))
            def _(half=half, span=span, count=count):
                rs_up(k, z_at, half).wait_recv()
                fetch_part(from_below.at[z_at], half, half).start()
                fetch_part(from_below.at[z_at], half, half).wait()
                add_blocks(mine.at[k, span], [landed.at[half, span]], count)
                rs_up(k, z_at, half).start()

            @pl.when((z > 0) & (z < 3) & (z_at < z))
            def _(half=half, span=span, count=count):
                rs_down(k, z_at, half).wait_recv()
                fetch_part(from_above.at[z_at], half, half).start()
                fetch_part(from_above.at[z_at], half, half).wait()
                add_blocks(mine.at[k, span], [landed.at[half, span]], count)
                rs_down(k, z_at, half).start()

    tile = x_tile.shape[1]

    def load_tile(source, target, t, sem):
        cut = pl.ds(pl.multiple_of(t * tile, tile), tile)
        return pltpu.make_async_copy(source.at[:, cut], target, load_sem.at[sem])

    def tile_stores(t, kind):
        cut = pl.ds(pl.multiple_of(t * tile, tile), tile)
        return (
            pltpu.make_async_copy(
                tile_out.at[kind, pl.ds(0, expert_width)],
                expert_grads_ref.at[kind, :, cut],
                store_sem.at[kind],
            ),
            pltpu.make_async_copy(
                shared_out.at[kind], shared_grads_ref.at[t, kind], store_sem.at[3 + kind]
            ),
        )

    def weight_tile(t, kind):
        @pl.when(t > 0)
        def _():
            for copy in tile_stores(t - 1, kind):
                copy.wait()

        if kind == 0:
            left, right = hidden_all[:, :filled], g_tile[...]
        else:
            left, right = both_all[:, (kind - 1) * width : (kind - 1) * width + filled], x_tile[...]
        result = inner_rows(left, right)
        tile_out[kind] = result
        shared_out[kind] = result[expert_width:, :].astype(jnp.bfloat16)
        for copy in tile_stores(t, kind):
            copy.start()

    own = pltpu.make_async_copy(x_ref, spot(z, 0, 0), own_sem)
    over_b(z, 0, x_ref).start()
    over_a(z, x_ref).start()

    @pl.when(z < 3)
    def _():
        up(z, x_ref).start()

    @pl.when(z > 0)
    def _():
        down(z, x_ref).start()

    to_sibling(z, 0, 0, x_ref).start()
    own.start()
    load_g(0, 0).start()

    def kept_to(i):
        return remote(
            kept_ref, kept_held.at[ep], kept_send.at[i - 1], kept_recv.at[i - 1], others[i - 1]
        )

    for i in range(1, sources):
        kept_to(i).start()
    own_kept = pltpu.make_async_copy(kept_ref, kept_held.at[ep], weight_sem.at[7])
    own_kept.start()
    pieces = [
        (expert_down_ref, down_ref, 0),
        (
            shared_down_ref.at[pl.ds(pl.multiple_of(ep * shared_width, 16), shared_width), :],
            down_ref,
            expert_width,
        ),
        (expert_gate_ref, in_ref, 0),
        (shared_gate_ref, in_ref, expert_width),
        (extra_ref, in_ref, filled),
        (expert_up_ref, in_ref, width),
        (shared_up_ref, in_ref, width + expert_width),
    ]
    weight_copies = [
        pltpu.make_async_copy(piece, target.at[pl.ds(at_row, piece.shape[0]), :], weight_sem.at[i])
        for i, (piece, target, at_row) in enumerate(pieces)
    ]
    for copy in weight_copies:
        copy.start()
    for target, first, last_row in (
        (in_ref, filled + 16, width),
        (in_ref, width + filled, 2 * width),
        (down_ref, filled, width),
    ):
        target[first:last_row, :] = jnp.zeros((last_row - first, target.shape[1]), target.dtype)
    for copy in weight_copies:
        copy.wait()
    load_g(0, 0).wait()
    project_grad()
    own_kept.wait()
    for i in range(1, sources):
        kept_to(i).wait_recv()
    own.wait()

    def ready(k, dy):
        if k > 0:
            pass_b(turns[k], dy)
        sibling_blocks(k, dy)
        load_x(k, dy).start()

    order = [(0, 0)] + [(k, dy) for k in range(1, 4) for dy in range(2)] + [(0, 1)]
    pass_a(z)
    pass_b(z, 0)
    ready(0, 0)
    for s, (k, dy) in enumerate(order):
        following = order[s + 1] if s < 7 else None
        load_x(k, dy).wait()
        project()
        if s == 0:
            pass_z(coming[1])
        if s >= 1:
            load_g(k, dy).wait()
            project_grad()
        if following is not None:
            load_g(*following).start()
        if s == 0:
            pass_z(coming[2])
            pass_b(z, 1)
            pass_a(coming[1])
        if s == 1:
            pass_z(coming[3])
        if s >= 1:
            reduce_sibling(*order[s - 1])
        if s in (4, 6):
            reduce_b(s // 2 - 1)
        activate(k, dy)
        if s == 0:
            pass_a(coming[2])
        if s == 2:
            pass_a(coming[3])
        if following is not None:
            ready(*following)
        if s in (5, 7):
            reduce_a((s - 3) // 2)
        if s >= 1:
            staged_free(*order[s - 1])
        if s == 5:
            for da in range(2):
                rs_over_b(1, da).wait_send()
            rs_over_a(1).wait_send()
        block_rows(k, dy)

    load_tile(g_ref, g_tile, 0, 2).start()
    load_tile(all_ref, x_tile, 0, 3).start()
    tiles = shared_grads_ref.shape[0]
    services = {
        (0, 1): lambda: reduce_sibling(0, 1),
        (0, 2): lambda: chain(2),
        (1, 1): lambda: reduce_b(3),
        (1, 2): lambda: reduce_b(0),
        (2, 0): lambda: chain(1),
        (3, 0): lambda: reduce_a(3),
        (4, 0): lambda: chain(3),
        (5, 1): lambda: reduce_a(0),
    }

    def tile_step(t, carry):
        for kind in range(3):
            if kind == 0:
                load_tile(g_ref, g_tile, t, 2).wait()
            if kind == 1:
                load_tile(all_ref, x_tile, t, 3).wait()
            weight_tile(t, kind)

            @pl.when(t + 1 < tiles)
            def _(kind=kind):
                if kind == 0:
                    load_tile(g_ref, g_tile, t + 1, 2).start()
                if kind == 2:
                    load_tile(all_ref, x_tile, t + 1, 3).start()

            for (at_tile, at_kind), service in services.items():
                if at_kind == kind:
                    pl.when(t == at_tile)(service)
        return carry

    lax.fori_loop(0, tiles, tile_step, 0)
    for kind in range(3):
        for copy in tile_stores(tiles - 1, kind):
            copy.wait()

    for half in range(2):

        @pl.when(z > 0)
        def _(half=half):
            rs_up(0, z, half).wait_recv()
            fetch_part(from_below.at[z], half, 0).start()
            fetch_part(from_below.at[z], half, 0).wait()

        @pl.when(z < 3)
        def _(half=half):
            rs_down(0, z, half).wait_recv()
            fetch_part(from_above.at[z], half, 1).start()
            fetch_part(from_above.at[z], half, 1).wait()

    def total(parts):
        def body(i, carry):
            for target, first in ((grad_ref, 0), (ffn_ref, out_at)):
                span = pl.ds(pl.multiple_of(i * 16, 16), 16)
                source = pl.ds(pl.multiple_of(first + i * 16, 16), 16)
                value = mine[0, source, :].astype(jnp.float32)
                for part in parts:
                    value = value + landed[part, source, :].astype(jnp.float32)
                target[span, :] = value
            return carry

        lax.fori_loop(0, rows // 16, body, 0)
        value = mine[0, rows:out_at, :].astype(jnp.float32)
        for part in parts:
            value = value + landed[part, rows:out_at, :].astype(jnp.float32)
        grad_ref[rows:, :] = value

    @pl.when(z == 0)
    def _():
        total([1])

    @pl.when(z == 3)
    def _():
        total([0])

    @pl.when((z > 0) & (z < 3))
    def _():
        total([0, 1])

    for i in range(1, sources):
        kept_to(i).wait_send()
    staged_free(0, 1)
    for k in (0, 2, 3):
        rs_over_a(k).wait_send()
        for da in range(2):
            rs_over_b(k, da).wait_send()

    def finish(i, carry):
        over_a(i, x_ref).wait_send()
        over_b(i, 0, x_ref).wait_send()
        over_b(i, 1, x_ref).wait_send()
        for n in range(4):
            block = spot(0, 0, 0)
            remote(block, block, s_sem.at[i * 4 + n], sib_sem.at[i * 4 + n], sibling).wait_send()

        @pl.when((z < 3) & (i <= z))
        def _():
            up(i, x_ref).wait_send()

        @pl.when((z > 0) & (i >= z))
        def _():
            down(i, x_ref).wait_send()

        for half in range(2):

            @pl.when(i > z)
            def _(half=half):
                rs_up(0, i, half).wait_send()

            @pl.when(i < z)
            def _(half=half):
                rs_down(0, i, half).wait_send()

        return carry

    lax.fori_loop(0, 4, finish, 0)


def experts(x_cols, grads_all, kept_rows, weights, expert_total, cid):
    rows, cols = x_cols.shape
    total, model_dim = grads_all.shape
    sources = total // rows
    expert_width, shared_width = weights[0].shape[0], weights[1].shape[0]
    filled = expert_width + shared_width
    width = -(-(filled + expert_total + 1) // 128) * 128
    tall = 2 * rows + 16
    tile = model_dim // sources
    low, dma = jnp.bfloat16, pltpu.SemaphoreType.DMA
    vmem, hbm = pl.BlockSpec(memory_space=pltpu.VMEM), pl.BlockSpec(memory_space=pl.ANY)

    def landing(count):
        return jax.ShapeDtypeStruct((count, tall, cols), low)

    return pl.pallas_call(
        functools.partial(experts_kernel, expert_width, shared_width, expert_total),
        out_shape=[
            jax.ShapeDtypeStruct((rows + 16, cols), jnp.float32),
            jax.ShapeDtypeStruct((rows, cols), jnp.float32),
            jax.ShapeDtypeStruct((rows, 128), jnp.float32),
            jax.ShapeDtypeStruct((3, expert_width, model_dim), jnp.float32),
            jax.ShapeDtypeStruct((sources, 3, shared_width, tile), low),
            jax.ShapeDtypeStruct((total, model_dim), low),
            landing(16),
            landing(8),
            landing(4),
            landing(4),
            landing(4),
        ],
        in_specs=[hbm] * 10,
        out_specs=[vmem, vmem, vmem] + [hbm] * 8,
        scratch_shapes=[
            pltpu.VMEM((2 * width, model_dim), low),
            pltpu.VMEM((width, model_dim), low),
            pltpu.VMEM((rows, 128), jnp.float32),
            pltpu.VMEM((sources, 16, rows), low),
            pltpu.VMEM((rows, model_dim), low),
            pltpu.VMEM((rows, model_dim), low),
            pltpu.VMEM((rows, 2 * width), jnp.float32),
            pltpu.VMEM((rows, width), jnp.float32),
            pltpu.VMEM((total, width), low),
            pltpu.VMEM((total, 2 * width), low),
            pltpu.VMEM((rows, 128), jnp.float32),
            pltpu.VMEM((2, tall, cols), low),
            pltpu.VMEM((13, tall, cols), low),
            pltpu.VMEM((2, tall, cols), low),
            pltpu.VMEM((total, tile), low),
            pltpu.VMEM((total, tile), low),
            pltpu.VMEM((3, filled, tile), jnp.float32),
            pltpu.VMEM((3, shared_width, tile), low),
        ]
        + [dma((4,)), dma((4,)), dma((4,)), dma((8,)), dma((16,)), dma((16,)), dma((16,)), dma]
        + [dma((4,)), dma((2,)), dma((6,)), dma((8,)), dma((7,)), dma((7,))]
        + [dma((16,)), dma((16,)), dma((8,)), dma((8,)), dma((4,)), dma((4,))]
        + [dma((8,))] * 4,
        compiler_params=pltpu.CompilerParams(
            collective_id=cid, has_side_effects=True, vmem_limit_bytes=63 * 2**20
        ),
        name="experts",
    )(x_cols, grads_all, kept_rows, *weights)


def row_of(columns):
    part = columns[:, :128]
    for i in range(1, columns.shape[1] // 128):
        part = part + columns[:, i * 128 : (i + 1) * 128]
    total = jnp.sum(part.T, axis=0, keepdims=True)
    return jnp.broadcast_to(total, (8, total.shape[1]))


def unwind_kernel(
    dn2_ref,
    unit_ref,
    inv_ref,
    second_ref,
    grad_ref,
    tokens_ref,
    inv_one_ref,
    first_ref,
    small_ref,
    q_ref,
    k_ref,
    v_ref,
    ke_ref,
    ve_ref,
    context_ref,
    log_ref,
    cos_ref,
    sin_ref,
    n1_hbm,
    wq_hbm,
    wk_hbm,
    wv_hbm,
    wo_hbm,
    tokens_grad_ref,
    weight_grads_ref,
    sums_ref,
    n1,
    wq,
    wk,
    wv,
    wo,
    grad_all,
    grad_own,
    hidden_grad,
    dc,
    dq,
    dk,
    dv,
    lin_grads,
    dke,
    dve,
    later_k,
    later_v,
    staged,
    mine,
    from_y,
    from_below,
    from_above,
    tp_staged,
    tp_mine,
    tp_sib,
    tp_x,
    dn1,
    row_mine,
    row_sib,
    row_x,
    smalls,
    load_sem,
    g_send,
    g_recv,
    row_send,
    row_recv,
    kv_send,
    kv_recv,
    y_send,
    y_recv,
    up_send,
    up_recv,
    down_send,
    down_recv,
    tp_send,
    tp_recv,
    small_send,
    small_recv,
):
    ep, tp, z, y, x, core = place()
    rows, cols = unit_ref.shape
    model_dim = n1.shape[1]
    heads = cols // HD
    block = mine.shape[1]
    low, full = jnp.bfloat16, jnp.float32
    score_scale = HD ** (-0.5)
    sibling, across = (ep, tp + 1 - 2 * core), (ep, tp + 2 - 4 * x)
    beside = (ep + 1 - 2 * y, tp)
    above, below = (ep + 2, tp), (ep - 2, tp)
    sources = smalls.shape[0]
    others = [(lax.rem(ep + i, sources), tp) for i in range(1, sources)]
    loads = [
        pltpu.make_async_copy(source, target, load_sem.at[i])
        for i, (source, target) in enumerate(
            ((wo_hbm, wo), (n1_hbm, n1), (wq_hbm, wq), (wk_hbm, wk), (wv_hbm, wv))
        )
    ]
    for copy in loads:
        copy.start()
    greet([across, sibling] + others)

    step = 64

    def by_rows(body):
        def one(i, carry):
            body(pl.ds(pl.multiple_of(i * step, step), step))
            return carry

        lax.fori_loop(0, rows // step, one, 0)

    def row_exchange(i, values):
        row_mine[2 * i] = values
        first = remote(
            row_mine.at[2 * i], row_sib.at[i], row_send.at[2 * i], row_recv.at[2 * i], sibling
        )
        first.start()
        first.wait_recv()
        row_mine[2 * i + 1] = row_mine[2 * i] + row_sib[i]
        second = remote(
            row_mine.at[2 * i + 1],
            row_x.at[i],
            row_send.at[2 * i + 1],
            row_recv.at[2 * i + 1],
            across,
        )
        second.start()
        second.wait_recv()
        first.wait_send()
        second.wait_send()
        return (row_mine[2 * i + 1] + row_x[i]).T[:, :1]

    dn1[...] = dn2_ref[...] * second_ref[:1, :] * unit_ref[...]
    mean = row_exchange(0, row_of(dn1[...])) * (1.0 / model_dim)
    dn1[:, :128] = jnp.broadcast_to(mean, (rows, 128))

    def norm_two(span):
        scaled = dn2_ref[span, :] * second_ref[:1, :]
        value = grad_ref[span, :].astype(full) + inv_ref[span, :1] * (
            scaled - unit_ref[span, :] * dn1[span, :1]
        )
        hidden_grad[span, :] = value
        grad_own[span, :] = value.astype(low)

    by_rows(norm_two)

    def quarter(at):
        return grad_all.at[:, pl.ds(pl.multiple_of(at * cols, cols), cols)]

    g_x = remote(grad_own, quarter(tp), g_send.at[0], g_recv.at[0], across)
    g_s = remote(grad_own, quarter(tp), g_send.at[1], g_recv.at[1], sibling)
    g_x.start()
    g_s.start()
    own_cut = pl.ds(pl.multiple_of(tp * cols, cols), cols)
    grad_all[:, own_cut] = grad_own[...]
    g_x.wait_recv()
    theirs = quarter(tp + 2 - 4 * x)
    g_f = remote(theirs, theirs, g_send.at[2], g_recv.at[2], sibling)
    g_f.start()
    g_s.wait_recv()
    g_f.wait_recv()
    loads[0].wait()
    dc[...] = times_transpose(grad_all[...], wo[...]).astype(low)

    def over_y(kind, z_at):
        n = kind * 4 + z_at
        return remote(staged.at[n], from_y.at[n], y_send.at[n], y_recv.at[n], beside)

    def weight_blocks(kind, left, right):
        def other(i, carry):
            z_at = lax.rem(i * 3, 4)
            cut = pl.ds(pl.multiple_of((z_at * 2 + 1 - y) * block, block), block)
            staged[kind * 4 + z_at] = inner_rows(left[:, cut], right[...]).astype(low)
            over_y(kind, z_at).start()
            return carry

        def ours(i, carry):
            z_at = lax.rem(i * 3, 4)
            cut = pl.ds(pl.multiple_of((z_at * 2 + y) * block, block), block)
            mine[kind * 4 + z_at] = inner_rows(left[:, cut], right[...]).astype(low)
            return carry

        lax.fori_loop(0, 4, other, 0)
        lax.fori_loop(0, 4, ours, 0)

    def up(kind, z_at):
        n = kind * 4 + z_at
        return remote(mine.at[n], from_below.at[n], up_send.at[n], up_recv.at[n], above)

    def down(kind, z_at):
        n = kind * 4 + z_at
        return remote(mine.at[n], from_above.at[n], down_send.at[n], down_recv.at[n], below)

    def y_stage(kind):
        def one(i, carry):
            z_at = lax.rem(i * 3, 4)
            n = kind * 4 + z_at
            over_y(kind, z_at).wait_recv()
            add_blocks(mine.at[n], [from_y.at[n]], block)

            @pl.when((z == 0) & (z_at > 0))
            def _():
                up(kind, z_at).start()

            @pl.when((z == 3) & (z_at < 3))
            def _():
                down(kind, z_at).start()

            return carry

        lax.fori_loop(0, 4, one, 0)

    def chain(kind):
        def rise(z_at):
            n = kind * 4 + z_at
            up(kind, z_at).wait_recv()
            add_blocks(mine.at[n], [from_below.at[n]], block)
            up(kind, z_at).start()

        def fall(z_at):
            n = kind * 4 + z_at
            down(kind, z_at).wait_recv()
            add_blocks(mine.at[n], [from_above.at[n]], block)
            down(kind, z_at).start()

        @pl.when(z == 1)
        def _():
            rise(3)
            rise(2)
            fall(0)

        @pl.when(z == 2)
        def _():
            fall(0)
            fall(1)
            rise(3)

    def final(kind):
        n = kind * 4 + z

        @pl.when(z > 0)
        def _():
            up(kind, z).wait_recv()

        @pl.when(z < 3)
        def _():
            down(kind, z).wait_recv()

        def one(i, carry):
            span = pl.ds(pl.multiple_of(i * 32, 32), 32)
            value = mine[n, span, :].astype(full)
            low_part = from_below[n, span, :].astype(full)
            high_part = from_above[n, span, :].astype(full)
            value = value + jnp.where(z > 0, low_part, 0.0) + jnp.where(z < 3, high_part, 0.0)
            weight_grads_ref[kind, span, :] = value
            return carry

        lax.fori_loop(0, block // 32, one, 0)

    weight_blocks(0, grad_all, context_ref)

    half = rows // 2

    def terms(h, qb, key_count, keys, values):
        cut = pl.ds(pl.multiple_of(h * HD, HD), HD)
        span = pl.ds(qb * half, half)
        lane = lax.broadcasted_iota(jnp.int32, (1, 128), 1)
        log_total = jnp.sum(jnp.where(lane == h, log_ref[span, :], 0.0), axis=1, keepdims=True)
        queries, grads = q_ref[span, cut], dc[span, cut]
        delta = jnp.sum(
            grads.astype(full) * context_ref[span, cut].astype(full), axis=1, keepdims=True
        )
        key_part, value_part = keys[:key_count, cut], values[:key_count, cut]
        probs = jnp.exp(times_transpose(queries, key_part) * score_scale - log_total)
        scores_grad = (probs * (times_transpose(grads, value_part) - delta)).astype(low)
        return (
            jnp.dot(scores_grad, key_part, preferred_element_type=full),
            inner_rows(scores_grad, queries),
            inner_rows(probs.astype(low), grads),
        )

    def spans(h, qb):
        return pl.ds(qb * half, half), pl.ds(pl.multiple_of(h * HD, HD), HD)

    later = (
        remote(dke, later_k, kv_send.at[0], kv_recv.at[0], beside),
        remote(dve, later_v, kv_send.at[1], kv_recv.at[1], beside),
    )

    @pl.when(y == 1)
    def _():
        def head(h, carry):
            cut = pl.ds(pl.multiple_of(h * HD, HD), HD)
            first = terms(h, 0, rows, ke_ref, ve_ref)
            dq[spans(h, 0)[0], cut] = first[0]
            dk[:, cut] = first[1]
            dv[:, cut] = first[2]
            second = terms(h, 1, rows, ke_ref, ve_ref)
            dq[spans(h, 1)[0], cut] = second[0]
            dke[:, cut] = ((dk[:, cut] + second[1]) * score_scale).astype(low)
            dve[:, cut] = (dv[:, cut] + second[2]).astype(low)
            return carry

        lax.fori_loop(0, heads, head, 0)
        for copy in later:
            copy.start()

    @pl.when(y == 0)
    def _():
        dq[...] = jnp.zeros_like(dq)

    y_stage(0)

    def head(h, carry):
        cut = pl.ds(pl.multiple_of(h * HD, HD), HD)
        second = terms(h, 1, rows, k_ref, v_ref)
        dq[half:, cut] = dq[half:, cut] + second[0]
        dk[:, cut] = second[1] * score_scale
        dv[:, cut] = second[2]
        first = terms(h, 0, half, k_ref, v_ref)
        dq[:half, cut] = dq[:half, cut] + first[0]
        dk[:half, cut] = dk[:half, cut] + first[1] * score_scale
        dv[:half, cut] = dv[:half, cut] + first[2]
        return carry

    lax.fori_loop(0, heads, head, 0)

    def rotate_back(source, target, scale):
        def one(h, carry):
            cut = pl.ds(pl.multiple_of(h * HD, HD), HD)
            value = source[:, cut] * scale
            turned = value * cos_ref[...] - pltpu.roll(value, HD // 2, 1) * sin_ref[...]
            lin_grads[target, :, cut] = turned.astype(low)
            return carry

        lax.fori_loop(0, heads, one, 0)

    rotate_back(dq, 0, score_scale)
    loads[1].wait()
    weight_blocks(1, n1, lin_grads.at[0])
    chain(0)

    @pl.when(y == 0)
    def _():
        for copy in later:
            copy.wait_recv()

        def add(span):
            dk[span, :] = dk[span, :] + later_k[span, :].astype(full)
            dv[span, :] = dv[span, :] + later_v[span, :].astype(full)

        by_rows(add)

    rotate_back(dk, 1, 1.0)
    lin_grads[2] = dv[...].astype(low)
    weight_blocks(2, n1, lin_grads.at[1])
    weight_blocks(3, n1, lin_grads.at[2])
    y_stage(1)
    for copy in loads[2:]:
        copy.wait()

    def dn1_part(at, target):
        cut = pl.ds(pl.multiple_of(at * cols, cols), cols)
        total = times_transpose(lin_grads[0], wq[cut, :])
        total = total + times_transpose(lin_grads[1], wk[cut, :])
        total = total + times_transpose(lin_grads[2], wv[cut, :])
        target[...] = total.astype(low)

    def to_sibling(i):
        return remote(tp_staged.at[i], tp_sib.at[i], tp_send.at[i], tp_recv.at[i], sibling)

    def part_of(i):
        x_at = 1 - x + (2 * x - 1) * i
        dn1_part(x_at * 2 + 1 - core, tp_staged.at[i])
        to_sibling(i).start()
        dn1_part(x_at * 2 + core, tp_mine.at[i])

    out_x = remote(tp_mine.at[0], tp_x, tp_send.at[2], tp_recv.at[2], across)
    part_of(0)
    to_sibling(0).wait_recv()
    add_blocks(tp_mine.at[0], [tp_sib.at[0]], rows)
    out_x.start()
    part_of(1)
    chain(1)
    to_sibling(1).wait_recv()
    out_x.wait_recv()

    def sum_parts(span):
        dn1[span, :] = (
            tp_mine[1, span, :].astype(full)
            + tp_sib[1, span, :].astype(full)
            + tp_x[span, :].astype(full)
        )

    by_rows(sum_parts)

    def unit_one(span):
        return tokens_ref[span, :].astype(full) * inv_one_ref[span, :1]

    def products(span):
        dq[span, :] = dn1[span, :] * unit_one(span)

    by_rows(products)
    gain_grad = jnp.sum(dq[...], axis=0, keepdims=True)
    dq[...] = dq[...] * first_ref[:1, :]
    total = row_exchange(1, row_of(dq[...]))
    dk[:, :128] = jnp.broadcast_to(total * (1.0 / model_dim), (rows, 128))

    def norm_one(span):
        scaled = dn1[span, :] * first_ref[:1, :]
        value = hidden_grad[span, :] + inv_one_ref[span, :1] * (
            scaled - unit_one(span) * dk[span, :1]
        )
        tokens_grad_ref[span, :] = value.astype(low)

    by_rows(norm_one)

    own = smalls.at[ep]
    own[...] = small_ref[...]
    own[0:1, :] = gain_grad
    for i in range(3):
        own[i + 1 : i + 2, :] = jnp.sum(lin_grads[i].astype(full), axis=0, keepdims=True)

    def small_to(i):
        return remote(own, own, small_send.at[i - 1], small_recv.at[i - 1], others[i - 1])

    for i in range(1, sources):
        small_to(i).start()
    y_stage(2)
    final(0)
    chain(2)
    y_stage(3)
    final(1)
    chain(3)
    for i in range(1, sources):
        small_to(i).wait_recv()
    total = smalls[0]
    for i in range(1, sources):
        total = total + smalls[i]
    sums_ref[...] = total
    final(2)
    final(3)

    for copy in (g_x, g_s, g_f, out_x, to_sibling(0), to_sibling(1)):
        copy.wait_send()

    @pl.when(y == 1)
    def _():
        for copy in later:
            copy.wait_send()

    for i in range(1, sources):
        small_to(i).wait_send()

    def finish(n, carry):
        remote(staged.at[0], from_y.at[0], y_send.at[n], y_recv.at[n], beside).wait_send()
        z_at = lax.rem(n, 4)

        @pl.when(z_at > z)
        def _():
            remote(mine.at[0], from_below.at[0], up_send.at[n], up_recv.at[n], above).wait_send()

        @pl.when(z_at < z)
        def _():
            remote(mine.at[0], from_above.at[0], down_send.at[n], down_recv.at[n], below).wait_send()

        return carry

    lax.fori_loop(0, 16, finish, 0)


def unwind(vmem_args, hbm_args, cid):
    rows, cols = vmem_args[0].shape
    model_dim = hbm_args[0].shape[1]
    sources = 8
    block = model_dim // sources
    low, full, dma = jnp.bfloat16, jnp.float32, pltpu.SemaphoreType.DMA
    vmem, hbm = pl.BlockSpec(memory_space=pltpu.VMEM), pl.BlockSpec(memory_space=pl.ANY)

    def buffers(*shape, dtype=low):
        return pltpu.VMEM(shape, dtype)

    return pl.pallas_call(
        unwind_kernel,
        out_shape=[
            jax.ShapeDtypeStruct((rows, cols), low),
            jax.ShapeDtypeStruct((4, block, cols), full),
            jax.ShapeDtypeStruct((16, cols), full),
        ],
        in_specs=[vmem] * len(vmem_args) + [hbm] * len(hbm_args),
        out_specs=[vmem] * 3,
        scratch_shapes=[buffers(*arg.shape) for arg in hbm_args]
        + [
            buffers(rows, model_dim),
            buffers(rows, cols),
            buffers(rows, cols, dtype=full),
            buffers(rows, cols),
            buffers(rows, cols, dtype=full),
            buffers(rows, cols, dtype=full),
            buffers(rows, cols, dtype=full),
            buffers(3, rows, cols),
            buffers(rows, cols),
            buffers(rows, cols),
            buffers(rows, cols),
            buffers(rows, cols),
        ]
        + [buffers(16, block, cols)] * 5
        + [
            buffers(2, rows, cols),
            buffers(2, rows, cols),
            buffers(2, rows, cols),
            buffers(rows, cols),
            buffers(rows, cols, dtype=full),
            buffers(4, 8, rows, dtype=full),
            buffers(2, 8, rows, dtype=full),
            buffers(2, 8, rows, dtype=full),
            buffers(sources, 16, cols, dtype=full),
        ]
        + [dma((5,)), dma((3,)), dma((3,)), dma((4,)), dma((4,)), dma((2,)), dma((2,))]
        + [dma((16,))] * 6
        + [dma((3,)), dma((3,)), dma((7,)), dma((7,))],
        compiler_params=pltpu.CompilerParams(
            collective_id=cid, has_side_effects=True, vmem_limit_bytes=60 * 2**20
        ),
        name="unwind",
    )(*vmem_args, *hbm_args)


def attend_kernel(
    first_ref,
    bias_ref,
    second_ref,
    cos_ref,
    sin_ref,
    tokens_hbm,
    grad_hbm,
    wq_hbm,
    wk_hbm,
    wv_hbm,
    wo_hbm,
    hidden_ref,
    unit_ref,
    inv_ref,
    normed_ref,
    n1_ref,
    inv_one_ref,
    q_ref,
    k_ref,
    v_ref,
    ke_ref,
    ve_ref,
    context_ref,
    log_ref,
    all_ref,
    wq,
    wk,
    wv,
    wo,
    tokens,
    lin,
    total,
    most,
    weight,
    earlier_k,
    earlier_v,
    tp_staged,
    tp_mine,
    tp_sib,
    tp_x,
    row_mine,
    row_sib,
    row_x,
    load_sem,
    t_send,
    t_recv,
    kv_send,
    kv_recv,
    tp_send,
    tp_recv,
    row_send,
    row_recv,
    up_sem,
    down_sem,
    a_sem,
    b_sem,
    s_sem,
    recv_sem,
    sib_sem,
):
    ep, tp, z, y, x, core = place()
    rows, cols = hidden_ref.shape
    model_dim = n1_ref.shape[1]
    heads = cols // HD
    low, full = jnp.bfloat16, jnp.float32
    score_scale = HD ** (-0.5)
    sibling, across = (ep, tp + 1 - 2 * core), (ep, tp + 2 - 4 * x)
    beside = (ep + 1 - 2 * y, tp)
    peer_a, peer_b, _, above, below = lane_peers()

    def quarter(at):
        return tokens.at[:, pl.ds(pl.multiple_of(at * cols, cols), cols)]

    loads = [
        pltpu.make_async_copy(source, target, load_sem.at[i])
        for i, (source, target) in enumerate(
            (
                (tokens_hbm, quarter(tp)),
                (wk_hbm, wk),
                (wv_hbm, wv),
                (wq_hbm, wq),
                (wo_hbm, wo),
            )
        )
    ]
    for copy in loads:
        copy.start()
    greet([across, beside, sibling], True)

    t_x = remote(tokens_hbm, quarter(tp), t_send.at[0], t_recv.at[0], across)
    t_s = remote(tokens_hbm, quarter(tp), t_send.at[1], t_recv.at[1], sibling)
    t_x.start()
    t_s.start()

    def choose(*values):
        return jnp.where(
            z == 0, values[0], jnp.where(z == 1, values[1], jnp.where(z == 2, values[2], values[3]))
        )

    coming = (z, choose(1, 0, 3, 2), choose(2, 2, 1, 1), choose(3, 3, 0, 0))

    def spot(z_at, da, db):
        group, at_quarter = lane_spot(z_at, da, db, core)
        return all_ref.at[
            pl.ds(pl.multiple_of(group * rows, rows), rows),
            pl.ds(pl.multiple_of(at_quarter * cols, cols), cols),
        ]

    def at(z_at, da, db):
        return z_at * 4 + da * 2 + db

    def arrived(z_at, da, db):
        block, n = spot(z_at, da, db), at(z_at, da, db)
        remote(block, block, s_sem.at[n], recv_sem.at[n], sibling).wait_recv()
        return block

    def up(z_at, source):
        return remote(source, spot(z_at, 0, 0), up_sem.at[z_at], recv_sem.at[at(z_at, 0, 0)], above)

    def down(z_at, source):
        return remote(source, spot(z_at, 0, 0), down_sem.at[z_at], recv_sem.at[at(z_at, 0, 0)], below)

    def over_a(z_at, source):
        return remote(source, spot(z_at, 0, 0), a_sem.at[z_at], recv_sem.at[at(z_at, 1, 0)], peer_a)

    def over_b(z_at, da, source):
        return remote(
            source, spot(z_at, da, 0), b_sem.at[z_at * 2 + da], recv_sem.at[at(z_at, da, 1)], peer_b
        )

    def to_sibling(z_at, da, db, source):
        n = at(z_at, da, db)
        return remote(source, spot(z_at, da, db), s_sem.at[n], sib_sem.at[n], sibling)

    def pass_z(k):
        z_at = coming[k]
        block = arrived(z_at, 0, 0)

        @pl.when((z_at > z) & (z > 0))
        def _():
            down(z_at, block).start()

        @pl.when((z_at < z) & (z < 3))
        def _():
            up(z_at, block).start()

        over_a(z_at, block).start()
        over_b(z_at, 0, block).start()
        to_sibling(z_at, 0, 0, block).start()

    def pass_a(k):
        block = arrived(coming[k], 1, 0)
        over_b(coming[k], 1, block).start()
        to_sibling(coming[k], 1, 0, block).start()

    def pass_b(k, da):
        block = arrived(coming[k], da, 1)
        to_sibling(coming[k], da, 1, block).start()

    own = pltpu.make_async_copy(grad_hbm, spot(z, 0, 0), load_sem.at[5])
    over_b(z, 0, grad_hbm).start()
    over_a(z, grad_hbm).start()

    @pl.when(z < 3)
    def _():
        up(z, grad_hbm).start()

    @pl.when(z > 0)
    def _():
        down(z, grad_hbm).start()

    to_sibling(z, 0, 0, grad_hbm).start()
    own.start()

    t_x.wait_recv()
    theirs = quarter(tp + 2 - 4 * x)
    t_f = remote(theirs, theirs, t_send.at[2], t_recv.at[2], sibling)
    t_f.start()
    loads[0].wait()
    t_s.wait_recv()
    t_f.wait_recv()

    def by_rows(step, body):
        def one(i, carry):
            body(pl.ds(pl.multiple_of(i * step, step), step))
            return carry

        lax.fori_loop(0, rows // step, one, 0)

    def norm_one(span):
        values = tokens[span, :].astype(full)
        inv = lax.rsqrt(jnp.mean(values * values, axis=1, keepdims=True) + norm_eps)
        n1_ref[span, :] = (values * inv * first_ref[:1, :]).astype(low)
        inv_one_ref[span, :] = jnp.broadcast_to(inv, (inv.shape[0], 128))

    by_rows(32, norm_one)
    pass_z(1)
    pass_a(0)

    def project(weights, bias_at):
        def one(i, carry):
            cut = pl.ds(pl.multiple_of(i * 256, 256), 256)
            lin[:, cut] = (
                jnp.dot(n1_ref[...], weights[:, cut], preferred_element_type=full)
                + bias_ref[bias_at : bias_at + 1, cut]
            )
            return carry

        lax.fori_loop(0, cols // 256, one, 0)

    def rotate_into(target):
        def one(h, carry):
            cut = pl.ds(pl.multiple_of(h * HD, HD), HD)
            value = lin[:, cut]
            turned = value * cos_ref[...] + pltpu.roll(value, HD // 2, 1) * sin_ref[...]
            target[:, cut] = turned.astype(low)
            return carry

        lax.fori_loop(0, heads, one, 0)

    loads[1].wait()
    project(wk, 1)
    rotate_into(k_ref)
    loads[2].wait()
    project(wv, 2)
    v_ref[...] = lin[...].astype(low)
    earlier = (
        remote(k_ref, earlier_k, kv_send.at[0], kv_recv.at[0], beside),
        remote(v_ref, earlier_v, kv_send.at[1], kv_recv.at[1], beside),
    )

    @pl.when(y == 0)
    def _():
        for copy in earlier:
            copy.start()

    pass_b(0, 0)
    pass_z(2)
    pass_a(1)
    loads[3].wait()
    project(wq, 0)
    rotate_into(q_ref)

    half = rows // 2
    lane = lax.broadcasted_iota(jnp.int32, (1, 128), 1)

    def pick(held, span, h):
        return jnp.sum(jnp.where(lane == h, held[span, :], 0.0), axis=1, keepdims=True)

    def put(held, span, h, value):
        held[span, :] = jnp.where(lane == h, value, held[span, :])

    most[...] = jnp.zeros_like(most)
    weight[...] = jnp.ones_like(weight)

    def local_head(h, carry):
        cut = pl.ds(pl.multiple_of(h * HD, HD), HD)
        for qb in range(2):
            span, count = pl.ds(qb * half, half), (qb + 1) * half
            scores = times_transpose(q_ref[span, cut], k_ref[:count, cut]) * score_scale
            top = jnp.max(scores, axis=1, keepdims=True)
            powers = jnp.exp(scores - top)
            put(most, span, h, top)
            put(weight, span, h, jnp.sum(powers, axis=1, keepdims=True))
            total[span, cut] = jnp.dot(
                powers.astype(low), v_ref[:count, cut], preferred_element_type=full
            )
        return carry

    lax.fori_loop(0, heads, local_head, 0)
    pass_z(3)
    pass_a(2)
    pass_b(0, 1)
    pass_b(1, 0)

    @pl.when(y == 0)
    def _():
        ke_ref[...] = jnp.zeros_like(ke_ref)
        ve_ref[...] = jnp.zeros_like(ve_ref)

    @pl.when(y == 1)
    def _():
        for copy in earlier:
            copy.wait_recv()
        ke_ref[...] = earlier_k[...]
        ve_ref[...] = earlier_v[...]

        def remote_head(h, carry):
            cut = pl.ds(pl.multiple_of(h * HD, HD), HD)
            for qb in range(2):
                span = pl.ds(qb * half, half)
                scores = times_transpose(q_ref[span, cut], ke_ref[:, cut]) * score_scale
                before = pick(most, span, h)
                top = jnp.maximum(before, jnp.max(scores, axis=1, keepdims=True))
                powers = jnp.exp(scores - top)
                shrink = jnp.exp(before - top)
                put(most, span, h, top)
                put(
                    weight,
                    span,
                    h,
                    pick(weight, span, h) * shrink + jnp.sum(powers, axis=1, keepdims=True),
                )
                total[span, cut] = total[span, cut] * shrink + jnp.dot(
                    powers.astype(low), ve_ref[:, cut], preferred_element_type=full
                )
            return carry

        lax.fori_loop(0, heads, remote_head, 0)

    def finish_head(h, carry):
        cut = pl.ds(pl.multiple_of(h * HD, HD), HD)
        context_ref[:, cut] = (total[:, cut] / pick(weight, slice(None), h)).astype(low)
        return carry

    lax.fori_loop(0, heads, finish_head, 0)
    log_ref[...] = most[...] + jnp.log(weight[...])

    loads[4].wait()

    def out_part(at_quarter, target):
        cut = pl.ds(pl.multiple_of(at_quarter * cols, cols), cols)
        target[...] = jnp.dot(context_ref[...], wo[:, cut], preferred_element_type=full).astype(low)

    def part_to_sibling(i):
        return remote(tp_staged.at[i], tp_sib.at[i], tp_send.at[i], tp_recv.at[i], sibling)

    def part_of(i):
        x_at = 1 - x + (2 * x - 1) * i
        out_part(x_at * 2 + 1 - core, tp_staged.at[i])
        part_to_sibling(i).start()
        out_part(x_at * 2 + core, tp_mine.at[i])

    out_x = remote(tp_mine.at[0], tp_x, tp_send.at[2], tp_recv.at[2], across)
    part_of(0)
    part_to_sibling(0).wait_recv()
    add_blocks(tp_mine.at[0], [tp_sib.at[0]], rows)
    out_x.start()
    part_of(1)
    pass_a(3)
    pass_b(1, 1)
    pass_b(2, 0)
    part_to_sibling(1).wait_recv()
    out_x.wait_recv()
    own_cut = pl.ds(pl.multiple_of(tp * cols, cols), cols)

    def sum_parts(span):
        value = tokens[span, own_cut].astype(full) + (
            tp_mine[1, span, :].astype(full)
            + tp_sib[1, span, :].astype(full)
            + tp_x[span, :].astype(full)
        )
        hidden_ref[span, :] = value
        lin[span, :] = value * value

    by_rows(64, sum_parts)

    row_mine[0] = row_of(lin[...])
    first = remote(row_mine.at[0], row_sib, row_send.at[0], row_recv.at[0], sibling)
    first.start()
    first.wait_recv()
    row_mine[1] = row_mine[0] + row_sib[...]
    second = remote(row_mine.at[1], row_x, row_send.at[1], row_recv.at[1], across)
    second.start()
    second.wait_recv()
    squares = (row_mine[1] + row_x[...]).T[:, :1]
    inv_two = lax.rsqrt(squares * (1.0 / model_dim) + norm_eps)
    inv_ref[...] = jnp.broadcast_to(inv_two, (rows, 128))

    def norm_two(span):
        unit = hidden_ref[span, :] * inv_ref[span, :1]
        unit_ref[span, :] = unit
        normed_ref[span, :] = (unit * second_ref[:1, :]).astype(low)

    by_rows(64, norm_two)

    pass_b(2, 1)
    pass_b(3, 0)
    pass_b(3, 1)

    def finish_sibling(i, carry):
        block = spot(0, 0, 0)
        copy = remote(block, block, s_sem.at[i], sib_sem.at[i], sibling)
        copy.wait_recv()
        copy.wait_send()
        return carry

    lax.fori_loop(0, 16, finish_sibling, 0)

    def finish_links(i, carry):
        over_a(i, grad_hbm).wait_send()
        over_b(i, 0, grad_hbm).wait_send()
        over_b(i, 1, grad_hbm).wait_send()

        @pl.when((z < 3) & (i <= z))
        def _():
            up(i, grad_hbm).wait_send()

        @pl.when((z > 0) & (i >= z))
        def _():
            down(i, grad_hbm).wait_send()

        return carry

    lax.fori_loop(0, 4, finish_links, 0)
    own.wait()
    for copy in (t_x, t_s, t_f, out_x, part_to_sibling(0), part_to_sibling(1), first, second):
        copy.wait_send()

    @pl.when(y == 0)
    def _():
        for copy in earlier:
            copy.wait_send()


def attend(vmem_args, hbm_args, cid):
    rows, cols = hbm_args[0].shape
    model_dim = vmem_args[0].shape[1]
    low, full, dma = jnp.bfloat16, jnp.float32, pltpu.SemaphoreType.DMA
    vmem, hbm = pl.BlockSpec(memory_space=pltpu.VMEM), pl.BlockSpec(memory_space=pl.ANY)

    def buffers(*shape, dtype=low):
        return pltpu.VMEM(shape, dtype)

    def result(*shape, dtype=low):
        return jax.ShapeDtypeStruct(shape, dtype)

    return pl.pallas_call(
        attend_kernel,
        out_shape=[
            result(rows, cols, dtype=full),
            result(rows, cols, dtype=full),
            result(rows, 128, dtype=full),
            result(rows, cols),
            result(rows, model_dim),
            result(rows, 128, dtype=full),
        ]
        + [result(rows, cols)] * 6
        + [result(rows, 128, dtype=full), result(8 * rows, model_dim)],
        in_specs=[vmem] * len(vmem_args) + [hbm] * len(hbm_args),
        out_specs=[vmem] * 13 + [hbm],
        scratch_shapes=[buffers(*arg.shape) for arg in hbm_args[2:]]
        + [
            buffers(rows, model_dim),
            buffers(rows, cols, dtype=full),
            buffers(rows, cols, dtype=full),
            buffers(rows, 128, dtype=full),
            buffers(rows, 128, dtype=full),
            buffers(rows, cols),
            buffers(rows, cols),
            buffers(2, rows, cols),
            buffers(2, rows, cols),
            buffers(2, rows, cols),
            buffers(rows, cols),
            buffers(2, 8, rows, dtype=full),
            buffers(8, rows, dtype=full),
            buffers(8, rows, dtype=full),
        ]
        + [dma((6,)), dma((3,)), dma((3,)), dma((2,)), dma((2,)), dma((3,)), dma((3,))]
        + [dma((2,)), dma((2,))]
        + [dma((4,)), dma((4,)), dma((4,)), dma((8,)), dma((16,)), dma((16,)), dma((16,))],
        compiler_params=pltpu.CompilerParams(
            collective_id=cid, has_side_effects=True, vmem_limit_bytes=60 * 2**20
        ),
        name="attend",
    )(*vmem_args, *hbm_args)


def kept_choice(expert_ids, pair_order, expert_total, capacity):
    tok_count, top_count = expert_ids.shape
    pair_count = tok_count * top_count
    order = pair_order.reshape(-1)
    pairs = jnp.arange(pair_count, dtype=jnp.int32)
    turn = jnp.sum(jnp.where(order[None, :] == pairs[:, None], pairs[None, :], 0), axis=1)
    turn = turn.reshape(tok_count, top_count)
    picked = expert_ids[:, :, None] == jnp.arange(expert_total, dtype=jnp.int32)[None, None, :]
    experts_apart = jnp.arange(expert_total, dtype=jnp.int32)[:, None, None]
    picked = expert_ids.T[None] == experts_apart
    named = jnp.any(picked, axis=1)
    turn_of = jnp.sum(jnp.where(picked, turn.T[None], 0), axis=1)
    turn_of = jnp.where(named, turn_of, pair_count)
    slot = jnp.sum((turn_of[:, None, :] < turn_of[:, :, None]).astype(jnp.int32), axis=2)
    return (named & (slot < capacity)).astype(jnp.float32)


def dense_plan(
    tokens,
    out_grad,
    first_gain,
    query_weight,
    key_weight,
    value_weight,
    query_bias,
    key_bias,
    value_bias,
    output_weight,
    second_gain,
    router_weight,
    shared_gate_weight,
    shared_up_weight,
    shared_down_weight,
    switch_vector,
    expert_gate_weight,
    expert_up_weight,
    expert_down_weight,
    expert_ids,
    pair_order,
):
    ep, tp = lax.axis_index("ep"), lax.axis_index("tp")
    tok_count, col_width = tokens.shape
    model_dim = query_weight.shape[0]
    sources = lax.axis_size("ep")
    place_in_seq = ep % SPAN
    expert_total = router_weight.shape[1]
    capacity = 9 * tok_count * expert_ids.shape[1] // (8 * expert_total)
    head_count = query_weight.shape[1] // HD
    expert_width = expert_gate_weight.shape[2]
    shared_width = shared_gate_weight.shape[1] // sources
    width = expert_width + shared_width

    def own_cols(vector):
        return lax.dynamic_slice_in_dim(vector, tp * col_width, col_width, vector.ndim - 1)

    kept_own = kept_choice(expert_ids, pair_order, expert_total, capacity)

    def tall(vector):
        return jnp.broadcast_to(vector[None, :], (8, vector.shape[0]))

    cosine, sine_part = rope_tables(tok_count, HD, place_in_seq * tok_count)
    cos_wide = jnp.concatenate([cosine[:, 0], cosine[:, 0]], axis=1)
    sin_wide = jnp.concatenate([-sine_part[:, 0], sine_part[:, 0]], axis=1)
    second_cols = own_cols(second_gain)
    biases = jnp.pad(jnp.stack([query_bias, key_bias, value_bias]), ((0, 5), (0, 0)))
    (
        hidden_cols,
        unit_two,
        inv_two,
        normed_cols,
        normed_one,
        inv_one,
        queries,
        keys_rot,
        values_all,
        earlier_keys,
        earlier_values,
        context,
        log_rows,
        grads_all,
    ) = attend(
        [tall(first_gain), biases, tall(second_cols), cos_wide, sin_wide],
        [tokens, out_grad, query_weight, key_weight, value_weight, output_weight],
        2,
    )

    def shared_rows(weight):
        return lax.dynamic_slice_in_dim(weight, ep * shared_width, shared_width, 1).T

    extra_rows = jnp.concatenate([router_weight.T, switch_vector[None, :]], axis=0)
    extra_rows = jnp.pad(extra_rows, ((0, 16 - extra_rows.shape[0]), (0, 0)))
    kept_rows = jnp.pad(kept_own, ((0, 16 - expert_total), (0, 0))).astype(jnp.bfloat16)
    reduced, ffn_cols, logit_tile, expert_grads, shared_parts, *_ = experts(
        normed_cols,
        grads_all,
        kept_rows,
        [
            expert_gate_weight[0].T,
            shared_rows(shared_gate_weight),
            extra_rows,
            expert_up_weight[0].T,
            shared_rows(shared_up_weight),
            expert_down_weight[0],
            shared_down_weight,
        ],
        expert_total,
        4,
    )
    layer_out = (hidden_cols + ffn_cols).astype(jnp.bfloat16)
    shared_parts = lax.all_to_all(shared_parts, "ep", split_axis=0, concat_axis=0, tiled=True)
    shared_parts = shared_parts.transpose(1, 0, 2, 3).reshape(3, sources * shared_width, -1)
    shared_parts = shared_parts.astype(jnp.float32)
    shared_gate_grad = shared_parts[1].T
    shared_up_grad = shared_parts[2].T
    shared_down_grad = shared_parts[0]

    normed_grad = reduced[:tok_count]
    probs_grad = (reduced[tok_count : tok_count + expert_total] * kept_own).T
    switch_grad = reduced[tok_count + expert_total]
    logit_at = width % 128
    probs_own = softmax_rows(logit_tile[:, logit_at : logit_at + expert_total])
    switch = jax.nn.sigmoid(logit_tile[:, logit_at + expert_total])
    logit_grad = (
        probs_own * (probs_grad - jnp.sum(probs_own * probs_grad, axis=-1, keepdims=True))
    ).astype(jnp.bfloat16)
    router_grad = inner_rows(normed_cols, logit_grad)
    switch_lin_grad = switch_grad * switch * (1.0 - switch)
    switch_vector_grad = jnp.dot(switch_lin_grad, normed_cols, preferred_element_type=jnp.float32)
    router_cols = lax.dynamic_slice_in_dim(router_weight, tp * col_width, col_width, 0)
    normed_grad = normed_grad + times_transpose(logit_grad, router_cols)
    normed_grad = (
        normed_grad
        + switch_lin_grad[:, None] * own_cols(switch_vector).astype(jnp.float32)[None, :]
    )
    second_gain_grad = jnp.sum(normed_grad * unit_two, axis=0)

    small = jnp.concatenate(
        [second_gain_grad[None], switch_vector_grad[None], router_grad.T], axis=0
    )
    small_rows = small.shape[0]
    small = jnp.pad(small, ((4, 12 - small_rows), (0, 0)))
    tokens_grad, weight_grads, sums = unwind(
        [
            normed_grad,
            unit_two,
            inv_two,
            tall(second_cols),
            out_grad,
            tokens,
            inv_one,
            tall(own_cols(first_gain)),
            small,
            queries,
            keys_rot,
            values_all,
            earlier_keys,
            earlier_values,
            context,
            log_rows,
            cos_wide,
            sin_wide,
        ],
        [normed_one, query_weight, key_weight, value_weight, output_weight],
        5,
    )
    share = model_dim // sources
    bias_width = HD // sources
    bias_sums = lax.dynamic_slice_in_dim(
        sums[1:4].reshape(3, head_count, HD), ep * bias_width, bias_width, 2
    )
    spread = jnp.concatenate([sums[:1], sums[4 : 4 + small_rows]], axis=0)
    spread = lax.all_gather(spread, "tp", axis=1, tiled=True)
    spread = lax.dynamic_slice_in_dim(spread, ep * share, share, 1)
    return (
        layer_out,
        tokens_grad,
        spread[0],
        weight_grads[1],
        weight_grads[2],
        weight_grads[3],
        bias_sums[0],
        bias_sums[1],
        bias_sums[2],
        weight_grads[0].T,
        spread[1],
        spread[3:].T,
        shared_gate_grad,
        shared_up_grad,
        shared_down_grad,
        spread[2],
        expert_grads[1].T[None],
        expert_grads[2].T[None],
        expert_grads[0][None],
    )


def solution(mesh):
    plan = dense_plan if dict(mesh.shape) == {"ep": 8, "tp": 4} else slot_plan
    return jax.shard_map(
        plan,
        mesh=mesh,
        in_specs=(
            P("ep", "tp"),
            P("ep", "tp"),
            P(),
            P(None, "tp"),
            P(None, "tp"),
            P(None, "tp"),
            P("tp"),
            P("tp"),
            P("tp"),
            P("tp", None),
            P(),
            P(),
            P(None, "tp"),
            P(None, "tp"),
            P("tp", None),
            P(),
            P("ep", None, "tp"),
            P("ep", None, "tp"),
            P("ep", "tp", None),
            P("ep", None),
            P("ep", None),
        ),
        out_specs=(
            P("ep", "tp"),
            P("ep", "tp"),
            P("ep"),
            P("ep", "tp"),
            P("ep", "tp"),
            P("ep", "tp"),
            P("tp", "ep"),
            P("tp", "ep"),
            P("tp", "ep"),
            P("tp", "ep"),
            P("ep"),
            P("ep", None),
            P("ep", "tp"),
            P("ep", "tp"),
            P("tp", "ep"),
            P("ep"),
            P("ep", None, "tp"),
            P("ep", None, "tp"),
            P("ep", "tp", None),
        ),
        check_vma=False,
    )
```

```python
import functools
import math

import jax
import jax.numpy as jnp
from jax import lax
from jax.experimental import pallas as pl
from jax.experimental.pallas import tpu as pltpu
from jax.sharding import PartitionSpec as P

HD = 128
BLOCK = 256
SPAN = 2


rope_theta = 1000000.0
norm_eps = 1e-06
masked_score = -1e30


def passed_along(value, axis, steps):
    count = lax.axis_size(axis)
    leading, last = (max(0, -steps), min(count, count - steps))
    return lax.ppermute(value, axis, [(source, source + steps) for source in range(leading, last)])


def rope_tables(row_count, head_dim, first_position):
    positions = jnp.arange(row_count, dtype=jnp.float32) + first_position.astype(jnp.float32)
    frequency = jnp.exp(
        jnp.arange(head_dim // 2, dtype=jnp.float32) * (-2.0 * math.log(rope_theta) / head_dim)
    )
    angles = positions[:, None] * frequency[None, :]
    return (jnp.cos(angles)[:, None, :], jnp.sin(angles)[:, None, :])


def rotate(values, cosine, sine_part):
    half_dim = values.shape[-1] // 2
    first_half = values[..., :half_dim]
    second_half = values[..., half_dim:]
    return jnp.concatenate(
        [
            first_half * cosine - second_half * sine_part,
            second_half * cosine + first_half * sine_part,
        ],
        axis=-1,
    )


def inner_rows(left_side, right_side):
    return lax.dot_general(
        left_side, right_side, (((0,), (0,)), ((), ())), preferred_element_type=jnp.float32
    )


def times_transpose(left_side, right_side):
    return lax.dot_general(
        left_side, right_side, (((1,), (1,)), ((), ())), preferred_element_type=jnp.float32
    )


def row_stats(values):
    inv_rms = lax.rsqrt(jnp.mean(values * values, axis=-1, keepdims=True) + norm_eps)
    return (values * inv_rms, inv_rms)


def norm_back(grad_rows, unit_rows, inv_rms, gain_vec):
    scaled = grad_rows * gain_vec
    return inv_rms * (scaled - unit_rows * jnp.mean(scaled * unit_rows, axis=-1, keepdims=True))


def softmax_rows(scores):
    row_max = jnp.max(scores, axis=-1, keepdims=True)
    powers = jnp.exp(scores - row_max)
    return powers / jnp.sum(powers, axis=-1, keepdims=True)


def to_experts(block_rows, local_count):
    sources, span_rows, col_count = block_rows.shape
    slot_count = span_rows // local_count
    shaped = block_rows.reshape(sources, local_count, slot_count, col_count)
    return shaped.swapaxes(0, 1).reshape(local_count, sources * slot_count, col_count)


def to_sources(block_rows, sources):
    local_count, rows_all, col_count = block_rows.shape
    slot_count = rows_all // sources
    shaped = block_rows.reshape(local_count, sources, slot_count, col_count)
    return shaped.swapaxes(0, 1).reshape(sources, local_count * slot_count, col_count)


def deliver(block_rows):
    arrived = lax.all_to_all(block_rows, "ep", split_axis=0, concat_axis=0, tiled=True)
    return arrived


def collect(block_rows):
    return lax.all_to_all(block_rows, "ep", split_axis=0, concat_axis=0, tiled=True)


def slot_plan(
    tokens,
    out_grad,
    first_gain,
    query_weight,
    key_weight,
    value_weight,
    query_bias,
    key_bias,
    value_bias,
    output_weight,
    second_gain,
    router_weight,
    shared_gate_weight,
    shared_up_weight,
    shared_down_weight,
    switch_vector,
    expert_gate_weight,
    expert_up_weight,
    expert_down_weight,
    expert_ids,
    pair_order,
):
    whole_in, whole_grad = (
        lax.all_gather(tokens, "tp", axis=1, tiled=True),
        lax.all_gather(out_grad, "tp", axis=1, tiled=True),
    )
    tok_count = whole_in.shape[0]
    model_dim = whole_in.shape[1]
    col_width = tokens.shape[1]
    col_start = lax.axis_index("tp") * col_width
    sources = lax.axis_size("ep")
    place_in_seq = lax.axis_index("ep") % SPAN
    has_earlier = place_in_seq > 0
    local_experts = expert_gate_weight.shape[0]
    expert_total = router_weight.shape[1]
    top_count = expert_ids.shape[1]
    pair_count = tok_count * top_count
    capacity = 9 * pair_count // (8 * expert_total)
    head_count = query_weight.shape[1] // HD
    score_scale = HD ** (-0.5)
    inputs_full = whole_in.astype(jnp.float32)
    unit_one, inv_one = row_stats(inputs_full)
    normed_one = (unit_one * first_gain).astype(jnp.bfloat16)
    query_lin = jnp.dot(normed_one, query_weight, preferred_element_type=jnp.float32) + query_bias
    key_lin = jnp.dot(normed_one, key_weight, preferred_element_type=jnp.float32) + key_bias
    value_lin = jnp.dot(normed_one, value_weight, preferred_element_type=jnp.float32) + value_bias
    cosine, sine_part = rope_tables(tok_count, HD, place_in_seq * tok_count)
    queries = rotate(query_lin.reshape(tok_count, head_count, HD), cosine, sine_part).astype(
        jnp.bfloat16
    )
    keys_rot = rotate(key_lin.reshape(tok_count, head_count, HD), cosine, sine_part).astype(
        jnp.bfloat16
    )
    values_all = value_lin.reshape(tok_count, head_count, HD).astype(jnp.bfloat16)
    earlier_keys, earlier_values = passed_along((keys_rot, values_all), "ep", 1)
    keys_both = jnp.concatenate([earlier_keys, keys_rot], axis=0)
    values_both = jnp.concatenate([earlier_values, values_all], axis=0)
    blocks = jnp.arange(tok_count) // BLOCK
    local_allowed = blocks[None, :] <= blocks[:, None]
    remote_allowed = jnp.broadcast_to(has_earlier, (tok_count, tok_count))
    allowed = jnp.concatenate([remote_allowed, local_allowed], axis=1)[None]

    def attention_scores():
        scored = (
            jnp.einsum("qhd,khd->hqk", queries, keys_both, preferred_element_type=jnp.float32)
            * score_scale
        )
        return jnp.where(allowed, scored, masked_score)

    scores = attention_scores()
    row_max = jnp.max(scores, axis=-1, keepdims=True)
    powers = jnp.exp(scores - row_max)
    totals = jnp.sum(powers, axis=-1, keepdims=True)
    log_total = row_max + jnp.log(totals)
    probs_low = (powers / totals).astype(jnp.bfloat16)
    context = jnp.einsum("hqk,khd->qhd", probs_low, values_both, preferred_element_type=jnp.float32)
    context = context.reshape(tok_count, head_count * HD).astype(jnp.bfloat16)
    attn_part = jnp.dot(context, output_weight, preferred_element_type=jnp.float32)
    attended = lax.psum(attn_part, "tp")
    hidden_one = inputs_full + attended
    unit_two, inv_two = row_stats(hidden_one)
    normed_two = (unit_two * second_gain).astype(jnp.bfloat16)
    logits = jnp.dot(normed_two, router_weight, preferred_element_type=jnp.float32)
    router_probs = softmax_rows(logits)
    gate_values = jnp.take_along_axis(router_probs, expert_ids, axis=1)
    switch = jax.nn.sigmoid(jnp.dot(normed_two, switch_vector, preferred_element_type=jnp.float32))
    flat_ids = expert_ids.reshape(-1)
    turn_order = pair_order.reshape(-1)
    in_turn = flat_ids[turn_order]
    onehot = (in_turn[:, None] == jnp.arange(expert_total, dtype=jnp.int32)[None, :]).astype(
        jnp.int32
    )
    earlier = jnp.cumsum(onehot, axis=0) - onehot
    turn_slot = jnp.sum(earlier * onehot, axis=1)
    slot_index = jnp.zeros((pair_count,), jnp.int32).at[turn_order].set(turn_slot)
    kept_pair = slot_index < capacity
    slot_rows = expert_total * capacity
    target = jnp.where(kept_pair, flat_ids * capacity + slot_index, slot_rows)
    pair_token = jnp.arange(pair_count, dtype=jnp.int32) // top_count
    slot_token = (
        jnp.full((slot_rows + 1,), tok_count, jnp.int32).at[target].set(pair_token)[:slot_rows]
    )
    slot_gate = (
        jnp.zeros((slot_rows + 1,), jnp.float32).at[target].set(gate_values.reshape(-1))[:slot_rows]
    )
    padded_two = jnp.concatenate([normed_two, jnp.zeros((1, model_dim), jnp.bfloat16)], axis=0)
    send_rows = padded_two[slot_token].reshape(sources, local_experts * capacity, model_dim)
    expert_rows = to_experts(deliver(send_rows), local_experts)
    gate_lin = jnp.einsum(
        "erd,edf->erf", expert_rows, expert_gate_weight, preferred_element_type=jnp.float32
    )
    up_lin = jnp.einsum(
        "erd,edf->erf", expert_rows, expert_up_weight, preferred_element_type=jnp.float32
    )
    gate_sig = jax.nn.sigmoid(gate_lin)
    gate_act = gate_lin * gate_sig
    expert_hidden = (gate_act * up_lin).astype(jnp.bfloat16)
    expert_part = jnp.einsum(
        "erf,efd->erd", expert_hidden, expert_down_weight, preferred_element_type=jnp.float32
    )
    shared_gate_lin = jnp.dot(normed_two, shared_gate_weight, preferred_element_type=jnp.float32)
    shared_up_lin = jnp.dot(normed_two, shared_up_weight, preferred_element_type=jnp.float32)
    shared_sig = jax.nn.sigmoid(shared_gate_lin)
    shared_act = shared_gate_lin * shared_sig
    shared_hidden = (shared_act * shared_up_lin).astype(jnp.bfloat16)
    shared_part = jnp.dot(shared_hidden, shared_down_weight, preferred_element_type=jnp.float32)
    expert_cols, shared_cols = (
        lax.psum_scatter(expert_part.reshape(-1, model_dim), "tp", scatter_dimension=1, tiled=True),
        lax.psum_scatter(shared_part, "tp", scatter_dimension=1, tiled=True),
    )
    returned = collect(
        to_sources(expert_cols.astype(jnp.bfloat16).reshape(local_experts, -1, col_width), sources)
    )
    back_flat = jnp.concatenate(
        [returned.reshape(slot_rows, col_width), jnp.zeros((1, col_width), jnp.bfloat16)], axis=0
    )
    pair_out = back_flat[target].astype(jnp.float32).reshape(tok_count, top_count, col_width)
    routed = jnp.sum(gate_values[:, :, None] * pair_out, axis=1)
    hidden_cols = lax.dynamic_slice_in_dim(hidden_one, col_start, col_width, 1)
    layer_out = (hidden_cols + switch[:, None] * shared_cols + routed).astype(jnp.bfloat16)
    grad_full = whole_grad.astype(jnp.float32)
    grad_cols = out_grad.astype(jnp.float32)
    gate_part = jnp.sum(pair_out * grad_cols[:, None, :], axis=-1)
    switch_part = jnp.sum(grad_cols * shared_cols, axis=-1)
    gate_grad, switch_grad = lax.psum((gate_part, switch_part), "tp")
    padded_grad = jnp.concatenate([whole_grad, jnp.zeros((1, model_dim), jnp.bfloat16)], axis=0)
    send_grads = (slot_gate[:, None] * padded_grad[slot_token].astype(jnp.float32)).astype(
        jnp.bfloat16
    )
    expert_grads = to_experts(
        deliver(send_grads.reshape(sources, local_experts * capacity, model_dim)), local_experts
    )
    hidden_grad = jnp.einsum(
        "erd,efd->erf", expert_grads, expert_down_weight, preferred_element_type=jnp.float32
    )
    gate_lin_grad = (hidden_grad * up_lin * gate_sig * (1.0 + gate_lin * (1.0 - gate_sig))).astype(
        jnp.bfloat16
    )
    up_lin_grad = (hidden_grad * gate_act).astype(jnp.bfloat16)
    expert_down_grad = jnp.einsum(
        "erf,erd->efd", expert_hidden, expert_grads, preferred_element_type=jnp.float32
    )
    expert_gate_grad = jnp.einsum(
        "erd,erf->edf", expert_rows, gate_lin_grad, preferred_element_type=jnp.float32
    )
    expert_up_grad = jnp.einsum(
        "erd,erf->edf", expert_rows, up_lin_grad, preferred_element_type=jnp.float32
    )
    rows_grad = jnp.einsum(
        "erf,edf->erd", gate_lin_grad, expert_gate_weight, preferred_element_type=jnp.float32
    )
    rows_grad = rows_grad + jnp.einsum(
        "erf,edf->erd", up_lin_grad, expert_up_weight, preferred_element_type=jnp.float32
    )
    rows_grad_cols = lax.psum_scatter(
        rows_grad.reshape(-1, model_dim), "tp", scatter_dimension=1, tiled=True
    )
    returned_grad = collect(
        to_sources(
            rows_grad_cols.astype(jnp.bfloat16).reshape(local_experts, -1, col_width), sources
        )
    )
    back_grad = jnp.concatenate(
        [returned_grad.reshape(slot_rows, col_width), jnp.zeros((1, col_width), jnp.bfloat16)],
        axis=0,
    )
    routed_grad = jnp.sum(
        back_grad[target].astype(jnp.float32).reshape(tok_count, top_count, col_width), axis=1
    )
    shared_out_grad = (switch[:, None] * grad_full).astype(jnp.bfloat16)
    shared_hidden_grad = times_transpose(shared_out_grad, shared_down_weight)
    shared_gate_lin_grad = (
        shared_hidden_grad
        * shared_up_lin
        * shared_sig
        * (1.0 + shared_gate_lin * (1.0 - shared_sig))
    ).astype(jnp.bfloat16)
    shared_up_lin_grad = (shared_hidden_grad * shared_act).astype(jnp.bfloat16)
    shared_down_grad = inner_rows(shared_hidden, shared_out_grad)
    shared_gate_grad = inner_rows(normed_two, shared_gate_lin_grad)
    shared_up_grad = inner_rows(normed_two, shared_up_lin_grad)
    normed_grad = times_transpose(shared_gate_lin_grad, shared_gate_weight) + times_transpose(
        shared_up_lin_grad, shared_up_weight
    )
    normed_grad = normed_grad + lax.dynamic_update_slice_in_dim(
        jnp.zeros_like(normed_grad), routed_grad, col_start, 1
    )
    normed_grad = lax.psum(normed_grad, "tp")
    picked = (
        expert_ids[:, :, None] == jnp.arange(expert_total, dtype=jnp.int32)[None, None, :]
    ).astype(jnp.float32)
    probs_grad = jnp.sum(picked * gate_grad[:, :, None], axis=1)
    logit_grad = (
        router_probs * (probs_grad - jnp.sum(router_probs * probs_grad, axis=-1, keepdims=True))
    ).astype(jnp.bfloat16)
    router_grad = inner_rows(normed_two, logit_grad)
    switch_lin_grad = switch_grad * switch * (1.0 - switch)
    switch_vector_grad = jnp.dot(switch_lin_grad, normed_two, preferred_element_type=jnp.float32)
    normed_grad = normed_grad + times_transpose(logit_grad, router_weight)
    normed_grad = (
        normed_grad + switch_lin_grad[:, None] * switch_vector.astype(jnp.float32)[None, :]
    )
    second_gain_grad = jnp.sum(normed_grad * unit_two, axis=0)
    hidden_grad_one = grad_full + norm_back(normed_grad, unit_two, inv_two, second_gain)
    attended_grad = hidden_grad_one.astype(jnp.bfloat16)
    output_grad = inner_rows(context, attended_grad)
    context_grad = (
        times_transpose(attended_grad, output_weight)
        .astype(jnp.bfloat16)
        .reshape(tok_count, head_count, HD)
    )
    scores = attention_scores()
    attn_probs = jnp.exp(scores - log_total)
    probs_again = attn_probs.astype(jnp.bfloat16)
    probs_grad_att = jnp.einsum(
        "qhd,khd->hqk", context_grad, values_both, preferred_element_type=jnp.float32
    )
    values_both_grad = jnp.einsum(
        "hqk,qhd->khd", probs_again, context_grad, preferred_element_type=jnp.float32
    )
    scores_grad = (
        attn_probs * (probs_grad_att - jnp.sum(attn_probs * probs_grad_att, axis=-1, keepdims=True))
    ).astype(jnp.bfloat16)
    queries_grad = (
        jnp.einsum("hqk,khd->qhd", scores_grad, keys_both, preferred_element_type=jnp.float32)
        * score_scale
    )
    keys_both_grad = (
        jnp.einsum("hqk,qhd->khd", scores_grad, queries, preferred_element_type=jnp.float32)
        * score_scale
    )
    later_keys_grad, later_values_grad = passed_along(
        (keys_both_grad[:tok_count], values_both_grad[:tok_count]), "ep", -1
    )
    keep_later = jnp.where(has_earlier, 0.0, 1.0).astype(jnp.float32)
    keys_grad = keys_both_grad[tok_count:] + keep_later * later_keys_grad
    values_grad = values_both_grad[tok_count:] + keep_later * later_values_grad
    value_lin_grad = values_grad.reshape(tok_count, head_count * HD).astype(jnp.bfloat16)
    query_lin_grad = (
        rotate(queries_grad, cosine, -sine_part)
        .reshape(tok_count, head_count * HD)
        .astype(jnp.bfloat16)
    )
    key_lin_grad = (
        rotate(keys_grad, cosine, -sine_part)
        .reshape(tok_count, head_count * HD)
        .astype(jnp.bfloat16)
    )
    query_grad = inner_rows(normed_one, query_lin_grad)
    key_grad = inner_rows(normed_one, key_lin_grad)
    value_grad = inner_rows(normed_one, value_lin_grad)
    query_bias_grad = jnp.sum(query_lin_grad.astype(jnp.float32), axis=0).reshape(head_count, HD)
    key_bias_grad = jnp.sum(key_lin_grad.astype(jnp.float32), axis=0).reshape(head_count, HD)
    value_bias_grad = jnp.sum(value_lin_grad.astype(jnp.float32), axis=0).reshape(head_count, HD)
    normed_one_grad = times_transpose(query_lin_grad, query_weight) + times_transpose(
        key_lin_grad, key_weight
    )
    normed_one_grad = normed_one_grad + times_transpose(value_lin_grad, value_weight)
    normed_one_grad = lax.psum(normed_one_grad.astype(jnp.bfloat16), "tp").astype(jnp.float32)
    first_gain_grad = jnp.sum(normed_one_grad * unit_one, axis=0)
    input_grad = hidden_grad_one + norm_back(normed_one_grad, unit_one, inv_one, first_gain)
    tokens_grad = lax.dynamic_slice_in_dim(input_grad, col_start, col_width, 1).astype(jnp.bfloat16)
    reduced = (
        lax.psum_scatter(
            first_gain_grad.astype(jnp.bfloat16), "ep", scatter_dimension=0, tiled=True
        ).astype(jnp.float32),
        lax.psum_scatter(
            query_grad.astype(jnp.bfloat16), "ep", scatter_dimension=0, tiled=True
        ).astype(jnp.float32),
        lax.psum_scatter(
            key_grad.astype(jnp.bfloat16), "ep", scatter_dimension=0, tiled=True
        ).astype(jnp.float32),
        lax.psum_scatter(
            value_grad.astype(jnp.bfloat16), "ep", scatter_dimension=0, tiled=True
        ).astype(jnp.float32),
        lax.psum_scatter(
            query_bias_grad.astype(jnp.bfloat16), "ep", scatter_dimension=1, tiled=True
        ).astype(jnp.float32),
        lax.psum_scatter(
            key_bias_grad.astype(jnp.bfloat16), "ep", scatter_dimension=1, tiled=True
        ).astype(jnp.float32),
        lax.psum_scatter(
            value_bias_grad.astype(jnp.bfloat16), "ep", scatter_dimension=1, tiled=True
        ).astype(jnp.float32),
        lax.psum_scatter(
            output_grad.astype(jnp.bfloat16), "ep", scatter_dimension=1, tiled=True
        ).astype(jnp.float32),
        lax.psum_scatter(
            second_gain_grad.astype(jnp.bfloat16), "ep", scatter_dimension=0, tiled=True
        ).astype(jnp.float32),
        lax.psum_scatter(
            router_grad.astype(jnp.bfloat16), "ep", scatter_dimension=0, tiled=True
        ).astype(jnp.float32),
        lax.psum_scatter(
            shared_gate_grad.astype(jnp.bfloat16), "ep", scatter_dimension=0, tiled=True
        ).astype(jnp.float32),
        lax.psum_scatter(
            shared_up_grad.astype(jnp.bfloat16), "ep", scatter_dimension=0, tiled=True
        ).astype(jnp.float32),
        lax.psum_scatter(
            shared_down_grad.astype(jnp.bfloat16), "ep", scatter_dimension=1, tiled=True
        ).astype(jnp.float32),
        lax.psum_scatter(
            switch_vector_grad.astype(jnp.bfloat16), "ep", scatter_dimension=0, tiled=True
        ).astype(jnp.float32),
    )
    return (
        layer_out,
        tokens_grad,
        reduced[0],
        reduced[1],
        reduced[2],
        reduced[3],
        reduced[4],
        reduced[5],
        reduced[6],
        reduced[7],
        reduced[8],
        reduced[9],
        reduced[10],
        reduced[11],
        reduced[12],
        reduced[13],
        expert_gate_grad,
        expert_up_grad,
        expert_down_grad,
    )


MESH = pl.DeviceIdType.MESH
Z_ORDER = (0, 3, 1, 2)


def place():
    ep, tp = lax.axis_index("ep"), lax.axis_index("tp")
    return ep, tp, ep // 2, lax.rem(ep, 2), tp // 2, lax.rem(tp, 2)


def greet(always, along_z=False):
    barrier = pltpu.get_barrier_semaphore()
    for device in always:
        pl.semaphore_signal(barrier, inc=1, device_id=device, device_id_type=MESH)
    count = len(always)
    if along_z:
        ep, tp, z, _, _, _ = place()

        @pl.when(z < 3)
        def _():
            pl.semaphore_signal(barrier, inc=1, device_id=(ep + 2, tp), device_id_type=MESH)

        @pl.when(z > 0)
        def _():
            pl.semaphore_signal(barrier, inc=1, device_id=(ep - 2, tp), device_id_type=MESH)

        count = count + lax.min(z, 1) + lax.min(3 - z, 1)
    pl.semaphore_wait(barrier, count)


def remote(source, target, send_sem, recv_sem, device):
    return pltpu.make_async_remote_copy(
        src_ref=source,
        dst_ref=target,
        send_sem=send_sem,
        recv_sem=recv_sem,
        device_id=device,
        device_id_type=MESH,
    )


def add_blocks(target, sources, rows):
    step = next(size for size in (80, 64, 48, 16) if rows % size == 0)

    def body(i, carry):
        span = pl.ds(pl.multiple_of(i * step, 16), step)
        total = target[span, :]
        for source in sources:
            total = total + source[span, :].astype(target.dtype)
        target[span, :] = total
        return carry

    lax.fori_loop(0, rows // step, body, 0)


def gather_tp_kernel(x_ref, o_ref, send_sem, recv_sem, own_sem):
    ep, tp, _, _, x, core = place()
    cols = x_ref.shape[1]
    sibling = (ep, tp + 1 - 2 * core)
    across = (ep, tp + 2 - 4 * x)
    greet([sibling, across])
    mine = o_ref.at[:, pl.ds(pl.multiple_of(tp * cols, cols), cols)]
    theirs = o_ref.at[:, pl.ds(pl.multiple_of((tp + 2 - 4 * x) * cols, cols), cols)]
    out_x = remote(x_ref, mine, send_sem.at[0], recv_sem.at[0], across)
    out_s = remote(x_ref, mine, send_sem.at[1], recv_sem.at[1], sibling)
    own = pltpu.make_async_copy(x_ref, mine, own_sem)
    out_x.start()
    out_s.start()
    own.start()
    remote(x_ref, theirs, send_sem.at[0], recv_sem.at[0], across).wait_recv()
    passing = remote(theirs, theirs, send_sem.at[2], recv_sem.at[2], sibling)
    passing.start()
    out_s.wait_recv()
    passing.wait_recv()
    own.wait()
    out_x.wait_send()
    out_s.wait_send()
    passing.wait_send()


def gather_tp(value, cid):
    rows, cols = value.shape
    return pl.pallas_call(
        gather_tp_kernel,
        out_shape=jax.ShapeDtypeStruct((rows, 4 * cols), value.dtype),
        in_specs=[pl.BlockSpec(memory_space=pl.ANY)],
        out_specs=pl.BlockSpec(memory_space=pl.ANY),
        scratch_shapes=[
            pltpu.SemaphoreType.DMA((3,)),
            pltpu.SemaphoreType.DMA((3,)),
            pltpu.SemaphoreType.DMA,
        ],
        compiler_params=pltpu.CompilerParams(collective_id=cid, has_side_effects=True),
        name="gather_tp",
    )(value)


def scatter_tp_kernel(p_ref, o_ref, mine, from_sib, from_x, own_sem, send_sem, recv_sem):
    ep, tp, _, _, x, core = place()
    rows, cols = o_ref.shape
    sibling = (ep, tp + 1 - 2 * core)
    across = (ep, tp + 2 - 4 * x)
    greet([sibling, across])

    def part(x_at, core_at):
        return p_ref.at[:, pl.ds(pl.multiple_of((x_at * 2 + core_at) * cols, cols), cols)]

    sends, owns = [], []
    for i, x_at in enumerate((1 - x, x)):
        owns.append(pltpu.make_async_copy(part(x_at, core), mine.at[i], own_sem.at[i]))
        sends.append(
            remote(part(x_at, 1 - core), from_sib.at[i], send_sem.at[i], recv_sem.at[i], sibling)
        )
        sends[-1].start()
        owns[-1].start()
    owns[0].wait()
    sends[0].wait_recv()
    add_blocks(mine.at[0], [from_sib.at[0]], rows)
    out_x = remote(mine.at[0], from_x, send_sem.at[2], recv_sem.at[2], across)
    out_x.start()
    owns[1].wait()
    sends[1].wait_recv()
    out_x.wait_recv()
    o_ref[...] = jnp.zeros_like(o_ref)
    add_blocks(o_ref, [mine.at[1], from_sib.at[1], from_x], rows)
    out_x.wait_send()
    sends[0].wait_send()
    sends[1].wait_send()


def scatter_tp(value, cid):
    rows, cols = value.shape[0], value.shape[1] // 4
    return pl.pallas_call(
        scatter_tp_kernel,
        out_shape=jax.ShapeDtypeStruct((rows, cols), jnp.float32),
        in_specs=[pl.BlockSpec(memory_space=pl.ANY)],
        out_specs=pl.BlockSpec(memory_space=pltpu.VMEM),
        scratch_shapes=[
            pltpu.VMEM((2, rows, cols), value.dtype),
            pltpu.VMEM((2, rows, cols), value.dtype),
            pltpu.VMEM((rows, cols), value.dtype),
            pltpu.SemaphoreType.DMA((2,)),
            pltpu.SemaphoreType.DMA((3,)),
            pltpu.SemaphoreType.DMA((3,)),
        ],
        compiler_params=pltpu.CompilerParams(
            collective_id=cid, has_side_effects=True, vmem_limit_bytes=32 * 2**20
        ),
        name="scatter_tp",
    )(value)


def lane_peers():
    ep, tp, z, y, x, core = place()
    to_y, to_x = 1 - 2 * y, 1 - 2 * x
    peer_a = (ep + (1 - core) * to_y, tp + core * 2 * to_x)
    peer_b = (ep + core * to_y, tp + (1 - core) * 2 * to_x)
    sibling = (ep, tp + 1 - 2 * core)
    above, below = (ep + 2, tp), (ep - 2, tp)
    return peer_a, peer_b, sibling, above, below


def lane_spot(z_at, da, db, core_at):
    _, _, _, y, x, _ = place()
    y_at = y + (1 - 2 * y) * ((1 - core_at) * da + core_at * db)
    x_at = x + (1 - 2 * x) * (core_at * da + (1 - core_at) * db)
    return z_at * 2 + y_at, x_at * 2 + core_at


def gather_all_kernel(x_ref, o_ref, up_sem, down_sem, a_sem, b_sem, s_sem, recv_sem, sib_sem, own_sem):
    ep, tp, z, y, x, core = place()
    rows, cols = x_ref.shape
    peer_a, peer_b, sibling, above, below = lane_peers()
    greet([peer_a, peer_b, sibling], True)

    def spot(z_at, da, db):
        group, quarter = lane_spot(z_at, da, db, core)
        return o_ref.at[
            pl.ds(pl.multiple_of(group * rows, rows), rows),
            pl.ds(pl.multiple_of(quarter * cols, cols), cols),
        ]

    def at(z_at, da, db):
        return z_at * 4 + da * 2 + db

    def arrived(z_at, da, db):
        block = spot(z_at, da, db)
        remote(block, block, s_sem.at[at(z_at, da, db)], recv_sem.at[at(z_at, da, db)], sibling).wait_recv()

    def up(z_at, source):
        return remote(source, spot(z_at, 0, 0), up_sem.at[z_at], recv_sem.at[at(z_at, 0, 0)], above)

    def down(z_at, source):
        return remote(source, spot(z_at, 0, 0), down_sem.at[z_at], recv_sem.at[at(z_at, 0, 0)], below)

    def over_a(z_at, source):
        return remote(source, spot(z_at, 0, 0), a_sem.at[z_at], recv_sem.at[at(z_at, 1, 0)], peer_a)

    def over_b(z_at, da, source):
        return remote(
            source, spot(z_at, da, 0), b_sem.at[z_at * 2 + da], recv_sem.at[at(z_at, da, 1)], peer_b
        )

    def to_sibling(z_at, da, db, source):
        n = at(z_at, da, db)
        return remote(source, spot(z_at, da, db), s_sem.at[n], sib_sem.at[n], sibling)

    own = pltpu.make_async_copy(x_ref, spot(z, 0, 0), own_sem)
    over_b(z, 0, x_ref).start()
    over_a(z, x_ref).start()

    @pl.when(z < 3)
    def _():
        up(z, x_ref).start()

    @pl.when(z > 0)
    def _():
        down(z, x_ref).start()

    to_sibling(z, 0, 0, x_ref).start()
    own.start()

    def from_a(z_at):
        arrived(z_at, 1, 0)
        block = spot(z_at, 1, 0)
        over_b(z_at, 1, block).start()
        to_sibling(z_at, 1, 0, block).start()

    def from_z(z_at, onward):
        arrived(z_at, 0, 0)
        block = spot(z_at, 0, 0)
        onward(block)
        over_a(z_at, block).start()
        over_b(z_at, 0, block).start()
        to_sibling(z_at, 0, 0, block).start()

    def from_below(z_at):
        def onward(block):
            @pl.when(z < 3)
            def _():
                up(z_at, block).start()

        from_z(z_at, onward)

    def from_above(z_at):
        def onward(block):
            @pl.when(z > 0)
            def _():
                down(z_at, block).start()

        from_z(z_at, onward)

    for d in range(1, 4):

        @pl.when(z >= d)
        def _(d=d):
            from_below(z - d)

        @pl.when(z + d <= 3)
        def _(d=d):
            from_above(z + d)

        if d == 1:
            from_a(z)
        else:

            @pl.when(z >= d - 1)
            def _(d=d):
                from_a(z - d + 1)

            @pl.when(z + d - 1 <= 3)
            def _(d=d):
                from_a(z + d - 1)

    @pl.when(z >= 3)
    def _():
        from_a(z - 3)

    @pl.when(z + 3 <= 3)
    def _():
        from_a(z + 3)

    def from_b(z_at, da):
        arrived(z_at, da, 1)
        to_sibling(z_at, da, 1, spot(z_at, da, 1)).start()

    for da in range(2):
        from_b(z, da)
    for d in range(1, 4):
        for da in range(2):

            @pl.when(z >= d)
            def _(d=d, da=da):
                from_b(z - d, da)

            @pl.when(z + d <= 3)
            def _(d=d, da=da):
                from_b(z + d, da)

    def finish_sibling(i, carry):
        block = spot(0, 0, 0)
        copy = remote(block, block, s_sem.at[i], sib_sem.at[i], sibling)
        copy.wait_recv()
        copy.wait_send()
        return carry

    lax.fori_loop(0, 16, finish_sibling, 0)

    def finish_links(i, carry):
        over_a(i, x_ref).wait_send()
        over_b(i, 0, x_ref).wait_send()
        over_b(i, 1, x_ref).wait_send()

        @pl.when((z < 3) & (i <= z))
        def _():
            up(i, x_ref).wait_send()

        @pl.when((z > 0) & (i >= z))
        def _():
            down(i, x_ref).wait_send()

        return carry

    lax.fori_loop(0, 4, finish_links, 0)
    own.wait()


def gather_all(value, cid):
    rows, cols = value.shape
    return pl.pallas_call(
        gather_all_kernel,
        out_shape=jax.ShapeDtypeStruct((8 * rows, 4 * cols), value.dtype),
        in_specs=[pl.BlockSpec(memory_space=pl.ANY)],
        out_specs=pl.BlockSpec(memory_space=pl.ANY),
        scratch_shapes=[
            pltpu.SemaphoreType.DMA((4,)),
            pltpu.SemaphoreType.DMA((4,)),
            pltpu.SemaphoreType.DMA((4,)),
            pltpu.SemaphoreType.DMA((8,)),
            pltpu.SemaphoreType.DMA((16,)),
            pltpu.SemaphoreType.DMA((16,)),
            pltpu.SemaphoreType.DMA((16,)),
            pltpu.SemaphoreType.DMA,
        ],
        compiler_params=pltpu.CompilerParams(collective_id=cid, has_side_effects=True),
        name="gather_all",
    )(value)


def z_chain(blocks, totals, from_below, from_above, up_send, up_recv, down_send, down_recv, rows, final):
    ep, tp, z, _, _, _ = place()
    above, below = (ep + 2, tp), (ep - 2, tp)

    def up(z_at):
        return remote(totals(z_at), from_below.at[z_at], up_send.at[z_at], up_recv.at[z_at], above)

    def down(z_at):
        return remote(totals(z_at), from_above.at[z_at], down_send.at[z_at], down_recv.at[z_at], below)

    for z_at in Z_ORDER:
        blocks(z_at)

        @pl.when(z_at > z)
        def _(z_at=z_at):
            @pl.when(z > 0)
            def _():
                up(z_at).wait_recv()
                add_blocks(totals(z_at), [from_below.at[z_at]], rows)

            up(z_at).start()

        @pl.when(z_at < z)
        def _(z_at=z_at):
            @pl.when(z < 3)
            def _():
                down(z_at).wait_recv()
                add_blocks(totals(z_at), [from_above.at[z_at]], rows)

            down(z_at).start()

    for z_at in range(4):

        @pl.when(z_at == z)
        def _(z_at=z_at):
            @pl.when(z > 0)
            def _():
                up(z_at).wait_recv()

            @pl.when(z < 3)
            def _():
                down(z_at).wait_recv()

            @pl.when(z == 0)
            def _():
                final(z_at, [from_above.at[z_at]])

            @pl.when(z == 3)
            def _():
                final(z_at, [from_below.at[z_at]])

            @pl.when((z > 0) & (z < 3))
            def _():
                final(z_at, [from_below.at[z_at], from_above.at[z_at]])

    for z_at in range(4):

        @pl.when(z_at > z)
        def _(z_at=z_at):
            up(z_at).wait_send()

        @pl.when(z_at < z)
        def _(z_at=z_at):
            down(z_at).wait_send()


def scatter_all_kernel(
    p_ref,
    o_ref,
    mine,
    from_sib,
    from_b,
    from_a,
    from_below,
    from_above,
    own_sem,
    s_send,
    s_recv,
    b_send,
    b_recv,
    a_send,
    a_recv,
    up_send,
    up_recv,
    down_send,
    down_recv,
):
    ep, tp, z, y, x, core = place()
    rows, cols = o_ref.shape
    peer_a, peer_b, sibling, above, below = lane_peers()
    greet([peer_a, peer_b, sibling], True)

    def part(z_at, da, db, core_at):
        group, quarter = lane_spot(z_at, da, db, core_at)
        return p_ref.at[
            pl.ds(pl.multiple_of(group * rows, rows), rows),
            pl.ds(pl.multiple_of(quarter * cols, cols), cols),
        ]

    def at(z_at, da, db):
        return z_at * 4 + da * 2 + db

    def own(z_at, da, db):
        n = at(z_at, da, db)
        return pltpu.make_async_copy(part(z_at, da, db, core), mine.at[n], own_sem.at[n])

    def to_sibling(z_at, da, db):
        n = at(z_at, da, db)
        return remote(
            part(z_at, da, db, 1 - core), from_sib.at[n], s_send.at[n], s_recv.at[n], sibling
        )

    for da, db in ((1, 1), (0, 1), (1, 0), (0, 0)):
        for z_at in Z_ORDER:
            to_sibling(z_at, da, db).start()
            own(z_at, da, db).start()

    def here(z_at, da, db):
        own(z_at, da, db).wait()
        to_sibling(z_at, da, db).wait_recv()
        return mine.at[at(z_at, da, db)], from_sib.at[at(z_at, da, db)]

    def over_b(z_at, da):
        n = z_at * 2 + da
        return remote(mine.at[at(z_at, da, 1)], from_b.at[n], b_send.at[n], b_recv.at[n], peer_b)

    def over_a(z_at):
        return remote(mine.at[at(z_at, 1, 0)], from_a.at[z_at], a_send.at[z_at], a_recv.at[z_at], peer_a)

    for da in (1, 0):
        for z_at in Z_ORDER:
            own_part, sib_part = here(z_at, da, 1)
            add_blocks(own_part, [sib_part], rows)
            over_b(z_at, da).start()
    for z_at in Z_ORDER:
        own_part, sib_part = here(z_at, 1, 0)
        over_b(z_at, 1).wait_recv()
        add_blocks(own_part, [sib_part, from_b.at[z_at * 2 + 1]], rows)
        over_a(z_at).start()

    def blocks(z_at):
        own_part, sib_part = here(z_at, 0, 0)
        over_b(z_at, 0).wait_recv()
        over_a(z_at).wait_recv()
        add_blocks(own_part, [sib_part, from_b.at[z_at * 2], from_a.at[z_at]], rows)

    def final(z_at, others):
        o_ref[...] = jnp.zeros_like(o_ref)
        add_blocks(o_ref, [mine.at[at(z_at, 0, 0)], *others], rows)

    z_chain(
        blocks,
        lambda z_at: mine.at[at(z_at, 0, 0)],
        from_below,
        from_above,
        up_send,
        up_recv,
        down_send,
        down_recv,
        rows,
        final,
    )
    for z_at in range(4):
        over_a(z_at).wait_send()
        for da in range(2):
            over_b(z_at, da).wait_send()
            for db in range(2):
                to_sibling(z_at, da, db).wait_send()


def scatter_all(value, cid):
    rows, cols = value.shape[0] // 8, value.shape[1] // 4
    dma = pltpu.SemaphoreType.DMA

    def held(count):
        return pltpu.VMEM((count, rows, cols), value.dtype)

    return pl.pallas_call(
        scatter_all_kernel,
        out_shape=jax.ShapeDtypeStruct((rows, cols), jnp.float32),
        in_specs=[pl.BlockSpec(memory_space=pl.ANY)],
        out_specs=pl.BlockSpec(memory_space=pltpu.VMEM),
        scratch_shapes=[held(16), held(16), held(8), held(4), held(4), held(4)]
        + [dma((16,)), dma((16,)), dma((16,)), dma((8,)), dma((8,))]
        + [dma((4,))] * 6,
        compiler_params=pltpu.CompilerParams(
            collective_id=cid, has_side_effects=True, vmem_limit_bytes=48 * 2**20
        ),
        name="scatter_all",
    )(value)


def scatter_ep_kernel(
    p_ref, e_ref, o_ref, mine, from_y, from_below, from_above, own_sem, y_send, y_recv, up_send, up_recv, down_send, down_recv
):
    ep, tp, z, y, _, _ = place()
    rows, extra = p_ref.shape[0] // 8, e_ref.shape[0]
    tall = rows + extra
    across = (ep + 1 - 2 * y, tp)
    greet([across], True)

    def part(z_at, y_at):
        return p_ref.at[pl.ds(pl.multiple_of((z_at * 2 + y_at) * rows, rows), rows), :]

    def own(z_at):
        return (
            pltpu.make_async_copy(part(z_at, y), mine.at[z_at, pl.ds(0, rows)], own_sem.at[z_at]),
            pltpu.make_async_copy(e_ref, mine.at[z_at, pl.ds(rows, extra)], own_sem.at[4 + z_at]),
        )

    def over_y(z_at):
        return (
            remote(
                part(z_at, 1 - y),
                from_y.at[z_at, pl.ds(0, rows)],
                y_send.at[z_at],
                y_recv.at[z_at],
                across,
            ),
            remote(
                e_ref,
                from_y.at[z_at, pl.ds(rows, extra)],
                y_send.at[4 + z_at],
                y_recv.at[4 + z_at],
                across,
            ),
        )

    for z_at in Z_ORDER:
        for copy in over_y(z_at) + own(z_at):
            copy.start()

    def blocks(z_at):
        for copy in own(z_at):
            copy.wait()
        for copy in over_y(z_at):
            copy.wait_recv()
        add_blocks(mine.at[z_at], [from_y.at[z_at]], tall)

    def final(z_at, others):
        o_ref[...] = jnp.zeros_like(o_ref)
        add_blocks(o_ref, [mine.at[z_at], *others], tall)

    z_chain(
        blocks,
        lambda z_at: mine.at[z_at],
        from_below,
        from_above,
        up_send,
        up_recv,
        down_send,
        down_recv,
        tall,
        final,
    )
    for z_at in range(4):
        for copy in over_y(z_at):
            copy.wait_send()


def scatter_ep(value, extra, cid):
    rows, cols = value.shape[0] // 8, value.shape[1]
    tall = rows + extra.shape[0]
    dma = pltpu.SemaphoreType.DMA

    def held():
        return pltpu.VMEM((4, tall, cols), value.dtype)

    return pl.pallas_call(
        scatter_ep_kernel,
        out_shape=jax.ShapeDtypeStruct((tall, cols), jnp.float32),
        in_specs=[pl.BlockSpec(memory_space=pl.ANY)] * 2,
        out_specs=pl.BlockSpec(memory_space=pltpu.VMEM),
        scratch_shapes=[held(), held(), held(), held()] + [dma((8,))] * 3 + [dma((4,))] * 4,
        compiler_params=pltpu.CompilerParams(
            collective_id=cid, has_side_effects=True, vmem_limit_bytes=40 * 2**20
        ),
        name="scatter_ep",
    )(value, extra)


def experts_kernel(
    expert_width,
    shared_width,
    expert_total,
    x_ref,
    g_ref,
    kept_ref,
    expert_gate_ref,
    shared_gate_ref,
    extra_ref,
    expert_up_ref,
    shared_up_ref,
    expert_down_ref,
    shared_down_ref,
    grad_ref,
    ffn_ref,
    logit_ref,
    expert_grads_ref,
    shared_grads_ref,
    all_ref,
    from_sib,
    from_b,
    from_a,
    from_below,
    from_above,
    in_ref,
    down_ref,
    scalars,
    kept_held,
    x_held,
    g_held,
    lin,
    hidden_grad,
    hidden_all,
    both_all,
    kept_cols,
    staged,
    mine,
    landed,
    x_tile,
    g_tile,
    tile_out,
    shared_out,
    up_sem,
    down_sem,
    a_sem,
    b_sem,
    s_sem,
    recv_sem,
    sib_sem,
    own_sem,
    load_sem,
    fetch_sem,
    store_sem,
    weight_sem,
    kept_send,
    kept_recv,
    rs_send,
    rs_recv,
    rb_send,
    rb_recv,
    ra_send,
    ra_recv,
    ru_send,
    ru_recv,
    rd_send,
    rd_recv,
):
    ep, tp, z, y, x, core = place()
    rows, cols = x_ref.shape
    width = down_ref.shape[0]
    filled = expert_width + shared_width
    tall = mine.shape[1]
    out_at = rows + 16
    cuts = ((0, out_at), (out_at, tall - out_at))
    peer_a, peer_b, sibling, above, below = lane_peers()
    sources = kept_held.shape[0]
    others = [(lax.rem(ep + i, sources), tp) for i in range(1, sources)]
    greet([(ep, tp + 2 - 4 * x), sibling] + others)

    def spot(z_at, da, db):
        group, quarter = lane_spot(z_at, da, db, core)
        return all_ref.at[
            pl.ds(pl.multiple_of(group * rows, rows), rows),
            pl.ds(pl.multiple_of(quarter * cols, cols), cols),
        ]

    def at(z_at, da, db):
        return z_at * 4 + da * 2 + db

    def choose(*values):
        return jnp.where(
            z == 0, values[0], jnp.where(z == 1, values[1], jnp.where(z == 2, values[2], values[3]))
        )

    coming = (z, choose(1, 0, 3, 2), choose(2, 2, 1, 1), choose(3, 3, 0, 0))
    turns = (z, choose(1, 0, 3, 2), choose(3, 3, 0, 0), choose(2, 2, 1, 1))

    def arrived(z_at, da, db):
        block, n = spot(z_at, da, db), at(z_at, da, db)
        remote(block, block, s_sem.at[n], recv_sem.at[n], sibling).wait_recv()
        return block

    def up(z_at, source):
        return remote(source, spot(z_at, 0, 0), up_sem.at[z_at], recv_sem.at[at(z_at, 0, 0)], above)

    def down(z_at, source):
        return remote(source, spot(z_at, 0, 0), down_sem.at[z_at], recv_sem.at[at(z_at, 0, 0)], below)

    def over_a(z_at, source):
        return remote(source, spot(z_at, 0, 0), a_sem.at[z_at], recv_sem.at[at(z_at, 1, 0)], peer_a)

    def over_b(z_at, da, source):
        return remote(
            source, spot(z_at, da, 0), b_sem.at[z_at * 2 + da], recv_sem.at[at(z_at, da, 1)], peer_b
        )

    def to_sibling(z_at, da, db, source):
        n = at(z_at, da, db)
        return remote(source, spot(z_at, da, db), s_sem.at[n], sib_sem.at[n], sibling)

    def pass_z(z_at):
        block = arrived(z_at, 0, 0)

        @pl.when((z_at > z) & (z > 0))
        def _():
            down(z_at, block).start()

        @pl.when((z_at < z) & (z < 3))
        def _():
            up(z_at, block).start()

        over_a(z_at, block).start()
        over_b(z_at, 0, block).start()
        to_sibling(z_at, 0, 0, block).start()

    def pass_a(z_at, onward=True):
        block = arrived(z_at, 1, 0)
        if onward:
            over_b(z_at, 1, block).start()
        to_sibling(z_at, 1, 0, block).start()

    def pass_b(z_at, da):
        block = arrived(z_at, da, 1)
        to_sibling(z_at, da, 1, block).start()

    def sibling_blocks(k, dy):
        for dx in range(2):
            da, db = core * dy + (1 - core) * dx, core * dx + (1 - core) * dy
            n = at(turns[k], da, db)
            block = spot(0, 0, 0)
            remote(block, block, s_sem.at[n], sib_sem.at[n], sibling).wait_recv()

    def group_rows(k, dy):
        group = turns[k] * 2 + y + (1 - 2 * y) * dy
        return group, pl.ds(pl.multiple_of(group * rows, rows), rows)

    def load_x(k, dy):
        _, span = group_rows(k, dy)
        return pltpu.make_async_copy(all_ref.at[span, :], x_held, load_sem.at[0])

    def load_g(k, dy):
        _, span = group_rows(k, dy)
        return pltpu.make_async_copy(g_ref.at[span, :], g_held, load_sem.at[1])

    def project():
        def body(i, carry):
            cut = pl.ds(pl.multiple_of(i * width, width), width)
            lin[:, cut] = times_transpose(x_held[...], in_ref[cut, :])
            return carry

        lax.fori_loop(0, 2, body, 0)

    def project_grad():
        hidden_grad[...] = times_transpose(g_held[...], down_ref[...])

    step = 64
    tile_start = width - 128
    logit_at = filled - tile_start

    def activate(k, dy):
        group, _ = group_rows(k, dy)
        lane = lax.broadcasted_iota(jnp.int32, (1, width), 1)
        near = lax.broadcasted_iota(jnp.int32, (1, 128), 1)
        is_logit = (near >= logit_at) & (near < logit_at + expert_total)
        kept_cols[:, :16] = kept_held[group].astype(jnp.float32).T

        def body(i, carry):
            span = pl.ds(pl.multiple_of(i * step, step), step)
            whole = pl.ds(pl.multiple_of(group * rows + i * step, step), step)
            gate_lin, up_lin = lin[span, :width], lin[span, width:]
            grad = hidden_grad[span, :]
            tail = lin[span, tile_start:width]
            if k == 0 and dy == 0:
                logit_ref[span, :] = tail
            most = jnp.max(jnp.where(is_logit, tail, -1e30), axis=1, keepdims=True)
            powers = jnp.where(is_logit, jnp.exp(jnp.minimum(tail - most, 0.0)), 0.0)
            kept = jnp.sum(jnp.where(near == ep, kept_cols[span, :], 0.0), axis=1, keepdims=True)
            gate = jnp.sum(jnp.where(near == logit_at + ep, powers, 0.0), axis=1, keepdims=True)
            gate = gate / jnp.sum(powers, axis=1, keepdims=True) * kept
            switch = jax.nn.sigmoid(
                jnp.sum(
                    jnp.where(near == logit_at + expert_total, tail, 0.0), axis=1, keepdims=True
                )
            )
            scale = jnp.where(lane < expert_width, gate, switch)
            sig = jax.nn.sigmoid(gate_lin)
            act = gate_lin * sig
            hidden = act * up_lin
            agreement = hidden * grad
            gate_part = jnp.sum(jnp.where(lane < expert_width, agreement, 0.0), axis=1, keepdims=True)
            switch_part = jnp.sum(
                jnp.where(lane < expert_width, 0.0, agreement), axis=1, keepdims=True
            )
            scaled = grad * scale
            hidden_all[whole, :] = (hidden * scale).astype(jnp.bfloat16)
            both_all[whole, :width] = (
                scaled * up_lin * sig * (1.0 + gate_lin * (1.0 - sig))
            ).astype(jnp.bfloat16)
            both_all[whole, width:] = (scaled * act).astype(jnp.bfloat16)
            scalars[span, :] = jnp.where(
                near == ep, gate_part, jnp.where(near == expert_total, switch_part, 0.0)
            )
            return carry

        lax.fori_loop(0, rows // step, body, 0)

    def hold(k, da, db):
        slot = 2 if k == 0 else k % 2
        return db * (7 + slot * 2 + da) + (1 - db) * (da * (4 + slot) + (1 - da) * k)

    def lane_offsets(dx, dy, core_at):
        return (1 - core_at) * dy + core_at * dx, (1 - core_at) * dx + core_at * dy

    def rs_sibling(k, dx, dy):
        n = at(turns[k], *lane_offsets(dx, dy, 1 - core))
        return remote(staged.at[dx], from_sib.at[n], rs_send.at[n], rs_recv.at[n], sibling)

    def block_rows(k, dy):
        sums = scalars[...].T[:16, :].astype(jnp.bfloat16)
        _, span = group_rows(k, dy)

        def fill(target, cut):
            target[:rows, :] = jnp.dot(
                both_all[span, :], in_ref[:, cut], preferred_element_type=jnp.float32
            ).astype(jnp.bfloat16)
            target[rows:out_at, :] = sums
            target[out_at:, :] = jnp.dot(
                hidden_all[span, :], down_ref[:, cut], preferred_element_type=jnp.float32
            ).astype(jnp.bfloat16)

        def body(dx, carry):
            x_at = x + (1 - 2 * x) * dx
            fill(staged.at[dx], pl.ds(pl.multiple_of((x_at * 2 + 1 - core) * cols, cols), cols))
            rs_sibling(k, dx, dy).start()
            fill(
                mine.at[hold(k, *lane_offsets(dx, dy, core))],
                pl.ds(pl.multiple_of((x_at * 2 + core) * cols, cols), cols),
            )
            return carry

        lax.fori_loop(0, 2, body, 0)

    def staged_free(k, dy):
        for dx in range(2):
            rs_sibling(k, dx, dy).wait_send()

    def rs_over_b(k, da, part):
        n, span = turns[k] * 2 + da, pl.ds(*cuts[part])
        return remote(
            mine.at[hold(k, da, 1), span],
            from_b.at[n, span],
            rb_send.at[n * 2 + part],
            rb_recv.at[n * 2 + part],
            peer_b,
        )

    def rs_over_a(k, part):
        z_at, span = turns[k], pl.ds(*cuts[part])
        return remote(
            mine.at[hold(k, 1, 0), span],
            from_a.at[z_at, span],
            ra_send.at[z_at * 2 + part],
            ra_recv.at[z_at * 2 + part],
            peer_a,
        )

    def rs_up(k, z_at, half):
        first, count = cuts[half]
        n = z_at * 2 + half
        span = pl.ds(first, count)
        return remote(
            mine.at[k, span], from_below.at[z_at, span], ru_send.at[n], ru_recv.at[n], above
        )

    def rs_down(k, z_at, half):
        first, count = cuts[half]
        n = z_at * 2 + half
        span = pl.ds(first, count)
        return remote(
            mine.at[k, span], from_above.at[z_at, span], rd_send.at[n], rd_recv.at[n], below
        )

    def fetch(source, i):
        return pltpu.make_async_copy(source, landed.at[i], fetch_sem.at[i])

    def fetch_part(source, half, i):
        span = pl.ds(*cuts[half])
        return pltpu.make_async_copy(source.at[span], landed.at[i, span], fetch_sem.at[i])

    def fetch_sibling(k, dy):
        for dx in range(2):
            n = at(turns[k], *lane_offsets(dx, dy, core))
            remote(staged.at[0], from_sib.at[n], rs_send.at[n], rs_recv.at[n], sibling).wait_recv()
            fetch(from_sib.at[n], dx).start()

    def reduce_sibling(k, dy):
        for dx in range(2):
            n = at(turns[k], *lane_offsets(dx, dy, core))
            fetch(from_sib.at[n], dx).wait()
            add_blocks(mine.at[hold(k, *lane_offsets(dx, dy, core))], [landed.at[dx]], tall)

        for part in range(2):

            @pl.when(core == 0)
            def _(part=part):
                rs_over_b(k, dy, part).start()

            if dy == 1:

                @pl.when(core == 1)
                def _(part=part):
                    rs_over_b(k, 0, part).start()
                    rs_over_b(k, 1, part).start()

    def add_part(target, part, copies):
        first, count = cuts[part]
        span = pl.ds(first, count)
        for copy in copies:
            copy.wait()
        add_blocks(
            mine.at[target, span], [landed.at[i, span] for i in range(len(copies))], count
        )

    def reduce_b(k, part):
        rs_over_b(k, 1, part).wait_recv()
        copy = fetch_part(from_b.at[turns[k] * 2 + 1], part, 0)
        copy.start()
        add_part(hold(k, 1, 0), part, [copy])
        rs_over_a(k, part).start()

    def reduce_a(k, part):
        z_at = turns[k]
        rs_over_b(k, 0, part).wait_recv()
        rs_over_a(k, part).wait_recv()
        copies = [
            fetch_part(from_b.at[z_at * 2], part, 0),
            fetch_part(from_a.at[z_at], part, 1),
        ]
        for copy in copies:
            copy.start()
        add_part(k, part, copies)
        if k > 0:

            @pl.when(z == 0)
            def _():
                rs_up(k, z_at, part).start()

            @pl.when(z == 3)
            def _():
                rs_down(k, z_at, part).start()

    def chain(k, part):
        z_at = turns[k]

        @pl.when((z > 0) & (z < 3) & (z_at > z))
        def _():
            rs_up(k, z_at, part).wait_recv()
            copy = fetch_part(from_below.at[z_at], part, 0)
            copy.start()
            add_part(k, part, [copy])
            rs_up(k, z_at, part).start()

        @pl.when((z > 0) & (z < 3) & (z_at < z))
        def _():
            rs_down(k, z_at, part).wait_recv()
            copy = fetch_part(from_above.at[z_at], part, 0)
            copy.start()
            add_part(k, part, [copy])
            rs_down(k, z_at, part).start()

    tile = x_tile.shape[1]

    def load_tile(source, target, t, sem):
        cut = pl.ds(pl.multiple_of(t * tile, tile), tile)
        return pltpu.make_async_copy(source.at[:, cut], target, load_sem.at[sem])

    def tile_stores(t, kind):
        cut = pl.ds(pl.multiple_of(t * tile, tile), tile)
        return (
            pltpu.make_async_copy(
                tile_out.at[kind, pl.ds(0, expert_width)],
                expert_grads_ref.at[kind, :, cut],
                store_sem.at[kind],
            ),
            pltpu.make_async_copy(
                shared_out.at[kind], shared_grads_ref.at[t, kind], store_sem.at[3 + kind]
            ),
        )

    def weight_tile(t, kind):
        @pl.when(t > 0)
        def _():
            for copy in tile_stores(t - 1, kind):
                copy.wait()

        if kind == 0:
            left, right = hidden_all[:, :filled], g_tile[...]
        else:
            left, right = both_all[:, (kind - 1) * width : (kind - 1) * width + filled], x_tile[...]
        result = inner_rows(left, right)
        tile_out[kind] = result
        shared_out[kind] = result[expert_width:, :].astype(jnp.bfloat16)
        for copy in tile_stores(t, kind):
            copy.start()

    own = pltpu.make_async_copy(x_ref, spot(z, 0, 0), own_sem)
    over_b(z, 0, x_ref).start()
    over_a(z, x_ref).start()

    @pl.when(z < 3)
    def _():
        up(z, x_ref).start()

    @pl.when(z > 0)
    def _():
        down(z, x_ref).start()

    to_sibling(z, 0, 0, x_ref).start()
    own.start()
    load_g(0, 0).start()

    def kept_to(i):
        return remote(
            kept_ref, kept_held.at[ep], kept_send.at[i - 1], kept_recv.at[i - 1], others[i - 1]
        )

    for i in range(1, sources):
        kept_to(i).start()
    own_kept = pltpu.make_async_copy(kept_ref, kept_held.at[ep], weight_sem.at[7])
    own_kept.start()
    pieces = [
        (expert_down_ref, down_ref, 0),
        (
            shared_down_ref.at[pl.ds(pl.multiple_of(ep * shared_width, 16), shared_width), :],
            down_ref,
            expert_width,
        ),
        (expert_gate_ref, in_ref, 0),
        (shared_gate_ref, in_ref, expert_width),
        (extra_ref, in_ref, filled),
        (expert_up_ref, in_ref, width),
        (shared_up_ref, in_ref, width + expert_width),
    ]
    weight_copies = [
        pltpu.make_async_copy(piece, target.at[pl.ds(at_row, piece.shape[0]), :], weight_sem.at[i])
        for i, (piece, target, at_row) in enumerate(pieces)
    ]
    for copy in weight_copies:
        copy.start()
    for target, first, last_row in (
        (in_ref, filled + 16, width),
        (in_ref, width + filled, 2 * width),
        (down_ref, filled, width),
    ):
        target[first:last_row, :] = jnp.zeros((last_row - first, target.shape[1]), target.dtype)
    for copy in weight_copies:
        copy.wait()
    load_g(0, 0).wait()
    project_grad()
    own_kept.wait()
    for i in range(1, sources):
        kept_to(i).wait_recv()
    own.wait()

    def ready(k, dy):
        if k > 0:
            pass_b(turns[k], dy)
        sibling_blocks(k, dy)
        load_x(k, dy).start()

    order = [(0, 0)] + [(k, dy) for k in range(1, 4) for dy in range(2)] + [(0, 1)]
    edge = (z == 0) | (z == 3)
    pass_z(coming[1])
    pass_a(z, False)
    pass_b(z, 0)

    @pl.when(jnp.logical_not(edge))
    def _():
        pass_z(coming[2])

    ready(0, 0)
    for s, (k, dy) in enumerate(order):
        following = order[s + 1] if s < 7 else None
        load_x(k, dy).wait()
        if s >= 1:
            fetch_sibling(*order[s - 1])
        project()
        if s >= 1:
            load_g(k, dy).wait()
            project_grad()
        if following is not None:
            load_g(*following).start()
        if s >= 1:
            reduce_sibling(*order[s - 1])
        if s == 1:
            pass_z(coming[3])
            over_b(z, 1, spot(z, 1, 0)).start()
        if s in (4, 6):
            reduce_b(s // 2 - 1, 0)
        activate(k, dy)
        if s == 0:

            @pl.when(edge)
            def _():
                pass_z(coming[2])

            pass_a(coming[1])
        if s == 1:
            pass_a(coming[2])
        if s == 2:
            pass_a(coming[3])
        if s == 4:
            pass_b(z, 1)
        if following is not None:
            ready(*following)
        if s in (4, 6):
            reduce_b(s // 2 - 1, 1)
        if s in (5, 7):
            reduce_a((s - 3) // 2, 0)
        if s >= 1:
            staged_free(*order[s - 1])
        if s == 5:
            for part in range(2):
                for da in range(2):
                    rs_over_b(1, da, part).wait_send()
                rs_over_a(1, part).wait_send()
        block_rows(k, dy)
        if s in (5, 7):
            reduce_a((s - 3) // 2, 1)

    load_tile(g_ref, g_tile, 0, 2).start()
    load_tile(all_ref, x_tile, 0, 3).start()
    tiles = shared_grads_ref.shape[0]
    services = {
        (0, 0): lambda: fetch_sibling(0, 1),
        (0, 1): lambda: reduce_sibling(0, 1),
        (0, 2): lambda: chain(2, 0),
        (1, 0): lambda: reduce_b(3, 0),
        (1, 1): lambda: chain(2, 1),
        (2, 0): lambda: chain(1, 0),
        (2, 2): lambda: chain(1, 1),
        (4, 0): lambda: reduce_b(3, 1),
        (4, 2): lambda: reduce_a(3, 0),
        (5, 1): lambda: reduce_b(0, 0),
        (6, 0): lambda: chain(3, 0),
        (6, 2): lambda: reduce_a(3, 1),
        (7, 0): lambda: reduce_b(0, 1),
        (7, 2): lambda: chain(3, 1),
    }

    def tile_step(t, carry):
        for kind in range(3):
            if kind == 0:
                load_tile(g_ref, g_tile, t, 2).wait()
            if kind == 1:
                load_tile(all_ref, x_tile, t, 3).wait()
            weight_tile(t, kind)

            @pl.when(t + 1 < tiles)
            def _(kind=kind):
                if kind == 0:
                    load_tile(g_ref, g_tile, t + 1, 2).start()
                if kind == 2:
                    load_tile(all_ref, x_tile, t + 1, 3).start()

            for (at_tile, at_kind), service in services.items():
                if at_kind == kind:
                    pl.when(t == at_tile)(service)
        return carry

    lax.fori_loop(0, tiles, tile_step, 0)
    for kind in range(3):
        for copy in tile_stores(tiles - 1, kind):
            copy.wait()

    reduce_a(0, 0)
    reduce_a(0, 1)

    for half in range(2):

        @pl.when(z > 0)
        def _(half=half):
            rs_up(0, z, half).wait_recv()
            fetch_part(from_below.at[z], half, 0).start()
            fetch_part(from_below.at[z], half, 0).wait()

        @pl.when(z < 3)
        def _(half=half):
            rs_down(0, z, half).wait_recv()
            fetch_part(from_above.at[z], half, 1).start()
            fetch_part(from_above.at[z], half, 1).wait()

    def total(parts):
        def body(i, carry):
            for target, first in ((grad_ref, 0), (ffn_ref, out_at)):
                span = pl.ds(pl.multiple_of(i * 16, 16), 16)
                source = pl.ds(pl.multiple_of(first + i * 16, 16), 16)
                value = mine[0, source, :].astype(jnp.float32)
                for part in parts:
                    value = value + landed[part, source, :].astype(jnp.float32)
                target[span, :] = value
            return carry

        lax.fori_loop(0, rows // 16, body, 0)
        value = mine[0, rows:out_at, :].astype(jnp.float32)
        for part in parts:
            value = value + landed[part, rows:out_at, :].astype(jnp.float32)
        grad_ref[rows:, :] = value

    @pl.when(z == 0)
    def _():
        total([1])

    @pl.when(z == 3)
    def _():
        total([0])

    @pl.when((z > 0) & (z < 3))
    def _():
        total([0, 1])

    for i in range(1, sources):
        kept_to(i).wait_send()
    staged_free(0, 1)
    for k in (0, 2, 3):
        for part in range(2):
            rs_over_a(k, part).wait_send()
            for da in range(2):
                rs_over_b(k, da, part).wait_send()

    def finish(i, carry):
        over_a(i, x_ref).wait_send()
        over_b(i, 0, x_ref).wait_send()
        over_b(i, 1, x_ref).wait_send()
        for n in range(4):
            block = spot(0, 0, 0)
            remote(block, block, s_sem.at[i * 4 + n], sib_sem.at[i * 4 + n], sibling).wait_send()

        @pl.when((z < 3) & (i <= z))
        def _():
            up(i, x_ref).wait_send()

        @pl.when((z > 0) & (i >= z))
        def _():
            down(i, x_ref).wait_send()

        for half in range(2):

            @pl.when(i > z)
            def _(half=half):
                rs_up(0, i, half).wait_send()

            @pl.when(i < z)
            def _(half=half):
                rs_down(0, i, half).wait_send()

        return carry

    lax.fori_loop(0, 4, finish, 0)


def experts(x_cols, grads_all, kept_rows, weights, expert_total, cid):
    rows, cols = x_cols.shape
    total, model_dim = grads_all.shape
    sources = total // rows
    expert_width, shared_width = weights[0].shape[0], weights[1].shape[0]
    filled = expert_width + shared_width
    width = -(-(filled + expert_total + 1) // 128) * 128
    tall = 2 * rows + 16
    tile = model_dim // sources
    low, dma = jnp.bfloat16, pltpu.SemaphoreType.DMA
    vmem, hbm = pl.BlockSpec(memory_space=pltpu.VMEM), pl.BlockSpec(memory_space=pl.ANY)

    def landing(count):
        return jax.ShapeDtypeStruct((count, tall, cols), low)

    return pl.pallas_call(
        functools.partial(experts_kernel, expert_width, shared_width, expert_total),
        out_shape=[
            jax.ShapeDtypeStruct((rows + 16, cols), jnp.float32),
            jax.ShapeDtypeStruct((rows, cols), jnp.float32),
            jax.ShapeDtypeStruct((rows, 128), jnp.float32),
            jax.ShapeDtypeStruct((3, expert_width, model_dim), jnp.float32),
            jax.ShapeDtypeStruct((sources, 3, shared_width, tile), low),
            jax.ShapeDtypeStruct((total, model_dim), low),
            landing(16),
            landing(8),
            landing(4),
            landing(4),
            landing(4),
        ],
        in_specs=[hbm] * 10,
        out_specs=[vmem, vmem, vmem] + [hbm] * 8,
        scratch_shapes=[
            pltpu.VMEM((2 * width, model_dim), low),
            pltpu.VMEM((width, model_dim), low),
            pltpu.VMEM((rows, 128), jnp.float32),
            pltpu.VMEM((sources, 16, rows), low),
            pltpu.VMEM((rows, model_dim), low),
            pltpu.VMEM((rows, model_dim), low),
            pltpu.VMEM((rows, 2 * width), jnp.float32),
            pltpu.VMEM((rows, width), jnp.float32),
            pltpu.VMEM((total, width), low),
            pltpu.VMEM((total, 2 * width), low),
            pltpu.VMEM((rows, 128), jnp.float32),
            pltpu.VMEM((2, tall, cols), low),
            pltpu.VMEM((13, tall, cols), low),
            pltpu.VMEM((2, tall, cols), low),
            pltpu.VMEM((total, tile), low),
            pltpu.VMEM((total, tile), low),
            pltpu.VMEM((3, filled, tile), jnp.float32),
            pltpu.VMEM((3, shared_width, tile), low),
        ]
        + [dma((4,)), dma((4,)), dma((4,)), dma((8,)), dma((16,)), dma((16,)), dma((16,)), dma]
        + [dma((4,)), dma((2,)), dma((6,)), dma((8,)), dma((7,)), dma((7,))]
        + [dma((16,))] * 4
        + [dma((8,))] * 6,
        compiler_params=pltpu.CompilerParams(
            collective_id=cid, has_side_effects=True, vmem_limit_bytes=63 * 2**20
        ),
        name="experts",
    )(x_cols, grads_all, kept_rows, *weights)


def row_of(columns):
    part = columns[:, :128]
    for i in range(1, columns.shape[1] // 128):
        part = part + columns[:, i * 128 : (i + 1) * 128]
    total = jnp.sum(part.T, axis=0, keepdims=True)
    return jnp.broadcast_to(total, (8, total.shape[1]))


def unwind_kernel(
    dn2_ref,
    unit_ref,
    inv_ref,
    second_ref,
    grad_ref,
    tokens_ref,
    inv_one_ref,
    first_ref,
    small_ref,
    q_ref,
    k_ref,
    v_ref,
    ke_ref,
    ve_ref,
    context_ref,
    log_ref,
    cos_ref,
    sin_ref,
    n1_hbm,
    wq_hbm,
    wk_hbm,
    wv_hbm,
    wo_hbm,
    tokens_grad_ref,
    weight_grads_ref,
    sums_ref,
    n1,
    wq,
    wk,
    wv,
    wo,
    grad_all,
    grad_own,
    hidden_grad,
    dc,
    dq,
    dk,
    dv,
    lin_grads,
    dke,
    dve,
    later_k,
    later_v,
    staged,
    mine,
    from_y,
    from_below,
    from_above,
    tp_staged,
    tp_mine,
    tp_sib,
    tp_x,
    dn1,
    row_mine,
    row_sib,
    row_x,
    smalls,
    load_sem,
    g_send,
    g_recv,
    row_send,
    row_recv,
    kv_send,
    kv_recv,
    y_send,
    y_recv,
    up_send,
    up_recv,
    down_send,
    down_recv,
    tp_send,
    tp_recv,
    small_send,
    small_recv,
):
    ep, tp, z, y, x, core = place()
    rows, cols = unit_ref.shape
    model_dim = n1.shape[1]
    heads = cols // HD
    block = mine.shape[1]
    low, full = jnp.bfloat16, jnp.float32
    score_scale = HD ** (-0.5)
    sibling, across = (ep, tp + 1 - 2 * core), (ep, tp + 2 - 4 * x)
    beside = (ep + 1 - 2 * y, tp)
    above, below = (ep + 2, tp), (ep - 2, tp)
    sources = smalls.shape[0]
    others = [(lax.rem(ep + i, sources), tp) for i in range(1, sources)]
    loads = [
        pltpu.make_async_copy(source, target, load_sem.at[i])
        for i, (source, target) in enumerate(
            ((wo_hbm, wo), (n1_hbm, n1), (wq_hbm, wq), (wk_hbm, wk), (wv_hbm, wv))
        )
    ]
    for copy in loads:
        copy.start()
    greet([across, sibling] + others)

    step = 64

    def by_rows(body):
        def one(i, carry):
            body(pl.ds(pl.multiple_of(i * step, step), step))
            return carry

        lax.fori_loop(0, rows // step, one, 0)

    def row_exchange(i, values):
        row_mine[2 * i] = values
        first = remote(
            row_mine.at[2 * i], row_sib.at[i], row_send.at[2 * i], row_recv.at[2 * i], sibling
        )
        first.start()
        first.wait_recv()
        row_mine[2 * i + 1] = row_mine[2 * i] + row_sib[i]
        second = remote(
            row_mine.at[2 * i + 1],
            row_x.at[i],
            row_send.at[2 * i + 1],
            row_recv.at[2 * i + 1],
            across,
        )
        second.start()
        second.wait_recv()
        first.wait_send()
        second.wait_send()
        return (row_mine[2 * i + 1] + row_x[i]).T[:, :1]

    dn1[...] = dn2_ref[...] * second_ref[:1, :] * unit_ref[...]
    mean = row_exchange(0, row_of(dn1[...])) * (1.0 / model_dim)
    dn1[:, :128] = jnp.broadcast_to(mean, (rows, 128))

    def norm_two(span):
        scaled = dn2_ref[span, :] * second_ref[:1, :]
        value = grad_ref[span, :].astype(full) + inv_ref[span, :1] * (
            scaled - unit_ref[span, :] * dn1[span, :1]
        )
        hidden_grad[span, :] = value
        grad_own[span, :] = value.astype(low)

    by_rows(norm_two)

    def quarter(at):
        return grad_all.at[:, pl.ds(pl.multiple_of(at * cols, cols), cols)]

    g_x = remote(grad_own, quarter(tp), g_send.at[0], g_recv.at[0], across)
    g_s = remote(grad_own, quarter(tp), g_send.at[1], g_recv.at[1], sibling)
    g_x.start()
    g_s.start()
    own_cut = pl.ds(pl.multiple_of(tp * cols, cols), cols)
    grad_all[:, own_cut] = grad_own[...]
    g_x.wait_recv()
    theirs = quarter(tp + 2 - 4 * x)
    g_f = remote(theirs, theirs, g_send.at[2], g_recv.at[2], sibling)
    g_f.start()
    g_s.wait_recv()
    g_f.wait_recv()
    loads[0].wait()
    dc[...] = times_transpose(grad_all[...], wo[...]).astype(low)

    def over_y(kind, z_at):
        n = kind * 4 + z_at
        return remote(staged.at[n], from_y.at[n], y_send.at[n], y_recv.at[n], beside)

    def weight_blocks(kind, left, right):
        def other(i, carry):
            z_at = lax.rem(i * 3, 4)
            cut = pl.ds(pl.multiple_of((z_at * 2 + 1 - y) * block, block), block)
            staged[kind * 4 + z_at] = inner_rows(left[:, cut], right[...]).astype(low)
            over_y(kind, z_at).start()
            return carry

        def ours(i, carry):
            z_at = lax.rem(i * 3, 4)
            cut = pl.ds(pl.multiple_of((z_at * 2 + y) * block, block), block)
            mine[kind * 4 + z_at] = inner_rows(left[:, cut], right[...]).astype(low)
            return carry

        lax.fori_loop(0, 4, other, 0)
        lax.fori_loop(0, 4, ours, 0)

    def up(kind, z_at):
        n = kind * 4 + z_at
        return remote(mine.at[n], from_below.at[n], up_send.at[n], up_recv.at[n], above)

    def down(kind, z_at):
        n = kind * 4 + z_at
        return remote(mine.at[n], from_above.at[n], down_send.at[n], down_recv.at[n], below)

    def y_stage(kind):
        def one(i, carry):
            z_at = lax.rem(i * 3, 4)
            n = kind * 4 + z_at
            over_y(kind, z_at).wait_recv()
            add_blocks(mine.at[n], [from_y.at[n]], block)

            @pl.when((z == 0) & (z_at > 0))
            def _():
                up(kind, z_at).start()

            @pl.when((z == 3) & (z_at < 3))
            def _():
                down(kind, z_at).start()

            return carry

        lax.fori_loop(0, 4, one, 0)

    def chain(kind):
        def rise(z_at):
            n = kind * 4 + z_at
            up(kind, z_at).wait_recv()
            add_blocks(mine.at[n], [from_below.at[n]], block)
            up(kind, z_at).start()

        def fall(z_at):
            n = kind * 4 + z_at
            down(kind, z_at).wait_recv()
            add_blocks(mine.at[n], [from_above.at[n]], block)
            down(kind, z_at).start()

        @pl.when(z == 1)
        def _():
            rise(3)
            rise(2)
            fall(0)

        @pl.when(z == 2)
        def _():
            fall(0)
            fall(1)
            rise(3)

    def final(kind):
        n = kind * 4 + z

        @pl.when(z > 0)
        def _():
            up(kind, z).wait_recv()

        @pl.when(z < 3)
        def _():
            down(kind, z).wait_recv()

        def one(i, carry):
            span = pl.ds(pl.multiple_of(i * 32, 32), 32)
            value = mine[n, span, :].astype(full)
            low_part = from_below[n, span, :].astype(full)
            high_part = from_above[n, span, :].astype(full)
            value = value + jnp.where(z > 0, low_part, 0.0) + jnp.where(z < 3, high_part, 0.0)
            weight_grads_ref[kind, span, :] = value
            return carry

        lax.fori_loop(0, block // 32, one, 0)

    weight_blocks(0, grad_all, context_ref)

    half = rows // 2

    def terms(h, qb, key_count, keys, values):
        cut = pl.ds(pl.multiple_of(h * HD, HD), HD)
        span = pl.ds(qb * half, half)
        lane = lax.broadcasted_iota(jnp.int32, (1, 128), 1)
        log_total = jnp.sum(jnp.where(lane == h, log_ref[span, :], 0.0), axis=1, keepdims=True)
        queries, grads = q_ref[span, cut], dc[span, cut]
        delta = jnp.sum(
            grads.astype(full) * context_ref[span, cut].astype(full), axis=1, keepdims=True
        )
        key_part, value_part = keys[:key_count, cut], values[:key_count, cut]
        probs = jnp.exp(times_transpose(queries, key_part) * score_scale - log_total)
        scores_grad = (probs * (times_transpose(grads, value_part) - delta)).astype(low)
        return (
            jnp.dot(scores_grad, key_part, preferred_element_type=full),
            inner_rows(scores_grad, queries),
            inner_rows(probs.astype(low), grads),
        )

    def spans(h, qb):
        return pl.ds(qb * half, half), pl.ds(pl.multiple_of(h * HD, HD), HD)

    later = (
        remote(dke, later_k, kv_send.at[0], kv_recv.at[0], beside),
        remote(dve, later_v, kv_send.at[1], kv_recv.at[1], beside),
    )

    @pl.when(y == 1)
    def _():
        def head(h, carry):
            cut = pl.ds(pl.multiple_of(h * HD, HD), HD)
            first = terms(h, 0, rows, ke_ref, ve_ref)
            dq[spans(h, 0)[0], cut] = first[0]
            dk[:, cut] = first[1]
            dv[:, cut] = first[2]
            second = terms(h, 1, rows, ke_ref, ve_ref)
            dq[spans(h, 1)[0], cut] = second[0]
            dke[:, cut] = ((dk[:, cut] + second[1]) * score_scale).astype(low)
            dve[:, cut] = (dv[:, cut] + second[2]).astype(low)
            return carry

        lax.fori_loop(0, heads, head, 0)
        for copy in later:
            copy.start()

    @pl.when(y == 0)
    def _():
        dq[...] = jnp.zeros_like(dq)

    y_stage(0)

    def head(h, carry):
        cut = pl.ds(pl.multiple_of(h * HD, HD), HD)
        second = terms(h, 1, rows, k_ref, v_ref)
        dq[half:, cut] = dq[half:, cut] + second[0]
        dk[:, cut] = second[1] * score_scale
        dv[:, cut] = second[2]
        first = terms(h, 0, half, k_ref, v_ref)
        dq[:half, cut] = dq[:half, cut] + first[0]
        dk[:half, cut] = dk[:half, cut] + first[1] * score_scale
        dv[:half, cut] = dv[:half, cut] + first[2]
        return carry

    lax.fori_loop(0, heads, head, 0)

    def rotate_back(source, target, scale):
        def one(h, carry):
            cut = pl.ds(pl.multiple_of(h * HD, HD), HD)
            value = source[:, cut] * scale
            turned = value * cos_ref[...] - pltpu.roll(value, HD // 2, 1) * sin_ref[...]
            lin_grads[target, :, cut] = turned.astype(low)
            return carry

        lax.fori_loop(0, heads, one, 0)

    rotate_back(dq, 0, score_scale)
    loads[1].wait()
    weight_blocks(1, n1, lin_grads.at[0])
    chain(0)

    @pl.when(y == 0)
    def _():
        for copy in later:
            copy.wait_recv()

        def add(span):
            dk[span, :] = dk[span, :] + later_k[span, :].astype(full)
            dv[span, :] = dv[span, :] + later_v[span, :].astype(full)

        by_rows(add)

    rotate_back(dk, 1, 1.0)
    lin_grads[2] = dv[...].astype(low)
    weight_blocks(2, n1, lin_grads.at[1])
    weight_blocks(3, n1, lin_grads.at[2])
    y_stage(1)
    for copy in loads[2:]:
        copy.wait()

    def dn1_part(at, target):
        cut = pl.ds(pl.multiple_of(at * cols, cols), cols)
        total = times_transpose(lin_grads[0], wq[cut, :])
        total = total + times_transpose(lin_grads[1], wk[cut, :])
        total = total + times_transpose(lin_grads[2], wv[cut, :])
        target[...] = total.astype(low)

    def to_sibling(i):
        return remote(tp_staged.at[i], tp_sib.at[i], tp_send.at[i], tp_recv.at[i], sibling)

    def part_of(i):
        x_at = 1 - x + (2 * x - 1) * i
        dn1_part(x_at * 2 + 1 - core, tp_staged.at[i])
        to_sibling(i).start()
        dn1_part(x_at * 2 + core, tp_mine.at[i])

    out_x = remote(tp_mine.at[0], tp_x, tp_send.at[2], tp_recv.at[2], across)
    part_of(0)
    to_sibling(0).wait_recv()
    add_blocks(tp_mine.at[0], [tp_sib.at[0]], rows)
    out_x.start()
    part_of(1)
    chain(1)
    to_sibling(1).wait_recv()
    out_x.wait_recv()

    def sum_parts(span):
        dn1[span, :] = (
            tp_mine[1, span, :].astype(full)
            + tp_sib[1, span, :].astype(full)
            + tp_x[span, :].astype(full)
        )

    by_rows(sum_parts)

    def unit_one(span):
        return tokens_ref[span, :].astype(full) * inv_one_ref[span, :1]

    def products(span):
        dq[span, :] = dn1[span, :] * unit_one(span)

    by_rows(products)
    gain_grad = jnp.sum(dq[...], axis=0, keepdims=True)
    dq[...] = dq[...] * first_ref[:1, :]
    total = row_exchange(1, row_of(dq[...]))
    dk[:, :128] = jnp.broadcast_to(total * (1.0 / model_dim), (rows, 128))

    def norm_one(span):
        scaled = dn1[span, :] * first_ref[:1, :]
        value = hidden_grad[span, :] + inv_one_ref[span, :1] * (
            scaled - unit_one(span) * dk[span, :1]
        )
        tokens_grad_ref[span, :] = value.astype(low)

    by_rows(norm_one)

    own = smalls.at[ep]
    own[...] = small_ref[...]
    own[0:1, :] = gain_grad
    for i in range(3):
        own[i + 1 : i + 2, :] = jnp.sum(lin_grads[i].astype(full), axis=0, keepdims=True)

    def small_to(i):
        return remote(own, own, small_send.at[i - 1], small_recv.at[i - 1], others[i - 1])

    for i in range(1, sources):
        small_to(i).start()
    y_stage(2)
    final(0)
    chain(2)
    y_stage(3)
    final(1)
    chain(3)
    for i in range(1, sources):
        small_to(i).wait_recv()
    total = smalls[0]
    for i in range(1, sources):
        total = total + smalls[i]
    sums_ref[...] = total
    final(2)
    final(3)

    for copy in (g_x, g_s, g_f, out_x, to_sibling(0), to_sibling(1)):
        copy.wait_send()

    @pl.when(y == 1)
    def _():
        for copy in later:
            copy.wait_send()

    for i in range(1, sources):
        small_to(i).wait_send()

    def finish(n, carry):
        remote(staged.at[0], from_y.at[0], y_send.at[n], y_recv.at[n], beside).wait_send()
        z_at = lax.rem(n, 4)

        @pl.when(z_at > z)
        def _():
            remote(mine.at[0], from_below.at[0], up_send.at[n], up_recv.at[n], above).wait_send()

        @pl.when(z_at < z)
        def _():
            remote(mine.at[0], from_above.at[0], down_send.at[n], down_recv.at[n], below).wait_send()

        return carry

    lax.fori_loop(0, 16, finish, 0)


def unwind(vmem_args, hbm_args, cid):
    rows, cols = vmem_args[0].shape
    model_dim = hbm_args[0].shape[1]
    sources = 8
    block = model_dim // sources
    low, full, dma = jnp.bfloat16, jnp.float32, pltpu.SemaphoreType.DMA
    vmem, hbm = pl.BlockSpec(memory_space=pltpu.VMEM), pl.BlockSpec(memory_space=pl.ANY)

    def buffers(*shape, dtype=low):
        return pltpu.VMEM(shape, dtype)

    return pl.pallas_call(
        unwind_kernel,
        out_shape=[
            jax.ShapeDtypeStruct((rows, cols), low),
            jax.ShapeDtypeStruct((4, block, cols), full),
            jax.ShapeDtypeStruct((16, cols), full),
        ],
        in_specs=[vmem] * len(vmem_args) + [hbm] * len(hbm_args),
        out_specs=[vmem] * 3,
        scratch_shapes=[buffers(*arg.shape) for arg in hbm_args]
        + [
            buffers(rows, model_dim),
            buffers(rows, cols),
            buffers(rows, cols, dtype=full),
            buffers(rows, cols),
            buffers(rows, cols, dtype=full),
            buffers(rows, cols, dtype=full),
            buffers(rows, cols, dtype=full),
            buffers(3, rows, cols),
            buffers(rows, cols),
            buffers(rows, cols),
            buffers(rows, cols),
            buffers(rows, cols),
        ]
        + [buffers(16, block, cols)] * 5
        + [
            buffers(2, rows, cols),
            buffers(2, rows, cols),
            buffers(2, rows, cols),
            buffers(rows, cols),
            buffers(rows, cols, dtype=full),
            buffers(4, 8, rows, dtype=full),
            buffers(2, 8, rows, dtype=full),
            buffers(2, 8, rows, dtype=full),
            buffers(sources, 16, cols, dtype=full),
        ]
        + [dma((5,)), dma((3,)), dma((3,)), dma((4,)), dma((4,)), dma((2,)), dma((2,))]
        + [dma((16,))] * 6
        + [dma((3,)), dma((3,)), dma((7,)), dma((7,))],
        compiler_params=pltpu.CompilerParams(
            collective_id=cid, has_side_effects=True, vmem_limit_bytes=60 * 2**20
        ),
        name="unwind",
    )(*vmem_args, *hbm_args)


def attend_kernel(
    first_ref,
    bias_ref,
    second_ref,
    cos_ref,
    sin_ref,
    tokens_hbm,
    grad_hbm,
    wq_hbm,
    wk_hbm,
    wv_hbm,
    wo_hbm,
    hidden_ref,
    unit_ref,
    inv_ref,
    normed_ref,
    n1_ref,
    inv_one_ref,
    q_ref,
    k_ref,
    v_ref,
    ke_ref,
    ve_ref,
    context_ref,
    log_ref,
    all_ref,
    wq,
    wk,
    wv,
    wo,
    tokens,
    lin,
    total,
    most,
    weight,
    earlier_k,
    earlier_v,
    tp_staged,
    tp_mine,
    tp_sib,
    tp_x,
    row_mine,
    row_sib,
    row_x,
    load_sem,
    t_send,
    t_recv,
    kv_send,
    kv_recv,
    tp_send,
    tp_recv,
    row_send,
    row_recv,
    up_sem,
    down_sem,
    a_sem,
    b_sem,
    s_sem,
    recv_sem,
    sib_sem,
):
    ep, tp, z, y, x, core = place()
    rows, cols = hidden_ref.shape
    model_dim = n1_ref.shape[1]
    heads = cols // HD
    low, full = jnp.bfloat16, jnp.float32
    score_scale = HD ** (-0.5)
    sibling, across = (ep, tp + 1 - 2 * core), (ep, tp + 2 - 4 * x)
    beside = (ep + 1 - 2 * y, tp)
    peer_a, peer_b, _, above, below = lane_peers()

    def quarter(at):
        return tokens.at[:, pl.ds(pl.multiple_of(at * cols, cols), cols)]

    loads = [
        pltpu.make_async_copy(source, target, load_sem.at[i])
        for i, (source, target) in enumerate(
            (
                (tokens_hbm, quarter(tp)),
                (wk_hbm, wk),
                (wv_hbm, wv),
                (wq_hbm, wq),
                (wo_hbm, wo),
            )
        )
    ]
    for copy in loads:
        copy.start()
    greet([across, beside, sibling], True)

    t_x = remote(tokens_hbm, quarter(tp), t_send.at[0], t_recv.at[0], across)
    t_s = remote(tokens_hbm, quarter(tp), t_send.at[1], t_recv.at[1], sibling)
    t_x.start()
    t_s.start()

    def choose(*values):
        return jnp.where(
            z == 0, values[0], jnp.where(z == 1, values[1], jnp.where(z == 2, values[2], values[3]))
        )

    coming = (z, choose(1, 0, 3, 2), choose(2, 2, 1, 1), choose(3, 3, 0, 0))

    def spot(z_at, da, db):
        group, at_quarter = lane_spot(z_at, da, db, core)
        return all_ref.at[
            pl.ds(pl.multiple_of(group * rows, rows), rows),
            pl.ds(pl.multiple_of(at_quarter * cols, cols), cols),
        ]

    def at(z_at, da, db):
        return z_at * 4 + da * 2 + db

    def arrived(z_at, da, db):
        block, n = spot(z_at, da, db), at(z_at, da, db)
        remote(block, block, s_sem.at[n], recv_sem.at[n], sibling).wait_recv()
        return block

    def up(z_at, da, source):
        n = z_at * 2 + da
        target = recv_sem.at[at(z_at, da, 0)]
        return remote(source, spot(z_at, da, 0), up_sem.at[n], target, above)

    def down(z_at, da, source):
        n = z_at * 2 + da
        target = recv_sem.at[at(z_at, da, 0)]
        return remote(source, spot(z_at, da, 0), down_sem.at[n], target, below)

    def over_a(source):
        return remote(source, spot(z, 0, 0), a_sem, recv_sem.at[at(z, 1, 0)], peer_a)

    def over_b(z_at, da, source):
        return remote(
            source, spot(z_at, da, 0), b_sem.at[z_at * 2 + da], recv_sem.at[at(z_at, da, 1)], peer_b
        )

    def to_sibling(z_at, da, db, source):
        n = at(z_at, da, db)
        return remote(source, spot(z_at, da, db), s_sem.at[n], sib_sem.at[n], sibling)

    def along_z(da, source):
        @pl.when(z < 3)
        def _():
            up(z, da, source).start()

        @pl.when(z > 0)
        def _():
            down(z, da, source).start()

    def pass_a():
        block = arrived(z, 1, 0)
        along_z(1, block)
        over_b(z, 1, block).start()
        to_sibling(z, 1, 0, block).start()

    def pass_z(k, da):
        z_at = coming[k]
        block = arrived(z_at, da, 0)

        @pl.when((z_at > z) & (z > 0))
        def _():
            down(z_at, da, block).start()

        @pl.when((z_at < z) & (z < 3))
        def _():
            up(z_at, da, block).start()

        over_b(z_at, da, block).start()
        to_sibling(z_at, da, 0, block).start()

    def pass_b(k, da):
        block = arrived(coming[k], da, 1)
        to_sibling(coming[k], da, 1, block).start()

    own = pltpu.make_async_copy(grad_hbm, spot(z, 0, 0), load_sem.at[5])
    over_a(grad_hbm).start()
    along_z(0, grad_hbm)
    over_b(z, 0, grad_hbm).start()
    to_sibling(z, 0, 0, grad_hbm).start()
    own.start()

    t_x.wait_recv()
    theirs = quarter(tp + 2 - 4 * x)
    t_f = remote(theirs, theirs, t_send.at[2], t_recv.at[2], sibling)
    t_f.start()
    loads[0].wait()
    t_s.wait_recv()
    t_f.wait_recv()

    def by_rows(step, body):
        def one(i, carry):
            body(pl.ds(pl.multiple_of(i * step, step), step))
            return carry

        lax.fori_loop(0, rows // step, one, 0)

    def norm_one(span):
        values = tokens[span, :].astype(full)
        inv = lax.rsqrt(jnp.mean(values * values, axis=1, keepdims=True) + norm_eps)
        n1_ref[span, :] = (values * inv * first_ref[:1, :]).astype(low)
        inv_one_ref[span, :] = jnp.broadcast_to(inv, (inv.shape[0], 128))

    by_rows(32, norm_one)
    pass_a()
    pass_z(1, 0)

    def project(weights, bias_at):
        def one(i, carry):
            cut = pl.ds(pl.multiple_of(i * 256, 256), 256)
            lin[:, cut] = (
                jnp.dot(n1_ref[...], weights[:, cut], preferred_element_type=full)
                + bias_ref[bias_at : bias_at + 1, cut]
            )
            return carry

        lax.fori_loop(0, cols // 256, one, 0)

    def rotate_into(target):
        def one(h, carry):
            cut = pl.ds(pl.multiple_of(h * HD, HD), HD)
            value = lin[:, cut]
            turned = value * cos_ref[...] + pltpu.roll(value, HD // 2, 1) * sin_ref[...]
            target[:, cut] = turned.astype(low)
            return carry

        lax.fori_loop(0, heads, one, 0)

    loads[1].wait()
    project(wk, 1)
    rotate_into(k_ref)
    loads[2].wait()
    project(wv, 2)
    v_ref[...] = lin[...].astype(low)
    earlier = (
        remote(k_ref, earlier_k, kv_send.at[0], kv_recv.at[0], beside),
        remote(v_ref, earlier_v, kv_send.at[1], kv_recv.at[1], beside),
    )

    @pl.when(y == 0)
    def _():
        for copy in earlier:
            copy.start()

    pass_b(0, 0)
    pass_z(2, 0)
    pass_z(1, 1)
    loads[3].wait()
    project(wq, 0)
    rotate_into(q_ref)

    half = rows // 2
    lane = lax.broadcasted_iota(jnp.int32, (1, 128), 1)

    def pick(held, span, h):
        return jnp.sum(jnp.where(lane == h, held[span, :], 0.0), axis=1, keepdims=True)

    def put(held, span, h, value):
        held[span, :] = jnp.where(lane == h, value, held[span, :])

    most[...] = jnp.zeros_like(most)
    weight[...] = jnp.ones_like(weight)

    def local_head(h, carry):
        cut = pl.ds(pl.multiple_of(h * HD, HD), HD)
        for qb in range(2):
            span, count = pl.ds(qb * half, half), (qb + 1) * half
            scores = times_transpose(q_ref[span, cut], k_ref[:count, cut]) * score_scale
            top = jnp.max(scores, axis=1, keepdims=True)
            powers = jnp.exp(scores - top)
            put(most, span, h, top)
            put(weight, span, h, jnp.sum(powers, axis=1, keepdims=True))
            total[span, cut] = jnp.dot(
                powers.astype(low), v_ref[:count, cut], preferred_element_type=full
            )
        return carry

    lax.fori_loop(0, heads, local_head, 0)
    pass_z(2, 1)
    pass_z(3, 0)
    pass_b(0, 1)
    pass_b(1, 0)

    @pl.when(y == 0)
    def _():
        ke_ref[...] = jnp.zeros_like(ke_ref)
        ve_ref[...] = jnp.zeros_like(ve_ref)

    @pl.when(y == 1)
    def _():
        for copy in earlier:
            copy.wait_recv()
        ke_ref[...] = earlier_k[...]
        ve_ref[...] = earlier_v[...]

        def remote_head(h, carry):
            cut = pl.ds(pl.multiple_of(h * HD, HD), HD)
            for qb in range(2):
                span = pl.ds(qb * half, half)
                scores = times_transpose(q_ref[span, cut], ke_ref[:, cut]) * score_scale
                before = pick(most, span, h)
                top = jnp.maximum(before, jnp.max(scores, axis=1, keepdims=True))
                powers = jnp.exp(scores - top)
                shrink = jnp.exp(before - top)
                put(most, span, h, top)
                put(
                    weight,
                    span,
                    h,
                    pick(weight, span, h) * shrink + jnp.sum(powers, axis=1, keepdims=True),
                )
                total[span, cut] = total[span, cut] * shrink + jnp.dot(
                    powers.astype(low), ve_ref[:, cut], preferred_element_type=full
                )
            return carry

        lax.fori_loop(0, heads, remote_head, 0)

    def finish_head(h, carry):
        cut = pl.ds(pl.multiple_of(h * HD, HD), HD)
        context_ref[:, cut] = (total[:, cut] / pick(weight, slice(None), h)).astype(low)
        return carry

    lax.fori_loop(0, heads, finish_head, 0)
    log_ref[...] = most[...] + jnp.log(weight[...])

    loads[4].wait()

    def out_part(at_quarter, target):
        cut = pl.ds(pl.multiple_of(at_quarter * cols, cols), cols)
        target[...] = jnp.dot(context_ref[...], wo[:, cut], preferred_element_type=full).astype(low)

    def part_to_sibling(i):
        return remote(tp_staged.at[i], tp_sib.at[i], tp_send.at[i], tp_recv.at[i], sibling)

    def part_of(i):
        x_at = 1 - x + (2 * x - 1) * i
        out_part(x_at * 2 + 1 - core, tp_staged.at[i])
        part_to_sibling(i).start()
        out_part(x_at * 2 + core, tp_mine.at[i])

    out_x = remote(tp_mine.at[0], tp_x, tp_send.at[2], tp_recv.at[2], across)
    part_of(0)
    part_to_sibling(0).wait_recv()
    add_blocks(tp_mine.at[0], [tp_sib.at[0]], rows)
    out_x.start()
    part_of(1)
    pass_z(3, 1)
    pass_b(1, 1)
    pass_b(2, 0)
    part_to_sibling(1).wait_recv()
    out_x.wait_recv()
    own_cut = pl.ds(pl.multiple_of(tp * cols, cols), cols)

    def sum_parts(span):
        value = tokens[span, own_cut].astype(full) + (
            tp_mine[1, span, :].astype(full)
            + tp_sib[1, span, :].astype(full)
            + tp_x[span, :].astype(full)
        )
        hidden_ref[span, :] = value
        lin[span, :] = value * value

    by_rows(64, sum_parts)

    row_mine[0] = row_of(lin[...])
    first = remote(row_mine.at[0], row_sib, row_send.at[0], row_recv.at[0], sibling)
    first.start()
    first.wait_recv()
    row_mine[1] = row_mine[0] + row_sib[...]
    second = remote(row_mine.at[1], row_x, row_send.at[1], row_recv.at[1], across)
    second.start()
    second.wait_recv()
    squares = (row_mine[1] + row_x[...]).T[:, :1]
    inv_two = lax.rsqrt(squares * (1.0 / model_dim) + norm_eps)
    inv_ref[...] = jnp.broadcast_to(inv_two, (rows, 128))

    def norm_two(span):
        unit = hidden_ref[span, :] * inv_ref[span, :1]
        unit_ref[span, :] = unit
        normed_ref[span, :] = (unit * second_ref[:1, :]).astype(low)

    by_rows(64, norm_two)

    pass_b(2, 1)
    pass_b(3, 0)
    pass_b(3, 1)

    def finish_sibling(i, carry):
        block = spot(0, 0, 0)
        copy = remote(block, block, s_sem.at[i], sib_sem.at[i], sibling)
        copy.wait_recv()
        copy.wait_send()
        return carry

    lax.fori_loop(0, 16, finish_sibling, 0)

    def finish_links(i, carry):
        for da in range(2):
            over_b(i, da, grad_hbm).wait_send()

            @pl.when((z < 3) & (i <= z))
            def _(da=da):
                up(i, da, grad_hbm).wait_send()

            @pl.when((z > 0) & (i >= z))
            def _(da=da):
                down(i, da, grad_hbm).wait_send()

        return carry

    lax.fori_loop(0, 4, finish_links, 0)
    over_a(grad_hbm).wait_send()
    own.wait()
    for copy in (t_x, t_s, t_f, out_x, part_to_sibling(0), part_to_sibling(1), first, second):
        copy.wait_send()

    @pl.when(y == 0)
    def _():
        for copy in earlier:
            copy.wait_send()


def attend(vmem_args, hbm_args, cid):
    rows, cols = hbm_args[0].shape
    model_dim = vmem_args[0].shape[1]
    low, full, dma = jnp.bfloat16, jnp.float32, pltpu.SemaphoreType.DMA
    vmem, hbm = pl.BlockSpec(memory_space=pltpu.VMEM), pl.BlockSpec(memory_space=pl.ANY)

    def buffers(*shape, dtype=low):
        return pltpu.VMEM(shape, dtype)

    def result(*shape, dtype=low):
        return jax.ShapeDtypeStruct(shape, dtype)

    return pl.pallas_call(
        attend_kernel,
        out_shape=[
            result(rows, cols, dtype=full),
            result(rows, cols, dtype=full),
            result(rows, 128, dtype=full),
            result(rows, cols),
            result(rows, model_dim),
            result(rows, 128, dtype=full),
        ]
        + [result(rows, cols)] * 6
        + [result(rows, 128, dtype=full), result(8 * rows, model_dim)],
        in_specs=[vmem] * len(vmem_args) + [hbm] * len(hbm_args),
        out_specs=[vmem] * 13 + [hbm],
        scratch_shapes=[buffers(*arg.shape) for arg in hbm_args[2:]]
        + [
            buffers(rows, model_dim),
            buffers(rows, cols, dtype=full),
            buffers(rows, cols, dtype=full),
            buffers(rows, 128, dtype=full),
            buffers(rows, 128, dtype=full),
            buffers(rows, cols),
            buffers(rows, cols),
            buffers(2, rows, cols),
            buffers(2, rows, cols),
            buffers(2, rows, cols),
            buffers(rows, cols),
            buffers(2, 8, rows, dtype=full),
            buffers(8, rows, dtype=full),
            buffers(8, rows, dtype=full),
        ]
        + [dma((6,)), dma((3,)), dma((3,)), dma((2,)), dma((2,)), dma((3,)), dma((3,))]
        + [dma((2,)), dma((2,))]
        + [dma((8,)), dma((8,)), dma, dma((8,)), dma((16,)), dma((16,)), dma((16,))],
        compiler_params=pltpu.CompilerParams(
            collective_id=cid, has_side_effects=True, vmem_limit_bytes=60 * 2**20
        ),
        name="attend",
    )(*vmem_args, *hbm_args)


def kept_choice(expert_ids, pair_order, expert_total, capacity):
    tok_count, top_count = expert_ids.shape
    pair_count = tok_count * top_count
    order = pair_order.reshape(-1)
    pairs = jnp.arange(pair_count, dtype=jnp.int32)
    turn = jnp.sum(jnp.where(order[None, :] == pairs[:, None], pairs[None, :], 0), axis=1)
    turn = turn.reshape(tok_count, top_count)
    picked = expert_ids[:, :, None] == jnp.arange(expert_total, dtype=jnp.int32)[None, None, :]
    experts_apart = jnp.arange(expert_total, dtype=jnp.int32)[:, None, None]
    picked = expert_ids.T[None] == experts_apart
    named = jnp.any(picked, axis=1)
    turn_of = jnp.sum(jnp.where(picked, turn.T[None], 0), axis=1)
    turn_of = jnp.where(named, turn_of, pair_count)
    slot = jnp.sum((turn_of[:, None, :] < turn_of[:, :, None]).astype(jnp.int32), axis=2)
    return (named & (slot < capacity)).astype(jnp.float32)


def dense_plan(
    tokens,
    out_grad,
    first_gain,
    query_weight,
    key_weight,
    value_weight,
    query_bias,
    key_bias,
    value_bias,
    output_weight,
    second_gain,
    router_weight,
    shared_gate_weight,
    shared_up_weight,
    shared_down_weight,
    switch_vector,
    expert_gate_weight,
    expert_up_weight,
    expert_down_weight,
    expert_ids,
    pair_order,
):
    ep, tp = lax.axis_index("ep"), lax.axis_index("tp")
    tok_count, col_width = tokens.shape
    model_dim = query_weight.shape[0]
    sources = lax.axis_size("ep")
    place_in_seq = ep % SPAN
    expert_total = router_weight.shape[1]
    capacity = 9 * tok_count * expert_ids.shape[1] // (8 * expert_total)
    head_count = query_weight.shape[1] // HD
    expert_width = expert_gate_weight.shape[2]
    shared_width = shared_gate_weight.shape[1] // sources
    width = expert_width + shared_width

    def own_cols(vector):
        return lax.dynamic_slice_in_dim(vector, tp * col_width, col_width, vector.ndim - 1)

    kept_own = kept_choice(expert_ids, pair_order, expert_total, capacity)

    def tall(vector):
        return jnp.broadcast_to(vector[None, :], (8, vector.shape[0]))

    cosine, sine_part = rope_tables(tok_count, HD, place_in_seq * tok_count)
    cos_wide = jnp.concatenate([cosine[:, 0], cosine[:, 0]], axis=1)
    sin_wide = jnp.concatenate([-sine_part[:, 0], sine_part[:, 0]], axis=1)
    second_cols = own_cols(second_gain)
    biases = jnp.pad(jnp.stack([query_bias, key_bias, value_bias]), ((0, 5), (0, 0)))
    (
        hidden_cols,
        unit_two,
        inv_two,
        normed_cols,
        normed_one,
        inv_one,
        queries,
        keys_rot,
        values_all,
        earlier_keys,
        earlier_values,
        context,
        log_rows,
        grads_all,
    ) = attend(
        [tall(first_gain), biases, tall(second_cols), cos_wide, sin_wide],
        [tokens, out_grad, query_weight, key_weight, value_weight, output_weight],
        2,
    )

    def shared_rows(weight):
        return lax.dynamic_slice_in_dim(weight, ep * shared_width, shared_width, 1).T

    extra_rows = jnp.concatenate([router_weight.T, switch_vector[None, :]], axis=0)
    extra_rows = jnp.pad(extra_rows, ((0, 16 - extra_rows.shape[0]), (0, 0)))
    kept_rows = jnp.pad(kept_own, ((0, 16 - expert_total), (0, 0))).astype(jnp.bfloat16)
    reduced, ffn_cols, logit_tile, expert_grads, shared_parts, *_ = experts(
        normed_cols,
        grads_all,
        kept_rows,
        [
            expert_gate_weight[0].T,
            shared_rows(shared_gate_weight),
            extra_rows,
            expert_up_weight[0].T,
            shared_rows(shared_up_weight),
            expert_down_weight[0],
            shared_down_weight,
        ],
        expert_total,
        4,
    )
    layer_out = (hidden_cols + ffn_cols).astype(jnp.bfloat16)
    shared_parts = lax.all_to_all(shared_parts, "ep", split_axis=0, concat_axis=0, tiled=True)
    shared_parts = shared_parts.transpose(1, 0, 2, 3).reshape(3, sources * shared_width, -1)
    shared_parts = shared_parts.astype(jnp.float32)
    shared_gate_grad = shared_parts[1].T
    shared_up_grad = shared_parts[2].T
    shared_down_grad = shared_parts[0]

    normed_grad = reduced[:tok_count]
    probs_grad = (reduced[tok_count : tok_count + expert_total] * kept_own).T
    switch_grad = reduced[tok_count + expert_total]
    logit_at = width % 128
    probs_own = softmax_rows(logit_tile[:, logit_at : logit_at + expert_total])
    switch = jax.nn.sigmoid(logit_tile[:, logit_at + expert_total])
    logit_grad = (
        probs_own * (probs_grad - jnp.sum(probs_own * probs_grad, axis=-1, keepdims=True))
    ).astype(jnp.bfloat16)
    router_grad = inner_rows(normed_cols, logit_grad)
    switch_lin_grad = switch_grad * switch * (1.0 - switch)
    switch_vector_grad = jnp.dot(switch_lin_grad, normed_cols, preferred_element_type=jnp.float32)
    router_cols = lax.dynamic_slice_in_dim(router_weight, tp * col_width, col_width, 0)
    normed_grad = normed_grad + times_transpose(logit_grad, router_cols)
    normed_grad = (
        normed_grad
        + switch_lin_grad[:, None] * own_cols(switch_vector).astype(jnp.float32)[None, :]
    )
    second_gain_grad = jnp.sum(normed_grad * unit_two, axis=0)

    small = jnp.concatenate(
        [second_gain_grad[None], switch_vector_grad[None], router_grad.T], axis=0
    )
    small_rows = small.shape[0]
    small = jnp.pad(small, ((4, 12 - small_rows), (0, 0)))
    tokens_grad, weight_grads, sums = unwind(
        [
            normed_grad,
            unit_two,
            inv_two,
            tall(second_cols),
            out_grad,
            tokens,
            inv_one,
            tall(own_cols(first_gain)),
            small,
            queries,
            keys_rot,
            values_all,
            earlier_keys,
            earlier_values,
            context,
            log_rows,
            cos_wide,
            sin_wide,
        ],
        [normed_one, query_weight, key_weight, value_weight, output_weight],
        5,
    )
    share = model_dim // sources
    bias_width = HD // sources
    bias_sums = lax.dynamic_slice_in_dim(
        sums[1:4].reshape(3, head_count, HD), ep * bias_width, bias_width, 2
    )
    spread = jnp.concatenate([sums[:1], sums[4 : 4 + small_rows]], axis=0)
    spread = lax.all_gather(spread, "tp", axis=1, tiled=True)
    spread = lax.dynamic_slice_in_dim(spread, ep * share, share, 1)
    return (
        layer_out,
        tokens_grad,
        spread[0],
        weight_grads[1],
        weight_grads[2],
        weight_grads[3],
        bias_sums[0],
        bias_sums[1],
        bias_sums[2],
        weight_grads[0].T,
        spread[1],
        spread[3:].T,
        shared_gate_grad,
        shared_up_grad,
        shared_down_grad,
        spread[2],
        expert_grads[1].T[None],
        expert_grads[2].T[None],
        expert_grads[0][None],
    )


def solution(mesh):
    plan = dense_plan if dict(mesh.shape) == {"ep": 8, "tp": 4} else slot_plan
    return jax.shard_map(
        plan,
        mesh=mesh,
        in_specs=(
            P("ep", "tp"),
            P("ep", "tp"),
            P(),
            P(None, "tp"),
            P(None, "tp"),
            P(None, "tp"),
            P("tp"),
            P("tp"),
            P("tp"),
            P("tp", None),
            P(),
            P(),
            P(None, "tp"),
            P(None, "tp"),
            P("tp", None),
            P(),
            P("ep", None, "tp"),
            P("ep", None, "tp"),
            P("ep", "tp", None),
            P("ep", None),
            P("ep", None),
        ),
        out_specs=(
            P("ep", "tp"),
            P("ep", "tp"),
            P("ep"),
            P("ep", "tp"),
            P("ep", "tp"),
            P("ep", "tp"),
            P("tp", "ep"),
            P("tp", "ep"),
            P("tp", "ep"),
            P("tp", "ep"),
            P("ep"),
            P("ep", None),
            P("ep", "tp"),
            P("ep", "tp"),
            P("tp", "ep"),
            P("ep"),
            P("ep", None, "tp"),
            P("ep", None, "tp"),
            P("ep", "tp", None),
        ),
        check_vma=False,
    )
```

```python
import functools
import math

import jax
import jax.numpy as jnp
from jax import lax
from jax.experimental import pallas as pl
from jax.experimental.pallas import tpu as pltpu
from jax.sharding import PartitionSpec as P

HD = 128
BLOCK = 256
SPAN = 2


rope_theta = 1000000.0
norm_eps = 1e-06
masked_score = -1e30


def passed_along(value, axis, steps):
    count = lax.axis_size(axis)
    leading, last = (max(0, -steps), min(count, count - steps))
    return lax.ppermute(value, axis, [(source, source + steps) for source in range(leading, last)])


def rope_tables(row_count, head_dim, first_position):
    positions = jnp.arange(row_count, dtype=jnp.float32) + first_position.astype(jnp.float32)
    frequency = jnp.exp(
        jnp.arange(head_dim // 2, dtype=jnp.float32) * (-2.0 * math.log(rope_theta) / head_dim)
    )
    angles = positions[:, None] * frequency[None, :]
    return (jnp.cos(angles)[:, None, :], jnp.sin(angles)[:, None, :])


def rotate(values, cosine, sine_part):
    half_dim = values.shape[-1] // 2
    first_half = values[..., :half_dim]
    second_half = values[..., half_dim:]
    return jnp.concatenate(
        [
            first_half * cosine - second_half * sine_part,
            second_half * cosine + first_half * sine_part,
        ],
        axis=-1,
    )


def inner_rows(left_side, right_side):
    return lax.dot_general(
        left_side, right_side, (((0,), (0,)), ((), ())), preferred_element_type=jnp.float32
    )


def times_transpose(left_side, right_side):
    return lax.dot_general(
        left_side, right_side, (((1,), (1,)), ((), ())), preferred_element_type=jnp.float32
    )


def row_stats(values):
    inv_rms = lax.rsqrt(jnp.mean(values * values, axis=-1, keepdims=True) + norm_eps)
    return (values * inv_rms, inv_rms)


def norm_back(grad_rows, unit_rows, inv_rms, gain_vec):
    scaled = grad_rows * gain_vec
    return inv_rms * (scaled - unit_rows * jnp.mean(scaled * unit_rows, axis=-1, keepdims=True))


def softmax_rows(scores):
    row_max = jnp.max(scores, axis=-1, keepdims=True)
    powers = jnp.exp(scores - row_max)
    return powers / jnp.sum(powers, axis=-1, keepdims=True)


def to_experts(block_rows, local_count):
    sources, span_rows, col_count = block_rows.shape
    slot_count = span_rows // local_count
    shaped = block_rows.reshape(sources, local_count, slot_count, col_count)
    return shaped.swapaxes(0, 1).reshape(local_count, sources * slot_count, col_count)


def to_sources(block_rows, sources):
    local_count, rows_all, col_count = block_rows.shape
    slot_count = rows_all // sources
    shaped = block_rows.reshape(local_count, sources, slot_count, col_count)
    return shaped.swapaxes(0, 1).reshape(sources, local_count * slot_count, col_count)


def deliver(block_rows):
    arrived = lax.all_to_all(block_rows, "ep", split_axis=0, concat_axis=0, tiled=True)
    return arrived


def collect(block_rows):
    return lax.all_to_all(block_rows, "ep", split_axis=0, concat_axis=0, tiled=True)


def slot_plan(
    tokens,
    out_grad,
    first_gain,
    query_weight,
    key_weight,
    value_weight,
    query_bias,
    key_bias,
    value_bias,
    output_weight,
    second_gain,
    router_weight,
    shared_gate_weight,
    shared_up_weight,
    shared_down_weight,
    switch_vector,
    expert_gate_weight,
    expert_up_weight,
    expert_down_weight,
    expert_ids,
    pair_order,
):
    whole_in, whole_grad = (
        lax.all_gather(tokens, "tp", axis=1, tiled=True),
        lax.all_gather(out_grad, "tp", axis=1, tiled=True),
    )
    tok_count = whole_in.shape[0]
    model_dim = whole_in.shape[1]
    col_width = tokens.shape[1]
    col_start = lax.axis_index("tp") * col_width
    sources = lax.axis_size("ep")
    place_in_seq = lax.axis_index("ep") % SPAN
    has_earlier = place_in_seq > 0
    local_experts = expert_gate_weight.shape[0]
    expert_total = router_weight.shape[1]
    top_count = expert_ids.shape[1]
    pair_count = tok_count * top_count
    capacity = 9 * pair_count // (8 * expert_total)
    head_count = query_weight.shape[1] // HD
    score_scale = HD ** (-0.5)
    inputs_full = whole_in.astype(jnp.float32)
    unit_one, inv_one = row_stats(inputs_full)
    normed_one = (unit_one * first_gain).astype(jnp.bfloat16)
    query_lin = jnp.dot(normed_one, query_weight, preferred_element_type=jnp.float32) + query_bias
    key_lin = jnp.dot(normed_one, key_weight, preferred_element_type=jnp.float32) + key_bias
    value_lin = jnp.dot(normed_one, value_weight, preferred_element_type=jnp.float32) + value_bias
    cosine, sine_part = rope_tables(tok_count, HD, place_in_seq * tok_count)
    queries = rotate(query_lin.reshape(tok_count, head_count, HD), cosine, sine_part).astype(
        jnp.bfloat16
    )
    keys_rot = rotate(key_lin.reshape(tok_count, head_count, HD), cosine, sine_part).astype(
        jnp.bfloat16
    )
    values_all = value_lin.reshape(tok_count, head_count, HD).astype(jnp.bfloat16)
    earlier_keys, earlier_values = passed_along((keys_rot, values_all), "ep", 1)
    keys_both = jnp.concatenate([earlier_keys, keys_rot], axis=0)
    values_both = jnp.concatenate([earlier_values, values_all], axis=0)
    blocks = jnp.arange(tok_count) // BLOCK
    local_allowed = blocks[None, :] <= blocks[:, None]
    remote_allowed = jnp.broadcast_to(has_earlier, (tok_count, tok_count))
    allowed = jnp.concatenate([remote_allowed, local_allowed], axis=1)[None]

    def attention_scores():
        scored = (
            jnp.einsum("qhd,khd->hqk", queries, keys_both, preferred_element_type=jnp.float32)
            * score_scale
        )
        return jnp.where(allowed, scored, masked_score)

    scores = attention_scores()
    row_max = jnp.max(scores, axis=-1, keepdims=True)
    powers = jnp.exp(scores - row_max)
    totals = jnp.sum(powers, axis=-1, keepdims=True)
    log_total = row_max + jnp.log(totals)
    probs_low = (powers / totals).astype(jnp.bfloat16)
    context = jnp.einsum("hqk,khd->qhd", probs_low, values_both, preferred_element_type=jnp.float32)
    context = context.reshape(tok_count, head_count * HD).astype(jnp.bfloat16)
    attn_part = jnp.dot(context, output_weight, preferred_element_type=jnp.float32)
    attended = lax.psum(attn_part, "tp")
    hidden_one = inputs_full + attended
    unit_two, inv_two = row_stats(hidden_one)
    normed_two = (unit_two * second_gain).astype(jnp.bfloat16)
    logits = jnp.dot(normed_two, router_weight, preferred_element_type=jnp.float32)
    router_probs = softmax_rows(logits)
    gate_values = jnp.take_along_axis(router_probs, expert_ids, axis=1)
    switch = jax.nn.sigmoid(jnp.dot(normed_two, switch_vector, preferred_element_type=jnp.float32))
    flat_ids = expert_ids.reshape(-1)
    turn_order = pair_order.reshape(-1)
    in_turn = flat_ids[turn_order]
    onehot = (in_turn[:, None] == jnp.arange(expert_total, dtype=jnp.int32)[None, :]).astype(
        jnp.int32
    )
    earlier = jnp.cumsum(onehot, axis=0) - onehot
    turn_slot = jnp.sum(earlier * onehot, axis=1)
    slot_index = jnp.zeros((pair_count,), jnp.int32).at[turn_order].set(turn_slot)
    kept_pair = slot_index < capacity
    slot_rows = expert_total * capacity
    target = jnp.where(kept_pair, flat_ids * capacity + slot_index, slot_rows)
    pair_token = jnp.arange(pair_count, dtype=jnp.int32) // top_count
    slot_token = (
        jnp.full((slot_rows + 1,), tok_count, jnp.int32).at[target].set(pair_token)[:slot_rows]
    )
    slot_gate = (
        jnp.zeros((slot_rows + 1,), jnp.float32).at[target].set(gate_values.reshape(-1))[:slot_rows]
    )
    padded_two = jnp.concatenate([normed_two, jnp.zeros((1, model_dim), jnp.bfloat16)], axis=0)
    send_rows = padded_two[slot_token].reshape(sources, local_experts * capacity, model_dim)
    expert_rows = to_experts(deliver(send_rows), local_experts)
    gate_lin = jnp.einsum(
        "erd,edf->erf", expert_rows, expert_gate_weight, preferred_element_type=jnp.float32
    )
    up_lin = jnp.einsum(
        "erd,edf->erf", expert_rows, expert_up_weight, preferred_element_type=jnp.float32
    )
    gate_sig = jax.nn.sigmoid(gate_lin)
    gate_act = gate_lin * gate_sig
    expert_hidden = (gate_act * up_lin).astype(jnp.bfloat16)
    expert_part = jnp.einsum(
        "erf,efd->erd", expert_hidden, expert_down_weight, preferred_element_type=jnp.float32
    )
    shared_gate_lin = jnp.dot(normed_two, shared_gate_weight, preferred_element_type=jnp.float32)
    shared_up_lin = jnp.dot(normed_two, shared_up_weight, preferred_element_type=jnp.float32)
    shared_sig = jax.nn.sigmoid(shared_gate_lin)
    shared_act = shared_gate_lin * shared_sig
    shared_hidden = (shared_act * shared_up_lin).astype(jnp.bfloat16)
    shared_part = jnp.dot(shared_hidden, shared_down_weight, preferred_element_type=jnp.float32)
    expert_cols, shared_cols = (
        lax.psum_scatter(expert_part.reshape(-1, model_dim), "tp", scatter_dimension=1, tiled=True),
        lax.psum_scatter(shared_part, "tp", scatter_dimension=1, tiled=True),
    )
    returned = collect(
        to_sources(expert_cols.astype(jnp.bfloat16).reshape(local_experts, -1, col_width), sources)
    )
    back_flat = jnp.concatenate(
        [returned.reshape(slot_rows, col_width), jnp.zeros((1, col_width), jnp.bfloat16)], axis=0
    )
    pair_out = back_flat[target].astype(jnp.float32).reshape(tok_count, top_count, col_width)
    routed = jnp.sum(gate_values[:, :, None] * pair_out, axis=1)
    hidden_cols = lax.dynamic_slice_in_dim(hidden_one, col_start, col_width, 1)
    layer_out = (hidden_cols + switch[:, None] * shared_cols + routed).astype(jnp.bfloat16)
    grad_full = whole_grad.astype(jnp.float32)
    grad_cols = out_grad.astype(jnp.float32)
    gate_part = jnp.sum(pair_out * grad_cols[:, None, :], axis=-1)
    switch_part = jnp.sum(grad_cols * shared_cols, axis=-1)
    gate_grad, switch_grad = lax.psum((gate_part, switch_part), "tp")
    padded_grad = jnp.concatenate([whole_grad, jnp.zeros((1, model_dim), jnp.bfloat16)], axis=0)
    send_grads = (slot_gate[:, None] * padded_grad[slot_token].astype(jnp.float32)).astype(
        jnp.bfloat16
    )
    expert_grads = to_experts(
        deliver(send_grads.reshape(sources, local_experts * capacity, model_dim)), local_experts
    )
    hidden_grad = jnp.einsum(
        "erd,efd->erf", expert_grads, expert_down_weight, preferred_element_type=jnp.float32
    )
    gate_lin_grad = (hidden_grad * up_lin * gate_sig * (1.0 + gate_lin * (1.0 - gate_sig))).astype(
        jnp.bfloat16
    )
    up_lin_grad = (hidden_grad * gate_act).astype(jnp.bfloat16)
    expert_down_grad = jnp.einsum(
        "erf,erd->efd", expert_hidden, expert_grads, preferred_element_type=jnp.float32
    )
    expert_gate_grad = jnp.einsum(
        "erd,erf->edf", expert_rows, gate_lin_grad, preferred_element_type=jnp.float32
    )
    expert_up_grad = jnp.einsum(
        "erd,erf->edf", expert_rows, up_lin_grad, preferred_element_type=jnp.float32
    )
    rows_grad = jnp.einsum(
        "erf,edf->erd", gate_lin_grad, expert_gate_weight, preferred_element_type=jnp.float32
    )
    rows_grad = rows_grad + jnp.einsum(
        "erf,edf->erd", up_lin_grad, expert_up_weight, preferred_element_type=jnp.float32
    )
    rows_grad_cols = lax.psum_scatter(
        rows_grad.reshape(-1, model_dim), "tp", scatter_dimension=1, tiled=True
    )
    returned_grad = collect(
        to_sources(
            rows_grad_cols.astype(jnp.bfloat16).reshape(local_experts, -1, col_width), sources
        )
    )
    back_grad = jnp.concatenate(
        [returned_grad.reshape(slot_rows, col_width), jnp.zeros((1, col_width), jnp.bfloat16)],
        axis=0,
    )
    routed_grad = jnp.sum(
        back_grad[target].astype(jnp.float32).reshape(tok_count, top_count, col_width), axis=1
    )
    shared_out_grad = (switch[:, None] * grad_full).astype(jnp.bfloat16)
    shared_hidden_grad = times_transpose(shared_out_grad, shared_down_weight)
    shared_gate_lin_grad = (
        shared_hidden_grad
        * shared_up_lin
        * shared_sig
        * (1.0 + shared_gate_lin * (1.0 - shared_sig))
    ).astype(jnp.bfloat16)
    shared_up_lin_grad = (shared_hidden_grad * shared_act).astype(jnp.bfloat16)
    shared_down_grad = inner_rows(shared_hidden, shared_out_grad)
    shared_gate_grad = inner_rows(normed_two, shared_gate_lin_grad)
    shared_up_grad = inner_rows(normed_two, shared_up_lin_grad)
    normed_grad = times_transpose(shared_gate_lin_grad, shared_gate_weight) + times_transpose(
        shared_up_lin_grad, shared_up_weight
    )
    normed_grad = normed_grad + lax.dynamic_update_slice_in_dim(
        jnp.zeros_like(normed_grad), routed_grad, col_start, 1
    )
    normed_grad = lax.psum(normed_grad, "tp")
    picked = (
        expert_ids[:, :, None] == jnp.arange(expert_total, dtype=jnp.int32)[None, None, :]
    ).astype(jnp.float32)
    probs_grad = jnp.sum(picked * gate_grad[:, :, None], axis=1)
    logit_grad = (
        router_probs * (probs_grad - jnp.sum(router_probs * probs_grad, axis=-1, keepdims=True))
    ).astype(jnp.bfloat16)
    router_grad = inner_rows(normed_two, logit_grad)
    switch_lin_grad = switch_grad * switch * (1.0 - switch)
    switch_vector_grad = jnp.dot(switch_lin_grad, normed_two, preferred_element_type=jnp.float32)
    normed_grad = normed_grad + times_transpose(logit_grad, router_weight)
    normed_grad = (
        normed_grad + switch_lin_grad[:, None] * switch_vector.astype(jnp.float32)[None, :]
    )
    second_gain_grad = jnp.sum(normed_grad * unit_two, axis=0)
    hidden_grad_one = grad_full + norm_back(normed_grad, unit_two, inv_two, second_gain)
    attended_grad = hidden_grad_one.astype(jnp.bfloat16)
    output_grad = inner_rows(context, attended_grad)
    context_grad = (
        times_transpose(attended_grad, output_weight)
        .astype(jnp.bfloat16)
        .reshape(tok_count, head_count, HD)
    )
    scores = attention_scores()
    attn_probs = jnp.exp(scores - log_total)
    probs_again = attn_probs.astype(jnp.bfloat16)
    probs_grad_att = jnp.einsum(
        "qhd,khd->hqk", context_grad, values_both, preferred_element_type=jnp.float32
    )
    values_both_grad = jnp.einsum(
        "hqk,qhd->khd", probs_again, context_grad, preferred_element_type=jnp.float32
    )
    scores_grad = (
        attn_probs * (probs_grad_att - jnp.sum(attn_probs * probs_grad_att, axis=-1, keepdims=True))
    ).astype(jnp.bfloat16)
    queries_grad = (
        jnp.einsum("hqk,khd->qhd", scores_grad, keys_both, preferred_element_type=jnp.float32)
        * score_scale
    )
    keys_both_grad = (
        jnp.einsum("hqk,qhd->khd", scores_grad, queries, preferred_element_type=jnp.float32)
        * score_scale
    )
    later_keys_grad, later_values_grad = passed_along(
        (keys_both_grad[:tok_count], values_both_grad[:tok_count]), "ep", -1
    )
    keep_later = jnp.where(has_earlier, 0.0, 1.0).astype(jnp.float32)
    keys_grad = keys_both_grad[tok_count:] + keep_later * later_keys_grad
    values_grad = values_both_grad[tok_count:] + keep_later * later_values_grad
    value_lin_grad = values_grad.reshape(tok_count, head_count * HD).astype(jnp.bfloat16)
    query_lin_grad = (
        rotate(queries_grad, cosine, -sine_part)
        .reshape(tok_count, head_count * HD)
        .astype(jnp.bfloat16)
    )
    key_lin_grad = (
        rotate(keys_grad, cosine, -sine_part)
        .reshape(tok_count, head_count * HD)
        .astype(jnp.bfloat16)
    )
    query_grad = inner_rows(normed_one, query_lin_grad)
    key_grad = inner_rows(normed_one, key_lin_grad)
    value_grad = inner_rows(normed_one, value_lin_grad)
    query_bias_grad = jnp.sum(query_lin_grad.astype(jnp.float32), axis=0).reshape(head_count, HD)
    key_bias_grad = jnp.sum(key_lin_grad.astype(jnp.float32), axis=0).reshape(head_count, HD)
    value_bias_grad = jnp.sum(value_lin_grad.astype(jnp.float32), axis=0).reshape(head_count, HD)
    normed_one_grad = times_transpose(query_lin_grad, query_weight) + times_transpose(
        key_lin_grad, key_weight
    )
    normed_one_grad = normed_one_grad + times_transpose(value_lin_grad, value_weight)
    normed_one_grad = lax.psum(normed_one_grad.astype(jnp.bfloat16), "tp").astype(jnp.float32)
    first_gain_grad = jnp.sum(normed_one_grad * unit_one, axis=0)
    input_grad = hidden_grad_one + norm_back(normed_one_grad, unit_one, inv_one, first_gain)
    tokens_grad = lax.dynamic_slice_in_dim(input_grad, col_start, col_width, 1).astype(jnp.bfloat16)
    reduced = (
        lax.psum_scatter(
            first_gain_grad.astype(jnp.bfloat16), "ep", scatter_dimension=0, tiled=True
        ).astype(jnp.float32),
        lax.psum_scatter(
            query_grad.astype(jnp.bfloat16), "ep", scatter_dimension=0, tiled=True
        ).astype(jnp.float32),
        lax.psum_scatter(
            key_grad.astype(jnp.bfloat16), "ep", scatter_dimension=0, tiled=True
        ).astype(jnp.float32),
        lax.psum_scatter(
            value_grad.astype(jnp.bfloat16), "ep", scatter_dimension=0, tiled=True
        ).astype(jnp.float32),
        lax.psum_scatter(
            query_bias_grad.astype(jnp.bfloat16), "ep", scatter_dimension=1, tiled=True
        ).astype(jnp.float32),
        lax.psum_scatter(
            key_bias_grad.astype(jnp.bfloat16), "ep", scatter_dimension=1, tiled=True
        ).astype(jnp.float32),
        lax.psum_scatter(
            value_bias_grad.astype(jnp.bfloat16), "ep", scatter_dimension=1, tiled=True
        ).astype(jnp.float32),
        lax.psum_scatter(
            output_grad.astype(jnp.bfloat16), "ep", scatter_dimension=1, tiled=True
        ).astype(jnp.float32),
        lax.psum_scatter(
            second_gain_grad.astype(jnp.bfloat16), "ep", scatter_dimension=0, tiled=True
        ).astype(jnp.float32),
        lax.psum_scatter(
            router_grad.astype(jnp.bfloat16), "ep", scatter_dimension=0, tiled=True
        ).astype(jnp.float32),
        lax.psum_scatter(
            shared_gate_grad.astype(jnp.bfloat16), "ep", scatter_dimension=0, tiled=True
        ).astype(jnp.float32),
        lax.psum_scatter(
            shared_up_grad.astype(jnp.bfloat16), "ep", scatter_dimension=0, tiled=True
        ).astype(jnp.float32),
        lax.psum_scatter(
            shared_down_grad.astype(jnp.bfloat16), "ep", scatter_dimension=1, tiled=True
        ).astype(jnp.float32),
        lax.psum_scatter(
            switch_vector_grad.astype(jnp.bfloat16), "ep", scatter_dimension=0, tiled=True
        ).astype(jnp.float32),
    )
    return (
        layer_out,
        tokens_grad,
        reduced[0],
        reduced[1],
        reduced[2],
        reduced[3],
        reduced[4],
        reduced[5],
        reduced[6],
        reduced[7],
        reduced[8],
        reduced[9],
        reduced[10],
        reduced[11],
        reduced[12],
        reduced[13],
        expert_gate_grad,
        expert_up_grad,
        expert_down_grad,
    )


MESH = pl.DeviceIdType.MESH
Z_ORDER = (0, 3, 1, 2)


def place():
    ep, tp = lax.axis_index("ep"), lax.axis_index("tp")
    return ep, tp, ep // 2, lax.rem(ep, 2), tp // 2, lax.rem(tp, 2)


def greet(always, along_z=False):
    barrier = pltpu.get_barrier_semaphore()
    for device in always:
        pl.semaphore_signal(barrier, inc=1, device_id=device, device_id_type=MESH)
    count = len(always)
    if along_z:
        ep, tp, z, _, _, _ = place()

        @pl.when(z < 3)
        def _():
            pl.semaphore_signal(barrier, inc=1, device_id=(ep + 2, tp), device_id_type=MESH)

        @pl.when(z > 0)
        def _():
            pl.semaphore_signal(barrier, inc=1, device_id=(ep - 2, tp), device_id_type=MESH)

        count = count + lax.min(z, 1) + lax.min(3 - z, 1)
    pl.semaphore_wait(barrier, count)


def remote(source, target, send_sem, recv_sem, device):
    return pltpu.make_async_remote_copy(
        src_ref=source,
        dst_ref=target,
        send_sem=send_sem,
        recv_sem=recv_sem,
        device_id=device,
        device_id_type=MESH,
    )


def add_blocks(target, sources, rows):
    step = next(size for size in (80, 64, 48, 16) if rows % size == 0)

    def body(i, carry):
        span = pl.ds(pl.multiple_of(i * step, 16), step)
        total = target[span, :]
        for source in sources:
            total = total + source[span, :].astype(target.dtype)
        target[span, :] = total
        return carry

    lax.fori_loop(0, rows // step, body, 0)


def gather_tp_kernel(x_ref, o_ref, send_sem, recv_sem, own_sem):
    ep, tp, _, _, x, core = place()
    cols = x_ref.shape[1]
    sibling = (ep, tp + 1 - 2 * core)
    across = (ep, tp + 2 - 4 * x)
    greet([sibling, across])
    mine = o_ref.at[:, pl.ds(pl.multiple_of(tp * cols, cols), cols)]
    theirs = o_ref.at[:, pl.ds(pl.multiple_of((tp + 2 - 4 * x) * cols, cols), cols)]
    out_x = remote(x_ref, mine, send_sem.at[0], recv_sem.at[0], across)
    out_s = remote(x_ref, mine, send_sem.at[1], recv_sem.at[1], sibling)
    own = pltpu.make_async_copy(x_ref, mine, own_sem)
    out_x.start()
    out_s.start()
    own.start()
    remote(x_ref, theirs, send_sem.at[0], recv_sem.at[0], across).wait_recv()
    passing = remote(theirs, theirs, send_sem.at[2], recv_sem.at[2], sibling)
    passing.start()
    out_s.wait_recv()
    passing.wait_recv()
    own.wait()
    out_x.wait_send()
    out_s.wait_send()
    passing.wait_send()


def gather_tp(value, cid):
    rows, cols = value.shape
    return pl.pallas_call(
        gather_tp_kernel,
        out_shape=jax.ShapeDtypeStruct((rows, 4 * cols), value.dtype),
        in_specs=[pl.BlockSpec(memory_space=pl.ANY)],
        out_specs=pl.BlockSpec(memory_space=pl.ANY),
        scratch_shapes=[
            pltpu.SemaphoreType.DMA((3,)),
            pltpu.SemaphoreType.DMA((3,)),
            pltpu.SemaphoreType.DMA,
        ],
        compiler_params=pltpu.CompilerParams(collective_id=cid, has_side_effects=True),
        name="gather_tp",
    )(value)


def scatter_tp_kernel(p_ref, o_ref, mine, from_sib, from_x, own_sem, send_sem, recv_sem):
    ep, tp, _, _, x, core = place()
    rows, cols = o_ref.shape
    sibling = (ep, tp + 1 - 2 * core)
    across = (ep, tp + 2 - 4 * x)
    greet([sibling, across])

    def part(x_at, core_at):
        return p_ref.at[:, pl.ds(pl.multiple_of((x_at * 2 + core_at) * cols, cols), cols)]

    sends, owns = [], []
    for i, x_at in enumerate((1 - x, x)):
        owns.append(pltpu.make_async_copy(part(x_at, core), mine.at[i], own_sem.at[i]))
        sends.append(
            remote(part(x_at, 1 - core), from_sib.at[i], send_sem.at[i], recv_sem.at[i], sibling)
        )
        sends[-1].start()
        owns[-1].start()
    owns[0].wait()
    sends[0].wait_recv()
    add_blocks(mine.at[0], [from_sib.at[0]], rows)
    out_x = remote(mine.at[0], from_x, send_sem.at[2], recv_sem.at[2], across)
    out_x.start()
    owns[1].wait()
    sends[1].wait_recv()
    out_x.wait_recv()
    o_ref[...] = jnp.zeros_like(o_ref)
    add_blocks(o_ref, [mine.at[1], from_sib.at[1], from_x], rows)
    out_x.wait_send()
    sends[0].wait_send()
    sends[1].wait_send()


def scatter_tp(value, cid):
    rows, cols = value.shape[0], value.shape[1] // 4
    return pl.pallas_call(
        scatter_tp_kernel,
        out_shape=jax.ShapeDtypeStruct((rows, cols), jnp.float32),
        in_specs=[pl.BlockSpec(memory_space=pl.ANY)],
        out_specs=pl.BlockSpec(memory_space=pltpu.VMEM),
        scratch_shapes=[
            pltpu.VMEM((2, rows, cols), value.dtype),
            pltpu.VMEM((2, rows, cols), value.dtype),
            pltpu.VMEM((rows, cols), value.dtype),
            pltpu.SemaphoreType.DMA((2,)),
            pltpu.SemaphoreType.DMA((3,)),
            pltpu.SemaphoreType.DMA((3,)),
        ],
        compiler_params=pltpu.CompilerParams(
            collective_id=cid, has_side_effects=True, vmem_limit_bytes=32 * 2**20
        ),
        name="scatter_tp",
    )(value)


def lane_peers():
    ep, tp, z, y, x, core = place()
    to_y, to_x = 1 - 2 * y, 1 - 2 * x
    peer_a = (ep + (1 - core) * to_y, tp + core * 2 * to_x)
    peer_b = (ep + core * to_y, tp + (1 - core) * 2 * to_x)
    sibling = (ep, tp + 1 - 2 * core)
    above, below = (ep + 2, tp), (ep - 2, tp)
    return peer_a, peer_b, sibling, above, below


def lane_spot(z_at, da, db, core_at):
    _, _, _, y, x, _ = place()
    y_at = y + (1 - 2 * y) * ((1 - core_at) * da + core_at * db)
    x_at = x + (1 - 2 * x) * (core_at * da + (1 - core_at) * db)
    return z_at * 2 + y_at, x_at * 2 + core_at


def gather_all_kernel(x_ref, o_ref, up_sem, down_sem, a_sem, b_sem, s_sem, recv_sem, sib_sem, own_sem):
    ep, tp, z, y, x, core = place()
    rows, cols = x_ref.shape
    peer_a, peer_b, sibling, above, below = lane_peers()
    greet([peer_a, peer_b, sibling], True)

    def spot(z_at, da, db):
        group, quarter = lane_spot(z_at, da, db, core)
        return o_ref.at[
            pl.ds(pl.multiple_of(group * rows, rows), rows),
            pl.ds(pl.multiple_of(quarter * cols, cols), cols),
        ]

    def at(z_at, da, db):
        return z_at * 4 + da * 2 + db

    def arrived(z_at, da, db):
        block = spot(z_at, da, db)
        remote(block, block, s_sem.at[at(z_at, da, db)], recv_sem.at[at(z_at, da, db)], sibling).wait_recv()

    def up(z_at, source):
        return remote(source, spot(z_at, 0, 0), up_sem.at[z_at], recv_sem.at[at(z_at, 0, 0)], above)

    def down(z_at, source):
        return remote(source, spot(z_at, 0, 0), down_sem.at[z_at], recv_sem.at[at(z_at, 0, 0)], below)

    def over_a(z_at, source):
        return remote(source, spot(z_at, 0, 0), a_sem.at[z_at], recv_sem.at[at(z_at, 1, 0)], peer_a)

    def over_b(z_at, da, source):
        return remote(
            source, spot(z_at, da, 0), b_sem.at[z_at * 2 + da], recv_sem.at[at(z_at, da, 1)], peer_b
        )

    def to_sibling(z_at, da, db, source):
        n = at(z_at, da, db)
        return remote(source, spot(z_at, da, db), s_sem.at[n], sib_sem.at[n], sibling)

    own = pltpu.make_async_copy(x_ref, spot(z, 0, 0), own_sem)
    over_b(z, 0, x_ref).start()
    over_a(z, x_ref).start()

    @pl.when(z < 3)
    def _():
        up(z, x_ref).start()

    @pl.when(z > 0)
    def _():
        down(z, x_ref).start()

    to_sibling(z, 0, 0, x_ref).start()
    own.start()

    def from_a(z_at):
        arrived(z_at, 1, 0)
        block = spot(z_at, 1, 0)
        over_b(z_at, 1, block).start()
        to_sibling(z_at, 1, 0, block).start()

    def from_z(z_at, onward):
        arrived(z_at, 0, 0)
        block = spot(z_at, 0, 0)
        onward(block)
        over_a(z_at, block).start()
        over_b(z_at, 0, block).start()
        to_sibling(z_at, 0, 0, block).start()

    def from_below(z_at):
        def onward(block):
            @pl.when(z < 3)
            def _():
                up(z_at, block).start()

        from_z(z_at, onward)

    def from_above(z_at):
        def onward(block):
            @pl.when(z > 0)
            def _():
                down(z_at, block).start()

        from_z(z_at, onward)

    for d in range(1, 4):

        @pl.when(z >= d)
        def _(d=d):
            from_below(z - d)

        @pl.when(z + d <= 3)
        def _(d=d):
            from_above(z + d)

        if d == 1:
            from_a(z)
        else:

            @pl.when(z >= d - 1)
            def _(d=d):
                from_a(z - d + 1)

            @pl.when(z + d - 1 <= 3)
            def _(d=d):
                from_a(z + d - 1)

    @pl.when(z >= 3)
    def _():
        from_a(z - 3)

    @pl.when(z + 3 <= 3)
    def _():
        from_a(z + 3)

    def from_b(z_at, da):
        arrived(z_at, da, 1)
        to_sibling(z_at, da, 1, spot(z_at, da, 1)).start()

    for da in range(2):
        from_b(z, da)
    for d in range(1, 4):
        for da in range(2):

            @pl.when(z >= d)
            def _(d=d, da=da):
                from_b(z - d, da)

            @pl.when(z + d <= 3)
            def _(d=d, da=da):
                from_b(z + d, da)

    def finish_sibling(i, carry):
        block = spot(0, 0, 0)
        copy = remote(block, block, s_sem.at[i], sib_sem.at[i], sibling)
        copy.wait_recv()
        copy.wait_send()
        return carry

    lax.fori_loop(0, 16, finish_sibling, 0)

    def finish_links(i, carry):
        over_a(i, x_ref).wait_send()
        over_b(i, 0, x_ref).wait_send()
        over_b(i, 1, x_ref).wait_send()

        @pl.when((z < 3) & (i <= z))
        def _():
            up(i, x_ref).wait_send()

        @pl.when((z > 0) & (i >= z))
        def _():
            down(i, x_ref).wait_send()

        return carry

    lax.fori_loop(0, 4, finish_links, 0)
    own.wait()


def gather_all(value, cid):
    rows, cols = value.shape
    return pl.pallas_call(
        gather_all_kernel,
        out_shape=jax.ShapeDtypeStruct((8 * rows, 4 * cols), value.dtype),
        in_specs=[pl.BlockSpec(memory_space=pl.ANY)],
        out_specs=pl.BlockSpec(memory_space=pl.ANY),
        scratch_shapes=[
            pltpu.SemaphoreType.DMA((4,)),
            pltpu.SemaphoreType.DMA((4,)),
            pltpu.SemaphoreType.DMA((4,)),
            pltpu.SemaphoreType.DMA((8,)),
            pltpu.SemaphoreType.DMA((16,)),
            pltpu.SemaphoreType.DMA((16,)),
            pltpu.SemaphoreType.DMA((16,)),
            pltpu.SemaphoreType.DMA,
        ],
        compiler_params=pltpu.CompilerParams(collective_id=cid, has_side_effects=True),
        name="gather_all",
    )(value)


def z_chain(blocks, totals, from_below, from_above, up_send, up_recv, down_send, down_recv, rows, final):
    ep, tp, z, _, _, _ = place()
    above, below = (ep + 2, tp), (ep - 2, tp)

    def up(z_at):
        return remote(totals(z_at), from_below.at[z_at], up_send.at[z_at], up_recv.at[z_at], above)

    def down(z_at):
        return remote(totals(z_at), from_above.at[z_at], down_send.at[z_at], down_recv.at[z_at], below)

    for z_at in Z_ORDER:
        blocks(z_at)

        @pl.when(z_at > z)
        def _(z_at=z_at):
            @pl.when(z > 0)
            def _():
                up(z_at).wait_recv()
                add_blocks(totals(z_at), [from_below.at[z_at]], rows)

            up(z_at).start()

        @pl.when(z_at < z)
        def _(z_at=z_at):
            @pl.when(z < 3)
            def _():
                down(z_at).wait_recv()
                add_blocks(totals(z_at), [from_above.at[z_at]], rows)

            down(z_at).start()

    for z_at in range(4):

        @pl.when(z_at == z)
        def _(z_at=z_at):
            @pl.when(z > 0)
            def _():
                up(z_at).wait_recv()

            @pl.when(z < 3)
            def _():
                down(z_at).wait_recv()

            @pl.when(z == 0)
            def _():
                final(z_at, [from_above.at[z_at]])

            @pl.when(z == 3)
            def _():
                final(z_at, [from_below.at[z_at]])

            @pl.when((z > 0) & (z < 3))
            def _():
                final(z_at, [from_below.at[z_at], from_above.at[z_at]])

    for z_at in range(4):

        @pl.when(z_at > z)
        def _(z_at=z_at):
            up(z_at).wait_send()

        @pl.when(z_at < z)
        def _(z_at=z_at):
            down(z_at).wait_send()


def scatter_all_kernel(
    p_ref,
    o_ref,
    mine,
    from_sib,
    from_b,
    from_a,
    from_below,
    from_above,
    own_sem,
    s_send,
    s_recv,
    b_send,
    b_recv,
    a_send,
    a_recv,
    up_send,
    up_recv,
    down_send,
    down_recv,
):
    ep, tp, z, y, x, core = place()
    rows, cols = o_ref.shape
    peer_a, peer_b, sibling, above, below = lane_peers()
    greet([peer_a, peer_b, sibling], True)

    def part(z_at, da, db, core_at):
        group, quarter = lane_spot(z_at, da, db, core_at)
        return p_ref.at[
            pl.ds(pl.multiple_of(group * rows, rows), rows),
            pl.ds(pl.multiple_of(quarter * cols, cols), cols),
        ]

    def at(z_at, da, db):
        return z_at * 4 + da * 2 + db

    def own(z_at, da, db):
        n = at(z_at, da, db)
        return pltpu.make_async_copy(part(z_at, da, db, core), mine.at[n], own_sem.at[n])

    def to_sibling(z_at, da, db):
        n = at(z_at, da, db)
        return remote(
            part(z_at, da, db, 1 - core), from_sib.at[n], s_send.at[n], s_recv.at[n], sibling
        )

    for da, db in ((1, 1), (0, 1), (1, 0), (0, 0)):
        for z_at in Z_ORDER:
            to_sibling(z_at, da, db).start()
            own(z_at, da, db).start()

    def here(z_at, da, db):
        own(z_at, da, db).wait()
        to_sibling(z_at, da, db).wait_recv()
        return mine.at[at(z_at, da, db)], from_sib.at[at(z_at, da, db)]

    def over_b(z_at, da):
        n = z_at * 2 + da
        return remote(mine.at[at(z_at, da, 1)], from_b.at[n], b_send.at[n], b_recv.at[n], peer_b)

    def over_a(z_at):
        return remote(mine.at[at(z_at, 1, 0)], from_a.at[z_at], a_send.at[z_at], a_recv.at[z_at], peer_a)

    for da in (1, 0):
        for z_at in Z_ORDER:
            own_part, sib_part = here(z_at, da, 1)
            add_blocks(own_part, [sib_part], rows)
            over_b(z_at, da).start()
    for z_at in Z_ORDER:
        own_part, sib_part = here(z_at, 1, 0)
        over_b(z_at, 1).wait_recv()
        add_blocks(own_part, [sib_part, from_b.at[z_at * 2 + 1]], rows)
        over_a(z_at).start()

    def blocks(z_at):
        own_part, sib_part = here(z_at, 0, 0)
        over_b(z_at, 0).wait_recv()
        over_a(z_at).wait_recv()
        add_blocks(own_part, [sib_part, from_b.at[z_at * 2], from_a.at[z_at]], rows)

    def final(z_at, others):
        o_ref[...] = jnp.zeros_like(o_ref)
        add_blocks(o_ref, [mine.at[at(z_at, 0, 0)], *others], rows)

    z_chain(
        blocks,
        lambda z_at: mine.at[at(z_at, 0, 0)],
        from_below,
        from_above,
        up_send,
        up_recv,
        down_send,
        down_recv,
        rows,
        final,
    )
    for z_at in range(4):
        over_a(z_at).wait_send()
        for da in range(2):
            over_b(z_at, da).wait_send()
            for db in range(2):
                to_sibling(z_at, da, db).wait_send()


def scatter_all(value, cid):
    rows, cols = value.shape[0] // 8, value.shape[1] // 4
    dma = pltpu.SemaphoreType.DMA

    def held(count):
        return pltpu.VMEM((count, rows, cols), value.dtype)

    return pl.pallas_call(
        scatter_all_kernel,
        out_shape=jax.ShapeDtypeStruct((rows, cols), jnp.float32),
        in_specs=[pl.BlockSpec(memory_space=pl.ANY)],
        out_specs=pl.BlockSpec(memory_space=pltpu.VMEM),
        scratch_shapes=[held(16), held(16), held(8), held(4), held(4), held(4)]
        + [dma((16,)), dma((16,)), dma((16,)), dma((8,)), dma((8,))]
        + [dma((4,))] * 6,
        compiler_params=pltpu.CompilerParams(
            collective_id=cid, has_side_effects=True, vmem_limit_bytes=48 * 2**20
        ),
        name="scatter_all",
    )(value)


def scatter_ep_kernel(
    p_ref, e_ref, o_ref, mine, from_y, from_below, from_above, own_sem, y_send, y_recv, up_send, up_recv, down_send, down_recv
):
    ep, tp, z, y, _, _ = place()
    rows, extra = p_ref.shape[0] // 8, e_ref.shape[0]
    tall = rows + extra
    across = (ep + 1 - 2 * y, tp)
    greet([across], True)

    def part(z_at, y_at):
        return p_ref.at[pl.ds(pl.multiple_of((z_at * 2 + y_at) * rows, rows), rows), :]

    def own(z_at):
        return (
            pltpu.make_async_copy(part(z_at, y), mine.at[z_at, pl.ds(0, rows)], own_sem.at[z_at]),
            pltpu.make_async_copy(e_ref, mine.at[z_at, pl.ds(rows, extra)], own_sem.at[4 + z_at]),
        )

    def over_y(z_at):
        return (
            remote(
                part(z_at, 1 - y),
                from_y.at[z_at, pl.ds(0, rows)],
                y_send.at[z_at],
                y_recv.at[z_at],
                across,
            ),
            remote(
                e_ref,
                from_y.at[z_at, pl.ds(rows, extra)],
                y_send.at[4 + z_at],
                y_recv.at[4 + z_at],
                across,
            ),
        )

    for z_at in Z_ORDER:
        for copy in over_y(z_at) + own(z_at):
            copy.start()

    def blocks(z_at):
        for copy in own(z_at):
            copy.wait()
        for copy in over_y(z_at):
            copy.wait_recv()
        add_blocks(mine.at[z_at], [from_y.at[z_at]], tall)

    def final(z_at, others):
        o_ref[...] = jnp.zeros_like(o_ref)
        add_blocks(o_ref, [mine.at[z_at], *others], tall)

    z_chain(
        blocks,
        lambda z_at: mine.at[z_at],
        from_below,
        from_above,
        up_send,
        up_recv,
        down_send,
        down_recv,
        tall,
        final,
    )
    for z_at in range(4):
        for copy in over_y(z_at):
            copy.wait_send()


def scatter_ep(value, extra, cid):
    rows, cols = value.shape[0] // 8, value.shape[1]
    tall = rows + extra.shape[0]
    dma = pltpu.SemaphoreType.DMA

    def held():
        return pltpu.VMEM((4, tall, cols), value.dtype)

    return pl.pallas_call(
        scatter_ep_kernel,
        out_shape=jax.ShapeDtypeStruct((tall, cols), jnp.float32),
        in_specs=[pl.BlockSpec(memory_space=pl.ANY)] * 2,
        out_specs=pl.BlockSpec(memory_space=pltpu.VMEM),
        scratch_shapes=[held(), held(), held(), held()] + [dma((8,))] * 3 + [dma((4,))] * 4,
        compiler_params=pltpu.CompilerParams(
            collective_id=cid, has_side_effects=True, vmem_limit_bytes=40 * 2**20
        ),
        name="scatter_ep",
    )(value, extra)


def experts_kernel(
    expert_width,
    shared_width,
    expert_total,
    x_ref,
    g_ref,
    kept_ref,
    expert_gate_ref,
    shared_gate_ref,
    extra_ref,
    expert_up_ref,
    shared_up_ref,
    expert_down_ref,
    shared_down_ref,
    residual_ref,
    grad_ref,
    mixed_ref,
    logit_ref,
    expert_grads_ref,
    shared_grads_ref,
    all_ref,
    from_sib,
    from_b,
    from_a,
    from_z,
    in_ref,
    down_ref,
    scalars,
    kept_held,
    x_held,
    g_held,
    lin,
    hidden_grad,
    hidden_all,
    both_all,
    kept_cols,
    staged,
    mine,
    landed,
    x_tile,
    g_tile,
    tile_out,
    shared_out,
    up_sem,
    down_sem,
    a_sem,
    b_sem,
    s_sem,
    recv_sem,
    sib_sem,
    own_sem,
    load_sem,
    fetch_sem,
    store_sem,
    weight_sem,
    kept_send,
    kept_recv,
    rs_send,
    rs_recv,
    rb_send,
    rb_recv,
    ra_send,
    ra_recv,
    rz_send,
    rz_recv,
):
    ep, tp, z, y, x, core = place()
    rows, cols = x_ref.shape
    width = down_ref.shape[0]
    filled = expert_width + shared_width
    tall = mine.shape[1]
    out_at = rows + 16
    cuts = ((0, out_at), (out_at, tall - out_at))
    peer_a, peer_b, sibling, above, below = lane_peers()
    sources = kept_held.shape[0]
    others = [(lax.rem(ep + i, sources), tp) for i in range(1, sources)]
    greet([(ep, tp + 2 - 4 * x), sibling] + others)

    def spot(z_at, da, db):
        group, quarter = lane_spot(z_at, da, db, core)
        return all_ref.at[
            pl.ds(pl.multiple_of(group * rows, rows), rows),
            pl.ds(pl.multiple_of(quarter * cols, cols), cols),
        ]

    def at(z_at, da, db):
        return z_at * 4 + da * 2 + db

    def choose(*values):
        return jnp.where(
            z == 0, values[0], jnp.where(z == 1, values[1], jnp.where(z == 2, values[2], values[3]))
        )

    coming = (z, choose(1, 2, 1, 2), choose(2, 0, 3, 1), choose(3, 3, 0, 0))
    turns = (z, choose(1, 2, 1, 2), choose(3, 3, 0, 0), choose(2, 0, 3, 1))

    def arrived(z_at, da, db):
        block, n = spot(z_at, da, db), at(z_at, da, db)
        remote(block, block, s_sem.at[n], recv_sem.at[n], sibling).wait_recv()
        return block

    def up(z_at, source):
        return remote(source, spot(z_at, 0, 0), up_sem.at[z_at], recv_sem.at[at(z_at, 0, 0)], above)

    def down(z_at, source):
        return remote(source, spot(z_at, 0, 0), down_sem.at[z_at], recv_sem.at[at(z_at, 0, 0)], below)

    def over_a(z_at, source):
        return remote(source, spot(z_at, 0, 0), a_sem.at[z_at], recv_sem.at[at(z_at, 1, 0)], peer_a)

    def over_b(z_at, da, source):
        return remote(
            source, spot(z_at, da, 0), b_sem.at[z_at * 2 + da], recv_sem.at[at(z_at, da, 1)], peer_b
        )

    def to_sibling(z_at, da, db, source):
        n = at(z_at, da, db)
        return remote(source, spot(z_at, da, db), s_sem.at[n], sib_sem.at[n], sibling)

    def pass_z(z_at):
        block = arrived(z_at, 0, 0)

        @pl.when((z_at > z) & (z > 0))
        def _():
            down(z_at, block).start()

        @pl.when((z_at < z) & (z < 3))
        def _():
            up(z_at, block).start()

        over_a(z_at, block).start()
        over_b(z_at, 0, block).start()
        to_sibling(z_at, 0, 0, block).start()

    def pass_a(z_at, onward=True):
        block = arrived(z_at, 1, 0)
        if onward:
            over_b(z_at, 1, block).start()
        to_sibling(z_at, 1, 0, block).start()

    def pass_b(z_at, da):
        block = arrived(z_at, da, 1)
        to_sibling(z_at, da, 1, block).start()

    def sibling_blocks(k, dy):
        for dx in range(2):
            da, db = core * dy + (1 - core) * dx, core * dx + (1 - core) * dy
            n = at(turns[k], da, db)
            block = spot(0, 0, 0)
            remote(block, block, s_sem.at[n], sib_sem.at[n], sibling).wait_recv()

    def group_rows(k, dy):
        group = turns[k] * 2 + y + (1 - 2 * y) * dy
        return group, pl.ds(pl.multiple_of(group * rows, rows), rows)

    def load_x(k, dy):
        _, span = group_rows(k, dy)
        return pltpu.make_async_copy(all_ref.at[span, :], x_held, load_sem.at[0])

    def load_g(k, dy):
        _, span = group_rows(k, dy)
        return pltpu.make_async_copy(g_ref.at[span, :], g_held, load_sem.at[1])

    def project():
        def body(i, carry):
            cut = pl.ds(pl.multiple_of(i * width, width), width)
            lin[:, cut] = times_transpose(x_held[...], in_ref[cut, :])
            return carry

        lax.fori_loop(0, 2, body, 0)

    def project_grad():
        hidden_grad[...] = times_transpose(g_held[...], down_ref[...])

    step = 64
    tile_start = width - 128
    logit_at = filled - tile_start

    def activate(k, dy):
        group, _ = group_rows(k, dy)
        lane = lax.broadcasted_iota(jnp.int32, (1, width), 1)
        near = lax.broadcasted_iota(jnp.int32, (1, 128), 1)
        is_logit = (near >= logit_at) & (near < logit_at + expert_total)
        kept_cols[:, :16] = kept_held[group].astype(jnp.float32).T

        def body(i, carry):
            span = pl.ds(pl.multiple_of(i * step, step), step)
            whole = pl.ds(pl.multiple_of(group * rows + i * step, step), step)
            gate_lin, up_lin = lin[span, :width], lin[span, width:]
            grad = hidden_grad[span, :]
            tail = lin[span, tile_start:width]
            if k == 0 and dy == 0:
                logit_ref[span, :] = tail
            most = jnp.max(jnp.where(is_logit, tail, -1e30), axis=1, keepdims=True)
            powers = jnp.where(is_logit, jnp.exp(jnp.minimum(tail - most, 0.0)), 0.0)
            kept = jnp.sum(jnp.where(near == ep, kept_cols[span, :], 0.0), axis=1, keepdims=True)
            gate = jnp.sum(jnp.where(near == logit_at + ep, powers, 0.0), axis=1, keepdims=True)
            gate = gate / jnp.sum(powers, axis=1, keepdims=True) * kept
            switch = jax.nn.sigmoid(
                jnp.sum(
                    jnp.where(near == logit_at + expert_total, tail, 0.0), axis=1, keepdims=True
                )
            )
            scale = jnp.where(lane < expert_width, gate, switch)
            sig = jax.nn.sigmoid(gate_lin)
            act = gate_lin * sig
            hidden = act * up_lin
            agreement = hidden * grad
            gate_part = jnp.sum(jnp.where(lane < expert_width, agreement, 0.0), axis=1, keepdims=True)
            switch_part = jnp.sum(
                jnp.where(lane < expert_width, 0.0, agreement), axis=1, keepdims=True
            )
            scaled = grad * scale
            hidden_all[whole, :] = (hidden * scale).astype(jnp.bfloat16)
            both_all[whole, :width] = (
                scaled * up_lin * sig * (1.0 + gate_lin * (1.0 - sig))
            ).astype(jnp.bfloat16)
            both_all[whole, width:] = (scaled * act).astype(jnp.bfloat16)
            scalars[span, :] = jnp.where(
                near == ep, gate_part, jnp.where(near == expert_total, switch_part, 0.0)
            )
            return carry

        lax.fori_loop(0, rows // step, body, 0)

    def hold(k, da, db):
        slot = 2 if k == 0 else k % 2
        return db * (7 + slot * 2 + da) + (1 - db) * (da * (4 + slot) + (1 - da) * k)

    def lane_offsets(dx, dy, core_at):
        return (1 - core_at) * dy + core_at * dx, (1 - core_at) * dx + core_at * dy

    def rs_sibling(k, dx, dy):
        n = at(turns[k], *lane_offsets(dx, dy, 1 - core))
        return remote(staged.at[dx], from_sib.at[n], rs_send.at[n], rs_recv.at[n], sibling)

    def block_rows(k, dy):
        sums = scalars[...].T[:16, :].astype(jnp.bfloat16)
        _, span = group_rows(k, dy)

        def fill(target, cut):
            target[:rows, :] = jnp.dot(
                both_all[span, :], in_ref[:, cut], preferred_element_type=jnp.float32
            ).astype(jnp.bfloat16)
            target[rows:out_at, :] = sums
            target[out_at:, :] = jnp.dot(
                hidden_all[span, :], down_ref[:, cut], preferred_element_type=jnp.float32
            ).astype(jnp.bfloat16)

        def body(dx, carry):
            x_at = x + (1 - 2 * x) * dx
            fill(staged.at[dx], pl.ds(pl.multiple_of((x_at * 2 + 1 - core) * cols, cols), cols))
            rs_sibling(k, dx, dy).start()
            fill(
                mine.at[hold(k, *lane_offsets(dx, dy, core))],
                pl.ds(pl.multiple_of((x_at * 2 + core) * cols, cols), cols),
            )
            return carry

        lax.fori_loop(0, 2, body, 0)

    def staged_free(k, dy):
        for dx in range(2):
            rs_sibling(k, dx, dy).wait_send()

    def rs_over_b(k, da, part):
        n, span = turns[k] * 2 + da, pl.ds(*cuts[part])
        return remote(
            mine.at[hold(k, da, 1), span],
            from_b.at[n, span],
            rb_send.at[n * 2 + part],
            rb_recv.at[n * 2 + part],
            peer_b,
        )

    def rs_over_a(k, part):
        z_at, span = turns[k], pl.ds(*cuts[part])
        return remote(
            mine.at[hold(k, 1, 0), span],
            from_a.at[z_at, span],
            ra_send.at[z_at * 2 + part],
            ra_recv.at[z_at * 2 + part],
            peer_a,
        )

    def rs_along_z(k, part):
        span = pl.ds(*cuts[part])
        return remote(
            mine.at[k, span],
            from_z.at[z, span],
            rz_send.at[k * 2 + part],
            rz_recv.at[z * 2 + part],
            (ep + 2 * (turns[k] - z), tp),
        )

    def fetch(source, i):
        return pltpu.make_async_copy(source, landed.at[i], fetch_sem.at[i])

    def fetch_part(source, half, i):
        span = pl.ds(*cuts[half])
        return pltpu.make_async_copy(source.at[span], landed.at[i, span], fetch_sem.at[i])

    def fetch_sibling(k, dy):
        for dx in range(2):
            n = at(turns[k], *lane_offsets(dx, dy, core))
            remote(staged.at[0], from_sib.at[n], rs_send.at[n], rs_recv.at[n], sibling).wait_recv()
            fetch(from_sib.at[n], dx).start()

    def reduce_sibling(k, dy):
        for dx in range(2):
            n = at(turns[k], *lane_offsets(dx, dy, core))
            fetch(from_sib.at[n], dx).wait()
            add_blocks(mine.at[hold(k, *lane_offsets(dx, dy, core))], [landed.at[dx]], tall)

        for part in range(2):

            @pl.when(core == 0)
            def _(part=part):
                rs_over_b(k, dy, part).start()

            if dy == 1:

                @pl.when(core == 1)
                def _(part=part):
                    rs_over_b(k, 0, part).start()
                    rs_over_b(k, 1, part).start()

    def add_part(target, part, copies):
        first, count = cuts[part]
        span = pl.ds(first, count)
        for copy in copies:
            copy.wait()
        add_blocks(
            mine.at[target, span], [landed.at[i, span] for i in range(len(copies))], count
        )

    def reduce_b(k, part):
        rs_over_b(k, 1, part).wait_recv()
        copy = fetch_part(from_b.at[turns[k] * 2 + 1], part, 0)
        copy.start()
        add_part(hold(k, 1, 0), part, [copy])
        rs_over_a(k, part).start()

    def reduce_a(k, part):
        z_at = turns[k]
        rs_over_b(k, 0, part).wait_recv()
        rs_over_a(k, part).wait_recv()
        copies = [
            fetch_part(from_b.at[z_at * 2], part, 0),
            fetch_part(from_a.at[z_at], part, 1),
        ]
        for copy in copies:
            copy.start()
        add_part(k, part, copies)
        if k > 0:
            rs_along_z(k, part).start()

    def reduce_z(i, part):
        source = (choose(3, 0, 3, 0), choose(2, 2, 1, 1), choose(1, 3, 0, 2))[i]
        span = pl.ds(*cuts[part])
        remote(
            mine.at[0, span],
            from_z.at[source, span],
            rz_send.at[0],
            rz_recv.at[source * 2 + part],
            sibling,
        ).wait_recv()
        copy = fetch_part(from_z.at[source], part, 0)
        copy.start()
        add_part(0, part, [copy])

    tile = x_tile.shape[1]

    def load_tile(source, target, t, sem):
        cut = pl.ds(pl.multiple_of(t * tile, tile), tile)
        return pltpu.make_async_copy(source.at[:, cut], target, load_sem.at[sem])

    def tile_stores(t, kind):
        cut = pl.ds(pl.multiple_of(t * tile, tile), tile)
        return (
            pltpu.make_async_copy(
                tile_out.at[kind, pl.ds(0, expert_width)],
                expert_grads_ref.at[kind, :, cut],
                store_sem.at[kind],
            ),
            pltpu.make_async_copy(
                shared_out.at[kind], shared_grads_ref.at[t, kind], store_sem.at[3 + kind]
            ),
        )

    def weight_tile(t, kind):
        @pl.when(t > 0)
        def _():
            for copy in tile_stores(t - 1, kind):
                copy.wait()

        if kind == 0:
            left, right = hidden_all[:, :filled], g_tile[...]
        else:
            left, right = both_all[:, (kind - 1) * width : (kind - 1) * width + filled], x_tile[...]
        result = inner_rows(left, right)
        tile_out[kind] = result
        shared_out[kind] = result[expert_width:, :].astype(jnp.bfloat16)
        for copy in tile_stores(t, kind):
            copy.start()

    own = pltpu.make_async_copy(x_ref, spot(z, 0, 0), own_sem)
    over_b(z, 0, x_ref).start()
    over_a(z, x_ref).start()

    @pl.when(z < 3)
    def _():
        up(z, x_ref).start()

    @pl.when(z > 0)
    def _():
        down(z, x_ref).start()

    to_sibling(z, 0, 0, x_ref).start()
    own.start()
    load_g(0, 0).start()

    def kept_to(i):
        return remote(
            kept_ref, kept_held.at[ep], kept_send.at[i - 1], kept_recv.at[i - 1], others[i - 1]
        )

    for i in range(1, sources):
        kept_to(i).start()
    own_kept = pltpu.make_async_copy(kept_ref, kept_held.at[ep], weight_sem.at[7])
    own_kept.start()
    pieces = [
        (expert_down_ref, down_ref, 0),
        (
            shared_down_ref.at[pl.ds(pl.multiple_of(ep * shared_width, 16), shared_width), :],
            down_ref,
            expert_width,
        ),
        (expert_gate_ref, in_ref, 0),
        (shared_gate_ref, in_ref, expert_width),
        (extra_ref, in_ref, filled),
        (expert_up_ref, in_ref, width),
        (shared_up_ref, in_ref, width + expert_width),
    ]
    weight_copies = [
        pltpu.make_async_copy(piece, target.at[pl.ds(at_row, piece.shape[0]), :], weight_sem.at[i])
        for i, (piece, target, at_row) in enumerate(pieces)
    ]
    for copy in weight_copies:
        copy.start()
    for target, first, last_row in (
        (in_ref, filled + 16, width),
        (in_ref, width + filled, 2 * width),
        (down_ref, filled, width),
    ):
        target[first:last_row, :] = jnp.zeros((last_row - first, target.shape[1]), target.dtype)
    for copy in weight_copies:
        copy.wait()
    load_g(0, 0).wait()
    project_grad()
    own_kept.wait()
    for i in range(1, sources):
        kept_to(i).wait_recv()
    own.wait()

    def ready(k, dy):
        if k > 0:
            pass_b(turns[k], dy)
        sibling_blocks(k, dy)
        load_x(k, dy).start()

    order = [(0, 0)] + [(k, dy) for k in range(1, 4) for dy in range(2)] + [(0, 1)]
    edge = (z == 0) | (z == 3)
    pass_z(coming[1])
    pass_a(z, False)
    pass_b(z, 0)

    @pl.when(jnp.logical_not(edge))
    def _():
        pass_z(coming[2])

    ready(0, 0)
    for s, (k, dy) in enumerate(order):
        following = order[s + 1] if s < 7 else None
        load_x(k, dy).wait()
        if s >= 1:
            fetch_sibling(*order[s - 1])
        project()
        if s >= 1:
            load_g(k, dy).wait()
            project_grad()
        if following is not None:
            load_g(*following).start()
        if s >= 1:
            reduce_sibling(*order[s - 1])
        if s == 1:
            pass_z(coming[3])
            over_b(z, 1, spot(z, 1, 0)).start()
        if s in (4, 6):
            reduce_b(s // 2 - 1, 0)
        activate(k, dy)
        if s == 0:

            @pl.when(edge)
            def _():
                pass_z(coming[2])

            pass_a(coming[1])
        if s == 1:
            pass_a(coming[2])
        if s == 2:
            pass_a(coming[3])
        if s == 4:
            pass_b(z, 1)
        if following is not None:
            ready(*following)
        if s in (4, 6):
            reduce_b(s // 2 - 1, 1)
        if s in (5, 7):
            reduce_a((s - 3) // 2, 0)
        if s >= 1:
            staged_free(*order[s - 1])
        if s == 5:
            for part in range(2):
                for da in range(2):
                    rs_over_b(1, da, part).wait_send()
                rs_over_a(1, part).wait_send()
        block_rows(k, dy)
        if s in (5, 7):
            reduce_a((s - 3) // 2, 1)

    load_tile(g_ref, g_tile, 0, 2).start()
    load_tile(all_ref, x_tile, 0, 3).start()
    tiles = shared_grads_ref.shape[0]
    services = {
        (0, 0): (fetch_sibling, 0, 1),
        (0, 1): (reduce_sibling, 0, 1),
        (1, 0): (reduce_b, 3, 0),
        (0, 2): (reduce_z, 0, 0),
        (1, 1): (reduce_z, 0, 1),
        (2, 0): (reduce_z, 1, 0),
        (3, 0): (reduce_z, 1, 1),
        (4, 0): (reduce_b, 3, 1),
        (4, 2): (reduce_a, 3, 0),
        (5, 1): (reduce_b, 0, 0),
        (6, 2): (reduce_a, 3, 1),
        (7, 0): (reduce_b, 0, 1),
    }

    def tile_step(t, carry):
        for kind in range(3):
            if kind == 0:
                load_tile(g_ref, g_tile, t, 2).wait()
            if kind == 1:
                load_tile(all_ref, x_tile, t, 3).wait()
            weight_tile(t, kind)

            @pl.when(t + 1 < tiles)
            def _(kind=kind):
                if kind == 0:
                    load_tile(g_ref, g_tile, t + 1, 2).start()
                if kind == 2:
                    load_tile(all_ref, x_tile, t + 1, 3).start()

            for (at_tile, at_kind), (service, *which) in services.items():
                if at_kind == kind:
                    pl.when(t == at_tile)(functools.partial(service, *which))
        return carry

    lax.fori_loop(0, tiles, tile_step, 0)
    for kind in range(3):
        for copy in tile_stores(tiles - 1, kind):
            copy.wait()

    for part in range(2):
        reduce_a(0, part)
        reduce_z(2, part)

    def total(i, carry):
        span = pl.ds(pl.multiple_of(i * 64, 64), 64)
        out_span = pl.ds(pl.multiple_of(out_at + i * 64, 16), 64)
        grad_ref[span, :] = mine[0, span, :].astype(jnp.float32)
        mixed_ref[span, :] = (
            residual_ref[span, :] + mine[0, out_span, :].astype(jnp.float32)
        ).astype(jnp.bfloat16)
        return carry

    lax.fori_loop(0, rows // 64, total, 0)
    grad_ref[rows:, :] = mine[0, rows:out_at, :].astype(jnp.float32)

    for i in range(1, sources):
        kept_to(i).wait_send()
    staged_free(0, 1)
    for k in range(1, 4):
        for part in range(2):
            rs_along_z(k, part).wait_send()
    for k in (0, 2, 3):
        for part in range(2):
            rs_over_a(k, part).wait_send()
            for da in range(2):
                rs_over_b(k, da, part).wait_send()

    def finish(i, carry):
        over_a(i, x_ref).wait_send()
        over_b(i, 0, x_ref).wait_send()
        over_b(i, 1, x_ref).wait_send()
        for n in range(4):
            block = spot(0, 0, 0)
            remote(block, block, s_sem.at[i * 4 + n], sib_sem.at[i * 4 + n], sibling).wait_send()

        @pl.when((z < 3) & (i <= z))
        def _():
            up(i, x_ref).wait_send()

        @pl.when((z > 0) & (i >= z))
        def _():
            down(i, x_ref).wait_send()

        return carry

    lax.fori_loop(0, 4, finish, 0)


def experts(x_cols, grads_all, kept_rows, weights, residual, expert_total, cid):
    rows, cols = x_cols.shape
    total, model_dim = grads_all.shape
    sources = total // rows
    expert_width, shared_width = weights[0].shape[0], weights[1].shape[0]
    filled = expert_width + shared_width
    width = -(-(filled + expert_total + 1) // 128) * 128
    tall = 2 * rows + 16
    tile = model_dim // sources
    low, dma = jnp.bfloat16, pltpu.SemaphoreType.DMA
    vmem, hbm = pl.BlockSpec(memory_space=pltpu.VMEM), pl.BlockSpec(memory_space=pl.ANY)

    def landing(count):
        return jax.ShapeDtypeStruct((count, tall, cols), low)

    return pl.pallas_call(
        functools.partial(experts_kernel, expert_width, shared_width, expert_total),
        out_shape=[
            jax.ShapeDtypeStruct((rows + 16, cols), jnp.float32),
            jax.ShapeDtypeStruct((rows, cols), low),
            jax.ShapeDtypeStruct((rows, 128), jnp.float32),
            jax.ShapeDtypeStruct((3, expert_width, model_dim), jnp.float32),
            jax.ShapeDtypeStruct((sources, 3, shared_width, tile), low),
            jax.ShapeDtypeStruct((total, model_dim), low),
            landing(16),
            landing(8),
            landing(4),
            landing(4),
        ],
        in_specs=[hbm] * 10 + [vmem],
        out_specs=[vmem, vmem, vmem] + [hbm] * 7,
        scratch_shapes=[
            pltpu.VMEM((2 * width, model_dim), low),
            pltpu.VMEM((width, model_dim), low),
            pltpu.VMEM((rows, 128), jnp.float32),
            pltpu.VMEM((sources, 16, rows), low),
            pltpu.VMEM((rows, model_dim), low),
            pltpu.VMEM((rows, model_dim), low),
            pltpu.VMEM((rows, 2 * width), jnp.float32),
            pltpu.VMEM((rows, width), jnp.float32),
            pltpu.VMEM((total, width), low),
            pltpu.VMEM((total, 2 * width), low),
            pltpu.VMEM((rows, 128), jnp.float32),
            pltpu.VMEM((2, tall, cols), low),
            pltpu.VMEM((13, tall, cols), low),
            pltpu.VMEM((2, tall, cols), low),
            pltpu.VMEM((total, tile), low),
            pltpu.VMEM((total, tile), low),
            pltpu.VMEM((3, filled, tile), jnp.float32),
            pltpu.VMEM((3, shared_width, tile), low),
        ]
        + [dma((4,)), dma((4,)), dma((4,)), dma((8,)), dma((16,)), dma((16,)), dma((16,)), dma]
        + [dma((4,)), dma((2,)), dma((6,)), dma((8,)), dma((7,)), dma((7,))]
        + [dma((16,))] * 4
        + [dma((8,))] * 4,
        compiler_params=pltpu.CompilerParams(
            collective_id=cid, has_side_effects=True, vmem_limit_bytes=63 * 2**20
        ),
        name="experts",
    )(x_cols, grads_all, kept_rows, *weights, residual)


def row_of(columns):
    part = columns[:, :128]
    for i in range(1, columns.shape[1] // 128):
        part = part + columns[:, i * 128 : (i + 1) * 128]
    total = jnp.sum(part.T, axis=0, keepdims=True)
    return jnp.broadcast_to(total, (8, total.shape[1]))


def unwind_kernel(
    dn2_ref,
    unit_ref,
    inv_ref,
    second_ref,
    grad_ref,
    tokens_ref,
    inv_one_ref,
    first_ref,
    small_ref,
    q_ref,
    k_ref,
    v_ref,
    ke_ref,
    ve_ref,
    context_ref,
    log_ref,
    cos_ref,
    sin_ref,
    n1_hbm,
    wq_hbm,
    wk_hbm,
    wv_hbm,
    wo_hbm,
    tokens_grad_ref,
    weight_grads_ref,
    sums_ref,
    n1,
    wq,
    wk,
    wv,
    wo,
    grad_all,
    grad_own,
    hidden_grad,
    dc,
    dq,
    dk,
    dv,
    lin_grads,
    dke,
    dve,
    later_k,
    later_v,
    staged,
    mine,
    from_y,
    from_below,
    from_above,
    from_below_2,
    from_above_2,
    tp_staged,
    tp_mine,
    tp_sib,
    tp_x,
    dn1,
    row_mine,
    row_sib,
    row_x,
    smalls,
    quarters,
    load_sem,
    g_send,
    g_recv,
    row_send,
    row_recv,
    kv_send,
    kv_recv,
    y_send,
    y_recv,
    up_send,
    up_recv,
    down_send,
    down_recv,
    tp_send,
    tp_recv,
    small_send,
    small_recv,
    s_send,
    s_recv,
    up2_send,
    up2_recv,
    down2_send,
    down2_recv,
):
    ep, tp, z, y, x, core = place()
    rows, cols = unit_ref.shape
    model_dim = n1.shape[1]
    heads = cols // HD
    block = mine.shape[1]
    low, full = jnp.bfloat16, jnp.float32
    score_scale = HD ** (-0.5)
    sibling, across = (ep, tp + 1 - 2 * core), (ep, tp + 2 - 4 * x)
    beside = (ep + 1 - 2 * y, tp)
    above, below = (ep + 2, tp), (ep - 2, tp)
    sources = smalls.shape[0]
    others = [(lax.rem(ep + i, sources), tp) for i in range(1, sources)]
    loads = [
        pltpu.make_async_copy(source, target, load_sem.at[i])
        for i, (source, target) in enumerate(
            ((wo_hbm, wo), (n1_hbm, n1), (wq_hbm, wq), (wk_hbm, wk), (wv_hbm, wv))
        )
    ]
    for copy in loads:
        copy.start()
    greet([across, sibling] + others)

    step = 64

    def by_rows(body):
        def one(i, carry):
            body(pl.ds(pl.multiple_of(i * step, step), step))
            return carry

        lax.fori_loop(0, rows // step, one, 0)

    def row_exchange(i, values):
        row_mine[2 * i] = values
        first = remote(
            row_mine.at[2 * i], row_sib.at[i], row_send.at[2 * i], row_recv.at[2 * i], sibling
        )
        first.start()
        first.wait_recv()
        row_mine[2 * i + 1] = row_mine[2 * i] + row_sib[i]
        second = remote(
            row_mine.at[2 * i + 1],
            row_x.at[i],
            row_send.at[2 * i + 1],
            row_recv.at[2 * i + 1],
            across,
        )
        second.start()
        second.wait_recv()
        first.wait_send()
        second.wait_send()
        return (row_mine[2 * i + 1] + row_x[i]).T[:, :1]

    dn1[...] = dn2_ref[...] * second_ref[:1, :] * unit_ref[...]
    mean = row_exchange(0, row_of(dn1[...])) * (1.0 / model_dim)
    dn1[:, :128] = jnp.broadcast_to(mean, (rows, 128))

    def norm_two(span):
        scaled = dn2_ref[span, :] * second_ref[:1, :]
        value = grad_ref[span, :].astype(full) + inv_ref[span, :1] * (
            scaled - unit_ref[span, :] * dn1[span, :1]
        )
        hidden_grad[span, :] = value
        grad_own[span, :] = value.astype(low)

    by_rows(norm_two)

    def quarter(at):
        return grad_all.at[:, pl.ds(pl.multiple_of(at * cols, cols), cols)]

    g_x = remote(grad_own, quarter(tp), g_send.at[0], g_recv.at[0], across)
    g_s = remote(grad_own, quarter(tp), g_send.at[1], g_recv.at[1], sibling)
    g_x.start()
    g_s.start()
    own_cut = pl.ds(pl.multiple_of(tp * cols, cols), cols)
    grad_all[:, own_cut] = grad_own[...]
    g_x.wait_recv()
    theirs = quarter(tp + 2 - 4 * x)
    g_f = remote(theirs, theirs, g_send.at[2], g_recv.at[2], sibling)
    g_f.start()
    g_s.wait_recv()
    g_f.wait_recv()
    loads[0].wait()
    dc[...] = times_transpose(grad_all[...], wo[...]).astype(low)

    def over_y(kind, z_at):
        n = kind * 4 + z_at
        return remote(staged.at[n], from_y.at[n], y_send.at[n], y_recv.at[n], beside)

    def weight_blocks(kind, left, right):
        def other(i, carry):
            z_at = lax.rem(i * 3, 4)
            cut = pl.ds(pl.multiple_of((z_at * 2 + 1 - y) * block, block), block)
            staged[kind * 4 + z_at] = inner_rows(left[:, cut], right[...]).astype(low)
            over_y(kind, z_at).start()
            return carry

        def ours(i, carry):
            z_at = lax.rem(i * 3, 4)
            cut = pl.ds(pl.multiple_of((z_at * 2 + y) * block, block), block)
            mine[kind * 4 + z_at] = inner_rows(left[:, cut], right[...]).astype(low)
            return carry

        lax.fori_loop(0, 4, other, 0)
        lax.fori_loop(0, 4, ours, 0)

    def blocks_along_z(left, right):
        def one(i, carry):
            z_at = lax.rem(i * 3, 4)
            cut = pl.ds(pl.multiple_of((z_at * 2 + 1 - y) * block, block), block)
            staged[4 + z_at] = inner_rows(left[:, cut], right[...]).astype(low)
            cut = pl.ds(pl.multiple_of((z_at * 2 + y) * block, block), block)
            mine[4 + z_at] = inner_rows(left[:, cut], right[...]).astype(low)

            @pl.when((z == 0) & (z_at > 0))
            def _():
                up_2(z_at).start()
                up(1, z_at).start()

            @pl.when((z == 3) & (z_at < 3))
            def _():
                down_2(z_at).start()
                down(1, z_at).start()

            return carry

        lax.fori_loop(0, 4, one, 0)

    def up_2(z_at):
        return remote(
            staged.at[4 + z_at], from_below_2.at[z_at], up2_send.at[z_at], up2_recv.at[z_at], above
        )

    def down_2(z_at):
        return remote(
            staged.at[4 + z_at],
            from_above_2.at[z_at],
            down2_send.at[z_at],
            down2_recv.at[z_at],
            below,
        )

    def chain_2():
        def rise(z_at):
            up_2(z_at).wait_recv()
            add_blocks(staged.at[4 + z_at], [from_below_2.at[z_at]], block)
            up_2(z_at).start()

        def fall(z_at):
            down_2(z_at).wait_recv()
            add_blocks(staged.at[4 + z_at], [from_above_2.at[z_at]], block)
            down_2(z_at).start()

        @pl.when(z == 1)
        def _():
            rise(3)
            rise(2)
            fall(0)

        @pl.when(z == 2)
        def _():
            fall(0)
            fall(1)
            rise(3)

    def other_y_along_z():
        @pl.when(z > 0)
        def _():
            up_2(z).wait_recv()
            add_blocks(staged.at[4 + z], [from_below_2.at[z]], block)

        @pl.when(z < 3)
        def _():
            down_2(z).wait_recv()
            add_blocks(staged.at[4 + z], [from_above_2.at[z]], block)

        over_y(1, z).start()

    def own_first_along_z():
        over_y(1, z).wait_recv()
        add_blocks(mine.at[4 + z], [from_y.at[4 + z]], block)

    def up(kind, z_at):
        n = kind * 4 + z_at
        return remote(mine.at[n], from_below.at[n], up_send.at[n], up_recv.at[n], above)

    def down(kind, z_at):
        n = kind * 4 + z_at
        return remote(mine.at[n], from_above.at[n], down_send.at[n], down_recv.at[n], below)

    def y_stage(kind):
        def one(i, carry):
            z_at = lax.rem(i * 3, 4)
            n = kind * 4 + z_at
            over_y(kind, z_at).wait_recv()
            add_blocks(mine.at[n], [from_y.at[n]], block)

            @pl.when((z == 0) & (z_at > 0))
            def _():
                up(kind, z_at).start()

            @pl.when((z == 3) & (z_at < 3))
            def _():
                down(kind, z_at).start()

            return carry

        lax.fori_loop(0, 4, one, 0)

    def chain(kind):
        def rise(z_at):
            n = kind * 4 + z_at
            up(kind, z_at).wait_recv()
            add_blocks(mine.at[n], [from_below.at[n]], block)
            up(kind, z_at).start()

        def fall(z_at):
            n = kind * 4 + z_at
            down(kind, z_at).wait_recv()
            add_blocks(mine.at[n], [from_above.at[n]], block)
            down(kind, z_at).start()

        @pl.when(z == 1)
        def _():
            rise(3)
            rise(2)
            fall(0)

        @pl.when(z == 2)
        def _():
            fall(0)
            fall(1)
            rise(3)

    def final(kind):
        n = kind * 4 + z

        @pl.when(z > 0)
        def _():
            up(kind, z).wait_recv()

        @pl.when(z < 3)
        def _():
            down(kind, z).wait_recv()

        def one(i, carry):
            span = pl.ds(pl.multiple_of(i * 32, 32), 32)
            value = mine[n, span, :].astype(full)
            low_part = from_below[n, span, :].astype(full)
            high_part = from_above[n, span, :].astype(full)
            value = value + jnp.where(z > 0, low_part, 0.0) + jnp.where(z < 3, high_part, 0.0)
            weight_grads_ref[kind, span, :] = value
            return carry

        lax.fori_loop(0, block // 32, one, 0)

    weight_blocks(0, grad_all, context_ref)

    half = rows // 2

    def terms(h, qb, key_count, keys, values):
        cut = pl.ds(pl.multiple_of(h * HD, HD), HD)
        span = pl.ds(qb * half, half)
        lane = lax.broadcasted_iota(jnp.int32, (1, 128), 1)
        log_total = jnp.sum(jnp.where(lane == h, log_ref[span, :], 0.0), axis=1, keepdims=True)
        queries, grads = q_ref[span, cut], dc[span, cut]
        delta = jnp.sum(
            grads.astype(full) * context_ref[span, cut].astype(full), axis=1, keepdims=True
        )
        key_part, value_part = keys[:key_count, cut], values[:key_count, cut]
        probs = jnp.exp(times_transpose(queries, key_part) * score_scale - log_total)
        scores_grad = (probs * (times_transpose(grads, value_part) - delta)).astype(low)
        return (
            jnp.dot(scores_grad, key_part, preferred_element_type=full),
            inner_rows(scores_grad, queries),
            inner_rows(probs.astype(low), grads),
        )

    def spans(h, qb):
        return pl.ds(qb * half, half), pl.ds(pl.multiple_of(h * HD, HD), HD)

    later = (
        remote(dke, later_k, kv_send.at[0], kv_recv.at[0], beside),
        remote(dve, later_v, kv_send.at[1], kv_recv.at[1], beside),
    )

    @pl.when(y == 1)
    def _():
        def head(h, carry):
            cut = pl.ds(pl.multiple_of(h * HD, HD), HD)
            first = terms(h, 0, rows, ke_ref, ve_ref)
            dq[spans(h, 0)[0], cut] = first[0]
            dk[:, cut] = first[1]
            dv[:, cut] = first[2]
            second = terms(h, 1, rows, ke_ref, ve_ref)
            dq[spans(h, 1)[0], cut] = second[0]
            dke[:, cut] = ((dk[:, cut] + second[1]) * score_scale).astype(low)
            dve[:, cut] = (dv[:, cut] + second[2]).astype(low)
            return carry

        lax.fori_loop(0, heads, head, 0)
        for copy in later:
            copy.start()

    @pl.when(y == 0)
    def _():
        dq[...] = jnp.zeros_like(dq)

    y_stage(0)

    def head(h, carry):
        cut = pl.ds(pl.multiple_of(h * HD, HD), HD)
        second = terms(h, 1, rows, k_ref, v_ref)
        dq[half:, cut] = dq[half:, cut] + second[0]
        dk[:, cut] = second[1] * score_scale
        dv[:, cut] = second[2]
        first = terms(h, 0, half, k_ref, v_ref)
        dq[:half, cut] = dq[:half, cut] + first[0]
        dk[:half, cut] = dk[:half, cut] + first[1] * score_scale
        dv[:half, cut] = dv[:half, cut] + first[2]
        return carry

    lax.fori_loop(0, heads, head, 0)

    def rotate_back(source, target, scale):
        def one(h, carry):
            cut = pl.ds(pl.multiple_of(h * HD, HD), HD)
            value = source[:, cut] * scale
            turned = value * cos_ref[...] - pltpu.roll(value, HD // 2, 1) * sin_ref[...]
            lin_grads[target, :, cut] = turned.astype(low)
            return carry

        lax.fori_loop(0, heads, one, 0)

    rotate_back(dq, 0, score_scale)
    loads[1].wait()
    blocks_along_z(n1, lin_grads.at[0])
    chain(0)

    @pl.when(y == 0)
    def _():
        for copy in later:
            copy.wait_recv()

        def add(span):
            dk[span, :] = dk[span, :] + later_k[span, :].astype(full)
            dv[span, :] = dv[span, :] + later_v[span, :].astype(full)

        by_rows(add)

    rotate_back(dk, 1, 1.0)
    lin_grads[2] = dv[...].astype(low)
    weight_blocks(2, n1, lin_grads.at[1])
    weight_blocks(3, n1, lin_grads.at[2])
    for copy in loads[2:]:
        copy.wait()

    def dn1_part(at, target):
        cut = pl.ds(pl.multiple_of(at * cols, cols), cols)
        total = times_transpose(lin_grads[0], wq[cut, :])
        total = total + times_transpose(lin_grads[1], wk[cut, :])
        total = total + times_transpose(lin_grads[2], wv[cut, :])
        target[...] = total.astype(low)

    def to_sibling(i):
        return remote(tp_staged.at[i], tp_sib.at[i], tp_send.at[i], tp_recv.at[i], sibling)

    def part_of(i):
        x_at = 1 - x + (2 * x - 1) * i
        dn1_part(x_at * 2 + 1 - core, tp_staged.at[i])
        to_sibling(i).start()
        dn1_part(x_at * 2 + core, tp_mine.at[i])

    out_x = remote(tp_mine.at[0], tp_x, tp_send.at[2], tp_recv.at[2], across)
    part_of(0)
    to_sibling(0).wait_recv()
    add_blocks(tp_mine.at[0], [tp_sib.at[0]], rows)
    out_x.start()
    part_of(1)
    chain_2()
    to_sibling(1).wait_recv()
    out_x.wait_recv()

    def sum_parts(span):
        dn1[span, :] = (
            tp_mine[1, span, :].astype(full)
            + tp_sib[1, span, :].astype(full)
            + tp_x[span, :].astype(full)
        )

    by_rows(sum_parts)

    def unit_one(span):
        return tokens_ref[span, :].astype(full) * inv_one_ref[span, :1]

    def products(span):
        dq[span, :] = dn1[span, :] * unit_one(span)

    by_rows(products)
    gain_grad = jnp.sum(dq[...], axis=0, keepdims=True)
    dq[...] = dq[...] * first_ref[:1, :]
    total = row_exchange(1, row_of(dq[...]))
    dk[:, :128] = jnp.broadcast_to(total * (1.0 / model_dim), (rows, 128))

    def norm_one(span):
        scaled = dn1[span, :] * first_ref[:1, :]
        value = hidden_grad[span, :] + inv_one_ref[span, :1] * (
            scaled - unit_one(span) * dk[span, :1]
        )
        tokens_grad_ref[span, :] = value.astype(low)

    by_rows(norm_one)

    own = smalls.at[ep]
    own[...] = small_ref[...]
    own[0:1, :] = gain_grad
    for i in range(3):
        own[i + 1 : i + 2, :] = jnp.sum(lin_grads[i].astype(full), axis=0, keepdims=True)

    def small_to(i):
        return remote(own, own, small_send.at[i - 1], small_recv.at[i - 1], others[i - 1])

    for i in range(1, sources):
        small_to(i).start()
    other_y_along_z()
    chain(1)
    y_stage(2)
    final(0)
    chain(2)
    y_stage(3)
    chain(3)
    for i in range(1, sources):
        small_to(i).wait_recv()
    total = smalls[0]
    for i in range(1, sources):
        total = total + smalls[i]
    quarters[tp] = total
    s_x = remote(quarters.at[tp], quarters.at[tp], s_send.at[0], s_recv.at[0], across)
    s_s = remote(quarters.at[tp], quarters.at[tp], s_send.at[1], s_recv.at[1], sibling)
    s_x.start()
    s_s.start()
    final(2)
    own_first_along_z()
    s_x.wait_recv()
    other = quarters.at[tp + 2 - 4 * x]
    s_f = remote(other, other, s_send.at[2], s_recv.at[2], sibling)
    s_f.start()
    final(3)
    final(1)
    s_s.wait_recv()
    s_f.wait_recv()
    sums_ref[...] = quarters[...]

    for copy in (g_x, g_s, g_f, s_x, s_s, s_f, out_x, to_sibling(0), to_sibling(1)):
        copy.wait_send()

    @pl.when(y == 1)
    def _():
        for copy in later:
            copy.wait_send()

    for i in range(1, sources):
        small_to(i).wait_send()

    def finish(n, carry):
        z_at = lax.rem(n, 4)

        @pl.when((n < 4) | (n >= 8) | (n == 4 + z))
        def _():
            remote(staged.at[0], from_y.at[0], y_send.at[n], y_recv.at[n], beside).wait_send()


        @pl.when(z_at > z)
        def _():
            remote(mine.at[0], from_below.at[0], up_send.at[n], up_recv.at[n], above).wait_send()

        @pl.when(z_at < z)
        def _():
            remote(mine.at[0], from_above.at[0], down_send.at[n], down_recv.at[n], below).wait_send()

        return carry

    lax.fori_loop(0, 16, finish, 0)

    def finish_2(z_at, carry):
        @pl.when(z_at > z)
        def _():
            up_2(z_at).wait_send()

        @pl.when(z_at < z)
        def _():
            down_2(z_at).wait_send()

        return carry

    lax.fori_loop(0, 4, finish_2, 0)


def unwind(vmem_args, hbm_args, cid):
    rows, cols = vmem_args[0].shape
    model_dim = hbm_args[0].shape[1]
    sources = 8
    block = model_dim // sources
    low, full, dma = jnp.bfloat16, jnp.float32, pltpu.SemaphoreType.DMA
    vmem, hbm = pl.BlockSpec(memory_space=pltpu.VMEM), pl.BlockSpec(memory_space=pl.ANY)

    def buffers(*shape, dtype=low):
        return pltpu.VMEM(shape, dtype)

    return pl.pallas_call(
        unwind_kernel,
        out_shape=[
            jax.ShapeDtypeStruct((rows, cols), low),
            jax.ShapeDtypeStruct((4, block, cols), full),
            jax.ShapeDtypeStruct((4, 16, cols), full),
        ],
        in_specs=[vmem] * len(vmem_args) + [hbm] * len(hbm_args),
        out_specs=[vmem] * 3,
        scratch_shapes=[buffers(*arg.shape) for arg in hbm_args]
        + [
            buffers(rows, model_dim),
            buffers(rows, cols),
            buffers(rows, cols, dtype=full),
            buffers(rows, cols),
            buffers(rows, cols, dtype=full),
            buffers(rows, cols, dtype=full),
            buffers(rows, cols, dtype=full),
            buffers(3, rows, cols),
            buffers(rows, cols),
            buffers(rows, cols),
            buffers(rows, cols),
            buffers(rows, cols),
        ]
        + [buffers(16, block, cols)] * 5
        + [buffers(4, block, cols)] * 2
        + [
            buffers(2, rows, cols),
            buffers(2, rows, cols),
            buffers(2, rows, cols),
            buffers(rows, cols),
            buffers(rows, cols, dtype=full),
            buffers(4, 8, rows, dtype=full),
            buffers(2, 8, rows, dtype=full),
            buffers(2, 8, rows, dtype=full),
            buffers(sources, 16, cols, dtype=full),
            buffers(4, 16, cols, dtype=full),
        ]
        + [dma((5,)), dma((3,)), dma((3,)), dma((4,)), dma((4,)), dma((2,)), dma((2,))]
        + [dma((16,))] * 6
        + [dma((3,)), dma((3,)), dma((7,)), dma((7,)), dma((3,)), dma((3,))]
        + [dma((4,))] * 4,
        compiler_params=pltpu.CompilerParams(
            collective_id=cid, has_side_effects=True, vmem_limit_bytes=60 * 2**20
        ),
        name="unwind",
    )(*vmem_args, *hbm_args)


def attend_kernel(
    first_ref,
    bias_ref,
    second_ref,
    cos_ref,
    sin_ref,
    tokens_hbm,
    grad_hbm,
    wq_hbm,
    wk_hbm,
    wv_hbm,
    wo_hbm,
    hidden_ref,
    unit_ref,
    inv_ref,
    normed_ref,
    n1_ref,
    inv_one_ref,
    q_ref,
    k_ref,
    v_ref,
    ke_ref,
    ve_ref,
    context_ref,
    log_ref,
    all_ref,
    wq,
    wk,
    wv,
    wo,
    tokens,
    lin,
    total,
    most,
    weight,
    earlier_k,
    earlier_v,
    tp_staged,
    tp_mine,
    tp_sib,
    tp_x,
    row_mine,
    row_sib,
    row_x,
    load_sem,
    t_send,
    t_recv,
    kv_send,
    kv_recv,
    tp_send,
    tp_recv,
    row_send,
    row_recv,
    up_sem,
    down_sem,
    a_sem,
    b_sem,
    s_sem,
    recv_sem,
    sib_sem,
):
    ep, tp, z, y, x, core = place()
    rows, cols = hidden_ref.shape
    model_dim = n1_ref.shape[1]
    heads = cols // HD
    low, full = jnp.bfloat16, jnp.float32
    score_scale = HD ** (-0.5)
    sibling, across = (ep, tp + 1 - 2 * core), (ep, tp + 2 - 4 * x)
    beside = (ep + 1 - 2 * y, tp)
    peer_a, peer_b, _, above, below = lane_peers()

    def quarter(at):
        return tokens.at[:, pl.ds(pl.multiple_of(at * cols, cols), cols)]

    loads = [
        pltpu.make_async_copy(source, target, load_sem.at[i])
        for i, (source, target) in enumerate(
            (
                (tokens_hbm, quarter(tp)),
                (wk_hbm, wk),
                (wv_hbm, wv),
                (wq_hbm, wq),
                (wo_hbm, wo),
            )
        )
    ]
    for copy in loads:
        copy.start()
    greet([across, beside, sibling], True)

    t_x = remote(tokens_hbm, quarter(tp), t_send.at[0], t_recv.at[0], across)
    t_s = remote(tokens_hbm, quarter(tp), t_send.at[1], t_recv.at[1], sibling)
    t_x.start()
    t_s.start()

    def choose(*values):
        return jnp.where(
            z == 0, values[0], jnp.where(z == 1, values[1], jnp.where(z == 2, values[2], values[3]))
        )

    coming = (z, choose(1, 0, 3, 2), choose(2, 2, 1, 1), choose(3, 3, 0, 0))

    def spot(z_at, da, db):
        group, at_quarter = lane_spot(z_at, da, db, core)
        return all_ref.at[
            pl.ds(pl.multiple_of(group * rows, rows), rows),
            pl.ds(pl.multiple_of(at_quarter * cols, cols), cols),
        ]

    def at(z_at, da, db):
        return z_at * 4 + da * 2 + db

    def arrived(z_at, da, db):
        block, n = spot(z_at, da, db), at(z_at, da, db)
        remote(block, block, s_sem.at[n], recv_sem.at[n], sibling).wait_recv()
        return block

    def up(z_at, da, source):
        n = z_at * 2 + da
        target = recv_sem.at[at(z_at, da, 0)]
        return remote(source, spot(z_at, da, 0), up_sem.at[n], target, above)

    def down(z_at, da, source):
        n = z_at * 2 + da
        target = recv_sem.at[at(z_at, da, 0)]
        return remote(source, spot(z_at, da, 0), down_sem.at[n], target, below)

    def over_a(source):
        return remote(source, spot(z, 0, 0), a_sem, recv_sem.at[at(z, 1, 0)], peer_a)

    def over_b(z_at, da, source):
        return remote(
            source, spot(z_at, da, 0), b_sem.at[z_at * 2 + da], recv_sem.at[at(z_at, da, 1)], peer_b
        )

    def to_sibling(z_at, da, db, source):
        n = at(z_at, da, db)
        return remote(source, spot(z_at, da, db), s_sem.at[n], sib_sem.at[n], sibling)

    def along_z(da, source):
        @pl.when(z < 3)
        def _():
            up(z, da, source).start()

        @pl.when(z > 0)
        def _():
            down(z, da, source).start()

    def pass_a():
        block = arrived(z, 1, 0)
        along_z(1, block)
        over_b(z, 1, block).start()
        to_sibling(z, 1, 0, block).start()

    def pass_z(k, da):
        z_at = coming[k]
        block = arrived(z_at, da, 0)

        @pl.when((z_at > z) & (z > 0))
        def _():
            down(z_at, da, block).start()

        @pl.when((z_at < z) & (z < 3))
        def _():
            up(z_at, da, block).start()

        over_b(z_at, da, block).start()
        to_sibling(z_at, da, 0, block).start()

    def pass_b(k, da):
        block = arrived(coming[k], da, 1)
        to_sibling(coming[k], da, 1, block).start()

    own = pltpu.make_async_copy(grad_hbm, spot(z, 0, 0), load_sem.at[5])
    over_a(grad_hbm).start()
    along_z(0, grad_hbm)
    over_b(z, 0, grad_hbm).start()
    to_sibling(z, 0, 0, grad_hbm).start()
    own.start()

    t_x.wait_recv()
    theirs = quarter(tp + 2 - 4 * x)
    t_f = remote(theirs, theirs, t_send.at[2], t_recv.at[2], sibling)
    t_f.start()
    loads[0].wait()
    t_s.wait_recv()
    t_f.wait_recv()

    def by_rows(step, body):
        def one(i, carry):
            body(pl.ds(pl.multiple_of(i * step, step), step))
            return carry

        lax.fori_loop(0, rows // step, one, 0)

    def norm_one(span):
        values = tokens[span, :].astype(full)
        inv = lax.rsqrt(jnp.mean(values * values, axis=1, keepdims=True) + norm_eps)
        n1_ref[span, :] = (values * inv * first_ref[:1, :]).astype(low)
        inv_one_ref[span, :] = jnp.broadcast_to(inv, (inv.shape[0], 128))

    by_rows(32, norm_one)
    pass_a()
    pass_z(1, 0)

    def project(weights, bias_at):
        def one(i, carry):
            cut = pl.ds(pl.multiple_of(i * 256, 256), 256)
            lin[:, cut] = (
                jnp.dot(n1_ref[...], weights[:, cut], preferred_element_type=full)
                + bias_ref[bias_at : bias_at + 1, cut]
            )
            return carry

        lax.fori_loop(0, cols // 256, one, 0)

    def rotate_into(target):
        def one(h, carry):
            cut = pl.ds(pl.multiple_of(h * HD, HD), HD)
            value = lin[:, cut]
            turned = value * cos_ref[...] + pltpu.roll(value, HD // 2, 1) * sin_ref[...]
            target[:, cut] = turned.astype(low)
            return carry

        lax.fori_loop(0, heads, one, 0)

    loads[1].wait()
    project(wk, 1)
    rotate_into(k_ref)
    loads[2].wait()
    project(wv, 2)
    v_ref[...] = lin[...].astype(low)
    earlier = (
        remote(k_ref, earlier_k, kv_send.at[0], kv_recv.at[0], beside),
        remote(v_ref, earlier_v, kv_send.at[1], kv_recv.at[1], beside),
    )

    @pl.when(y == 0)
    def _():
        for copy in earlier:
            copy.start()

    pass_b(0, 0)
    pass_z(2, 0)
    pass_z(1, 1)
    loads[3].wait()
    project(wq, 0)
    rotate_into(q_ref)

    half = rows // 2
    lane = lax.broadcasted_iota(jnp.int32, (1, 128), 1)

    def pick(held, span, h):
        return jnp.sum(jnp.where(lane == h, held[span, :], 0.0), axis=1, keepdims=True)

    def put(held, span, h, value):
        held[span, :] = jnp.where(lane == h, value, held[span, :])

    most[...] = jnp.zeros_like(most)
    weight[...] = jnp.ones_like(weight)

    def local_head(h, carry):
        cut = pl.ds(pl.multiple_of(h * HD, HD), HD)
        for qb in range(2):
            span, count = pl.ds(qb * half, half), (qb + 1) * half
            scores = times_transpose(q_ref[span, cut], k_ref[:count, cut]) * score_scale
            top = jnp.max(scores, axis=1, keepdims=True)
            powers = jnp.exp(scores - top)
            put(most, span, h, top)
            put(weight, span, h, jnp.sum(powers, axis=1, keepdims=True))
            total[span, cut] = jnp.dot(
                powers.astype(low), v_ref[:count, cut], preferred_element_type=full
            )
        return carry

    lax.fori_loop(0, heads, local_head, 0)
    pass_z(2, 1)
    pass_z(3, 0)
    pass_b(0, 1)
    pass_b(1, 0)

    @pl.when(y == 0)
    def _():
        ke_ref[...] = jnp.zeros_like(ke_ref)
        ve_ref[...] = jnp.zeros_like(ve_ref)

    @pl.when(y == 1)
    def _():
        for copy in earlier:
            copy.wait_recv()
        ke_ref[...] = earlier_k[...]
        ve_ref[...] = earlier_v[...]

        def remote_head(h, carry):
            cut = pl.ds(pl.multiple_of(h * HD, HD), HD)
            for qb in range(2):
                span = pl.ds(qb * half, half)
                scores = times_transpose(q_ref[span, cut], ke_ref[:, cut]) * score_scale
                before = pick(most, span, h)
                top = jnp.maximum(before, jnp.max(scores, axis=1, keepdims=True))
                powers = jnp.exp(scores - top)
                shrink = jnp.exp(before - top)
                put(most, span, h, top)
                put(
                    weight,
                    span,
                    h,
                    pick(weight, span, h) * shrink + jnp.sum(powers, axis=1, keepdims=True),
                )
                total[span, cut] = total[span, cut] * shrink + jnp.dot(
                    powers.astype(low), ve_ref[:, cut], preferred_element_type=full
                )
            return carry

        lax.fori_loop(0, heads, remote_head, 0)

    def finish_head(h, carry):
        cut = pl.ds(pl.multiple_of(h * HD, HD), HD)
        context_ref[:, cut] = (total[:, cut] / pick(weight, slice(None), h)).astype(low)
        return carry

    lax.fori_loop(0, heads, finish_head, 0)
    log_ref[...] = most[...] + jnp.log(weight[...])

    loads[4].wait()

    def out_part(at_quarter, target):
        cut = pl.ds(pl.multiple_of(at_quarter * cols, cols), cols)
        target[...] = jnp.dot(context_ref[...], wo[:, cut], preferred_element_type=full).astype(low)

    def part_to_sibling(i):
        return remote(tp_staged.at[i], tp_sib.at[i], tp_send.at[i], tp_recv.at[i], sibling)

    def part_of(i):
        x_at = 1 - x + (2 * x - 1) * i
        out_part(x_at * 2 + 1 - core, tp_staged.at[i])
        part_to_sibling(i).start()
        out_part(x_at * 2 + core, tp_mine.at[i])

    out_x = remote(tp_mine.at[0], tp_x, tp_send.at[2], tp_recv.at[2], across)
    part_of(0)
    part_to_sibling(0).wait_recv()
    add_blocks(tp_mine.at[0], [tp_sib.at[0]], rows)
    out_x.start()
    part_of(1)
    pass_z(3, 1)
    pass_b(1, 1)
    pass_b(2, 0)
    part_to_sibling(1).wait_recv()
    out_x.wait_recv()
    own_cut = pl.ds(pl.multiple_of(tp * cols, cols), cols)

    def sum_parts(span):
        value = tokens[span, own_cut].astype(full) + (
            tp_mine[1, span, :].astype(full)
            + tp_sib[1, span, :].astype(full)
            + tp_x[span, :].astype(full)
        )
        hidden_ref[span, :] = value
        lin[span, :] = value * value

    by_rows(64, sum_parts)

    row_mine[0] = row_of(lin[...])
    first = remote(row_mine.at[0], row_sib, row_send.at[0], row_recv.at[0], sibling)
    first.start()
    first.wait_recv()
    row_mine[1] = row_mine[0] + row_sib[...]
    second = remote(row_mine.at[1], row_x, row_send.at[1], row_recv.at[1], across)
    second.start()
    second.wait_recv()
    squares = (row_mine[1] + row_x[...]).T[:, :1]
    inv_two = lax.rsqrt(squares * (1.0 / model_dim) + norm_eps)
    inv_ref[...] = jnp.broadcast_to(inv_two, (rows, 128))

    def norm_two(span):
        unit = hidden_ref[span, :] * inv_ref[span, :1]
        unit_ref[span, :] = unit
        normed_ref[span, :] = (unit * second_ref[:1, :]).astype(low)

    by_rows(64, norm_two)

    pass_b(2, 1)
    pass_b(3, 0)
    pass_b(3, 1)

    def finish_sibling(i, carry):
        block = spot(0, 0, 0)
        copy = remote(block, block, s_sem.at[i], sib_sem.at[i], sibling)
        copy.wait_recv()
        copy.wait_send()
        return carry

    lax.fori_loop(0, 16, finish_sibling, 0)

    def finish_links(i, carry):
        for da in range(2):
            over_b(i, da, grad_hbm).wait_send()

            @pl.when((z < 3) & (i <= z))
            def _(da=da):
                up(i, da, grad_hbm).wait_send()

            @pl.when((z > 0) & (i >= z))
            def _(da=da):
                down(i, da, grad_hbm).wait_send()

        return carry

    lax.fori_loop(0, 4, finish_links, 0)
    over_a(grad_hbm).wait_send()
    own.wait()
    for copy in (t_x, t_s, t_f, out_x, part_to_sibling(0), part_to_sibling(1), first, second):
        copy.wait_send()

    @pl.when(y == 0)
    def _():
        for copy in earlier:
            copy.wait_send()


def attend(vmem_args, hbm_args, cid):
    rows, cols = hbm_args[0].shape
    model_dim = vmem_args[0].shape[1]
    low, full, dma = jnp.bfloat16, jnp.float32, pltpu.SemaphoreType.DMA
    vmem, hbm = pl.BlockSpec(memory_space=pltpu.VMEM), pl.BlockSpec(memory_space=pl.ANY)

    def buffers(*shape, dtype=low):
        return pltpu.VMEM(shape, dtype)

    def result(*shape, dtype=low):
        return jax.ShapeDtypeStruct(shape, dtype)

    return pl.pallas_call(
        attend_kernel,
        out_shape=[
            result(rows, cols, dtype=full),
            result(rows, cols, dtype=full),
            result(rows, 128, dtype=full),
            result(rows, cols),
            result(rows, model_dim),
            result(rows, 128, dtype=full),
        ]
        + [result(rows, cols)] * 6
        + [result(rows, 128, dtype=full), result(8 * rows, model_dim)],
        in_specs=[vmem] * len(vmem_args) + [hbm] * len(hbm_args),
        out_specs=[vmem] * 13 + [hbm],
        scratch_shapes=[buffers(*arg.shape) for arg in hbm_args[2:]]
        + [
            buffers(rows, model_dim),
            buffers(rows, cols, dtype=full),
            buffers(rows, cols, dtype=full),
            buffers(rows, 128, dtype=full),
            buffers(rows, 128, dtype=full),
            buffers(rows, cols),
            buffers(rows, cols),
            buffers(2, rows, cols),
            buffers(2, rows, cols),
            buffers(2, rows, cols),
            buffers(rows, cols),
            buffers(2, 8, rows, dtype=full),
            buffers(8, rows, dtype=full),
            buffers(8, rows, dtype=full),
        ]
        + [dma((6,)), dma((3,)), dma((3,)), dma((2,)), dma((2,)), dma((3,)), dma((3,))]
        + [dma((2,)), dma((2,))]
        + [dma((8,)), dma((8,)), dma, dma((8,)), dma((16,)), dma((16,)), dma((16,))],
        compiler_params=pltpu.CompilerParams(
            collective_id=cid, has_side_effects=True, vmem_limit_bytes=60 * 2**20
        ),
        name="attend",
    )(*vmem_args, *hbm_args)


def kept_choice(expert_ids, pair_order, expert_total, capacity):
    tok_count, top_count = expert_ids.shape
    pair_count = tok_count * top_count
    order = pair_order.reshape(-1)
    pairs = jnp.arange(pair_count, dtype=jnp.int32)
    turn = jnp.sum(jnp.where(order[None, :] == pairs[:, None], pairs[None, :], 0), axis=1)
    turn = turn.reshape(tok_count, top_count)
    picked = expert_ids[:, :, None] == jnp.arange(expert_total, dtype=jnp.int32)[None, None, :]
    experts_apart = jnp.arange(expert_total, dtype=jnp.int32)[:, None, None]
    picked = expert_ids.T[None] == experts_apart
    named = jnp.any(picked, axis=1)
    turn_of = jnp.sum(jnp.where(picked, turn.T[None], 0), axis=1)
    turn_of = jnp.where(named, turn_of, pair_count)
    slot = jnp.sum((turn_of[:, None, :] < turn_of[:, :, None]).astype(jnp.int32), axis=2)
    return (named & (slot < capacity)).astype(jnp.float32)


def dense_plan(
    tokens,
    out_grad,
    first_gain,
    query_weight,
    key_weight,
    value_weight,
    query_bias,
    key_bias,
    value_bias,
    output_weight,
    second_gain,
    router_weight,
    shared_gate_weight,
    shared_up_weight,
    shared_down_weight,
    switch_vector,
    expert_gate_weight,
    expert_up_weight,
    expert_down_weight,
    expert_ids,
    pair_order,
):
    ep, tp = lax.axis_index("ep"), lax.axis_index("tp")
    tok_count, col_width = tokens.shape
    model_dim = query_weight.shape[0]
    sources = lax.axis_size("ep")
    place_in_seq = ep % SPAN
    expert_total = router_weight.shape[1]
    capacity = 9 * tok_count * expert_ids.shape[1] // (8 * expert_total)
    head_count = query_weight.shape[1] // HD
    expert_width = expert_gate_weight.shape[2]
    shared_width = shared_gate_weight.shape[1] // sources
    width = expert_width + shared_width

    def own_cols(vector):
        return lax.dynamic_slice_in_dim(vector, tp * col_width, col_width, vector.ndim - 1)

    kept_own = kept_choice(expert_ids, pair_order, expert_total, capacity)

    def tall(vector):
        return jnp.broadcast_to(vector[None, :], (8, vector.shape[0]))

    cosine, sine_part = rope_tables(tok_count, HD, place_in_seq * tok_count)
    cos_wide = jnp.concatenate([cosine[:, 0], cosine[:, 0]], axis=1)
    sin_wide = jnp.concatenate([-sine_part[:, 0], sine_part[:, 0]], axis=1)
    second_cols = own_cols(second_gain)
    biases = jnp.pad(jnp.stack([query_bias, key_bias, value_bias]), ((0, 5), (0, 0)))
    (
        hidden_cols,
        unit_two,
        inv_two,
        normed_cols,
        normed_one,
        inv_one,
        queries,
        keys_rot,
        values_all,
        earlier_keys,
        earlier_values,
        context,
        log_rows,
        grads_all,
    ) = attend(
        [tall(first_gain), biases, tall(second_cols), cos_wide, sin_wide],
        [tokens, out_grad, query_weight, key_weight, value_weight, output_weight],
        2,
    )

    def shared_rows(weight):
        return lax.dynamic_slice_in_dim(weight, ep * shared_width, shared_width, 1).T

    extra_rows = jnp.concatenate([router_weight.T, switch_vector[None, :]], axis=0)
    extra_rows = jnp.pad(extra_rows, ((0, 16 - extra_rows.shape[0]), (0, 0)))
    kept_rows = jnp.pad(kept_own, ((0, 16 - expert_total), (0, 0))).astype(jnp.bfloat16)
    reduced, layer_out, logit_tile, expert_grads, shared_parts, *_ = experts(
        normed_cols,
        grads_all,
        kept_rows,
        [
            expert_gate_weight[0].T,
            shared_rows(shared_gate_weight),
            extra_rows,
            expert_up_weight[0].T,
            shared_rows(shared_up_weight),
            expert_down_weight[0],
            shared_down_weight,
        ],
        hidden_cols,
        expert_total,
        4,
    )
    shared_parts = lax.all_to_all(shared_parts, "ep", split_axis=0, concat_axis=0, tiled=True)
    shared_parts = shared_parts.transpose(1, 0, 2, 3).reshape(3, sources * shared_width, -1)
    shared_parts = shared_parts.astype(jnp.float32)
    shared_gate_grad = shared_parts[1].T
    shared_up_grad = shared_parts[2].T
    shared_down_grad = shared_parts[0]

    normed_grad = reduced[:tok_count]
    probs_grad = (reduced[tok_count : tok_count + expert_total] * kept_own).T
    switch_grad = reduced[tok_count + expert_total]
    logit_at = width % 128
    probs_own = softmax_rows(logit_tile[:, logit_at : logit_at + expert_total])
    switch = jax.nn.sigmoid(logit_tile[:, logit_at + expert_total])
    logit_grad = (
        probs_own * (probs_grad - jnp.sum(probs_own * probs_grad, axis=-1, keepdims=True))
    ).astype(jnp.bfloat16)
    router_grad = inner_rows(normed_cols, logit_grad)
    switch_lin_grad = switch_grad * switch * (1.0 - switch)
    switch_vector_grad = jnp.dot(switch_lin_grad, normed_cols, preferred_element_type=jnp.float32)
    router_cols = lax.dynamic_slice_in_dim(router_weight, tp * col_width, col_width, 0)
    normed_grad = normed_grad + times_transpose(logit_grad, router_cols)
    normed_grad = (
        normed_grad
        + switch_lin_grad[:, None] * own_cols(switch_vector).astype(jnp.float32)[None, :]
    )
    second_gain_grad = jnp.sum(normed_grad * unit_two, axis=0)

    small = jnp.concatenate(
        [second_gain_grad[None], switch_vector_grad[None], router_grad.T], axis=0
    )
    small_rows = small.shape[0]
    small = jnp.pad(small, ((4, 12 - small_rows), (0, 0)))
    tokens_grad, weight_grads, sums = unwind(
        [
            normed_grad,
            unit_two,
            inv_two,
            tall(second_cols),
            out_grad,
            tokens,
            inv_one,
            tall(own_cols(first_gain)),
            small,
            queries,
            keys_rot,
            values_all,
            earlier_keys,
            earlier_values,
            context,
            log_rows,
            cos_wide,
            sin_wide,
        ],
        [normed_one, query_weight, key_weight, value_weight, output_weight],
        5,
    )
    share = model_dim // sources
    bias_width = HD // sources
    bias_sums = lax.dynamic_slice_in_dim(
        lax.dynamic_index_in_dim(sums, tp, 0, keepdims=False)[1:4].reshape(3, head_count, HD),
        ep * bias_width,
        bias_width,
        2,
    )
    per_quarter = col_width // share
    spread = lax.dynamic_index_in_dim(sums, ep // per_quarter, 0, keepdims=False)
    spread = lax.dynamic_slice_in_dim(spread, ep % per_quarter * share, share, 1)
    spread = jnp.concatenate([spread[:1], spread[4 : 4 + small_rows]], axis=0)
    return (
        layer_out,
        tokens_grad,
        spread[0],
        weight_grads[1],
        weight_grads[2],
        weight_grads[3],
        bias_sums[0],
        bias_sums[1],
        bias_sums[2],
        weight_grads[0].T,
        spread[1],
        spread[3:].T,
        shared_gate_grad,
        shared_up_grad,
        shared_down_grad,
        spread[2],
        expert_grads[1].T[None],
        expert_grads[2].T[None],
        expert_grads[0][None],
    )


def solution(mesh):
    plan = dense_plan if dict(mesh.shape) == {"ep": 8, "tp": 4} else slot_plan
    return jax.shard_map(
        plan,
        mesh=mesh,
        in_specs=(
            P("ep", "tp"),
            P("ep", "tp"),
            P(),
            P(None, "tp"),
            P(None, "tp"),
            P(None, "tp"),
            P("tp"),
            P("tp"),
            P("tp"),
            P("tp", None),
            P(),
            P(),
            P(None, "tp"),
            P(None, "tp"),
            P("tp", None),
            P(),
            P("ep", None, "tp"),
            P("ep", None, "tp"),
            P("ep", "tp", None),
            P("ep", None),
            P("ep", None),
        ),
        out_specs=(
            P("ep", "tp"),
            P("ep", "tp"),
            P("ep"),
            P("ep", "tp"),
            P("ep", "tp"),
            P("ep", "tp"),
            P("tp", "ep"),
            P("tp", "ep"),
            P("tp", "ep"),
            P("tp", "ep"),
            P("ep"),
            P("ep", None),
            P("ep", "tp"),
            P("ep", "tp"),
            P("tp", "ep"),
            P("ep"),
            P("ep", None, "tp"),
            P("ep", None, "tp"),
            P("ep", "tp", None),
        ),
        check_vma=False,
    )
```

```python
import functools
import math

import jax
import jax.numpy as jnp
from jax import lax
from jax.experimental import pallas as pl
from jax.experimental.pallas import tpu as pltpu
from jax.sharding import PartitionSpec as P

HD = 128
BLOCK = 256
SPAN = 2


rope_theta = 1000000.0
norm_eps = 1e-06
masked_score = -1e30


def passed_along(value, axis, steps):
    count = lax.axis_size(axis)
    leading, last = (max(0, -steps), min(count, count - steps))
    return lax.ppermute(value, axis, [(source, source + steps) for source in range(leading, last)])


def rope_tables(row_count, head_dim, first_position):
    positions = jnp.arange(row_count, dtype=jnp.float32) + first_position.astype(jnp.float32)
    frequency = jnp.exp(
        jnp.arange(head_dim // 2, dtype=jnp.float32) * (-2.0 * math.log(rope_theta) / head_dim)
    )
    angles = positions[:, None] * frequency[None, :]
    return (jnp.cos(angles)[:, None, :], jnp.sin(angles)[:, None, :])


def rotate(values, cosine, sine_part):
    half_dim = values.shape[-1] // 2
    first_half = values[..., :half_dim]
    second_half = values[..., half_dim:]
    return jnp.concatenate(
        [
            first_half * cosine - second_half * sine_part,
            second_half * cosine + first_half * sine_part,
        ],
        axis=-1,
    )


def inner_rows(left_side, right_side):
    return lax.dot_general(
        left_side, right_side, (((0,), (0,)), ((), ())), preferred_element_type=jnp.float32
    )


def times_transpose(left_side, right_side):
    return lax.dot_general(
        left_side, right_side, (((1,), (1,)), ((), ())), preferred_element_type=jnp.float32
    )


def row_stats(values):
    inv_rms = lax.rsqrt(jnp.mean(values * values, axis=-1, keepdims=True) + norm_eps)
    return (values * inv_rms, inv_rms)


def norm_back(grad_rows, unit_rows, inv_rms, gain_vec):
    scaled = grad_rows * gain_vec
    return inv_rms * (scaled - unit_rows * jnp.mean(scaled * unit_rows, axis=-1, keepdims=True))


def softmax_rows(scores):
    row_max = jnp.max(scores, axis=-1, keepdims=True)
    powers = jnp.exp(scores - row_max)
    return powers / jnp.sum(powers, axis=-1, keepdims=True)


def to_experts(block_rows, local_count):
    sources, span_rows, col_count = block_rows.shape
    slot_count = span_rows // local_count
    shaped = block_rows.reshape(sources, local_count, slot_count, col_count)
    return shaped.swapaxes(0, 1).reshape(local_count, sources * slot_count, col_count)


def to_sources(block_rows, sources):
    local_count, rows_all, col_count = block_rows.shape
    slot_count = rows_all // sources
    shaped = block_rows.reshape(local_count, sources, slot_count, col_count)
    return shaped.swapaxes(0, 1).reshape(sources, local_count * slot_count, col_count)


def deliver(block_rows):
    arrived = lax.all_to_all(block_rows, "ep", split_axis=0, concat_axis=0, tiled=True)
    return arrived


def collect(block_rows):
    return lax.all_to_all(block_rows, "ep", split_axis=0, concat_axis=0, tiled=True)


def slot_plan(
    tokens,
    out_grad,
    first_gain,
    query_weight,
    key_weight,
    value_weight,
    query_bias,
    key_bias,
    value_bias,
    output_weight,
    second_gain,
    router_weight,
    shared_gate_weight,
    shared_up_weight,
    shared_down_weight,
    switch_vector,
    expert_gate_weight,
    expert_up_weight,
    expert_down_weight,
    expert_ids,
    pair_order,
):
    whole_in, whole_grad = (
        lax.all_gather(tokens, "tp", axis=1, tiled=True),
        lax.all_gather(out_grad, "tp", axis=1, tiled=True),
    )
    tok_count = whole_in.shape[0]
    model_dim = whole_in.shape[1]
    col_width = tokens.shape[1]
    col_start = lax.axis_index("tp") * col_width
    sources = lax.axis_size("ep")
    place_in_seq = lax.axis_index("ep") % SPAN
    has_earlier = place_in_seq > 0
    local_experts = expert_gate_weight.shape[0]
    expert_total = router_weight.shape[1]
    top_count = expert_ids.shape[1]
    pair_count = tok_count * top_count
    capacity = 9 * pair_count // (8 * expert_total)
    head_count = query_weight.shape[1] // HD
    score_scale = HD ** (-0.5)
    inputs_full = whole_in.astype(jnp.float32)
    unit_one, inv_one = row_stats(inputs_full)
    normed_one = (unit_one * first_gain).astype(jnp.bfloat16)
    query_lin = jnp.dot(normed_one, query_weight, preferred_element_type=jnp.float32) + query_bias
    key_lin = jnp.dot(normed_one, key_weight, preferred_element_type=jnp.float32) + key_bias
    value_lin = jnp.dot(normed_one, value_weight, preferred_element_type=jnp.float32) + value_bias
    cosine, sine_part = rope_tables(tok_count, HD, place_in_seq * tok_count)
    queries = rotate(query_lin.reshape(tok_count, head_count, HD), cosine, sine_part).astype(
        jnp.bfloat16
    )
    keys_rot = rotate(key_lin.reshape(tok_count, head_count, HD), cosine, sine_part).astype(
        jnp.bfloat16
    )
    values_all = value_lin.reshape(tok_count, head_count, HD).astype(jnp.bfloat16)
    earlier_keys, earlier_values = passed_along((keys_rot, values_all), "ep", 1)
    keys_both = jnp.concatenate([earlier_keys, keys_rot], axis=0)
    values_both = jnp.concatenate([earlier_values, values_all], axis=0)
    blocks = jnp.arange(tok_count) // BLOCK
    local_allowed = blocks[None, :] <= blocks[:, None]
    remote_allowed = jnp.broadcast_to(has_earlier, (tok_count, tok_count))
    allowed = jnp.concatenate([remote_allowed, local_allowed], axis=1)[None]

    def attention_scores():
        scored = (
            jnp.einsum("qhd,khd->hqk", queries, keys_both, preferred_element_type=jnp.float32)
            * score_scale
        )
        return jnp.where(allowed, scored, masked_score)

    scores = attention_scores()
    row_max = jnp.max(scores, axis=-1, keepdims=True)
    powers = jnp.exp(scores - row_max)
    totals = jnp.sum(powers, axis=-1, keepdims=True)
    log_total = row_max + jnp.log(totals)
    probs_low = (powers / totals).astype(jnp.bfloat16)
    context = jnp.einsum("hqk,khd->qhd", probs_low, values_both, preferred_element_type=jnp.float32)
    context = context.reshape(tok_count, head_count * HD).astype(jnp.bfloat16)
    attn_part = jnp.dot(context, output_weight, preferred_element_type=jnp.float32)
    attended = lax.psum(attn_part, "tp")
    hidden_one = inputs_full + attended
    unit_two, inv_two = row_stats(hidden_one)
    normed_two = (unit_two * second_gain).astype(jnp.bfloat16)
    logits = jnp.dot(normed_two, router_weight, preferred_element_type=jnp.float32)
    router_probs = softmax_rows(logits)
    gate_values = jnp.take_along_axis(router_probs, expert_ids, axis=1)
    switch = jax.nn.sigmoid(jnp.dot(normed_two, switch_vector, preferred_element_type=jnp.float32))
    flat_ids = expert_ids.reshape(-1)
    turn_order = pair_order.reshape(-1)
    in_turn = flat_ids[turn_order]
    onehot = (in_turn[:, None] == jnp.arange(expert_total, dtype=jnp.int32)[None, :]).astype(
        jnp.int32
    )
    earlier = jnp.cumsum(onehot, axis=0) - onehot
    turn_slot = jnp.sum(earlier * onehot, axis=1)
    slot_index = jnp.zeros((pair_count,), jnp.int32).at[turn_order].set(turn_slot)
    kept_pair = slot_index < capacity
    slot_rows = expert_total * capacity
    target = jnp.where(kept_pair, flat_ids * capacity + slot_index, slot_rows)
    pair_token = jnp.arange(pair_count, dtype=jnp.int32) // top_count
    slot_token = (
        jnp.full((slot_rows + 1,), tok_count, jnp.int32).at[target].set(pair_token)[:slot_rows]
    )
    slot_gate = (
        jnp.zeros((slot_rows + 1,), jnp.float32).at[target].set(gate_values.reshape(-1))[:slot_rows]
    )
    padded_two = jnp.concatenate([normed_two, jnp.zeros((1, model_dim), jnp.bfloat16)], axis=0)
    send_rows = padded_two[slot_token].reshape(sources, local_experts * capacity, model_dim)
    expert_rows = to_experts(deliver(send_rows), local_experts)
    gate_lin = jnp.einsum(
        "erd,edf->erf", expert_rows, expert_gate_weight, preferred_element_type=jnp.float32
    )
    up_lin = jnp.einsum(
        "erd,edf->erf", expert_rows, expert_up_weight, preferred_element_type=jnp.float32
    )
    gate_sig = jax.nn.sigmoid(gate_lin)
    gate_act = gate_lin * gate_sig
    expert_hidden = (gate_act * up_lin).astype(jnp.bfloat16)
    expert_part = jnp.einsum(
        "erf,efd->erd", expert_hidden, expert_down_weight, preferred_element_type=jnp.float32
    )
    shared_gate_lin = jnp.dot(normed_two, shared_gate_weight, preferred_element_type=jnp.float32)
    shared_up_lin = jnp.dot(normed_two, shared_up_weight, preferred_element_type=jnp.float32)
    shared_sig = jax.nn.sigmoid(shared_gate_lin)
    shared_act = shared_gate_lin * shared_sig
    shared_hidden = (shared_act * shared_up_lin).astype(jnp.bfloat16)
    shared_part = jnp.dot(shared_hidden, shared_down_weight, preferred_element_type=jnp.float32)
    expert_cols, shared_cols = (
        lax.psum_scatter(expert_part.reshape(-1, model_dim), "tp", scatter_dimension=1, tiled=True),
        lax.psum_scatter(shared_part, "tp", scatter_dimension=1, tiled=True),
    )
    returned = collect(
        to_sources(expert_cols.astype(jnp.bfloat16).reshape(local_experts, -1, col_width), sources)
    )
    back_flat = jnp.concatenate(
        [returned.reshape(slot_rows, col_width), jnp.zeros((1, col_width), jnp.bfloat16)], axis=0
    )
    pair_out = back_flat[target].astype(jnp.float32).reshape(tok_count, top_count, col_width)
    routed = jnp.sum(gate_values[:, :, None] * pair_out, axis=1)
    hidden_cols = lax.dynamic_slice_in_dim(hidden_one, col_start, col_width, 1)
    layer_out = (hidden_cols + switch[:, None] * shared_cols + routed).astype(jnp.bfloat16)
    grad_full = whole_grad.astype(jnp.float32)
    grad_cols = out_grad.astype(jnp.float32)
    gate_part = jnp.sum(pair_out * grad_cols[:, None, :], axis=-1)
    switch_part = jnp.sum(grad_cols * shared_cols, axis=-1)
    gate_grad, switch_grad = lax.psum((gate_part, switch_part), "tp")
    padded_grad = jnp.concatenate([whole_grad, jnp.zeros((1, model_dim), jnp.bfloat16)], axis=0)
    send_grads = (slot_gate[:, None] * padded_grad[slot_token].astype(jnp.float32)).astype(
        jnp.bfloat16
    )
    expert_grads = to_experts(
        deliver(send_grads.reshape(sources, local_experts * capacity, model_dim)), local_experts
    )
    hidden_grad = jnp.einsum(
        "erd,efd->erf", expert_grads, expert_down_weight, preferred_element_type=jnp.float32
    )
    gate_lin_grad = (hidden_grad * up_lin * gate_sig * (1.0 + gate_lin * (1.0 - gate_sig))).astype(
        jnp.bfloat16
    )
    up_lin_grad = (hidden_grad * gate_act).astype(jnp.bfloat16)
    expert_down_grad = jnp.einsum(
        "erf,erd->efd", expert_hidden, expert_grads, preferred_element_type=jnp.float32
    )
    expert_gate_grad = jnp.einsum(
        "erd,erf->edf", expert_rows, gate_lin_grad, preferred_element_type=jnp.float32
    )
    expert_up_grad = jnp.einsum(
        "erd,erf->edf", expert_rows, up_lin_grad, preferred_element_type=jnp.float32
    )
    rows_grad = jnp.einsum(
        "erf,edf->erd", gate_lin_grad, expert_gate_weight, preferred_element_type=jnp.float32
    )
    rows_grad = rows_grad + jnp.einsum(
        "erf,edf->erd", up_lin_grad, expert_up_weight, preferred_element_type=jnp.float32
    )
    rows_grad_cols = lax.psum_scatter(
        rows_grad.reshape(-1, model_dim), "tp", scatter_dimension=1, tiled=True
    )
    returned_grad = collect(
        to_sources(
            rows_grad_cols.astype(jnp.bfloat16).reshape(local_experts, -1, col_width), sources
        )
    )
    back_grad = jnp.concatenate(
        [returned_grad.reshape(slot_rows, col_width), jnp.zeros((1, col_width), jnp.bfloat16)],
        axis=0,
    )
    routed_grad = jnp.sum(
        back_grad[target].astype(jnp.float32).reshape(tok_count, top_count, col_width), axis=1
    )
    shared_out_grad = (switch[:, None] * grad_full).astype(jnp.bfloat16)
    shared_hidden_grad = times_transpose(shared_out_grad, shared_down_weight)
    shared_gate_lin_grad = (
        shared_hidden_grad
        * shared_up_lin
        * shared_sig
        * (1.0 + shared_gate_lin * (1.0 - shared_sig))
    ).astype(jnp.bfloat16)
    shared_up_lin_grad = (shared_hidden_grad * shared_act).astype(jnp.bfloat16)
    shared_down_grad = inner_rows(shared_hidden, shared_out_grad)
    shared_gate_grad = inner_rows(normed_two, shared_gate_lin_grad)
    shared_up_grad = inner_rows(normed_two, shared_up_lin_grad)
    normed_grad = times_transpose(shared_gate_lin_grad, shared_gate_weight) + times_transpose(
        shared_up_lin_grad, shared_up_weight
    )
    normed_grad = normed_grad + lax.dynamic_update_slice_in_dim(
        jnp.zeros_like(normed_grad), routed_grad, col_start, 1
    )
    normed_grad = lax.psum(normed_grad, "tp")
    picked = (
        expert_ids[:, :, None] == jnp.arange(expert_total, dtype=jnp.int32)[None, None, :]
    ).astype(jnp.float32)
    probs_grad = jnp.sum(picked * gate_grad[:, :, None], axis=1)
    logit_grad = (
        router_probs * (probs_grad - jnp.sum(router_probs * probs_grad, axis=-1, keepdims=True))
    ).astype(jnp.bfloat16)
    router_grad = inner_rows(normed_two, logit_grad)
    switch_lin_grad = switch_grad * switch * (1.0 - switch)
    switch_vector_grad = jnp.dot(switch_lin_grad, normed_two, preferred_element_type=jnp.float32)
    normed_grad = normed_grad + times_transpose(logit_grad, router_weight)
    normed_grad = (
        normed_grad + switch_lin_grad[:, None] * switch_vector.astype(jnp.float32)[None, :]
    )
    second_gain_grad = jnp.sum(normed_grad * unit_two, axis=0)
    hidden_grad_one = grad_full + norm_back(normed_grad, unit_two, inv_two, second_gain)
    attended_grad = hidden_grad_one.astype(jnp.bfloat16)
    output_grad = inner_rows(context, attended_grad)
    context_grad = (
        times_transpose(attended_grad, output_weight)
        .astype(jnp.bfloat16)
        .reshape(tok_count, head_count, HD)
    )
    scores = attention_scores()
    attn_probs = jnp.exp(scores - log_total)
    probs_again = attn_probs.astype(jnp.bfloat16)
    probs_grad_att = jnp.einsum(
        "qhd,khd->hqk", context_grad, values_both, preferred_element_type=jnp.float32
    )
    values_both_grad = jnp.einsum(
        "hqk,qhd->khd", probs_again, context_grad, preferred_element_type=jnp.float32
    )
    scores_grad = (
        attn_probs * (probs_grad_att - jnp.sum(attn_probs * probs_grad_att, axis=-1, keepdims=True))
    ).astype(jnp.bfloat16)
    queries_grad = (
        jnp.einsum("hqk,khd->qhd", scores_grad, keys_both, preferred_element_type=jnp.float32)
        * score_scale
    )
    keys_both_grad = (
        jnp.einsum("hqk,qhd->khd", scores_grad, queries, preferred_element_type=jnp.float32)
        * score_scale
    )
    later_keys_grad, later_values_grad = passed_along(
        (keys_both_grad[:tok_count], values_both_grad[:tok_count]), "ep", -1
    )
    keep_later = jnp.where(has_earlier, 0.0, 1.0).astype(jnp.float32)
    keys_grad = keys_both_grad[tok_count:] + keep_later * later_keys_grad
    values_grad = values_both_grad[tok_count:] + keep_later * later_values_grad
    value_lin_grad = values_grad.reshape(tok_count, head_count * HD).astype(jnp.bfloat16)
    query_lin_grad = (
        rotate(queries_grad, cosine, -sine_part)
        .reshape(tok_count, head_count * HD)
        .astype(jnp.bfloat16)
    )
    key_lin_grad = (
        rotate(keys_grad, cosine, -sine_part)
        .reshape(tok_count, head_count * HD)
        .astype(jnp.bfloat16)
    )
    query_grad = inner_rows(normed_one, query_lin_grad)
    key_grad = inner_rows(normed_one, key_lin_grad)
    value_grad = inner_rows(normed_one, value_lin_grad)
    query_bias_grad = jnp.sum(query_lin_grad.astype(jnp.float32), axis=0).reshape(head_count, HD)
    key_bias_grad = jnp.sum(key_lin_grad.astype(jnp.float32), axis=0).reshape(head_count, HD)
    value_bias_grad = jnp.sum(value_lin_grad.astype(jnp.float32), axis=0).reshape(head_count, HD)
    normed_one_grad = times_transpose(query_lin_grad, query_weight) + times_transpose(
        key_lin_grad, key_weight
    )
    normed_one_grad = normed_one_grad + times_transpose(value_lin_grad, value_weight)
    normed_one_grad = lax.psum(normed_one_grad.astype(jnp.bfloat16), "tp").astype(jnp.float32)
    first_gain_grad = jnp.sum(normed_one_grad * unit_one, axis=0)
    input_grad = hidden_grad_one + norm_back(normed_one_grad, unit_one, inv_one, first_gain)
    tokens_grad = lax.dynamic_slice_in_dim(input_grad, col_start, col_width, 1).astype(jnp.bfloat16)
    reduced = (
        lax.psum_scatter(
            first_gain_grad.astype(jnp.bfloat16), "ep", scatter_dimension=0, tiled=True
        ).astype(jnp.float32),
        lax.psum_scatter(
            query_grad.astype(jnp.bfloat16), "ep", scatter_dimension=0, tiled=True
        ).astype(jnp.float32),
        lax.psum_scatter(
            key_grad.astype(jnp.bfloat16), "ep", scatter_dimension=0, tiled=True
        ).astype(jnp.float32),
        lax.psum_scatter(
            value_grad.astype(jnp.bfloat16), "ep", scatter_dimension=0, tiled=True
        ).astype(jnp.float32),
        lax.psum_scatter(
            query_bias_grad.astype(jnp.bfloat16), "ep", scatter_dimension=1, tiled=True
        ).astype(jnp.float32),
        lax.psum_scatter(
            key_bias_grad.astype(jnp.bfloat16), "ep", scatter_dimension=1, tiled=True
        ).astype(jnp.float32),
        lax.psum_scatter(
            value_bias_grad.astype(jnp.bfloat16), "ep", scatter_dimension=1, tiled=True
        ).astype(jnp.float32),
        lax.psum_scatter(
            output_grad.astype(jnp.bfloat16), "ep", scatter_dimension=1, tiled=True
        ).astype(jnp.float32),
        lax.psum_scatter(
            second_gain_grad.astype(jnp.bfloat16), "ep", scatter_dimension=0, tiled=True
        ).astype(jnp.float32),
        lax.psum_scatter(
            router_grad.astype(jnp.bfloat16), "ep", scatter_dimension=0, tiled=True
        ).astype(jnp.float32),
        lax.psum_scatter(
            shared_gate_grad.astype(jnp.bfloat16), "ep", scatter_dimension=0, tiled=True
        ).astype(jnp.float32),
        lax.psum_scatter(
            shared_up_grad.astype(jnp.bfloat16), "ep", scatter_dimension=0, tiled=True
        ).astype(jnp.float32),
        lax.psum_scatter(
            shared_down_grad.astype(jnp.bfloat16), "ep", scatter_dimension=1, tiled=True
        ).astype(jnp.float32),
        lax.psum_scatter(
            switch_vector_grad.astype(jnp.bfloat16), "ep", scatter_dimension=0, tiled=True
        ).astype(jnp.float32),
    )
    return (
        layer_out,
        tokens_grad,
        reduced[0],
        reduced[1],
        reduced[2],
        reduced[3],
        reduced[4],
        reduced[5],
        reduced[6],
        reduced[7],
        reduced[8],
        reduced[9],
        reduced[10],
        reduced[11],
        reduced[12],
        reduced[13],
        expert_gate_grad,
        expert_up_grad,
        expert_down_grad,
    )


MESH = pl.DeviceIdType.MESH
Z_ORDER = (0, 3, 1, 2)


def place():
    ep, tp = lax.axis_index("ep"), lax.axis_index("tp")
    return ep, tp, ep // 2, lax.rem(ep, 2), tp // 2, lax.rem(tp, 2)


def greet(always, along_z=False):
    barrier = pltpu.get_barrier_semaphore()
    for device in always:
        pl.semaphore_signal(barrier, inc=1, device_id=device, device_id_type=MESH)
    count = len(always)
    if along_z:
        ep, tp, z, _, _, _ = place()

        @pl.when(z < 3)
        def _():
            pl.semaphore_signal(barrier, inc=1, device_id=(ep + 2, tp), device_id_type=MESH)

        @pl.when(z > 0)
        def _():
            pl.semaphore_signal(barrier, inc=1, device_id=(ep - 2, tp), device_id_type=MESH)

        count = count + lax.min(z, 1) + lax.min(3 - z, 1)
    pl.semaphore_wait(barrier, count)


def remote(source, target, send_sem, recv_sem, device):
    return pltpu.make_async_remote_copy(
        src_ref=source,
        dst_ref=target,
        send_sem=send_sem,
        recv_sem=recv_sem,
        device_id=device,
        device_id_type=MESH,
    )


def add_blocks(target, sources, rows):
    step = next(size for size in (80, 64, 48, 16) if rows % size == 0)

    def body(i, carry):
        span = pl.ds(pl.multiple_of(i * step, 16), step)
        total = target[span, :]
        for source in sources:
            total = total + source[span, :].astype(target.dtype)
        target[span, :] = total
        return carry

    lax.fori_loop(0, rows // step, body, 0)


def gather_tp_kernel(x_ref, o_ref, send_sem, recv_sem, own_sem):
    ep, tp, _, _, x, core = place()
    cols = x_ref.shape[1]
    sibling = (ep, tp + 1 - 2 * core)
    across = (ep, tp + 2 - 4 * x)
    greet([sibling, across])
    mine = o_ref.at[:, pl.ds(pl.multiple_of(tp * cols, cols), cols)]
    theirs = o_ref.at[:, pl.ds(pl.multiple_of((tp + 2 - 4 * x) * cols, cols), cols)]
    out_x = remote(x_ref, mine, send_sem.at[0], recv_sem.at[0], across)
    out_s = remote(x_ref, mine, send_sem.at[1], recv_sem.at[1], sibling)
    own = pltpu.make_async_copy(x_ref, mine, own_sem)
    out_x.start()
    out_s.start()
    own.start()
    remote(x_ref, theirs, send_sem.at[0], recv_sem.at[0], across).wait_recv()
    passing = remote(theirs, theirs, send_sem.at[2], recv_sem.at[2], sibling)
    passing.start()
    out_s.wait_recv()
    passing.wait_recv()
    own.wait()
    out_x.wait_send()
    out_s.wait_send()
    passing.wait_send()


def gather_tp(value, cid):
    rows, cols = value.shape
    return pl.pallas_call(
        gather_tp_kernel,
        out_shape=jax.ShapeDtypeStruct((rows, 4 * cols), value.dtype),
        in_specs=[pl.BlockSpec(memory_space=pl.ANY)],
        out_specs=pl.BlockSpec(memory_space=pl.ANY),
        scratch_shapes=[
            pltpu.SemaphoreType.DMA((3,)),
            pltpu.SemaphoreType.DMA((3,)),
            pltpu.SemaphoreType.DMA,
        ],
        compiler_params=pltpu.CompilerParams(collective_id=cid, has_side_effects=True),
        name="gather_tp",
    )(value)


def scatter_tp_kernel(p_ref, o_ref, mine, from_sib, from_x, own_sem, send_sem, recv_sem):
    ep, tp, _, _, x, core = place()
    rows, cols = o_ref.shape
    sibling = (ep, tp + 1 - 2 * core)
    across = (ep, tp + 2 - 4 * x)
    greet([sibling, across])

    def part(x_at, core_at):
        return p_ref.at[:, pl.ds(pl.multiple_of((x_at * 2 + core_at) * cols, cols), cols)]

    sends, owns = [], []
    for i, x_at in enumerate((1 - x, x)):
        owns.append(pltpu.make_async_copy(part(x_at, core), mine.at[i], own_sem.at[i]))
        sends.append(
            remote(part(x_at, 1 - core), from_sib.at[i], send_sem.at[i], recv_sem.at[i], sibling)
        )
        sends[-1].start()
        owns[-1].start()
    owns[0].wait()
    sends[0].wait_recv()
    add_blocks(mine.at[0], [from_sib.at[0]], rows)
    out_x = remote(mine.at[0], from_x, send_sem.at[2], recv_sem.at[2], across)
    out_x.start()
    owns[1].wait()
    sends[1].wait_recv()
    out_x.wait_recv()
    o_ref[...] = jnp.zeros_like(o_ref)
    add_blocks(o_ref, [mine.at[1], from_sib.at[1], from_x], rows)
    out_x.wait_send()
    sends[0].wait_send()
    sends[1].wait_send()


def scatter_tp(value, cid):
    rows, cols = value.shape[0], value.shape[1] // 4
    return pl.pallas_call(
        scatter_tp_kernel,
        out_shape=jax.ShapeDtypeStruct((rows, cols), jnp.float32),
        in_specs=[pl.BlockSpec(memory_space=pl.ANY)],
        out_specs=pl.BlockSpec(memory_space=pltpu.VMEM),
        scratch_shapes=[
            pltpu.VMEM((2, rows, cols), value.dtype),
            pltpu.VMEM((2, rows, cols), value.dtype),
            pltpu.VMEM((rows, cols), value.dtype),
            pltpu.SemaphoreType.DMA((2,)),
            pltpu.SemaphoreType.DMA((3,)),
            pltpu.SemaphoreType.DMA((3,)),
        ],
        compiler_params=pltpu.CompilerParams(
            collective_id=cid, has_side_effects=True, vmem_limit_bytes=32 * 2**20
        ),
        name="scatter_tp",
    )(value)


def lane_peers():
    ep, tp, z, y, x, core = place()
    to_y, to_x = 1 - 2 * y, 1 - 2 * x
    peer_a = (ep + (1 - core) * to_y, tp + core * 2 * to_x)
    peer_b = (ep + core * to_y, tp + (1 - core) * 2 * to_x)
    sibling = (ep, tp + 1 - 2 * core)
    above, below = (ep + 2, tp), (ep - 2, tp)
    return peer_a, peer_b, sibling, above, below


def lane_spot(z_at, da, db, core_at):
    _, _, _, y, x, _ = place()
    y_at = y + (1 - 2 * y) * ((1 - core_at) * da + core_at * db)
    x_at = x + (1 - 2 * x) * (core_at * da + (1 - core_at) * db)
    return z_at * 2 + y_at, x_at * 2 + core_at


def gather_all_kernel(x_ref, o_ref, up_sem, down_sem, a_sem, b_sem, s_sem, recv_sem, sib_sem, own_sem):
    ep, tp, z, y, x, core = place()
    rows, cols = x_ref.shape
    peer_a, peer_b, sibling, above, below = lane_peers()
    greet([peer_a, peer_b, sibling], True)

    def spot(z_at, da, db):
        group, quarter = lane_spot(z_at, da, db, core)
        return o_ref.at[
            pl.ds(pl.multiple_of(group * rows, rows), rows),
            pl.ds(pl.multiple_of(quarter * cols, cols), cols),
        ]

    def at(z_at, da, db):
        return z_at * 4 + da * 2 + db

    def arrived(z_at, da, db):
        block = spot(z_at, da, db)
        remote(block, block, s_sem.at[at(z_at, da, db)], recv_sem.at[at(z_at, da, db)], sibling).wait_recv()

    def up(z_at, source):
        return remote(source, spot(z_at, 0, 0), up_sem.at[z_at], recv_sem.at[at(z_at, 0, 0)], above)

    def down(z_at, source):
        return remote(source, spot(z_at, 0, 0), down_sem.at[z_at], recv_sem.at[at(z_at, 0, 0)], below)

    def over_a(z_at, source):
        return remote(source, spot(z_at, 0, 0), a_sem.at[z_at], recv_sem.at[at(z_at, 1, 0)], peer_a)

    def over_b(z_at, da, source):
        return remote(
            source, spot(z_at, da, 0), b_sem.at[z_at * 2 + da], recv_sem.at[at(z_at, da, 1)], peer_b
        )

    def to_sibling(z_at, da, db, source):
        n = at(z_at, da, db)
        return remote(source, spot(z_at, da, db), s_sem.at[n], sib_sem.at[n], sibling)

    own = pltpu.make_async_copy(x_ref, spot(z, 0, 0), own_sem)
    over_b(z, 0, x_ref).start()
    over_a(z, x_ref).start()

    @pl.when(z < 3)
    def _():
        up(z, x_ref).start()

    @pl.when(z > 0)
    def _():
        down(z, x_ref).start()

    to_sibling(z, 0, 0, x_ref).start()
    own.start()

    def from_a(z_at):
        arrived(z_at, 1, 0)
        block = spot(z_at, 1, 0)
        over_b(z_at, 1, block).start()
        to_sibling(z_at, 1, 0, block).start()

    def from_z(z_at, onward):
        arrived(z_at, 0, 0)
        block = spot(z_at, 0, 0)
        onward(block)
        over_a(z_at, block).start()
        over_b(z_at, 0, block).start()
        to_sibling(z_at, 0, 0, block).start()

    def from_below(z_at):
        def onward(block):
            @pl.when(z < 3)
            def _():
                up(z_at, block).start()

        from_z(z_at, onward)

    def from_above(z_at):
        def onward(block):
            @pl.when(z > 0)
            def _():
                down(z_at, block).start()

        from_z(z_at, onward)

    for d in range(1, 4):

        @pl.when(z >= d)
        def _(d=d):
            from_below(z - d)

        @pl.when(z + d <= 3)
        def _(d=d):
            from_above(z + d)

        if d == 1:
            from_a(z)
        else:

            @pl.when(z >= d - 1)
            def _(d=d):
                from_a(z - d + 1)

            @pl.when(z + d - 1 <= 3)
            def _(d=d):
                from_a(z + d - 1)

    @pl.when(z >= 3)
    def _():
        from_a(z - 3)

    @pl.when(z + 3 <= 3)
    def _():
        from_a(z + 3)

    def from_b(z_at, da):
        arrived(z_at, da, 1)
        to_sibling(z_at, da, 1, spot(z_at, da, 1)).start()

    for da in range(2):
        from_b(z, da)
    for d in range(1, 4):
        for da in range(2):

            @pl.when(z >= d)
            def _(d=d, da=da):
                from_b(z - d, da)

            @pl.when(z + d <= 3)
            def _(d=d, da=da):
                from_b(z + d, da)

    def finish_sibling(i, carry):
        block = spot(0, 0, 0)
        copy = remote(block, block, s_sem.at[i], sib_sem.at[i], sibling)
        copy.wait_recv()
        copy.wait_send()
        return carry

    lax.fori_loop(0, 16, finish_sibling, 0)

    def finish_links(i, carry):
        over_a(i, x_ref).wait_send()
        over_b(i, 0, x_ref).wait_send()
        over_b(i, 1, x_ref).wait_send()

        @pl.when((z < 3) & (i <= z))
        def _():
            up(i, x_ref).wait_send()

        @pl.when((z > 0) & (i >= z))
        def _():
            down(i, x_ref).wait_send()

        return carry

    lax.fori_loop(0, 4, finish_links, 0)
    own.wait()


def gather_all(value, cid):
    rows, cols = value.shape
    return pl.pallas_call(
        gather_all_kernel,
        out_shape=jax.ShapeDtypeStruct((8 * rows, 4 * cols), value.dtype),
        in_specs=[pl.BlockSpec(memory_space=pl.ANY)],
        out_specs=pl.BlockSpec(memory_space=pl.ANY),
        scratch_shapes=[
            pltpu.SemaphoreType.DMA((4,)),
            pltpu.SemaphoreType.DMA((4,)),
            pltpu.SemaphoreType.DMA((4,)),
            pltpu.SemaphoreType.DMA((8,)),
            pltpu.SemaphoreType.DMA((16,)),
            pltpu.SemaphoreType.DMA((16,)),
            pltpu.SemaphoreType.DMA((16,)),
            pltpu.SemaphoreType.DMA,
        ],
        compiler_params=pltpu.CompilerParams(collective_id=cid, has_side_effects=True),
        name="gather_all",
    )(value)


def z_chain(blocks, totals, from_below, from_above, up_send, up_recv, down_send, down_recv, rows, final):
    ep, tp, z, _, _, _ = place()
    above, below = (ep + 2, tp), (ep - 2, tp)

    def up(z_at):
        return remote(totals(z_at), from_below.at[z_at], up_send.at[z_at], up_recv.at[z_at], above)

    def down(z_at):
        return remote(totals(z_at), from_above.at[z_at], down_send.at[z_at], down_recv.at[z_at], below)

    for z_at in Z_ORDER:
        blocks(z_at)

        @pl.when(z_at > z)
        def _(z_at=z_at):
            @pl.when(z > 0)
            def _():
                up(z_at).wait_recv()
                add_blocks(totals(z_at), [from_below.at[z_at]], rows)

            up(z_at).start()

        @pl.when(z_at < z)
        def _(z_at=z_at):
            @pl.when(z < 3)
            def _():
                down(z_at).wait_recv()
                add_blocks(totals(z_at), [from_above.at[z_at]], rows)

            down(z_at).start()

    for z_at in range(4):

        @pl.when(z_at == z)
        def _(z_at=z_at):
            @pl.when(z > 0)
            def _():
                up(z_at).wait_recv()

            @pl.when(z < 3)
            def _():
                down(z_at).wait_recv()

            @pl.when(z == 0)
            def _():
                final(z_at, [from_above.at[z_at]])

            @pl.when(z == 3)
            def _():
                final(z_at, [from_below.at[z_at]])

            @pl.when((z > 0) & (z < 3))
            def _():
                final(z_at, [from_below.at[z_at], from_above.at[z_at]])

    for z_at in range(4):

        @pl.when(z_at > z)
        def _(z_at=z_at):
            up(z_at).wait_send()

        @pl.when(z_at < z)
        def _(z_at=z_at):
            down(z_at).wait_send()


def scatter_all_kernel(
    p_ref,
    o_ref,
    mine,
    from_sib,
    from_b,
    from_a,
    from_below,
    from_above,
    own_sem,
    s_send,
    s_recv,
    b_send,
    b_recv,
    a_send,
    a_recv,
    up_send,
    up_recv,
    down_send,
    down_recv,
):
    ep, tp, z, y, x, core = place()
    rows, cols = o_ref.shape
    peer_a, peer_b, sibling, above, below = lane_peers()
    greet([peer_a, peer_b, sibling], True)

    def part(z_at, da, db, core_at):
        group, quarter = lane_spot(z_at, da, db, core_at)
        return p_ref.at[
            pl.ds(pl.multiple_of(group * rows, rows), rows),
            pl.ds(pl.multiple_of(quarter * cols, cols), cols),
        ]

    def at(z_at, da, db):
        return z_at * 4 + da * 2 + db

    def own(z_at, da, db):
        n = at(z_at, da, db)
        return pltpu.make_async_copy(part(z_at, da, db, core), mine.at[n], own_sem.at[n])

    def to_sibling(z_at, da, db):
        n = at(z_at, da, db)
        return remote(
            part(z_at, da, db, 1 - core), from_sib.at[n], s_send.at[n], s_recv.at[n], sibling
        )

    for da, db in ((1, 1), (0, 1), (1, 0), (0, 0)):
        for z_at in Z_ORDER:
            to_sibling(z_at, da, db).start()
            own(z_at, da, db).start()

    def here(z_at, da, db):
        own(z_at, da, db).wait()
        to_sibling(z_at, da, db).wait_recv()
        return mine.at[at(z_at, da, db)], from_sib.at[at(z_at, da, db)]

    def over_b(z_at, da):
        n = z_at * 2 + da
        return remote(mine.at[at(z_at, da, 1)], from_b.at[n], b_send.at[n], b_recv.at[n], peer_b)

    def over_a(z_at):
        return remote(mine.at[at(z_at, 1, 0)], from_a.at[z_at], a_send.at[z_at], a_recv.at[z_at], peer_a)

    for da in (1, 0):
        for z_at in Z_ORDER:
            own_part, sib_part = here(z_at, da, 1)
            add_blocks(own_part, [sib_part], rows)
            over_b(z_at, da).start()
    for z_at in Z_ORDER:
        own_part, sib_part = here(z_at, 1, 0)
        over_b(z_at, 1).wait_recv()
        add_blocks(own_part, [sib_part, from_b.at[z_at * 2 + 1]], rows)
        over_a(z_at).start()

    def blocks(z_at):
        own_part, sib_part = here(z_at, 0, 0)
        over_b(z_at, 0).wait_recv()
        over_a(z_at).wait_recv()
        add_blocks(own_part, [sib_part, from_b.at[z_at * 2], from_a.at[z_at]], rows)

    def final(z_at, others):
        o_ref[...] = jnp.zeros_like(o_ref)
        add_blocks(o_ref, [mine.at[at(z_at, 0, 0)], *others], rows)

    z_chain(
        blocks,
        lambda z_at: mine.at[at(z_at, 0, 0)],
        from_below,
        from_above,
        up_send,
        up_recv,
        down_send,
        down_recv,
        rows,
        final,
    )
    for z_at in range(4):
        over_a(z_at).wait_send()
        for da in range(2):
            over_b(z_at, da).wait_send()
            for db in range(2):
                to_sibling(z_at, da, db).wait_send()


def scatter_all(value, cid):
    rows, cols = value.shape[0] // 8, value.shape[1] // 4
    dma = pltpu.SemaphoreType.DMA

    def held(count):
        return pltpu.VMEM((count, rows, cols), value.dtype)

    return pl.pallas_call(
        scatter_all_kernel,
        out_shape=jax.ShapeDtypeStruct((rows, cols), jnp.float32),
        in_specs=[pl.BlockSpec(memory_space=pl.ANY)],
        out_specs=pl.BlockSpec(memory_space=pltpu.VMEM),
        scratch_shapes=[held(16), held(16), held(8), held(4), held(4), held(4)]
        + [dma((16,)), dma((16,)), dma((16,)), dma((8,)), dma((8,))]
        + [dma((4,))] * 6,
        compiler_params=pltpu.CompilerParams(
            collective_id=cid, has_side_effects=True, vmem_limit_bytes=48 * 2**20
        ),
        name="scatter_all",
    )(value)


def scatter_ep_kernel(
    p_ref, e_ref, o_ref, mine, from_y, from_below, from_above, own_sem, y_send, y_recv, up_send, up_recv, down_send, down_recv
):
    ep, tp, z, y, _, _ = place()
    rows, extra = p_ref.shape[0] // 8, e_ref.shape[0]
    tall = rows + extra
    across = (ep + 1 - 2 * y, tp)
    greet([across], True)

    def part(z_at, y_at):
        return p_ref.at[pl.ds(pl.multiple_of((z_at * 2 + y_at) * rows, rows), rows), :]

    def own(z_at):
        return (
            pltpu.make_async_copy(part(z_at, y), mine.at[z_at, pl.ds(0, rows)], own_sem.at[z_at]),
            pltpu.make_async_copy(e_ref, mine.at[z_at, pl.ds(rows, extra)], own_sem.at[4 + z_at]),
        )

    def over_y(z_at):
        return (
            remote(
                part(z_at, 1 - y),
                from_y.at[z_at, pl.ds(0, rows)],
                y_send.at[z_at],
                y_recv.at[z_at],
                across,
            ),
            remote(
                e_ref,
                from_y.at[z_at, pl.ds(rows, extra)],
                y_send.at[4 + z_at],
                y_recv.at[4 + z_at],
                across,
            ),
        )

    for z_at in Z_ORDER:
        for copy in over_y(z_at) + own(z_at):
            copy.start()

    def blocks(z_at):
        for copy in own(z_at):
            copy.wait()
        for copy in over_y(z_at):
            copy.wait_recv()
        add_blocks(mine.at[z_at], [from_y.at[z_at]], tall)

    def final(z_at, others):
        o_ref[...] = jnp.zeros_like(o_ref)
        add_blocks(o_ref, [mine.at[z_at], *others], tall)

    z_chain(
        blocks,
        lambda z_at: mine.at[z_at],
        from_below,
        from_above,
        up_send,
        up_recv,
        down_send,
        down_recv,
        tall,
        final,
    )
    for z_at in range(4):
        for copy in over_y(z_at):
            copy.wait_send()


def scatter_ep(value, extra, cid):
    rows, cols = value.shape[0] // 8, value.shape[1]
    tall = rows + extra.shape[0]
    dma = pltpu.SemaphoreType.DMA

    def held():
        return pltpu.VMEM((4, tall, cols), value.dtype)

    return pl.pallas_call(
        scatter_ep_kernel,
        out_shape=jax.ShapeDtypeStruct((tall, cols), jnp.float32),
        in_specs=[pl.BlockSpec(memory_space=pl.ANY)] * 2,
        out_specs=pl.BlockSpec(memory_space=pltpu.VMEM),
        scratch_shapes=[held(), held(), held(), held()] + [dma((8,))] * 3 + [dma((4,))] * 4,
        compiler_params=pltpu.CompilerParams(
            collective_id=cid, has_side_effects=True, vmem_limit_bytes=40 * 2**20
        ),
        name="scatter_ep",
    )(value, extra)


def experts_kernel(
    expert_width,
    shared_width,
    expert_total,
    x_ref,
    g_ref,
    kept_ref,
    expert_gate_ref,
    shared_gate_ref,
    extra_ref,
    expert_up_ref,
    shared_up_ref,
    expert_down_ref,
    shared_down_ref,
    residual_ref,
    grad_ref,
    mixed_ref,
    logit_ref,
    expert_grads_ref,
    shared_grads_ref,
    all_ref,
    from_sib,
    from_b,
    from_a,
    from_z,
    in_ref,
    down_ref,
    scalars,
    kept_held,
    x_held,
    g_held,
    lin,
    hidden_grad,
    hidden_all,
    both_all,
    kept_cols,
    staged,
    mine,
    landed,
    x_tile,
    g_tile,
    tile_out,
    shared_out,
    up_sem,
    down_sem,
    a_sem,
    b_sem,
    s_sem,
    recv_sem,
    sib_sem,
    own_sem,
    load_sem,
    fetch_sem,
    store_sem,
    weight_sem,
    kept_send,
    kept_recv,
    rs_send,
    rs_recv,
    rb_send,
    rb_recv,
    ra_send,
    ra_recv,
    rz_send,
    rz_recv,
):
    ep, tp, z, y, x, core = place()
    rows, cols = x_ref.shape
    width = down_ref.shape[0]
    filled = expert_width + shared_width
    tall = mine.shape[1]
    out_at = rows + 16
    cuts = ((0, out_at), (out_at, tall - out_at))
    peer_a, peer_b, sibling, above, below = lane_peers()
    sources = kept_held.shape[0]
    others = [(lax.rem(ep + i, sources), tp) for i in range(1, sources)]
    greet([(ep, tp + 2 - 4 * x), sibling] + others)

    def spot(z_at, da, db):
        group, quarter = lane_spot(z_at, da, db, core)
        return all_ref.at[
            pl.ds(pl.multiple_of(group * rows, rows), rows),
            pl.ds(pl.multiple_of(quarter * cols, cols), cols),
        ]

    def at(z_at, da, db):
        return z_at * 4 + da * 2 + db

    def choose(*values):
        return jnp.where(
            z == 0, values[0], jnp.where(z == 1, values[1], jnp.where(z == 2, values[2], values[3]))
        )

    coming = (z, choose(1, 2, 1, 2), choose(2, 0, 3, 1), choose(3, 3, 0, 0))
    turns = (z, choose(1, 2, 1, 2), choose(3, 3, 0, 0), choose(2, 0, 3, 1))

    def arrived(z_at, da, db):
        block, n = spot(z_at, da, db), at(z_at, da, db)
        remote(block, block, s_sem.at[n], recv_sem.at[n], sibling).wait_recv()
        return block

    def up(z_at, source):
        return remote(source, spot(z_at, 0, 0), up_sem.at[z_at], recv_sem.at[at(z_at, 0, 0)], above)

    def down(z_at, source):
        return remote(source, spot(z_at, 0, 0), down_sem.at[z_at], recv_sem.at[at(z_at, 0, 0)], below)

    def over_a(z_at, source):
        return remote(source, spot(z_at, 0, 0), a_sem.at[z_at], recv_sem.at[at(z_at, 1, 0)], peer_a)

    def over_b(z_at, da, source):
        return remote(
            source, spot(z_at, da, 0), b_sem.at[z_at * 2 + da], recv_sem.at[at(z_at, da, 1)], peer_b
        )

    def to_sibling(z_at, da, db, source):
        n = at(z_at, da, db)
        return remote(source, spot(z_at, da, db), s_sem.at[n], sib_sem.at[n], sibling)

    def pass_z(z_at):
        block = arrived(z_at, 0, 0)

        @pl.when((z_at > z) & (z > 0))
        def _():
            down(z_at, block).start()

        @pl.when((z_at < z) & (z < 3))
        def _():
            up(z_at, block).start()

        over_a(z_at, block).start()
        over_b(z_at, 0, block).start()
        to_sibling(z_at, 0, 0, block).start()

    def pass_a(z_at, onward=True):
        block = arrived(z_at, 1, 0)
        if onward:
            over_b(z_at, 1, block).start()
        to_sibling(z_at, 1, 0, block).start()

    def pass_b(z_at, da):
        block = arrived(z_at, da, 1)
        to_sibling(z_at, da, 1, block).start()

    def sibling_blocks(k, dy):
        for dx in range(2):
            da, db = core * dy + (1 - core) * dx, core * dx + (1 - core) * dy
            n = at(turns[k], da, db)
            block = spot(0, 0, 0)
            remote(block, block, s_sem.at[n], sib_sem.at[n], sibling).wait_recv()

    def group_rows(k, dy):
        group = turns[k] * 2 + y + (1 - 2 * y) * dy
        return group, pl.ds(pl.multiple_of(group * rows, rows), rows)

    def load_x(k, dy):
        _, span = group_rows(k, dy)
        return pltpu.make_async_copy(all_ref.at[span, :], x_held, load_sem.at[0])

    def load_g(k, dy):
        _, span = group_rows(k, dy)
        return pltpu.make_async_copy(g_ref.at[span, :], g_held, load_sem.at[1])

    def project():
        def body(i, carry):
            cut = pl.ds(pl.multiple_of(i * width, width), width)
            lin[:, cut] = times_transpose(x_held[...], in_ref[cut, :])
            return carry

        lax.fori_loop(0, 2, body, 0)

    def project_grad():
        hidden_grad[...] = times_transpose(g_held[...], down_ref[...])

    step = 64
    tile_start = width - 128
    logit_at = filled - tile_start

    def activate(k, dy):
        group, _ = group_rows(k, dy)
        lane = lax.broadcasted_iota(jnp.int32, (1, width), 1)
        near = lax.broadcasted_iota(jnp.int32, (1, 128), 1)
        is_logit = (near >= logit_at) & (near < logit_at + expert_total)
        kept_cols[:, :16] = kept_held[group].astype(jnp.float32).T

        def body(i, carry):
            span = pl.ds(pl.multiple_of(i * step, step), step)
            whole = pl.ds(pl.multiple_of(group * rows + i * step, step), step)
            gate_lin, up_lin = lin[span, :width], lin[span, width:]
            grad = hidden_grad[span, :]
            tail = lin[span, tile_start:width]
            if k == 0 and dy == 0:
                logit_ref[span, :] = tail
            most = jnp.max(jnp.where(is_logit, tail, -1e30), axis=1, keepdims=True)
            powers = jnp.where(is_logit, jnp.exp(jnp.minimum(tail - most, 0.0)), 0.0)
            kept = jnp.sum(jnp.where(near == ep, kept_cols[span, :], 0.0), axis=1, keepdims=True)
            gate = jnp.sum(jnp.where(near == logit_at + ep, powers, 0.0), axis=1, keepdims=True)
            gate = gate / jnp.sum(powers, axis=1, keepdims=True) * kept
            switch = jax.nn.sigmoid(
                jnp.sum(
                    jnp.where(near == logit_at + expert_total, tail, 0.0), axis=1, keepdims=True
                )
            )
            scale = jnp.where(lane < expert_width, gate, switch)
            sig = jax.nn.sigmoid(gate_lin)
            act = gate_lin * sig
            hidden = act * up_lin
            agreement = hidden * grad
            gate_part = jnp.sum(jnp.where(lane < expert_width, agreement, 0.0), axis=1, keepdims=True)
            switch_part = jnp.sum(
                jnp.where(lane < expert_width, 0.0, agreement), axis=1, keepdims=True
            )
            scaled = grad * scale
            hidden_all[whole, :] = (hidden * scale).astype(jnp.bfloat16)
            both_all[whole, :width] = (
                scaled * up_lin * sig * (1.0 + gate_lin * (1.0 - sig))
            ).astype(jnp.bfloat16)
            both_all[whole, width:] = (scaled * act).astype(jnp.bfloat16)
            scalars[span, :] = jnp.where(
                near == ep, gate_part, jnp.where(near == expert_total, switch_part, 0.0)
            )
            return carry

        lax.fori_loop(0, rows // step, body, 0)

    def hold(k, da, db):
        slot = 2 if k == 0 else k % 2
        return db * (7 + slot * 2 + da) + (1 - db) * (da * (4 + slot) + (1 - da) * k)

    def lane_offsets(dx, dy, core_at):
        return (1 - core_at) * dy + core_at * dx, (1 - core_at) * dx + core_at * dy

    def rs_sibling(k, dx, dy):
        n = at(turns[k], *lane_offsets(dx, dy, 1 - core))
        return remote(staged.at[dx], from_sib.at[n], rs_send.at[n], rs_recv.at[n], sibling)

    def block_rows(k, dy):
        sums = scalars[...].T[:16, :].astype(jnp.bfloat16)
        _, span = group_rows(k, dy)

        def fill(target, cut):
            target[:rows, :] = jnp.dot(
                both_all[span, :], in_ref[:, cut], preferred_element_type=jnp.float32
            ).astype(jnp.bfloat16)
            target[rows:out_at, :] = sums
            target[out_at:, :] = jnp.dot(
                hidden_all[span, :], down_ref[:, cut], preferred_element_type=jnp.float32
            ).astype(jnp.bfloat16)

        def body(dx, carry):
            x_at = x + (1 - 2 * x) * dx
            fill(staged.at[dx], pl.ds(pl.multiple_of((x_at * 2 + 1 - core) * cols, cols), cols))
            rs_sibling(k, dx, dy).start()
            fill(
                mine.at[hold(k, *lane_offsets(dx, dy, core))],
                pl.ds(pl.multiple_of((x_at * 2 + core) * cols, cols), cols),
            )
            return carry

        lax.fori_loop(0, 2, body, 0)

    def staged_free(k, dy):
        for dx in range(2):
            rs_sibling(k, dx, dy).wait_send()

    def rs_over_b(k, da, part):
        n, span = turns[k] * 2 + da, pl.ds(*cuts[part])
        return remote(
            mine.at[hold(k, da, 1), span],
            from_b.at[n, span],
            rb_send.at[n * 2 + part],
            rb_recv.at[n * 2 + part],
            peer_b,
        )

    def rs_over_a(k, part):
        z_at, span = turns[k], pl.ds(*cuts[part])
        return remote(
            mine.at[hold(k, 1, 0), span],
            from_a.at[z_at, span],
            ra_send.at[z_at * 2 + part],
            ra_recv.at[z_at * 2 + part],
            peer_a,
        )

    def rs_along_z(k, part):
        span = pl.ds(*cuts[part])
        return remote(
            mine.at[k, span],
            from_z.at[z, span],
            rz_send.at[k * 2 + part],
            rz_recv.at[z * 2 + part],
            (ep + 2 * (turns[k] - z), tp),
        )

    def fetch(source, i):
        return pltpu.make_async_copy(source, landed.at[i], fetch_sem.at[i])

    def fetch_part(source, half, i):
        span = pl.ds(*cuts[half])
        return pltpu.make_async_copy(source.at[span], landed.at[i, span], fetch_sem.at[i])

    def fetch_sibling(k, dy):
        for dx in range(2):
            n = at(turns[k], *lane_offsets(dx, dy, core))
            remote(staged.at[0], from_sib.at[n], rs_send.at[n], rs_recv.at[n], sibling).wait_recv()
            fetch(from_sib.at[n], dx).start()

    def reduce_sibling(k, dy):
        for dx in range(2):
            n = at(turns[k], *lane_offsets(dx, dy, core))
            fetch(from_sib.at[n], dx).wait()
            add_blocks(mine.at[hold(k, *lane_offsets(dx, dy, core))], [landed.at[dx]], tall)

        for part in range(2):

            @pl.when(core == 0)
            def _(part=part):
                rs_over_b(k, dy, part).start()

            if dy == 1:

                @pl.when(core == 1)
                def _(part=part):
                    rs_over_b(k, 0, part).start()
                    rs_over_b(k, 1, part).start()

    def add_part(target, part, copies):
        first, count = cuts[part]
        span = pl.ds(first, count)
        for copy in copies:
            copy.wait()
        add_blocks(
            mine.at[target, span], [landed.at[i, span] for i in range(len(copies))], count
        )

    def reduce_b(k, part):
        rs_over_b(k, 1, part).wait_recv()
        copy = fetch_part(from_b.at[turns[k] * 2 + 1], part, 0)
        copy.start()
        add_part(hold(k, 1, 0), part, [copy])
        rs_over_a(k, part).start()

    def reduce_a(k, part):
        z_at = turns[k]
        rs_over_b(k, 0, part).wait_recv()
        rs_over_a(k, part).wait_recv()
        copies = [
            fetch_part(from_b.at[z_at * 2], part, 0),
            fetch_part(from_a.at[z_at], part, 1),
        ]
        for copy in copies:
            copy.start()
        add_part(k, part, copies)
        if k > 0:
            rs_along_z(k, part).start()

    def reduce_z(i, part):
        source = (choose(3, 0, 3, 0), choose(2, 2, 1, 1), choose(1, 3, 0, 2))[i]
        span = pl.ds(*cuts[part])
        remote(
            mine.at[0, span],
            from_z.at[source, span],
            rz_send.at[0],
            rz_recv.at[source * 2 + part],
            sibling,
        ).wait_recv()
        copy = fetch_part(from_z.at[source], part, 0)
        copy.start()
        add_part(0, part, [copy])

    tile = x_tile.shape[1]

    def load_tile(source, target, t, sem):
        cut = pl.ds(pl.multiple_of(t * tile, tile), tile)
        return pltpu.make_async_copy(source.at[:, cut], target, load_sem.at[sem])

    def tile_stores(t, kind):
        cut = pl.ds(pl.multiple_of(t * tile, tile), tile)
        return (
            pltpu.make_async_copy(
                tile_out.at[kind, pl.ds(0, expert_width)],
                expert_grads_ref.at[kind, :, cut],
                store_sem.at[kind],
            ),
            pltpu.make_async_copy(
                shared_out.at[kind], shared_grads_ref.at[t, kind], store_sem.at[3 + kind]
            ),
        )

    def weight_tile(t, kind):
        @pl.when(t > 0)
        def _():
            for copy in tile_stores(t - 1, kind):
                copy.wait()

        if kind == 0:
            left, right = hidden_all[:, :filled], g_tile[...]
        else:
            left, right = both_all[:, (kind - 1) * width : (kind - 1) * width + filled], x_tile[...]
        result = inner_rows(left, right)
        tile_out[kind] = result
        shared_out[kind] = result[expert_width:, :].astype(jnp.bfloat16)
        for copy in tile_stores(t, kind):
            copy.start()

    own = pltpu.make_async_copy(x_ref, spot(z, 0, 0), own_sem)
    over_b(z, 0, x_ref).start()
    over_a(z, x_ref).start()

    @pl.when(z < 3)
    def _():
        up(z, x_ref).start()

    @pl.when(z > 0)
    def _():
        down(z, x_ref).start()

    to_sibling(z, 0, 0, x_ref).start()
    own.start()
    load_g(0, 0).start()

    def kept_to(i):
        return remote(
            kept_ref, kept_held.at[ep], kept_send.at[i - 1], kept_recv.at[i - 1], others[i - 1]
        )

    for i in range(1, sources):
        kept_to(i).start()
    own_kept = pltpu.make_async_copy(kept_ref, kept_held.at[ep], weight_sem.at[7])
    own_kept.start()
    pieces = [
        (expert_down_ref, down_ref, 0),
        (
            shared_down_ref.at[pl.ds(pl.multiple_of(ep * shared_width, 16), shared_width), :],
            down_ref,
            expert_width,
        ),
        (expert_gate_ref, in_ref, 0),
        (extra_ref, in_ref, filled),
        (expert_up_ref, in_ref, width),
    ]
    weight_copies = [
        pltpu.make_async_copy(piece, target.at[pl.ds(at_row, piece.shape[0]), :], weight_sem.at[i])
        for i, (piece, target, at_row) in enumerate(pieces)
    ]
    model_dim = in_ref.shape[1]
    window = (shared_width // 128 + 2) * 128
    first_tile = lax.min(ep * shared_width // 128, (shared_gate_ref.shape[1] - window) // 128)
    offset = ep * shared_width - first_tile * 128
    for i, source in enumerate((shared_gate_ref, shared_up_ref)):
        weight_copies.append(
            pltpu.make_async_copy(
                source.at[:, pl.ds(pl.multiple_of(first_tile * 128, 128), window)],
                both_all.at[pl.ds(i * model_dim, model_dim), pl.ds(0, window)],
                weight_sem.at[5 + i],
            )
        )
    for copy in weight_copies:
        copy.start()
    for target, first, last_row in (
        (in_ref, filled + 16, width),
        (in_ref, width + filled, 2 * width),
        (down_ref, filled, width),
    ):
        target[first:last_row, :] = jnp.zeros((last_row - first, target.shape[1]), target.dtype)
    for copy in weight_copies:
        copy.wait()
    picked = (
        lax.broadcasted_iota(jnp.int32, (shared_width, window), 1)
        == lax.broadcasted_iota(jnp.int32, (shared_width, window), 0) + offset
    ).astype(jnp.bfloat16)

    def pick_rows(i, carry):
        cut = pl.ds(pl.multiple_of(i * 512, 512), 512)
        for j in range(2):
            held = pl.ds(pl.multiple_of(j * model_dim + i * 512, 512), 512)
            at_row = j * width + expert_width
            in_ref[at_row : at_row + shared_width, cut] = times_transpose(
                picked, both_all[held, :window]
            ).astype(jnp.bfloat16)
        return carry

    lax.fori_loop(0, model_dim // 512, pick_rows, 0)
    load_g(0, 0).wait()
    project_grad()
    own_kept.wait()
    for i in range(1, sources):
        kept_to(i).wait_recv()
    own.wait()

    def ready(k, dy):
        if k > 0:
            pass_b(turns[k], dy)
        sibling_blocks(k, dy)
        load_x(k, dy).start()

    order = [(0, 0)] + [(k, dy) for k in range(1, 4) for dy in range(2)] + [(0, 1)]
    edge = (z == 0) | (z == 3)
    pass_z(coming[1])
    pass_a(z, False)
    pass_b(z, 0)

    @pl.when(jnp.logical_not(edge))
    def _():
        pass_z(coming[2])

    ready(0, 0)
    for s, (k, dy) in enumerate(order):
        following = order[s + 1] if s < 7 else None
        load_x(k, dy).wait()
        if s >= 1:
            fetch_sibling(*order[s - 1])
        project()
        if s >= 1:
            load_g(k, dy).wait()
            project_grad()
        if following is not None:
            load_g(*following).start()
        if s >= 1:
            reduce_sibling(*order[s - 1])
        if s == 1:
            pass_z(coming[3])
            over_b(z, 1, spot(z, 1, 0)).start()
        if s in (4, 6):
            reduce_b(s // 2 - 1, 0)
        activate(k, dy)
        if s == 0:

            @pl.when(edge)
            def _():
                pass_z(coming[2])

            pass_a(coming[1])
        if s == 1:
            pass_a(coming[2])
        if s == 2:
            pass_a(coming[3])
        if s == 4:
            pass_b(z, 1)
        if following is not None:
            ready(*following)
        if s in (4, 6):
            reduce_b(s // 2 - 1, 1)
        if s in (5, 7):
            reduce_a((s - 3) // 2, 0)
        if s >= 1:
            staged_free(*order[s - 1])
        if s == 5:
            for part in range(2):
                for da in range(2):
                    rs_over_b(1, da, part).wait_send()
                rs_over_a(1, part).wait_send()
        block_rows(k, dy)
        if s in (5, 7):
            reduce_a((s - 3) // 2, 1)

    load_tile(g_ref, g_tile, 0, 2).start()
    load_tile(all_ref, x_tile, 0, 3).start()
    tiles = shared_grads_ref.shape[0]
    services = {
        (0, 0): (fetch_sibling, 0, 1),
        (0, 1): (reduce_sibling, 0, 1),
        (1, 0): (reduce_b, 3, 0),
        (0, 2): (reduce_z, 0, 0),
        (1, 1): (reduce_z, 0, 1),
        (2, 0): (reduce_z, 1, 0),
        (3, 0): (reduce_z, 1, 1),
        (4, 0): (reduce_b, 3, 1),
        (4, 2): (reduce_a, 3, 0),
        (5, 1): (reduce_b, 0, 0),
        (6, 2): (reduce_a, 3, 1),
        (7, 0): (reduce_b, 0, 1),
    }

    def tile_step(t, carry):
        for kind in range(3):
            if kind == 0:
                load_tile(g_ref, g_tile, t, 2).wait()
            if kind == 1:
                load_tile(all_ref, x_tile, t, 3).wait()
            weight_tile(t, kind)

            @pl.when(t + 1 < tiles)
            def _(kind=kind):
                if kind == 0:
                    load_tile(g_ref, g_tile, t + 1, 2).start()
                if kind == 2:
                    load_tile(all_ref, x_tile, t + 1, 3).start()

            for (at_tile, at_kind), (service, *which) in services.items():
                if at_kind == kind:
                    pl.when(t == at_tile)(functools.partial(service, *which))
        return carry

    lax.fori_loop(0, tiles, tile_step, 0)
    for kind in range(3):
        for copy in tile_stores(tiles - 1, kind):
            copy.wait()

    for part in range(2):
        reduce_a(0, part)
        reduce_z(2, part)

    def total(i, carry):
        span = pl.ds(pl.multiple_of(i * 64, 64), 64)
        out_span = pl.ds(pl.multiple_of(out_at + i * 64, 16), 64)
        grad_ref[span, :] = mine[0, span, :].astype(jnp.float32)
        mixed_ref[span, :] = (
            residual_ref[span, :] + mine[0, out_span, :].astype(jnp.float32)
        ).astype(jnp.bfloat16)
        return carry

    lax.fori_loop(0, rows // 64, total, 0)
    grad_ref[rows:, :] = mine[0, rows:out_at, :].astype(jnp.float32)

    for i in range(1, sources):
        kept_to(i).wait_send()
    staged_free(0, 1)
    for k in range(1, 4):
        for part in range(2):
            rs_along_z(k, part).wait_send()
    for k in (0, 2, 3):
        for part in range(2):
            rs_over_a(k, part).wait_send()
            for da in range(2):
                rs_over_b(k, da, part).wait_send()

    def finish(i, carry):
        over_a(i, x_ref).wait_send()
        over_b(i, 0, x_ref).wait_send()
        over_b(i, 1, x_ref).wait_send()
        for n in range(4):
            block = spot(0, 0, 0)
            remote(block, block, s_sem.at[i * 4 + n], sib_sem.at[i * 4 + n], sibling).wait_send()

        @pl.when((z < 3) & (i <= z))
        def _():
            up(i, x_ref).wait_send()

        @pl.when((z > 0) & (i >= z))
        def _():
            down(i, x_ref).wait_send()

        return carry

    lax.fori_loop(0, 4, finish, 0)


def experts(x_cols, grads_all, kept_rows, weights, residual, expert_total, cid):
    rows, cols = x_cols.shape
    total, model_dim = grads_all.shape
    sources = total // rows
    expert_width, shared_width = weights[0].shape[0], weights[1].shape[1] // sources
    filled = expert_width + shared_width
    width = -(-(filled + expert_total + 1) // 128) * 128
    tall = 2 * rows + 16
    tile = model_dim // sources
    low, dma = jnp.bfloat16, pltpu.SemaphoreType.DMA
    vmem, hbm = pl.BlockSpec(memory_space=pltpu.VMEM), pl.BlockSpec(memory_space=pl.ANY)

    def landing(count):
        return jax.ShapeDtypeStruct((count, tall, cols), low)

    return pl.pallas_call(
        functools.partial(experts_kernel, expert_width, shared_width, expert_total),
        out_shape=[
            jax.ShapeDtypeStruct((rows + 16, cols), jnp.float32),
            jax.ShapeDtypeStruct((rows, cols), low),
            jax.ShapeDtypeStruct((rows, 128), jnp.float32),
            jax.ShapeDtypeStruct((3, expert_width, model_dim), jnp.float32),
            jax.ShapeDtypeStruct((sources, 3, shared_width, tile), low),
            jax.ShapeDtypeStruct((total, model_dim), low),
            landing(16),
            landing(8),
            landing(4),
            landing(4),
        ],
        in_specs=[hbm] * 10 + [vmem],
        out_specs=[vmem, vmem, vmem] + [hbm] * 7,
        scratch_shapes=[
            pltpu.VMEM((2 * width, model_dim), low),
            pltpu.VMEM((width, model_dim), low),
            pltpu.VMEM((rows, 128), jnp.float32),
            pltpu.VMEM((sources, 16, rows), low),
            pltpu.VMEM((rows, model_dim), low),
            pltpu.VMEM((rows, model_dim), low),
            pltpu.VMEM((rows, 2 * width), jnp.float32),
            pltpu.VMEM((rows, width), jnp.float32),
            pltpu.VMEM((total, width), low),
            pltpu.VMEM((total, 2 * width), low),
            pltpu.VMEM((rows, 128), jnp.float32),
            pltpu.VMEM((2, tall, cols), low),
            pltpu.VMEM((13, tall, cols), low),
            pltpu.VMEM((2, tall, cols), low),
            pltpu.VMEM((total, tile), low),
            pltpu.VMEM((total, tile), low),
            pltpu.VMEM((3, filled, tile), jnp.float32),
            pltpu.VMEM((3, shared_width, tile), low),
        ]
        + [dma((4,)), dma((4,)), dma((4,)), dma((8,)), dma((16,)), dma((16,)), dma((16,)), dma]
        + [dma((4,)), dma((2,)), dma((6,)), dma((8,)), dma((7,)), dma((7,))]
        + [dma((16,))] * 4
        + [dma((8,))] * 4,
        compiler_params=pltpu.CompilerParams(
            collective_id=cid, has_side_effects=True, vmem_limit_bytes=63 * 2**20
        ),
        name="experts",
    )(x_cols, grads_all, kept_rows, *weights, residual)


def row_of(columns):
    part = columns[:, :128]
    for i in range(1, columns.shape[1] // 128):
        part = part + columns[:, i * 128 : (i + 1) * 128]
    total = jnp.sum(part.T, axis=0, keepdims=True)
    return jnp.broadcast_to(total, (8, total.shape[1]))


def unwind_kernel(
    dn2_ref,
    unit_ref,
    inv_ref,
    second_ref,
    grad_ref,
    tokens_ref,
    inv_one_ref,
    first_ref,
    small_ref,
    q_ref,
    k_ref,
    v_ref,
    ke_ref,
    ve_ref,
    context_ref,
    log_ref,
    cos_ref,
    sin_ref,
    n1_hbm,
    wq_hbm,
    wk_hbm,
    wv_hbm,
    wo_hbm,
    tokens_grad_ref,
    weight_grads_ref,
    sums_ref,
    n1,
    wq,
    wk,
    wv,
    wo,
    grad_all,
    grad_own,
    hidden_grad,
    dc,
    dq,
    dk,
    dv,
    lin_grads,
    dke,
    dve,
    later_k,
    later_v,
    staged,
    mine,
    from_y,
    from_below,
    from_above,
    from_below_2,
    from_above_2,
    tp_staged,
    tp_mine,
    tp_sib,
    tp_x,
    dn1,
    row_mine,
    row_sib,
    row_x,
    smalls,
    quarters,
    load_sem,
    g_send,
    g_recv,
    row_send,
    row_recv,
    kv_send,
    kv_recv,
    y_send,
    y_recv,
    up_send,
    up_recv,
    down_send,
    down_recv,
    tp_send,
    tp_recv,
    small_send,
    small_recv,
    s_send,
    s_recv,
    up2_send,
    up2_recv,
    down2_send,
    down2_recv,
):
    ep, tp, z, y, x, core = place()
    rows, cols = unit_ref.shape
    model_dim = n1.shape[1]
    heads = cols // HD
    block = mine.shape[1]
    low, full = jnp.bfloat16, jnp.float32
    score_scale = HD ** (-0.5)
    sibling, across = (ep, tp + 1 - 2 * core), (ep, tp + 2 - 4 * x)
    beside = (ep + 1 - 2 * y, tp)
    above, below = (ep + 2, tp), (ep - 2, tp)
    sources = smalls.shape[0]
    others = [(lax.rem(ep + i, sources), tp) for i in range(1, sources)]
    loads = [
        pltpu.make_async_copy(source, target, load_sem.at[i])
        for i, (source, target) in enumerate(
            ((wo_hbm, wo), (n1_hbm, n1), (wq_hbm, wq), (wk_hbm, wk), (wv_hbm, wv))
        )
    ]
    for copy in loads:
        copy.start()
    greet([across, sibling] + others)

    step = 64

    def by_rows(body):
        def one(i, carry):
            body(pl.ds(pl.multiple_of(i * step, step), step))
            return carry

        lax.fori_loop(0, rows // step, one, 0)

    def row_exchange(i, values):
        row_mine[2 * i] = values
        first = remote(
            row_mine.at[2 * i], row_sib.at[i], row_send.at[2 * i], row_recv.at[2 * i], sibling
        )
        first.start()
        first.wait_recv()
        row_mine[2 * i + 1] = row_mine[2 * i] + row_sib[i]
        second = remote(
            row_mine.at[2 * i + 1],
            row_x.at[i],
            row_send.at[2 * i + 1],
            row_recv.at[2 * i + 1],
            across,
        )
        second.start()
        second.wait_recv()
        first.wait_send()
        second.wait_send()
        return (row_mine[2 * i + 1] + row_x[i]).T[:, :1]

    dn1[...] = dn2_ref[...] * second_ref[:1, :] * unit_ref[...]
    mean = row_exchange(0, row_of(dn1[...])) * (1.0 / model_dim)
    dn1[:, :128] = jnp.broadcast_to(mean, (rows, 128))

    def norm_two(span):
        scaled = dn2_ref[span, :] * second_ref[:1, :]
        value = grad_ref[span, :].astype(full) + inv_ref[span, :1] * (
            scaled - unit_ref[span, :] * dn1[span, :1]
        )
        hidden_grad[span, :] = value
        grad_own[span, :] = value.astype(low)

    by_rows(norm_two)

    def quarter(at):
        return grad_all.at[:, pl.ds(pl.multiple_of(at * cols, cols), cols)]

    g_x = remote(grad_own, quarter(tp), g_send.at[0], g_recv.at[0], across)
    g_s = remote(grad_own, quarter(tp), g_send.at[1], g_recv.at[1], sibling)
    g_x.start()
    g_s.start()
    own_cut = pl.ds(pl.multiple_of(tp * cols, cols), cols)
    grad_all[:, own_cut] = grad_own[...]
    g_x.wait_recv()
    theirs = quarter(tp + 2 - 4 * x)
    g_f = remote(theirs, theirs, g_send.at[2], g_recv.at[2], sibling)
    g_f.start()
    g_s.wait_recv()
    g_f.wait_recv()
    loads[0].wait()
    dc[...] = times_transpose(grad_all[...], wo[...]).astype(low)

    def over_y(kind, z_at):
        n = kind * 4 + z_at
        return remote(staged.at[n], from_y.at[n], y_send.at[n], y_recv.at[n], beside)

    def weight_blocks(kind, left, right):
        def other(i, carry):
            z_at = lax.rem(i * 3, 4)
            cut = pl.ds(pl.multiple_of((z_at * 2 + 1 - y) * block, block), block)
            staged[kind * 4 + z_at] = inner_rows(left[:, cut], right[...]).astype(low)
            over_y(kind, z_at).start()
            return carry

        def ours(i, carry):
            z_at = lax.rem(i * 3, 4)
            cut = pl.ds(pl.multiple_of((z_at * 2 + y) * block, block), block)
            mine[kind * 4 + z_at] = inner_rows(left[:, cut], right[...]).astype(low)
            return carry

        lax.fori_loop(0, 4, other, 0)
        lax.fori_loop(0, 4, ours, 0)

    def blocks_along_z(left, right):
        def one(i, carry):
            z_at = lax.rem(i * 3, 4)
            cut = pl.ds(pl.multiple_of((z_at * 2 + 1 - y) * block, block), block)
            staged[4 + z_at] = inner_rows(left[:, cut], right[...]).astype(low)
            cut = pl.ds(pl.multiple_of((z_at * 2 + y) * block, block), block)
            mine[4 + z_at] = inner_rows(left[:, cut], right[...]).astype(low)

            @pl.when((z == 0) & (z_at > 0))
            def _():
                up_2(z_at).start()
                up(1, z_at).start()

            @pl.when((z == 3) & (z_at < 3))
            def _():
                down_2(z_at).start()
                down(1, z_at).start()

            return carry

        lax.fori_loop(0, 4, one, 0)

    def up_2(z_at):
        return remote(
            staged.at[4 + z_at], from_below_2.at[z_at], up2_send.at[z_at], up2_recv.at[z_at], above
        )

    def down_2(z_at):
        return remote(
            staged.at[4 + z_at],
            from_above_2.at[z_at],
            down2_send.at[z_at],
            down2_recv.at[z_at],
            below,
        )

    def chain_2():
        def rise(z_at):
            up_2(z_at).wait_recv()
            add_blocks(staged.at[4 + z_at], [from_below_2.at[z_at]], block)
            up_2(z_at).start()

        def fall(z_at):
            down_2(z_at).wait_recv()
            add_blocks(staged.at[4 + z_at], [from_above_2.at[z_at]], block)
            down_2(z_at).start()

        @pl.when(z == 1)
        def _():
            rise(3)
            rise(2)
            fall(0)

        @pl.when(z == 2)
        def _():
            fall(0)
            fall(1)
            rise(3)

    def other_y_along_z():
        @pl.when(z > 0)
        def _():
            up_2(z).wait_recv()
            add_blocks(staged.at[4 + z], [from_below_2.at[z]], block)

        @pl.when(z < 3)
        def _():
            down_2(z).wait_recv()
            add_blocks(staged.at[4 + z], [from_above_2.at[z]], block)

        over_y(1, z).start()

    def own_first_along_z():
        over_y(1, z).wait_recv()
        add_blocks(mine.at[4 + z], [from_y.at[4 + z]], block)

    def up(kind, z_at):
        n = kind * 4 + z_at
        return remote(mine.at[n], from_below.at[n], up_send.at[n], up_recv.at[n], above)

    def down(kind, z_at):
        n = kind * 4 + z_at
        return remote(mine.at[n], from_above.at[n], down_send.at[n], down_recv.at[n], below)

    def y_stage(kind):
        def one(i, carry):
            z_at = lax.rem(i * 3, 4)
            n = kind * 4 + z_at
            over_y(kind, z_at).wait_recv()
            add_blocks(mine.at[n], [from_y.at[n]], block)

            @pl.when((z == 0) & (z_at > 0))
            def _():
                up(kind, z_at).start()

            @pl.when((z == 3) & (z_at < 3))
            def _():
                down(kind, z_at).start()

            return carry

        lax.fori_loop(0, 4, one, 0)

    def chain(kind):
        def rise(z_at):
            n = kind * 4 + z_at
            up(kind, z_at).wait_recv()
            add_blocks(mine.at[n], [from_below.at[n]], block)
            up(kind, z_at).start()

        def fall(z_at):
            n = kind * 4 + z_at
            down(kind, z_at).wait_recv()
            add_blocks(mine.at[n], [from_above.at[n]], block)
            down(kind, z_at).start()

        @pl.when(z == 1)
        def _():
            rise(3)
            rise(2)
            fall(0)

        @pl.when(z == 2)
        def _():
            fall(0)
            fall(1)
            rise(3)

    def final(kind):
        n = kind * 4 + z

        @pl.when(z > 0)
        def _():
            up(kind, z).wait_recv()

        @pl.when(z < 3)
        def _():
            down(kind, z).wait_recv()

        def one(i, carry):
            span = pl.ds(pl.multiple_of(i * 32, 32), 32)
            value = mine[n, span, :].astype(full)
            low_part = from_below[n, span, :].astype(full)
            high_part = from_above[n, span, :].astype(full)
            value = value + jnp.where(z > 0, low_part, 0.0) + jnp.where(z < 3, high_part, 0.0)
            weight_grads_ref[kind, span, :] = value
            return carry

        lax.fori_loop(0, block // 32, one, 0)

    weight_blocks(0, grad_all, context_ref)

    half = rows // 2

    def terms(h, qb, key_count, keys, values):
        cut = pl.ds(pl.multiple_of(h * HD, HD), HD)
        span = pl.ds(qb * half, half)
        lane = lax.broadcasted_iota(jnp.int32, (1, 128), 1)
        log_total = jnp.sum(jnp.where(lane == h, log_ref[span, :], 0.0), axis=1, keepdims=True)
        queries, grads = q_ref[span, cut], dc[span, cut]
        delta = jnp.sum(
            grads.astype(full) * context_ref[span, cut].astype(full), axis=1, keepdims=True
        )
        key_part, value_part = keys[:key_count, cut], values[:key_count, cut]
        probs = jnp.exp(times_transpose(queries, key_part) * score_scale - log_total)
        scores_grad = (probs * (times_transpose(grads, value_part) - delta)).astype(low)
        return (
            jnp.dot(scores_grad, key_part, preferred_element_type=full),
            inner_rows(scores_grad, queries),
            inner_rows(probs.astype(low), grads),
        )

    def spans(h, qb):
        return pl.ds(qb * half, half), pl.ds(pl.multiple_of(h * HD, HD), HD)

    later = (
        remote(dke, later_k, kv_send.at[0], kv_recv.at[0], beside),
        remote(dve, later_v, kv_send.at[1], kv_recv.at[1], beside),
    )

    @pl.when(y == 1)
    def _():
        def head(h, carry):
            cut = pl.ds(pl.multiple_of(h * HD, HD), HD)
            first = terms(h, 0, rows, ke_ref, ve_ref)
            dq[spans(h, 0)[0], cut] = first[0]
            dk[:, cut] = first[1]
            dv[:, cut] = first[2]
            second = terms(h, 1, rows, ke_ref, ve_ref)
            dq[spans(h, 1)[0], cut] = second[0]
            dke[:, cut] = ((dk[:, cut] + second[1]) * score_scale).astype(low)
            dve[:, cut] = (dv[:, cut] + second[2]).astype(low)
            return carry

        lax.fori_loop(0, heads, head, 0)
        for copy in later:
            copy.start()

    @pl.when(y == 0)
    def _():
        dq[...] = jnp.zeros_like(dq)

    y_stage(0)

    def head(h, carry):
        cut = pl.ds(pl.multiple_of(h * HD, HD), HD)
        second = terms(h, 1, rows, k_ref, v_ref)
        dq[half:, cut] = dq[half:, cut] + second[0]
        dk[:, cut] = second[1] * score_scale
        dv[:, cut] = second[2]
        first = terms(h, 0, half, k_ref, v_ref)
        dq[:half, cut] = dq[:half, cut] + first[0]
        dk[:half, cut] = dk[:half, cut] + first[1] * score_scale
        dv[:half, cut] = dv[:half, cut] + first[2]
        return carry

    lax.fori_loop(0, heads, head, 0)

    def rotate_back(source, target, scale):
        def one(h, carry):
            cut = pl.ds(pl.multiple_of(h * HD, HD), HD)
            value = source[:, cut] * scale
            turned = value * cos_ref[...] - pltpu.roll(value, HD // 2, 1) * sin_ref[...]
            lin_grads[target, :, cut] = turned.astype(low)
            return carry

        lax.fori_loop(0, heads, one, 0)

    rotate_back(dq, 0, score_scale)
    loads[1].wait()
    blocks_along_z(n1, lin_grads.at[0])
    chain(0)

    @pl.when(y == 0)
    def _():
        for copy in later:
            copy.wait_recv()

        def add(span):
            dk[span, :] = dk[span, :] + later_k[span, :].astype(full)
            dv[span, :] = dv[span, :] + later_v[span, :].astype(full)

        by_rows(add)

    rotate_back(dk, 1, 1.0)
    lin_grads[2] = dv[...].astype(low)
    weight_blocks(2, n1, lin_grads.at[1])
    weight_blocks(3, n1, lin_grads.at[2])
    for copy in loads[2:]:
        copy.wait()

    def dn1_part(at, target):
        cut = pl.ds(pl.multiple_of(at * cols, cols), cols)
        total = times_transpose(lin_grads[0], wq[cut, :])
        total = total + times_transpose(lin_grads[1], wk[cut, :])
        total = total + times_transpose(lin_grads[2], wv[cut, :])
        target[...] = total.astype(low)

    def to_sibling(i):
        return remote(tp_staged.at[i], tp_sib.at[i], tp_send.at[i], tp_recv.at[i], sibling)

    def part_of(i):
        x_at = 1 - x + (2 * x - 1) * i
        dn1_part(x_at * 2 + 1 - core, tp_staged.at[i])
        to_sibling(i).start()
        dn1_part(x_at * 2 + core, tp_mine.at[i])

    out_x = remote(tp_mine.at[0], tp_x, tp_send.at[2], tp_recv.at[2], across)
    part_of(0)
    to_sibling(0).wait_recv()
    add_blocks(tp_mine.at[0], [tp_sib.at[0]], rows)
    out_x.start()
    part_of(1)
    chain_2()
    to_sibling(1).wait_recv()
    out_x.wait_recv()

    def sum_parts(span):
        dn1[span, :] = (
            tp_mine[1, span, :].astype(full)
            + tp_sib[1, span, :].astype(full)
            + tp_x[span, :].astype(full)
        )

    by_rows(sum_parts)

    def unit_one(span):
        return tokens_ref[span, :].astype(full) * inv_one_ref[span, :1]

    def products(span):
        dq[span, :] = dn1[span, :] * unit_one(span)

    by_rows(products)
    gain_grad = jnp.sum(dq[...], axis=0, keepdims=True)
    dq[...] = dq[...] * first_ref[:1, :]
    total = row_exchange(1, row_of(dq[...]))
    dk[:, :128] = jnp.broadcast_to(total * (1.0 / model_dim), (rows, 128))

    def norm_one(span):
        scaled = dn1[span, :] * first_ref[:1, :]
        value = hidden_grad[span, :] + inv_one_ref[span, :1] * (
            scaled - unit_one(span) * dk[span, :1]
        )
        tokens_grad_ref[span, :] = value.astype(low)

    by_rows(norm_one)

    own = smalls.at[ep]
    own[...] = small_ref[...]
    own[0:1, :] = gain_grad
    for i in range(3):
        own[i + 1 : i + 2, :] = jnp.sum(lin_grads[i].astype(full), axis=0, keepdims=True)

    def small_to(i):
        return remote(own, own, small_send.at[i - 1], small_recv.at[i - 1], others[i - 1])

    for i in range(1, sources):
        small_to(i).start()
    other_y_along_z()
    chain(1)
    y_stage(2)
    final(0)
    chain(2)
    y_stage(3)
    chain(3)
    for i in range(1, sources):
        small_to(i).wait_recv()
    total = smalls[0]
    for i in range(1, sources):
        total = total + smalls[i]
    quarters[tp] = total
    s_x = remote(quarters.at[tp], quarters.at[tp], s_send.at[0], s_recv.at[0], across)
    s_s = remote(quarters.at[tp], quarters.at[tp], s_send.at[1], s_recv.at[1], sibling)
    s_x.start()
    s_s.start()
    final(2)
    own_first_along_z()
    s_x.wait_recv()
    other = quarters.at[tp + 2 - 4 * x]
    s_f = remote(other, other, s_send.at[2], s_recv.at[2], sibling)
    s_f.start()
    final(3)
    final(1)
    s_s.wait_recv()
    s_f.wait_recv()
    sums_ref[...] = quarters[...]

    for copy in (g_x, g_s, g_f, s_x, s_s, s_f, out_x, to_sibling(0), to_sibling(1)):
        copy.wait_send()

    @pl.when(y == 1)
    def _():
        for copy in later:
            copy.wait_send()

    for i in range(1, sources):
        small_to(i).wait_send()

    def finish(n, carry):
        z_at = lax.rem(n, 4)

        @pl.when((n < 4) | (n >= 8) | (n == 4 + z))
        def _():
            remote(staged.at[0], from_y.at[0], y_send.at[n], y_recv.at[n], beside).wait_send()


        @pl.when(z_at > z)
        def _():
            remote(mine.at[0], from_below.at[0], up_send.at[n], up_recv.at[n], above).wait_send()

        @pl.when(z_at < z)
        def _():
            remote(mine.at[0], from_above.at[0], down_send.at[n], down_recv.at[n], below).wait_send()

        return carry

    lax.fori_loop(0, 16, finish, 0)

    def finish_2(z_at, carry):
        @pl.when(z_at > z)
        def _():
            up_2(z_at).wait_send()

        @pl.when(z_at < z)
        def _():
            down_2(z_at).wait_send()

        return carry

    lax.fori_loop(0, 4, finish_2, 0)


def unwind(vmem_args, hbm_args, cid):
    rows, cols = vmem_args[0].shape
    model_dim = hbm_args[0].shape[1]
    sources = 8
    block = model_dim // sources
    low, full, dma = jnp.bfloat16, jnp.float32, pltpu.SemaphoreType.DMA
    vmem, hbm = pl.BlockSpec(memory_space=pltpu.VMEM), pl.BlockSpec(memory_space=pl.ANY)

    def buffers(*shape, dtype=low):
        return pltpu.VMEM(shape, dtype)

    return pl.pallas_call(
        unwind_kernel,
        out_shape=[
            jax.ShapeDtypeStruct((rows, cols), low),
            jax.ShapeDtypeStruct((4, block, cols), full),
            jax.ShapeDtypeStruct((4, 16, cols), full),
        ],
        in_specs=[vmem] * len(vmem_args) + [hbm] * len(hbm_args),
        out_specs=[vmem] * 3,
        scratch_shapes=[buffers(*arg.shape) for arg in hbm_args]
        + [
            buffers(rows, model_dim),
            buffers(rows, cols),
            buffers(rows, cols, dtype=full),
            buffers(rows, cols),
            buffers(rows, cols, dtype=full),
            buffers(rows, cols, dtype=full),
            buffers(rows, cols, dtype=full),
            buffers(3, rows, cols),
            buffers(rows, cols),
            buffers(rows, cols),
            buffers(rows, cols),
            buffers(rows, cols),
        ]
        + [buffers(16, block, cols)] * 5
        + [buffers(4, block, cols)] * 2
        + [
            buffers(2, rows, cols),
            buffers(2, rows, cols),
            buffers(2, rows, cols),
            buffers(rows, cols),
            buffers(rows, cols, dtype=full),
            buffers(4, 8, rows, dtype=full),
            buffers(2, 8, rows, dtype=full),
            buffers(2, 8, rows, dtype=full),
            buffers(sources, 16, cols, dtype=full),
            buffers(4, 16, cols, dtype=full),
        ]
        + [dma((5,)), dma((3,)), dma((3,)), dma((4,)), dma((4,)), dma((2,)), dma((2,))]
        + [dma((16,))] * 6
        + [dma((3,)), dma((3,)), dma((7,)), dma((7,)), dma((3,)), dma((3,))]
        + [dma((4,))] * 4,
        compiler_params=pltpu.CompilerParams(
            collective_id=cid, has_side_effects=True, vmem_limit_bytes=60 * 2**20
        ),
        name="unwind",
    )(*vmem_args, *hbm_args)


def attend_kernel(
    first_ref,
    bias_ref,
    second_ref,
    cos_ref,
    sin_ref,
    tokens_hbm,
    grad_hbm,
    wq_hbm,
    wk_hbm,
    wv_hbm,
    wo_hbm,
    hidden_ref,
    unit_ref,
    inv_ref,
    normed_ref,
    n1_ref,
    inv_one_ref,
    q_ref,
    k_ref,
    v_ref,
    ke_ref,
    ve_ref,
    context_ref,
    log_ref,
    all_ref,
    wq,
    wk,
    wv,
    wo,
    tokens,
    lin,
    total,
    most,
    weight,
    earlier_k,
    earlier_v,
    tp_staged,
    tp_mine,
    tp_sib,
    tp_x,
    row_mine,
    row_sib,
    row_x,
    load_sem,
    t_send,
    t_recv,
    kv_send,
    kv_recv,
    tp_send,
    tp_recv,
    row_send,
    row_recv,
    up_sem,
    down_sem,
    a_sem,
    b_sem,
    s_sem,
    recv_sem,
    sib_sem,
):
    ep, tp, z, y, x, core = place()
    rows, cols = hidden_ref.shape
    model_dim = n1_ref.shape[1]
    heads = cols // HD
    low, full = jnp.bfloat16, jnp.float32
    score_scale = HD ** (-0.5)
    sibling, across = (ep, tp + 1 - 2 * core), (ep, tp + 2 - 4 * x)
    beside = (ep + 1 - 2 * y, tp)
    peer_a, peer_b, _, above, below = lane_peers()

    def quarter(at):
        return tokens.at[:, pl.ds(pl.multiple_of(at * cols, cols), cols)]

    loads = [
        pltpu.make_async_copy(source, target, load_sem.at[i])
        for i, (source, target) in enumerate(
            (
                (tokens_hbm, quarter(tp)),
                (wk_hbm, wk),
                (wv_hbm, wv),
                (wq_hbm, wq),
                (wo_hbm, wo),
            )
        )
    ]
    for copy in loads:
        copy.start()
    greet([across, beside, sibling], True)

    t_x = remote(tokens_hbm, quarter(tp), t_send.at[0], t_recv.at[0], across)
    t_s = remote(tokens_hbm, quarter(tp), t_send.at[1], t_recv.at[1], sibling)
    t_x.start()
    t_s.start()

    def choose(*values):
        return jnp.where(
            z == 0, values[0], jnp.where(z == 1, values[1], jnp.where(z == 2, values[2], values[3]))
        )

    coming = (z, choose(1, 0, 3, 2), choose(2, 2, 1, 1), choose(3, 3, 0, 0))

    def spot(z_at, da, db):
        group, at_quarter = lane_spot(z_at, da, db, core)
        return all_ref.at[
            pl.ds(pl.multiple_of(group * rows, rows), rows),
            pl.ds(pl.multiple_of(at_quarter * cols, cols), cols),
        ]

    def at(z_at, da, db):
        return z_at * 4 + da * 2 + db

    def arrived(z_at, da, db):
        block, n = spot(z_at, da, db), at(z_at, da, db)
        remote(block, block, s_sem.at[n], recv_sem.at[n], sibling).wait_recv()
        return block

    def up(z_at, da, source):
        n = z_at * 2 + da
        target = recv_sem.at[at(z_at, da, 0)]
        return remote(source, spot(z_at, da, 0), up_sem.at[n], target, above)

    def down(z_at, da, source):
        n = z_at * 2 + da
        target = recv_sem.at[at(z_at, da, 0)]
        return remote(source, spot(z_at, da, 0), down_sem.at[n], target, below)

    def over_a(source):
        return remote(source, spot(z, 0, 0), a_sem, recv_sem.at[at(z, 1, 0)], peer_a)

    def over_b(z_at, da, source):
        return remote(
            source, spot(z_at, da, 0), b_sem.at[z_at * 2 + da], recv_sem.at[at(z_at, da, 1)], peer_b
        )

    def to_sibling(z_at, da, db, source):
        n = at(z_at, da, db)
        return remote(source, spot(z_at, da, db), s_sem.at[n], sib_sem.at[n], sibling)

    def along_z(da, source):
        @pl.when(z < 3)
        def _():
            up(z, da, source).start()

        @pl.when(z > 0)
        def _():
            down(z, da, source).start()

    def pass_a():
        block = arrived(z, 1, 0)
        along_z(1, block)
        over_b(z, 1, block).start()
        to_sibling(z, 1, 0, block).start()

    def pass_z(k, da):
        z_at = coming[k]
        block = arrived(z_at, da, 0)

        @pl.when((z_at > z) & (z > 0))
        def _():
            down(z_at, da, block).start()

        @pl.when((z_at < z) & (z < 3))
        def _():
            up(z_at, da, block).start()

        over_b(z_at, da, block).start()
        to_sibling(z_at, da, 0, block).start()

    def pass_b(k, da):
        block = arrived(coming[k], da, 1)
        to_sibling(coming[k], da, 1, block).start()

    own = pltpu.make_async_copy(grad_hbm, spot(z, 0, 0), load_sem.at[5])
    over_a(grad_hbm).start()
    along_z(0, grad_hbm)
    over_b(z, 0, grad_hbm).start()
    to_sibling(z, 0, 0, grad_hbm).start()
    own.start()

    t_x.wait_recv()
    theirs = quarter(tp + 2 - 4 * x)
    t_f = remote(theirs, theirs, t_send.at[2], t_recv.at[2], sibling)
    t_f.start()
    loads[0].wait()
    t_s.wait_recv()
    t_f.wait_recv()

    def by_rows(step, body):
        def one(i, carry):
            body(pl.ds(pl.multiple_of(i * step, step), step))
            return carry

        lax.fori_loop(0, rows // step, one, 0)

    def norm_one(span):
        values = tokens[span, :].astype(full)
        inv = lax.rsqrt(jnp.mean(values * values, axis=1, keepdims=True) + norm_eps)
        n1_ref[span, :] = (values * inv * first_ref[:1, :]).astype(low)
        inv_one_ref[span, :] = jnp.broadcast_to(inv, (inv.shape[0], 128))

    by_rows(32, norm_one)
    pass_a()
    pass_z(1, 0)

    def project(weights, bias_at):
        def one(i, carry):
            cut = pl.ds(pl.multiple_of(i * 256, 256), 256)
            lin[:, cut] = (
                jnp.dot(n1_ref[...], weights[:, cut], preferred_element_type=full)
                + bias_ref[bias_at : bias_at + 1, cut]
            )
            return carry

        lax.fori_loop(0, cols // 256, one, 0)

    def rotate_into(target):
        def one(h, carry):
            cut = pl.ds(pl.multiple_of(h * HD, HD), HD)
            value = lin[:, cut]
            turned = value * cos_ref[...] + pltpu.roll(value, HD // 2, 1) * sin_ref[...]
            target[:, cut] = turned.astype(low)
            return carry

        lax.fori_loop(0, heads, one, 0)

    loads[1].wait()
    project(wk, 1)
    rotate_into(k_ref)
    loads[2].wait()
    project(wv, 2)
    v_ref[...] = lin[...].astype(low)
    earlier = (
        remote(k_ref, earlier_k, kv_send.at[0], kv_recv.at[0], beside),
        remote(v_ref, earlier_v, kv_send.at[1], kv_recv.at[1], beside),
    )

    @pl.when(y == 0)
    def _():
        for copy in earlier:
            copy.start()

    pass_b(0, 0)
    pass_z(2, 0)
    pass_z(1, 1)
    loads[3].wait()
    project(wq, 0)
    rotate_into(q_ref)

    half = rows // 2
    lane = lax.broadcasted_iota(jnp.int32, (1, 128), 1)

    def pick(held, span, h):
        return jnp.sum(jnp.where(lane == h, held[span, :], 0.0), axis=1, keepdims=True)

    def put(held, span, h, value):
        held[span, :] = jnp.where(lane == h, value, held[span, :])

    most[...] = jnp.zeros_like(most)
    weight[...] = jnp.ones_like(weight)

    def local_head(h, carry):
        cut = pl.ds(pl.multiple_of(h * HD, HD), HD)
        for qb in range(2):
            span, count = pl.ds(qb * half, half), (qb + 1) * half
            scores = times_transpose(q_ref[span, cut], k_ref[:count, cut]) * score_scale
            top = jnp.max(scores, axis=1, keepdims=True)
            powers = jnp.exp(scores - top)
            put(most, span, h, top)
            put(weight, span, h, jnp.sum(powers, axis=1, keepdims=True))
            total[span, cut] = jnp.dot(
                powers.astype(low), v_ref[:count, cut], preferred_element_type=full
            )
        return carry

    lax.fori_loop(0, heads, local_head, 0)
    pass_z(2, 1)
    pass_z(3, 0)
    pass_b(0, 1)
    pass_b(1, 0)

    @pl.when(y == 0)
    def _():
        ke_ref[...] = jnp.zeros_like(ke_ref)
        ve_ref[...] = jnp.zeros_like(ve_ref)

    @pl.when(y == 1)
    def _():
        for copy in earlier:
            copy.wait_recv()
        ke_ref[...] = earlier_k[...]
        ve_ref[...] = earlier_v[...]

        def remote_head(h, carry):
            cut = pl.ds(pl.multiple_of(h * HD, HD), HD)
            for qb in range(2):
                span = pl.ds(qb * half, half)
                scores = times_transpose(q_ref[span, cut], ke_ref[:, cut]) * score_scale
                before = pick(most, span, h)
                top = jnp.maximum(before, jnp.max(scores, axis=1, keepdims=True))
                powers = jnp.exp(scores - top)
                shrink = jnp.exp(before - top)
                put(most, span, h, top)
                put(
                    weight,
                    span,
                    h,
                    pick(weight, span, h) * shrink + jnp.sum(powers, axis=1, keepdims=True),
                )
                total[span, cut] = total[span, cut] * shrink + jnp.dot(
                    powers.astype(low), ve_ref[:, cut], preferred_element_type=full
                )
            return carry

        lax.fori_loop(0, heads, remote_head, 0)

    def finish_head(h, carry):
        cut = pl.ds(pl.multiple_of(h * HD, HD), HD)
        context_ref[:, cut] = (total[:, cut] / pick(weight, slice(None), h)).astype(low)
        return carry

    lax.fori_loop(0, heads, finish_head, 0)
    log_ref[...] = most[...] + jnp.log(weight[...])

    loads[4].wait()

    def out_part(at_quarter, target):
        cut = pl.ds(pl.multiple_of(at_quarter * cols, cols), cols)
        target[...] = jnp.dot(context_ref[...], wo[:, cut], preferred_element_type=full).astype(low)

    def part_to_sibling(i):
        return remote(tp_staged.at[i], tp_sib.at[i], tp_send.at[i], tp_recv.at[i], sibling)

    def part_of(i):
        x_at = 1 - x + (2 * x - 1) * i
        out_part(x_at * 2 + 1 - core, tp_staged.at[i])
        part_to_sibling(i).start()
        out_part(x_at * 2 + core, tp_mine.at[i])

    out_x = remote(tp_mine.at[0], tp_x, tp_send.at[2], tp_recv.at[2], across)
    part_of(0)
    part_to_sibling(0).wait_recv()
    add_blocks(tp_mine.at[0], [tp_sib.at[0]], rows)
    out_x.start()
    part_of(1)
    pass_z(3, 1)
    pass_b(1, 1)
    pass_b(2, 0)
    part_to_sibling(1).wait_recv()
    out_x.wait_recv()
    own_cut = pl.ds(pl.multiple_of(tp * cols, cols), cols)

    def sum_parts(span):
        value = tokens[span, own_cut].astype(full) + (
            tp_mine[1, span, :].astype(full)
            + tp_sib[1, span, :].astype(full)
            + tp_x[span, :].astype(full)
        )
        hidden_ref[span, :] = value
        lin[span, :] = value * value

    by_rows(64, sum_parts)

    row_mine[0] = row_of(lin[...])
    first = remote(row_mine.at[0], row_sib, row_send.at[0], row_recv.at[0], sibling)
    first.start()
    first.wait_recv()
    row_mine[1] = row_mine[0] + row_sib[...]
    second = remote(row_mine.at[1], row_x, row_send.at[1], row_recv.at[1], across)
    second.start()
    second.wait_recv()
    squares = (row_mine[1] + row_x[...]).T[:, :1]
    inv_two = lax.rsqrt(squares * (1.0 / model_dim) + norm_eps)
    inv_ref[...] = jnp.broadcast_to(inv_two, (rows, 128))

    def norm_two(span):
        unit = hidden_ref[span, :] * inv_ref[span, :1]
        unit_ref[span, :] = unit
        normed_ref[span, :] = (unit * second_ref[:1, :]).astype(low)

    by_rows(64, norm_two)

    pass_b(2, 1)
    pass_b(3, 0)
    pass_b(3, 1)

    def finish_sibling(i, carry):
        block = spot(0, 0, 0)
        copy = remote(block, block, s_sem.at[i], sib_sem.at[i], sibling)
        copy.wait_recv()
        copy.wait_send()
        return carry

    lax.fori_loop(0, 16, finish_sibling, 0)

    def finish_links(i, carry):
        for da in range(2):
            over_b(i, da, grad_hbm).wait_send()

            @pl.when((z < 3) & (i <= z))
            def _(da=da):
                up(i, da, grad_hbm).wait_send()

            @pl.when((z > 0) & (i >= z))
            def _(da=da):
                down(i, da, grad_hbm).wait_send()

        return carry

    lax.fori_loop(0, 4, finish_links, 0)
    over_a(grad_hbm).wait_send()
    own.wait()
    for copy in (t_x, t_s, t_f, out_x, part_to_sibling(0), part_to_sibling(1), first, second):
        copy.wait_send()

    @pl.when(y == 0)
    def _():
        for copy in earlier:
            copy.wait_send()


def attend(vmem_args, hbm_args, cid):
    rows, cols = hbm_args[0].shape
    model_dim = vmem_args[0].shape[1]
    low, full, dma = jnp.bfloat16, jnp.float32, pltpu.SemaphoreType.DMA
    vmem, hbm = pl.BlockSpec(memory_space=pltpu.VMEM), pl.BlockSpec(memory_space=pl.ANY)

    def buffers(*shape, dtype=low):
        return pltpu.VMEM(shape, dtype)

    def result(*shape, dtype=low):
        return jax.ShapeDtypeStruct(shape, dtype)

    return pl.pallas_call(
        attend_kernel,
        out_shape=[
            result(rows, cols, dtype=full),
            result(rows, cols, dtype=full),
            result(rows, 128, dtype=full),
            result(rows, cols),
            result(rows, model_dim),
            result(rows, 128, dtype=full),
        ]
        + [result(rows, cols)] * 6
        + [result(rows, 128, dtype=full), result(8 * rows, model_dim)],
        in_specs=[vmem] * len(vmem_args) + [hbm] * len(hbm_args),
        out_specs=[vmem] * 13 + [hbm],
        scratch_shapes=[buffers(*arg.shape) for arg in hbm_args[2:]]
        + [
            buffers(rows, model_dim),
            buffers(rows, cols, dtype=full),
            buffers(rows, cols, dtype=full),
            buffers(rows, 128, dtype=full),
            buffers(rows, 128, dtype=full),
            buffers(rows, cols),
            buffers(rows, cols),
            buffers(2, rows, cols),
            buffers(2, rows, cols),
            buffers(2, rows, cols),
            buffers(rows, cols),
            buffers(2, 8, rows, dtype=full),
            buffers(8, rows, dtype=full),
            buffers(8, rows, dtype=full),
        ]
        + [dma((6,)), dma((3,)), dma((3,)), dma((2,)), dma((2,)), dma((3,)), dma((3,))]
        + [dma((2,)), dma((2,))]
        + [dma((8,)), dma((8,)), dma, dma((8,)), dma((16,)), dma((16,)), dma((16,))],
        compiler_params=pltpu.CompilerParams(
            collective_id=cid, has_side_effects=True, vmem_limit_bytes=60 * 2**20
        ),
        name="attend",
    )(*vmem_args, *hbm_args)


def kept_choice(expert_ids, pair_order, expert_total, capacity):
    tok_count, top_count = expert_ids.shape
    pair_count = tok_count * top_count
    order = pair_order.reshape(-1)
    pairs = jnp.arange(pair_count, dtype=jnp.int32)
    turn = jnp.sum(jnp.where(order[None, :] == pairs[:, None], pairs[None, :], 0), axis=1)
    turn = turn.reshape(tok_count, top_count)
    picked = expert_ids[:, :, None] == jnp.arange(expert_total, dtype=jnp.int32)[None, None, :]
    experts_apart = jnp.arange(expert_total, dtype=jnp.int32)[:, None, None]
    picked = expert_ids.T[None] == experts_apart
    named = jnp.any(picked, axis=1)
    turn_of = jnp.sum(jnp.where(picked, turn.T[None], 0), axis=1)
    turn_of = jnp.where(named, turn_of, pair_count)
    slot = jnp.sum((turn_of[:, None, :] < turn_of[:, :, None]).astype(jnp.int32), axis=2)
    return (named & (slot < capacity)).astype(jnp.float32)


def dense_plan(
    tokens,
    out_grad,
    first_gain,
    query_weight,
    key_weight,
    value_weight,
    query_bias,
    key_bias,
    value_bias,
    output_weight,
    second_gain,
    router_weight,
    shared_gate_weight,
    shared_up_weight,
    shared_down_weight,
    switch_vector,
    expert_gate_weight,
    expert_up_weight,
    expert_down_weight,
    expert_ids,
    pair_order,
):
    ep, tp = lax.axis_index("ep"), lax.axis_index("tp")
    tok_count, col_width = tokens.shape
    model_dim = query_weight.shape[0]
    sources = lax.axis_size("ep")
    place_in_seq = ep % SPAN
    expert_total = router_weight.shape[1]
    capacity = 9 * tok_count * expert_ids.shape[1] // (8 * expert_total)
    head_count = query_weight.shape[1] // HD
    expert_width = expert_gate_weight.shape[2]
    shared_width = shared_gate_weight.shape[1] // sources
    width = expert_width + shared_width

    def own_cols(vector):
        return lax.dynamic_slice_in_dim(vector, tp * col_width, col_width, vector.ndim - 1)

    kept_own = kept_choice(expert_ids, pair_order, expert_total, capacity)

    cosine, sine_part = rope_tables(tok_count, HD, place_in_seq * tok_count)
    cos_wide = jnp.concatenate([cosine[:, 0], cosine[:, 0]], axis=1)
    sin_wide = jnp.concatenate([-sine_part[:, 0], sine_part[:, 0]], axis=1)
    second_cols = own_cols(second_gain)
    biases = jnp.stack([query_bias, key_bias, value_bias])
    (
        hidden_cols,
        unit_two,
        inv_two,
        normed_cols,
        normed_one,
        inv_one,
        queries,
        keys_rot,
        values_all,
        earlier_keys,
        earlier_values,
        context,
        log_rows,
        grads_all,
    ) = attend(
        [first_gain[None], biases, second_cols[None], cos_wide, sin_wide],
        [tokens, out_grad, query_weight, key_weight, value_weight, output_weight],
        2,
    )

    extra_rows = jnp.concatenate([router_weight.T, switch_vector[None, :]], axis=0)
    extra_rows = jnp.pad(extra_rows, ((0, 16 - extra_rows.shape[0]), (0, 0)))
    kept_rows = jnp.pad(kept_own, ((0, 16 - expert_total), (0, 0))).astype(jnp.bfloat16)
    reduced, layer_out, logit_tile, expert_grads, shared_parts, *_ = experts(
        normed_cols,
        grads_all,
        kept_rows,
        [
            expert_gate_weight[0].T,
            shared_gate_weight,
            extra_rows,
            expert_up_weight[0].T,
            shared_up_weight,
            expert_down_weight[0],
            shared_down_weight,
        ],
        hidden_cols,
        expert_total,
        4,
    )
    shared_parts = lax.all_to_all(shared_parts, "ep", split_axis=0, concat_axis=0, tiled=True)
    shared_parts = shared_parts.transpose(1, 0, 2, 3).reshape(3, sources * shared_width, -1)
    shared_parts = shared_parts.astype(jnp.float32)
    shared_gate_grad = shared_parts[1].T
    shared_up_grad = shared_parts[2].T
    shared_down_grad = shared_parts[0]

    normed_grad = reduced[:tok_count]
    probs_grad = (reduced[tok_count : tok_count + expert_total] * kept_own).T
    switch_grad = reduced[tok_count + expert_total]
    logit_at = width % 128
    probs_own = softmax_rows(logit_tile[:, logit_at : logit_at + expert_total])
    switch = jax.nn.sigmoid(logit_tile[:, logit_at + expert_total])
    logit_grad = (
        probs_own * (probs_grad - jnp.sum(probs_own * probs_grad, axis=-1, keepdims=True))
    ).astype(jnp.bfloat16)
    router_grad = inner_rows(normed_cols, logit_grad)
    switch_lin_grad = switch_grad * switch * (1.0 - switch)
    switch_vector_grad = jnp.dot(switch_lin_grad, normed_cols, preferred_element_type=jnp.float32)
    router_cols = lax.dynamic_slice_in_dim(router_weight, tp * col_width, col_width, 0)
    normed_grad = normed_grad + times_transpose(logit_grad, router_cols)
    normed_grad = (
        normed_grad
        + switch_lin_grad[:, None] * own_cols(switch_vector).astype(jnp.float32)[None, :]
    )
    second_gain_grad = jnp.sum(normed_grad * unit_two, axis=0)

    small = jnp.concatenate(
        [second_gain_grad[None], switch_vector_grad[None], router_grad.T], axis=0
    )
    small_rows = small.shape[0]
    small = jnp.pad(small, ((4, 12 - small_rows), (0, 0)))
    tokens_grad, weight_grads, sums = unwind(
        [
            normed_grad,
            unit_two,
            inv_two,
            second_cols[None],
            out_grad,
            tokens,
            inv_one,
            own_cols(first_gain)[None],
            small,
            queries,
            keys_rot,
            values_all,
            earlier_keys,
            earlier_values,
            context,
            log_rows,
            cos_wide,
            sin_wide,
        ],
        [normed_one, query_weight, key_weight, value_weight, output_weight],
        5,
    )
    share = model_dim // sources
    bias_width = HD // sources
    bias_sums = lax.dynamic_slice_in_dim(
        lax.dynamic_index_in_dim(sums, tp, 0, keepdims=False)[1:4].reshape(3, head_count, HD),
        ep * bias_width,
        bias_width,
        2,
    )
    per_quarter = col_width // share
    spread = lax.dynamic_index_in_dim(sums, ep // per_quarter, 0, keepdims=False)
    spread = lax.dynamic_slice_in_dim(spread, ep % per_quarter * share, share, 1)
    spread = jnp.concatenate([spread[:1], spread[4 : 4 + small_rows]], axis=0)
    return (
        layer_out,
        tokens_grad,
        spread[0],
        weight_grads[1],
        weight_grads[2],
        weight_grads[3],
        bias_sums[0],
        bias_sums[1],
        bias_sums[2],
        weight_grads[0].T,
        spread[1],
        spread[3:].T,
        shared_gate_grad,
        shared_up_grad,
        shared_down_grad,
        spread[2],
        expert_grads[1].T[None],
        expert_grads[2].T[None],
        expert_grads[0][None],
    )


def solution(mesh):
    plan = dense_plan if dict(mesh.shape) == {"ep": 8, "tp": 4} else slot_plan
    return jax.shard_map(
        plan,
        mesh=mesh,
        in_specs=(
            P("ep", "tp"),
            P("ep", "tp"),
            P(),
            P(None, "tp"),
            P(None, "tp"),
            P(None, "tp"),
            P("tp"),
            P("tp"),
            P("tp"),
            P("tp", None),
            P(),
            P(),
            P(None, "tp"),
            P(None, "tp"),
            P("tp", None),
            P(),
            P("ep", None, "tp"),
            P("ep", None, "tp"),
            P("ep", "tp", None),
            P("ep", None),
            P("ep", None),
        ),
        out_specs=(
            P("ep", "tp"),
            P("ep", "tp"),
            P("ep"),
            P("ep", "tp"),
            P("ep", "tp"),
            P("ep", "tp"),
            P("tp", "ep"),
            P("tp", "ep"),
            P("tp", "ep"),
            P("tp", "ep"),
            P("ep"),
            P("ep", None),
            P("ep", "tp"),
            P("ep", "tp"),
            P("tp", "ep"),
            P("ep"),
            P("ep", None, "tp"),
            P("ep", None, "tp"),
            P("ep", "tp", None),
        ),
        check_vma=False,
    )
```

```python
import functools
import math

import jax
import jax.numpy as jnp
from jax import lax
from jax.experimental import pallas as pl
from jax.experimental.pallas import tpu as pltpu
from jax.sharding import PartitionSpec as P

HD = 128
BLOCK = 256
SPAN = 2


rope_theta = 1000000.0
norm_eps = 1e-06
masked_score = -1e30


def passed_along(value, axis, steps):
    count = lax.axis_size(axis)
    leading, last = (max(0, -steps), min(count, count - steps))
    return lax.ppermute(value, axis, [(source, source + steps) for source in range(leading, last)])


def rope_tables(row_count, head_dim, first_position):
    positions = jnp.arange(row_count, dtype=jnp.float32) + first_position.astype(jnp.float32)
    frequency = jnp.exp(
        jnp.arange(head_dim // 2, dtype=jnp.float32) * (-2.0 * math.log(rope_theta) / head_dim)
    )
    angles = positions[:, None] * frequency[None, :]
    return (jnp.cos(angles)[:, None, :], jnp.sin(angles)[:, None, :])


def rotate(values, cosine, sine_part):
    half_dim = values.shape[-1] // 2
    first_half = values[..., :half_dim]
    second_half = values[..., half_dim:]
    return jnp.concatenate(
        [
            first_half * cosine - second_half * sine_part,
            second_half * cosine + first_half * sine_part,
        ],
        axis=-1,
    )


def inner_rows(left_side, right_side):
    return lax.dot_general(
        left_side, right_side, (((0,), (0,)), ((), ())), preferred_element_type=jnp.float32
    )


def times_transpose(left_side, right_side):
    return lax.dot_general(
        left_side, right_side, (((1,), (1,)), ((), ())), preferred_element_type=jnp.float32
    )


def row_stats(values):
    inv_rms = lax.rsqrt(jnp.mean(values * values, axis=-1, keepdims=True) + norm_eps)
    return (values * inv_rms, inv_rms)


def norm_back(grad_rows, unit_rows, inv_rms, gain_vec):
    scaled = grad_rows * gain_vec
    return inv_rms * (scaled - unit_rows * jnp.mean(scaled * unit_rows, axis=-1, keepdims=True))


def softmax_rows(scores):
    row_max = jnp.max(scores, axis=-1, keepdims=True)
    powers = jnp.exp(scores - row_max)
    return powers / jnp.sum(powers, axis=-1, keepdims=True)


def to_experts(block_rows, local_count):
    sources, span_rows, col_count = block_rows.shape
    slot_count = span_rows // local_count
    shaped = block_rows.reshape(sources, local_count, slot_count, col_count)
    return shaped.swapaxes(0, 1).reshape(local_count, sources * slot_count, col_count)


def to_sources(block_rows, sources):
    local_count, rows_all, col_count = block_rows.shape
    slot_count = rows_all // sources
    shaped = block_rows.reshape(local_count, sources, slot_count, col_count)
    return shaped.swapaxes(0, 1).reshape(sources, local_count * slot_count, col_count)


def deliver(block_rows):
    arrived = lax.all_to_all(block_rows, "ep", split_axis=0, concat_axis=0, tiled=True)
    return arrived


def collect(block_rows):
    return lax.all_to_all(block_rows, "ep", split_axis=0, concat_axis=0, tiled=True)


def slot_plan(
    tokens,
    out_grad,
    first_gain,
    query_weight,
    key_weight,
    value_weight,
    query_bias,
    key_bias,
    value_bias,
    output_weight,
    second_gain,
    router_weight,
    shared_gate_weight,
    shared_up_weight,
    shared_down_weight,
    switch_vector,
    expert_gate_weight,
    expert_up_weight,
    expert_down_weight,
    expert_ids,
    pair_order,
):
    whole_in, whole_grad = (
        lax.all_gather(tokens, "tp", axis=1, tiled=True),
        lax.all_gather(out_grad, "tp", axis=1, tiled=True),
    )
    tok_count = whole_in.shape[0]
    model_dim = whole_in.shape[1]
    col_width = tokens.shape[1]
    col_start = lax.axis_index("tp") * col_width
    sources = lax.axis_size("ep")
    place_in_seq = lax.axis_index("ep") % SPAN
    has_earlier = place_in_seq > 0
    local_experts = expert_gate_weight.shape[0]
    expert_total = router_weight.shape[1]
    top_count = expert_ids.shape[1]
    pair_count = tok_count * top_count
    capacity = 9 * pair_count // (8 * expert_total)
    head_count = query_weight.shape[1] // HD
    score_scale = HD ** (-0.5)
    inputs_full = whole_in.astype(jnp.float32)
    unit_one, inv_one = row_stats(inputs_full)
    normed_one = (unit_one * first_gain).astype(jnp.bfloat16)
    query_lin = jnp.dot(normed_one, query_weight, preferred_element_type=jnp.float32) + query_bias
    key_lin = jnp.dot(normed_one, key_weight, preferred_element_type=jnp.float32) + key_bias
    value_lin = jnp.dot(normed_one, value_weight, preferred_element_type=jnp.float32) + value_bias
    cosine, sine_part = rope_tables(tok_count, HD, place_in_seq * tok_count)
    queries = rotate(query_lin.reshape(tok_count, head_count, HD), cosine, sine_part).astype(
        jnp.bfloat16
    )
    keys_rot = rotate(key_lin.reshape(tok_count, head_count, HD), cosine, sine_part).astype(
        jnp.bfloat16
    )
    values_all = value_lin.reshape(tok_count, head_count, HD).astype(jnp.bfloat16)
    earlier_keys, earlier_values = passed_along((keys_rot, values_all), "ep", 1)
    keys_both = jnp.concatenate([earlier_keys, keys_rot], axis=0)
    values_both = jnp.concatenate([earlier_values, values_all], axis=0)
    blocks = jnp.arange(tok_count) // BLOCK
    local_allowed = blocks[None, :] <= blocks[:, None]
    remote_allowed = jnp.broadcast_to(has_earlier, (tok_count, tok_count))
    allowed = jnp.concatenate([remote_allowed, local_allowed], axis=1)[None]

    def attention_scores():
        scored = (
            jnp.einsum("qhd,khd->hqk", queries, keys_both, preferred_element_type=jnp.float32)
            * score_scale
        )
        return jnp.where(allowed, scored, masked_score)

    scores = attention_scores()
    row_max = jnp.max(scores, axis=-1, keepdims=True)
    powers = jnp.exp(scores - row_max)
    totals = jnp.sum(powers, axis=-1, keepdims=True)
    log_total = row_max + jnp.log(totals)
    probs_low = (powers / totals).astype(jnp.bfloat16)
    context = jnp.einsum("hqk,khd->qhd", probs_low, values_both, preferred_element_type=jnp.float32)
    context = context.reshape(tok_count, head_count * HD).astype(jnp.bfloat16)
    attn_part = jnp.dot(context, output_weight, preferred_element_type=jnp.float32)
    attended = lax.psum(attn_part, "tp")
    hidden_one = inputs_full + attended
    unit_two, inv_two = row_stats(hidden_one)
    normed_two = (unit_two * second_gain).astype(jnp.bfloat16)
    logits = jnp.dot(normed_two, router_weight, preferred_element_type=jnp.float32)
    router_probs = softmax_rows(logits)
    gate_values = jnp.take_along_axis(router_probs, expert_ids, axis=1)
    switch = jax.nn.sigmoid(jnp.dot(normed_two, switch_vector, preferred_element_type=jnp.float32))
    flat_ids = expert_ids.reshape(-1)
    turn_order = pair_order.reshape(-1)
    in_turn = flat_ids[turn_order]
    onehot = (in_turn[:, None] == jnp.arange(expert_total, dtype=jnp.int32)[None, :]).astype(
        jnp.int32
    )
    earlier = jnp.cumsum(onehot, axis=0) - onehot
    turn_slot = jnp.sum(earlier * onehot, axis=1)
    slot_index = jnp.zeros((pair_count,), jnp.int32).at[turn_order].set(turn_slot)
    kept_pair = slot_index < capacity
    slot_rows = expert_total * capacity
    target = jnp.where(kept_pair, flat_ids * capacity + slot_index, slot_rows)
    pair_token = jnp.arange(pair_count, dtype=jnp.int32) // top_count
    slot_token = (
        jnp.full((slot_rows + 1,), tok_count, jnp.int32).at[target].set(pair_token)[:slot_rows]
    )
    slot_gate = (
        jnp.zeros((slot_rows + 1,), jnp.float32).at[target].set(gate_values.reshape(-1))[:slot_rows]
    )
    padded_two = jnp.concatenate([normed_two, jnp.zeros((1, model_dim), jnp.bfloat16)], axis=0)
    send_rows = padded_two[slot_token].reshape(sources, local_experts * capacity, model_dim)
    expert_rows = to_experts(deliver(send_rows), local_experts)
    gate_lin = jnp.einsum(
        "erd,edf->erf", expert_rows, expert_gate_weight, preferred_element_type=jnp.float32
    )
    up_lin = jnp.einsum(
        "erd,edf->erf", expert_rows, expert_up_weight, preferred_element_type=jnp.float32
    )
    gate_sig = jax.nn.sigmoid(gate_lin)
    gate_act = gate_lin * gate_sig
    expert_hidden = (gate_act * up_lin).astype(jnp.bfloat16)
    expert_part = jnp.einsum(
        "erf,efd->erd", expert_hidden, expert_down_weight, preferred_element_type=jnp.float32
    )
    shared_gate_lin = jnp.dot(normed_two, shared_gate_weight, preferred_element_type=jnp.float32)
    shared_up_lin = jnp.dot(normed_two, shared_up_weight, preferred_element_type=jnp.float32)
    shared_sig = jax.nn.sigmoid(shared_gate_lin)
    shared_act = shared_gate_lin * shared_sig
    shared_hidden = (shared_act * shared_up_lin).astype(jnp.bfloat16)
    shared_part = jnp.dot(shared_hidden, shared_down_weight, preferred_element_type=jnp.float32)
    expert_cols, shared_cols = (
        lax.psum_scatter(expert_part.reshape(-1, model_dim), "tp", scatter_dimension=1, tiled=True),
        lax.psum_scatter(shared_part, "tp", scatter_dimension=1, tiled=True),
    )
    returned = collect(
        to_sources(expert_cols.astype(jnp.bfloat16).reshape(local_experts, -1, col_width), sources)
    )
    back_flat = jnp.concatenate(
        [returned.reshape(slot_rows, col_width), jnp.zeros((1, col_width), jnp.bfloat16)], axis=0
    )
    pair_out = back_flat[target].astype(jnp.float32).reshape(tok_count, top_count, col_width)
    routed = jnp.sum(gate_values[:, :, None] * pair_out, axis=1)
    hidden_cols = lax.dynamic_slice_in_dim(hidden_one, col_start, col_width, 1)
    layer_out = (hidden_cols + switch[:, None] * shared_cols + routed).astype(jnp.bfloat16)
    grad_full = whole_grad.astype(jnp.float32)
    grad_cols = out_grad.astype(jnp.float32)
    gate_part = jnp.sum(pair_out * grad_cols[:, None, :], axis=-1)
    switch_part = jnp.sum(grad_cols * shared_cols, axis=-1)
    gate_grad, switch_grad = lax.psum((gate_part, switch_part), "tp")
    padded_grad = jnp.concatenate([whole_grad, jnp.zeros((1, model_dim), jnp.bfloat16)], axis=0)
    send_grads = (slot_gate[:, None] * padded_grad[slot_token].astype(jnp.float32)).astype(
        jnp.bfloat16
    )
    expert_grads = to_experts(
        deliver(send_grads.reshape(sources, local_experts * capacity, model_dim)), local_experts
    )
    hidden_grad = jnp.einsum(
        "erd,efd->erf", expert_grads, expert_down_weight, preferred_element_type=jnp.float32
    )
    gate_lin_grad = (hidden_grad * up_lin * gate_sig * (1.0 + gate_lin * (1.0 - gate_sig))).astype(
        jnp.bfloat16
    )
    up_lin_grad = (hidden_grad * gate_act).astype(jnp.bfloat16)
    expert_down_grad = jnp.einsum(
        "erf,erd->efd", expert_hidden, expert_grads, preferred_element_type=jnp.float32
    )
    expert_gate_grad = jnp.einsum(
        "erd,erf->edf", expert_rows, gate_lin_grad, preferred_element_type=jnp.float32
    )
    expert_up_grad = jnp.einsum(
        "erd,erf->edf", expert_rows, up_lin_grad, preferred_element_type=jnp.float32
    )
    rows_grad = jnp.einsum(
        "erf,edf->erd", gate_lin_grad, expert_gate_weight, preferred_element_type=jnp.float32
    )
    rows_grad = rows_grad + jnp.einsum(
        "erf,edf->erd", up_lin_grad, expert_up_weight, preferred_element_type=jnp.float32
    )
    rows_grad_cols = lax.psum_scatter(
        rows_grad.reshape(-1, model_dim), "tp", scatter_dimension=1, tiled=True
    )
    returned_grad = collect(
        to_sources(
            rows_grad_cols.astype(jnp.bfloat16).reshape(local_experts, -1, col_width), sources
        )
    )
    back_grad = jnp.concatenate(
        [returned_grad.reshape(slot_rows, col_width), jnp.zeros((1, col_width), jnp.bfloat16)],
        axis=0,
    )
    routed_grad = jnp.sum(
        back_grad[target].astype(jnp.float32).reshape(tok_count, top_count, col_width), axis=1
    )
    shared_out_grad = (switch[:, None] * grad_full).astype(jnp.bfloat16)
    shared_hidden_grad = times_transpose(shared_out_grad, shared_down_weight)
    shared_gate_lin_grad = (
        shared_hidden_grad
        * shared_up_lin
        * shared_sig
        * (1.0 + shared_gate_lin * (1.0 - shared_sig))
    ).astype(jnp.bfloat16)
    shared_up_lin_grad = (shared_hidden_grad * shared_act).astype(jnp.bfloat16)
    shared_down_grad = inner_rows(shared_hidden, shared_out_grad)
    shared_gate_grad = inner_rows(normed_two, shared_gate_lin_grad)
    shared_up_grad = inner_rows(normed_two, shared_up_lin_grad)
    normed_grad = times_transpose(shared_gate_lin_grad, shared_gate_weight) + times_transpose(
        shared_up_lin_grad, shared_up_weight
    )
    normed_grad = normed_grad + lax.dynamic_update_slice_in_dim(
        jnp.zeros_like(normed_grad), routed_grad, col_start, 1
    )
    normed_grad = lax.psum(normed_grad, "tp")
    picked = (
        expert_ids[:, :, None] == jnp.arange(expert_total, dtype=jnp.int32)[None, None, :]
    ).astype(jnp.float32)
    probs_grad = jnp.sum(picked * gate_grad[:, :, None], axis=1)
    logit_grad = (
        router_probs * (probs_grad - jnp.sum(router_probs * probs_grad, axis=-1, keepdims=True))
    ).astype(jnp.bfloat16)
    router_grad = inner_rows(normed_two, logit_grad)
    switch_lin_grad = switch_grad * switch * (1.0 - switch)
    switch_vector_grad = jnp.dot(switch_lin_grad, normed_two, preferred_element_type=jnp.float32)
    normed_grad = normed_grad + times_transpose(logit_grad, router_weight)
    normed_grad = (
        normed_grad + switch_lin_grad[:, None] * switch_vector.astype(jnp.float32)[None, :]
    )
    second_gain_grad = jnp.sum(normed_grad * unit_two, axis=0)
    hidden_grad_one = grad_full + norm_back(normed_grad, unit_two, inv_two, second_gain)
    attended_grad = hidden_grad_one.astype(jnp.bfloat16)
    output_grad = inner_rows(context, attended_grad)
    context_grad = (
        times_transpose(attended_grad, output_weight)
        .astype(jnp.bfloat16)
        .reshape(tok_count, head_count, HD)
    )
    scores = attention_scores()
    attn_probs = jnp.exp(scores - log_total)
    probs_again = attn_probs.astype(jnp.bfloat16)
    probs_grad_att = jnp.einsum(
        "qhd,khd->hqk", context_grad, values_both, preferred_element_type=jnp.float32
    )
    values_both_grad = jnp.einsum(
        "hqk,qhd->khd", probs_again, context_grad, preferred_element_type=jnp.float32
    )
    scores_grad = (
        attn_probs * (probs_grad_att - jnp.sum(attn_probs * probs_grad_att, axis=-1, keepdims=True))
    ).astype(jnp.bfloat16)
    queries_grad = (
        jnp.einsum("hqk,khd->qhd", scores_grad, keys_both, preferred_element_type=jnp.float32)
        * score_scale
    )
    keys_both_grad = (
        jnp.einsum("hqk,qhd->khd", scores_grad, queries, preferred_element_type=jnp.float32)
        * score_scale
    )
    later_keys_grad, later_values_grad = passed_along(
        (keys_both_grad[:tok_count], values_both_grad[:tok_count]), "ep", -1
    )
    keep_later = jnp.where(has_earlier, 0.0, 1.0).astype(jnp.float32)
    keys_grad = keys_both_grad[tok_count:] + keep_later * later_keys_grad
    values_grad = values_both_grad[tok_count:] + keep_later * later_values_grad
    value_lin_grad = values_grad.reshape(tok_count, head_count * HD).astype(jnp.bfloat16)
    query_lin_grad = (
        rotate(queries_grad, cosine, -sine_part)
        .reshape(tok_count, head_count * HD)
        .astype(jnp.bfloat16)
    )
    key_lin_grad = (
        rotate(keys_grad, cosine, -sine_part)
        .reshape(tok_count, head_count * HD)
        .astype(jnp.bfloat16)
    )
    query_grad = inner_rows(normed_one, query_lin_grad)
    key_grad = inner_rows(normed_one, key_lin_grad)
    value_grad = inner_rows(normed_one, value_lin_grad)
    query_bias_grad = jnp.sum(query_lin_grad.astype(jnp.float32), axis=0).reshape(head_count, HD)
    key_bias_grad = jnp.sum(key_lin_grad.astype(jnp.float32), axis=0).reshape(head_count, HD)
    value_bias_grad = jnp.sum(value_lin_grad.astype(jnp.float32), axis=0).reshape(head_count, HD)
    normed_one_grad = times_transpose(query_lin_grad, query_weight) + times_transpose(
        key_lin_grad, key_weight
    )
    normed_one_grad = normed_one_grad + times_transpose(value_lin_grad, value_weight)
    normed_one_grad = lax.psum(normed_one_grad.astype(jnp.bfloat16), "tp").astype(jnp.float32)
    first_gain_grad = jnp.sum(normed_one_grad * unit_one, axis=0)
    input_grad = hidden_grad_one + norm_back(normed_one_grad, unit_one, inv_one, first_gain)
    tokens_grad = lax.dynamic_slice_in_dim(input_grad, col_start, col_width, 1).astype(jnp.bfloat16)
    reduced = (
        lax.psum_scatter(
            first_gain_grad.astype(jnp.bfloat16), "ep", scatter_dimension=0, tiled=True
        ).astype(jnp.float32),
        lax.psum_scatter(
            query_grad.astype(jnp.bfloat16), "ep", scatter_dimension=0, tiled=True
        ).astype(jnp.float32),
        lax.psum_scatter(
            key_grad.astype(jnp.bfloat16), "ep", scatter_dimension=0, tiled=True
        ).astype(jnp.float32),
        lax.psum_scatter(
            value_grad.astype(jnp.bfloat16), "ep", scatter_dimension=0, tiled=True
        ).astype(jnp.float32),
        lax.psum_scatter(
            query_bias_grad.astype(jnp.bfloat16), "ep", scatter_dimension=1, tiled=True
        ).astype(jnp.float32),
        lax.psum_scatter(
            key_bias_grad.astype(jnp.bfloat16), "ep", scatter_dimension=1, tiled=True
        ).astype(jnp.float32),
        lax.psum_scatter(
            value_bias_grad.astype(jnp.bfloat16), "ep", scatter_dimension=1, tiled=True
        ).astype(jnp.float32),
        lax.psum_scatter(
            output_grad.astype(jnp.bfloat16), "ep", scatter_dimension=1, tiled=True
        ).astype(jnp.float32),
        lax.psum_scatter(
            second_gain_grad.astype(jnp.bfloat16), "ep", scatter_dimension=0, tiled=True
        ).astype(jnp.float32),
        lax.psum_scatter(
            router_grad.astype(jnp.bfloat16), "ep", scatter_dimension=0, tiled=True
        ).astype(jnp.float32),
        lax.psum_scatter(
            shared_gate_grad.astype(jnp.bfloat16), "ep", scatter_dimension=0, tiled=True
        ).astype(jnp.float32),
        lax.psum_scatter(
            shared_up_grad.astype(jnp.bfloat16), "ep", scatter_dimension=0, tiled=True
        ).astype(jnp.float32),
        lax.psum_scatter(
            shared_down_grad.astype(jnp.bfloat16), "ep", scatter_dimension=1, tiled=True
        ).astype(jnp.float32),
        lax.psum_scatter(
            switch_vector_grad.astype(jnp.bfloat16), "ep", scatter_dimension=0, tiled=True
        ).astype(jnp.float32),
    )
    return (
        layer_out,
        tokens_grad,
        reduced[0],
        reduced[1],
        reduced[2],
        reduced[3],
        reduced[4],
        reduced[5],
        reduced[6],
        reduced[7],
        reduced[8],
        reduced[9],
        reduced[10],
        reduced[11],
        reduced[12],
        reduced[13],
        expert_gate_grad,
        expert_up_grad,
        expert_down_grad,
    )


MESH = pl.DeviceIdType.MESH


def place():
    ep, tp = lax.axis_index("ep"), lax.axis_index("tp")
    return ep, tp, ep // 2, lax.rem(ep, 2), tp // 2, lax.rem(tp, 2)


def greet(always, along_z=False):
    barrier = pltpu.get_barrier_semaphore()
    for device in always:
        pl.semaphore_signal(barrier, inc=1, device_id=device, device_id_type=MESH)
    count = len(always)
    if along_z:
        ep, tp, z, _, _, _ = place()

        @pl.when(z < 3)
        def _():
            pl.semaphore_signal(barrier, inc=1, device_id=(ep + 2, tp), device_id_type=MESH)

        @pl.when(z > 0)
        def _():
            pl.semaphore_signal(barrier, inc=1, device_id=(ep - 2, tp), device_id_type=MESH)

        count = count + lax.min(z, 1) + lax.min(3 - z, 1)
    pl.semaphore_wait(barrier, count)


def remote(source, target, send_sem, recv_sem, device):
    return pltpu.make_async_remote_copy(
        src_ref=source,
        dst_ref=target,
        send_sem=send_sem,
        recv_sem=recv_sem,
        device_id=device,
        device_id_type=MESH,
    )


def add_blocks(target, sources, rows):
    step = next(size for size in (80, 64, 48, 16) if rows % size == 0)

    def body(i, carry):
        span = pl.ds(pl.multiple_of(i * step, 16), step)
        total = target[span, :]
        for source in sources:
            total = total + source[span, :].astype(target.dtype)
        target[span, :] = total
        return carry

    lax.fori_loop(0, rows // step, body, 0)


def lane_peers():
    ep, tp, z, y, x, core = place()
    to_y, to_x = 1 - 2 * y, 1 - 2 * x
    peer_a = (ep + (1 - core) * to_y, tp + core * 2 * to_x)
    peer_b = (ep + core * to_y, tp + (1 - core) * 2 * to_x)
    sibling = (ep, tp + 1 - 2 * core)
    above, below = (ep + 2, tp), (ep - 2, tp)
    return peer_a, peer_b, sibling, above, below


def lane_spot(z_at, da, db, core_at):
    _, _, _, y, x, _ = place()
    y_at = y + (1 - 2 * y) * ((1 - core_at) * da + core_at * db)
    x_at = x + (1 - 2 * x) * (core_at * da + (1 - core_at) * db)
    return z_at * 2 + y_at, x_at * 2 + core_at


def experts_kernel(
    expert_width,
    shared_width,
    expert_total,
    x_ref,
    g_ref,
    kept_ref,
    expert_gate_ref,
    shared_gate_ref,
    extra_ref,
    expert_up_ref,
    shared_up_ref,
    expert_down_ref,
    shared_down_ref,
    residual_ref,
    grad_ref,
    mixed_ref,
    logit_ref,
    down_grad_ref,
    gate_grad_ref,
    up_grad_ref,
    shared_grads_ref,
    all_ref,
    from_sib,
    from_b,
    from_a,
    from_z,
    in_ref,
    down_ref,
    scalars,
    kept_held,
    x_held,
    g_held,
    lin,
    hidden_grad,
    hidden_all,
    both_all,
    kept_cols,
    staged,
    mine,
    landed,
    x_tile,
    g_tile,
    tile_out,
    shared_out,
    up_sem,
    down_sem,
    a_sem,
    b_sem,
    s_sem,
    recv_sem,
    sib_sem,
    own_sem,
    load_sem,
    fetch_sem,
    store_sem,
    weight_sem,
    kept_send,
    kept_recv,
    rs_send,
    rs_recv,
    rb_send,
    rb_recv,
    ra_send,
    ra_recv,
    rz_send,
    rz_recv,
):
    ep, tp, z, y, x, core = place()
    rows, cols = x_ref.shape
    width = down_ref.shape[0]
    filled = expert_width + shared_width
    tall = mine.shape[1]
    out_at = rows + 16
    cuts = ((0, out_at), (out_at, tall - out_at))
    peer_a, peer_b, sibling, above, below = lane_peers()
    sources = kept_held.shape[0]
    others = [(lax.rem(ep + i, sources), tp) for i in range(1, sources)]
    greet([(ep, tp + 2 - 4 * x), sibling] + others)

    def spot(z_at, da, db):
        group, quarter = lane_spot(z_at, da, db, core)
        return all_ref.at[
            pl.ds(pl.multiple_of(group * rows, rows), rows),
            pl.ds(pl.multiple_of(quarter * cols, cols), cols),
        ]

    def at(z_at, da, db):
        return z_at * 4 + da * 2 + db

    def choose(*values):
        return jnp.where(
            z == 0, values[0], jnp.where(z == 1, values[1], jnp.where(z == 2, values[2], values[3]))
        )

    coming = (z, choose(1, 2, 1, 2), choose(2, 0, 3, 1), choose(3, 3, 0, 0))
    turns = (z, choose(1, 2, 1, 2), choose(3, 3, 0, 0), choose(2, 0, 3, 1))

    def arrived(z_at, da, db):
        block, n = spot(z_at, da, db), at(z_at, da, db)
        remote(block, block, s_sem.at[n], recv_sem.at[n], sibling).wait_recv()
        return block

    def up(z_at, source):
        return remote(source, spot(z_at, 0, 0), up_sem.at[z_at], recv_sem.at[at(z_at, 0, 0)], above)

    def down(z_at, source):
        return remote(source, spot(z_at, 0, 0), down_sem.at[z_at], recv_sem.at[at(z_at, 0, 0)], below)

    def over_a(z_at, source):
        return remote(source, spot(z_at, 0, 0), a_sem.at[z_at], recv_sem.at[at(z_at, 1, 0)], peer_a)

    def over_b(z_at, da, source):
        return remote(
            source, spot(z_at, da, 0), b_sem.at[z_at * 2 + da], recv_sem.at[at(z_at, da, 1)], peer_b
        )

    def to_sibling(z_at, da, db, source):
        n = at(z_at, da, db)
        return remote(source, spot(z_at, da, db), s_sem.at[n], sib_sem.at[n], sibling)

    def pass_z(z_at):
        block = arrived(z_at, 0, 0)

        @pl.when((z_at > z) & (z > 0))
        def _():
            down(z_at, block).start()

        @pl.when((z_at < z) & (z < 3))
        def _():
            up(z_at, block).start()

        over_a(z_at, block).start()
        over_b(z_at, 0, block).start()
        to_sibling(z_at, 0, 0, block).start()

    def pass_a(z_at, onward=True):
        block = arrived(z_at, 1, 0)
        if onward:
            over_b(z_at, 1, block).start()
        to_sibling(z_at, 1, 0, block).start()

    def pass_b(z_at, da):
        block = arrived(z_at, da, 1)
        to_sibling(z_at, da, 1, block).start()

    def sibling_blocks(k, dy):
        for dx in range(2):
            da, db = core * dy + (1 - core) * dx, core * dx + (1 - core) * dy
            n = at(turns[k], da, db)
            block = spot(0, 0, 0)
            remote(block, block, s_sem.at[n], sib_sem.at[n], sibling).wait_recv()

    def group_rows(k, dy):
        group = turns[k] * 2 + y + (1 - 2 * y) * dy
        return group, pl.ds(pl.multiple_of(group * rows, rows), rows)

    def load_x(k, dy):
        _, span = group_rows(k, dy)
        return pltpu.make_async_copy(all_ref.at[span, :], x_held, load_sem.at[0])

    def load_g(k, dy):
        _, span = group_rows(k, dy)
        return pltpu.make_async_copy(g_ref.at[span, :], g_held, load_sem.at[1])

    def project():
        def body(i, carry):
            cut = pl.ds(pl.multiple_of(i * width, width), width)
            lin[:, cut] = times_transpose(x_held[...], in_ref[cut, :])
            return carry

        lax.fori_loop(0, 2, body, 0)

    def project_grad():
        hidden_grad[...] = times_transpose(g_held[...], down_ref[...])

    step = 64
    tile_start = width - 128
    logit_at = filled - tile_start

    def activate(k, dy):
        group, _ = group_rows(k, dy)
        lane = lax.broadcasted_iota(jnp.int32, (1, width), 1)
        near = lax.broadcasted_iota(jnp.int32, (1, 128), 1)
        is_logit = (near >= logit_at) & (near < logit_at + expert_total)
        kept_cols[:, :16] = kept_held[group].astype(jnp.float32).T

        def body(i, carry):
            span = pl.ds(pl.multiple_of(i * step, step), step)
            whole = pl.ds(pl.multiple_of(group * rows + i * step, step), step)
            gate_lin, up_lin = lin[span, :width], lin[span, width:]
            grad = hidden_grad[span, :]
            tail = lin[span, tile_start:width]
            if k == 0 and dy == 0:
                logit_ref[span, :] = tail
            most = jnp.max(jnp.where(is_logit, tail, -1e30), axis=1, keepdims=True)
            powers = jnp.where(is_logit, jnp.exp(jnp.minimum(tail - most, 0.0)), 0.0)
            kept = jnp.sum(jnp.where(near == ep, kept_cols[span, :], 0.0), axis=1, keepdims=True)
            gate = jnp.sum(jnp.where(near == logit_at + ep, powers, 0.0), axis=1, keepdims=True)
            gate = gate / jnp.sum(powers, axis=1, keepdims=True) * kept
            switch = jax.nn.sigmoid(
                jnp.sum(
                    jnp.where(near == logit_at + expert_total, tail, 0.0), axis=1, keepdims=True
                )
            )
            scale = jnp.where(lane < expert_width, gate, switch)
            sig = jax.nn.sigmoid(gate_lin)
            act = gate_lin * sig
            hidden = act * up_lin
            agreement = hidden * grad
            gate_part = jnp.sum(jnp.where(lane < expert_width, agreement, 0.0), axis=1, keepdims=True)
            switch_part = jnp.sum(
                jnp.where(lane < expert_width, 0.0, agreement), axis=1, keepdims=True
            )
            scaled = grad * scale
            hidden_all[whole, :] = (hidden * scale).astype(jnp.bfloat16)
            both_all[whole, :width] = (
                scaled * up_lin * sig * (1.0 + gate_lin * (1.0 - sig))
            ).astype(jnp.bfloat16)
            both_all[whole, width:] = (scaled * act).astype(jnp.bfloat16)
            scalars[span, :] = jnp.where(
                near == ep, gate_part, jnp.where(near == expert_total, switch_part, 0.0)
            )
            return carry

        lax.fori_loop(0, rows // step, body, 0)

    def hold(k, da, db):
        slot = 2 if k == 0 else k % 2
        return db * (7 + slot * 2 + da) + (1 - db) * (da * (4 + slot) + (1 - da) * k)

    def lane_offsets(dx, dy, core_at):
        return (1 - core_at) * dy + core_at * dx, (1 - core_at) * dx + core_at * dy

    def rs_sibling(k, dx, dy):
        n = at(turns[k], *lane_offsets(dx, dy, 1 - core))
        return remote(staged.at[dx], from_sib.at[n], rs_send.at[n], rs_recv.at[n], sibling)

    def block_rows(k, dy):
        sums = scalars[...].T[:16, :].astype(jnp.bfloat16)
        _, span = group_rows(k, dy)

        def fill(target, cut):
            target[:rows, :] = jnp.dot(
                both_all[span, :], in_ref[:, cut], preferred_element_type=jnp.float32
            ).astype(jnp.bfloat16)
            target[rows:out_at, :] = sums
            target[out_at:, :] = jnp.dot(
                hidden_all[span, :], down_ref[:, cut], preferred_element_type=jnp.float32
            ).astype(jnp.bfloat16)

        def body(dx, carry):
            x_at = x + (1 - 2 * x) * dx
            fill(staged.at[dx], pl.ds(pl.multiple_of((x_at * 2 + 1 - core) * cols, cols), cols))
            rs_sibling(k, dx, dy).start()
            fill(
                mine.at[hold(k, *lane_offsets(dx, dy, core))],
                pl.ds(pl.multiple_of((x_at * 2 + core) * cols, cols), cols),
            )
            return carry

        lax.fori_loop(0, 2, body, 0)

    def staged_free(k, dy):
        for dx in range(2):
            rs_sibling(k, dx, dy).wait_send()

    def rs_over_b(k, da, part):
        n, span = turns[k] * 2 + da, pl.ds(*cuts[part])
        return remote(
            mine.at[hold(k, da, 1), span],
            from_b.at[n, span],
            rb_send.at[n * 2 + part],
            rb_recv.at[n * 2 + part],
            peer_b,
        )

    def rs_over_a(k, part):
        z_at, span = turns[k], pl.ds(*cuts[part])
        return remote(
            mine.at[hold(k, 1, 0), span],
            from_a.at[z_at, span],
            ra_send.at[z_at * 2 + part],
            ra_recv.at[z_at * 2 + part],
            peer_a,
        )

    def rs_along_z(k, part):
        span = pl.ds(*cuts[part])
        return remote(
            mine.at[k, span],
            from_z.at[z, span],
            rz_send.at[k * 2 + part],
            rz_recv.at[z * 2 + part],
            (ep + 2 * (turns[k] - z), tp),
        )

    def fetch(source, i):
        return pltpu.make_async_copy(source, landed.at[i], fetch_sem.at[i])

    def fetch_part(source, half, i):
        span = pl.ds(*cuts[half])
        return pltpu.make_async_copy(source.at[span], landed.at[i, span], fetch_sem.at[i])

    def fetch_sibling(k, dy):
        for dx in range(2):
            n = at(turns[k], *lane_offsets(dx, dy, core))
            remote(staged.at[0], from_sib.at[n], rs_send.at[n], rs_recv.at[n], sibling).wait_recv()
            fetch(from_sib.at[n], dx).start()

    def reduce_sibling(k, dy):
        for dx in range(2):
            n = at(turns[k], *lane_offsets(dx, dy, core))
            fetch(from_sib.at[n], dx).wait()
            add_blocks(mine.at[hold(k, *lane_offsets(dx, dy, core))], [landed.at[dx]], tall)

        for part in range(2):

            @pl.when(core == 0)
            def _(part=part):
                rs_over_b(k, dy, part).start()

            if dy == 1:

                @pl.when(core == 1)
                def _(part=part):
                    rs_over_b(k, 0, part).start()
                    rs_over_b(k, 1, part).start()

    def add_part(target, part, copies):
        first, count = cuts[part]
        span = pl.ds(first, count)
        for copy in copies:
            copy.wait()
        add_blocks(
            mine.at[target, span], [landed.at[i, span] for i in range(len(copies))], count
        )

    def reduce_b(k, part):
        rs_over_b(k, 1, part).wait_recv()
        copy = fetch_part(from_b.at[turns[k] * 2 + 1], part, 0)
        copy.start()
        add_part(hold(k, 1, 0), part, [copy])
        rs_over_a(k, part).start()

    def reduce_a(k, part):
        z_at = turns[k]
        rs_over_b(k, 0, part).wait_recv()
        rs_over_a(k, part).wait_recv()
        copies = [
            fetch_part(from_b.at[z_at * 2], part, 0),
            fetch_part(from_a.at[z_at], part, 1),
        ]
        for copy in copies:
            copy.start()
        add_part(k, part, copies)
        if k > 0:
            rs_along_z(k, part).start()

    def reduce_z(i, part):
        source = (choose(3, 0, 3, 0), choose(2, 2, 1, 1), choose(1, 3, 0, 2))[i]
        span = pl.ds(*cuts[part])
        remote(
            mine.at[0, span],
            from_z.at[source, span],
            rz_send.at[0],
            rz_recv.at[source * 2 + part],
            sibling,
        ).wait_recv()
        copy = fetch_part(from_z.at[source], part, 0)
        copy.start()
        add_part(0, part, [copy])

    tile = x_tile.shape[1]

    def load_tile(source, target, t, sem):
        cut = pl.ds(pl.multiple_of(t * tile, tile), tile)
        return pltpu.make_async_copy(source.at[:, cut], target, load_sem.at[sem])

    def tile_stores(t, kind):
        cut = pl.ds(pl.multiple_of(t * tile, tile), tile)
        return (
            pltpu.make_async_copy(
                tile_out.at[kind, pl.ds(0, expert_width)],
                (down_grad_ref, gate_grad_ref, up_grad_ref)[kind].at[:, cut],
                store_sem.at[kind],
            ),
            pltpu.make_async_copy(
                shared_out.at[kind], shared_grads_ref.at[t, kind], store_sem.at[3 + kind]
            ),
        )

    def weight_tile(t, kind):
        @pl.when(t > 0)
        def _():
            for copy in tile_stores(t - 1, kind):
                copy.wait()

        if kind == 0:
            left, right = hidden_all[:, :filled], g_tile[...]
        else:
            left, right = both_all[:, (kind - 1) * width : (kind - 1) * width + filled], x_tile[...]
        result = inner_rows(left, right)
        tile_out[kind] = result
        shared_out[kind] = result[expert_width:, :].astype(jnp.bfloat16)
        for copy in tile_stores(t, kind):
            copy.start()

    own = pltpu.make_async_copy(x_ref, spot(z, 0, 0), own_sem)
    over_b(z, 0, x_ref).start()
    over_a(z, x_ref).start()

    @pl.when(z < 3)
    def _():
        up(z, x_ref).start()

    @pl.when(z > 0)
    def _():
        down(z, x_ref).start()

    to_sibling(z, 0, 0, x_ref).start()
    own.start()
    load_g(0, 0).start()

    def kept_to(i):
        return remote(
            kept_ref, kept_held.at[ep], kept_send.at[i - 1], kept_recv.at[i - 1], others[i - 1]
        )

    for i in range(1, sources):
        kept_to(i).start()
    own_kept = pltpu.make_async_copy(kept_ref, kept_held.at[ep], weight_sem.at[7])
    own_kept.start()
    pieces = [
        (expert_down_ref, down_ref, 0),
        (
            shared_down_ref.at[pl.ds(pl.multiple_of(ep * shared_width, 16), shared_width), :],
            down_ref,
            expert_width,
        ),
        (expert_gate_ref, in_ref, 0),
        (extra_ref, in_ref, filled),
        (expert_up_ref, in_ref, width),
    ]
    weight_copies = [
        pltpu.make_async_copy(piece, target.at[pl.ds(at_row, piece.shape[0]), :], weight_sem.at[i])
        for i, (piece, target, at_row) in enumerate(pieces)
    ]
    model_dim = in_ref.shape[1]
    window = (shared_width // 128 + 2) * 128
    first_tile = lax.min(ep * shared_width // 128, (shared_gate_ref.shape[1] - window) // 128)
    offset = ep * shared_width - first_tile * 128
    for i, source in enumerate((shared_gate_ref, shared_up_ref)):
        weight_copies.append(
            pltpu.make_async_copy(
                source.at[:, pl.ds(pl.multiple_of(first_tile * 128, 128), window)],
                both_all.at[pl.ds(i * model_dim, model_dim), pl.ds(0, window)],
                weight_sem.at[5 + i],
            )
        )
    for copy in weight_copies:
        copy.start()
    for target, first, last_row in (
        (in_ref, filled + 16, width),
        (in_ref, width + filled, 2 * width),
        (down_ref, filled, width),
    ):
        target[first:last_row, :] = jnp.zeros((last_row - first, target.shape[1]), target.dtype)
    for copy in weight_copies:
        copy.wait()
    picked = (
        lax.broadcasted_iota(jnp.int32, (shared_width, window), 1)
        == lax.broadcasted_iota(jnp.int32, (shared_width, window), 0) + offset
    ).astype(jnp.bfloat16)

    def pick_rows(i, carry):
        cut = pl.ds(pl.multiple_of(i * 512, 512), 512)
        for j in range(2):
            held = pl.ds(pl.multiple_of(j * model_dim + i * 512, 512), 512)
            at_row = j * width + expert_width
            in_ref[at_row : at_row + shared_width, cut] = times_transpose(
                picked, both_all[held, :window]
            ).astype(jnp.bfloat16)
        return carry

    lax.fori_loop(0, model_dim // 512, pick_rows, 0)
    load_g(0, 0).wait()
    project_grad()
    own_kept.wait()
    for i in range(1, sources):
        kept_to(i).wait_recv()
    own.wait()

    def ready(k, dy):
        if k > 0:
            pass_b(turns[k], dy)
        sibling_blocks(k, dy)
        load_x(k, dy).start()

    order = [(0, 0)] + [(k, dy) for k in range(1, 4) for dy in range(2)] + [(0, 1)]
    edge = (z == 0) | (z == 3)
    pass_z(coming[1])
    pass_a(z, False)
    pass_b(z, 0)

    @pl.when(jnp.logical_not(edge))
    def _():
        pass_z(coming[2])

    ready(0, 0)
    for s, (k, dy) in enumerate(order):
        following = order[s + 1] if s < 7 else None
        load_x(k, dy).wait()
        if s >= 1:
            fetch_sibling(*order[s - 1])
        project()
        if s >= 1:
            load_g(k, dy).wait()
            project_grad()
        if following is not None:
            load_g(*following).start()
        if s >= 1:
            reduce_sibling(*order[s - 1])
        if s == 1:
            pass_z(coming[3])
            over_b(z, 1, spot(z, 1, 0)).start()
        if s in (4, 6):
            reduce_b(s // 2 - 1, 0)
        activate(k, dy)
        if s == 0:

            @pl.when(edge)
            def _():
                pass_z(coming[2])

            pass_a(coming[1])
        if s == 1:
            pass_a(coming[2])
        if s == 2:
            pass_a(coming[3])
        if s == 4:
            pass_b(z, 1)
        if following is not None:
            ready(*following)
        if s in (4, 6):
            reduce_b(s // 2 - 1, 1)
        if s in (5, 7):
            reduce_a((s - 3) // 2, 0)
        if s >= 1:
            staged_free(*order[s - 1])
        if s == 5:
            for part in range(2):
                for da in range(2):
                    rs_over_b(1, da, part).wait_send()
                rs_over_a(1, part).wait_send()
        block_rows(k, dy)
        if s in (5, 7):
            reduce_a((s - 3) // 2, 1)

    load_tile(g_ref, g_tile, 0, 2).start()
    load_tile(all_ref, x_tile, 0, 3).start()
    tiles = shared_grads_ref.shape[0]
    services = {
        (0, 0): (fetch_sibling, 0, 1),
        (0, 1): (reduce_sibling, 0, 1),
        (1, 0): (reduce_b, 3, 0),
        (0, 2): (reduce_z, 0, 0),
        (1, 1): (reduce_z, 0, 1),
        (2, 0): (reduce_z, 1, 0),
        (3, 0): (reduce_z, 1, 1),
        (4, 0): (reduce_b, 3, 1),
        (4, 2): (reduce_a, 3, 0),
        (5, 1): (reduce_b, 0, 0),
        (6, 2): (reduce_a, 3, 1),
        (7, 0): (reduce_b, 0, 1),
    }

    def tile_step(t, carry):
        for kind in range(3):
            if kind == 0:
                load_tile(g_ref, g_tile, t, 2).wait()
            if kind == 1:
                load_tile(all_ref, x_tile, t, 3).wait()
            weight_tile(t, kind)

            @pl.when(t + 1 < tiles)
            def _(kind=kind):
                if kind == 0:
                    load_tile(g_ref, g_tile, t + 1, 2).start()
                if kind == 2:
                    load_tile(all_ref, x_tile, t + 1, 3).start()

            for (at_tile, at_kind), (service, *which) in services.items():
                if at_kind == kind:
                    pl.when(t == at_tile)(functools.partial(service, *which))
        return carry

    lax.fori_loop(0, tiles, tile_step, 0)
    for kind in range(3):
        for copy in tile_stores(tiles - 1, kind):
            copy.wait()

    for part in range(2):
        reduce_a(0, part)
        reduce_z(2, part)

    def total(i, carry):
        span = pl.ds(pl.multiple_of(i * 64, 64), 64)
        out_span = pl.ds(pl.multiple_of(out_at + i * 64, 16), 64)
        grad_ref[span, :] = mine[0, span, :].astype(jnp.float32)
        mixed_ref[span, :] = (
            residual_ref[span, :] + mine[0, out_span, :].astype(jnp.float32)
        ).astype(jnp.bfloat16)
        return carry

    lax.fori_loop(0, rows // 64, total, 0)
    grad_ref[rows:, :] = mine[0, rows:out_at, :].astype(jnp.float32)

    for i in range(1, sources):
        kept_to(i).wait_send()
    staged_free(0, 1)
    for k in range(1, 4):
        for part in range(2):
            rs_along_z(k, part).wait_send()
    for k in (0, 2, 3):
        for part in range(2):
            rs_over_a(k, part).wait_send()
            for da in range(2):
                rs_over_b(k, da, part).wait_send()

    def finish(i, carry):
        over_a(i, x_ref).wait_send()
        over_b(i, 0, x_ref).wait_send()
        over_b(i, 1, x_ref).wait_send()
        for n in range(4):
            block = spot(0, 0, 0)
            remote(block, block, s_sem.at[i * 4 + n], sib_sem.at[i * 4 + n], sibling).wait_send()

        @pl.when((z < 3) & (i <= z))
        def _():
            up(i, x_ref).wait_send()

        @pl.when((z > 0) & (i >= z))
        def _():
            down(i, x_ref).wait_send()

        return carry

    lax.fori_loop(0, 4, finish, 0)


def experts(x_cols, grads_all, kept_rows, weights, residual, expert_total, cid):
    rows, cols = x_cols.shape
    total, model_dim = grads_all.shape
    sources = total // rows
    expert_width, shared_width = weights[0].shape[0], weights[1].shape[1] // sources
    filled = expert_width + shared_width
    width = -(-(filled + expert_total + 1) // 128) * 128
    tall = 2 * rows + 16
    tile = model_dim // sources
    low, dma = jnp.bfloat16, pltpu.SemaphoreType.DMA
    vmem, hbm = pl.BlockSpec(memory_space=pltpu.VMEM), pl.BlockSpec(memory_space=pl.ANY)

    def landing(count):
        return jax.ShapeDtypeStruct((count, tall, cols), low)

    return pl.pallas_call(
        functools.partial(experts_kernel, expert_width, shared_width, expert_total),
        out_shape=[
            jax.ShapeDtypeStruct((rows + 16, cols), jnp.float32),
            jax.ShapeDtypeStruct((rows, cols), low),
            jax.ShapeDtypeStruct((rows, 128), jnp.float32),
            jax.ShapeDtypeStruct((expert_width, model_dim), jnp.float32),
            jax.ShapeDtypeStruct((expert_width, model_dim), jnp.float32),
            jax.ShapeDtypeStruct((expert_width, model_dim), jnp.float32),
            jax.ShapeDtypeStruct((sources, 3, shared_width, tile), low),
            jax.ShapeDtypeStruct((total, model_dim), low),
            landing(16),
            landing(8),
            landing(4),
            landing(4),
        ],
        in_specs=[hbm] * 10 + [vmem],
        out_specs=[vmem, vmem, vmem] + [hbm] * 9,
        scratch_shapes=[
            pltpu.VMEM((2 * width, model_dim), low),
            pltpu.VMEM((width, model_dim), low),
            pltpu.VMEM((rows, 128), jnp.float32),
            pltpu.VMEM((sources, 16, rows), low),
            pltpu.VMEM((rows, model_dim), low),
            pltpu.VMEM((rows, model_dim), low),
            pltpu.VMEM((rows, 2 * width), jnp.float32),
            pltpu.VMEM((rows, width), jnp.float32),
            pltpu.VMEM((total, width), low),
            pltpu.VMEM((total, 2 * width), low),
            pltpu.VMEM((rows, 128), jnp.float32),
            pltpu.VMEM((2, tall, cols), low),
            pltpu.VMEM((13, tall, cols), low),
            pltpu.VMEM((2, tall, cols), low),
            pltpu.VMEM((total, tile), low),
            pltpu.VMEM((total, tile), low),
            pltpu.VMEM((3, filled, tile), jnp.float32),
            pltpu.VMEM((3, shared_width, tile), low),
        ]
        + [dma((4,)), dma((4,)), dma((4,)), dma((8,)), dma((16,)), dma((16,)), dma((16,)), dma]
        + [dma((4,)), dma((2,)), dma((6,)), dma((8,)), dma((7,)), dma((7,))]
        + [dma((16,))] * 4
        + [dma((8,))] * 4,
        compiler_params=pltpu.CompilerParams(
            collective_id=cid, has_side_effects=True, vmem_limit_bytes=63 * 2**20
        ),
        name="experts",
    )(x_cols, grads_all, kept_rows, *weights, residual)


def row_of(columns):
    part = columns[:, :128]
    for i in range(1, columns.shape[1] // 128):
        part = part + columns[:, i * 128 : (i + 1) * 128]
    total = jnp.sum(part.T, axis=0, keepdims=True)
    return jnp.broadcast_to(total, (8, total.shape[1]))


def unwind_kernel(
    dn2_ref,
    unit_ref,
    inv_ref,
    second_ref,
    grad_ref,
    tokens_ref,
    inv_one_ref,
    first_ref,
    small_ref,
    q_ref,
    k_ref,
    v_ref,
    ke_ref,
    ve_ref,
    context_ref,
    log_ref,
    cos_ref,
    sin_ref,
    n1_hbm,
    wq_hbm,
    wk_hbm,
    wv_hbm,
    wo_hbm,
    tokens_grad_ref,
    weight_grads_ref,
    sums_ref,
    n1,
    wq,
    wk,
    wv,
    wo,
    grad_all,
    grad_own,
    hidden_grad,
    dc,
    dq,
    dk,
    dv,
    lin_grads,
    dke,
    dve,
    later_k,
    later_v,
    staged,
    mine,
    from_y,
    from_below,
    from_above,
    from_below_2,
    from_above_2,
    tp_staged,
    tp_mine,
    tp_sib,
    tp_x,
    dn1,
    row_mine,
    row_sib,
    row_x,
    smalls,
    quarters,
    load_sem,
    g_send,
    g_recv,
    row_send,
    row_recv,
    kv_send,
    kv_recv,
    y_send,
    y_recv,
    up_send,
    up_recv,
    down_send,
    down_recv,
    tp_send,
    tp_recv,
    small_send,
    small_recv,
    s_send,
    s_recv,
    up2_send,
    up2_recv,
    down2_send,
    down2_recv,
):
    ep, tp, z, y, x, core = place()
    rows, cols = unit_ref.shape
    model_dim = n1.shape[1]
    heads = cols // HD
    block = mine.shape[1]
    low, full = jnp.bfloat16, jnp.float32
    score_scale = HD ** (-0.5)
    sibling, across = (ep, tp + 1 - 2 * core), (ep, tp + 2 - 4 * x)
    beside = (ep + 1 - 2 * y, tp)
    above, below = (ep + 2, tp), (ep - 2, tp)
    sources = smalls.shape[0]
    others = [(lax.rem(ep + i, sources), tp) for i in range(1, sources)]
    loads = [
        pltpu.make_async_copy(source, target, load_sem.at[i])
        for i, (source, target) in enumerate(
            ((wo_hbm, wo), (n1_hbm, n1), (wq_hbm, wq), (wk_hbm, wk), (wv_hbm, wv))
        )
    ]
    for copy in loads:
        copy.start()
    greet([across, sibling] + others)

    step = 64

    def by_rows(body):
        def one(i, carry):
            body(pl.ds(pl.multiple_of(i * step, step), step))
            return carry

        lax.fori_loop(0, rows // step, one, 0)

    def row_exchange(i, values):
        row_mine[2 * i] = values
        first = remote(
            row_mine.at[2 * i], row_sib.at[i], row_send.at[2 * i], row_recv.at[2 * i], sibling
        )
        first.start()
        first.wait_recv()
        row_mine[2 * i + 1] = row_mine[2 * i] + row_sib[i]
        second = remote(
            row_mine.at[2 * i + 1],
            row_x.at[i],
            row_send.at[2 * i + 1],
            row_recv.at[2 * i + 1],
            across,
        )
        second.start()
        second.wait_recv()
        first.wait_send()
        second.wait_send()
        return (row_mine[2 * i + 1] + row_x[i]).T[:, :1]

    dn1[...] = dn2_ref[...] * second_ref[:1, :] * unit_ref[...]
    mean = row_exchange(0, row_of(dn1[...])) * (1.0 / model_dim)
    dn1[:, :128] = jnp.broadcast_to(mean, (rows, 128))

    def norm_two(span):
        scaled = dn2_ref[span, :] * second_ref[:1, :]
        value = grad_ref[span, :].astype(full) + inv_ref[span, :1] * (
            scaled - unit_ref[span, :] * dn1[span, :1]
        )
        hidden_grad[span, :] = value
        grad_own[span, :] = value.astype(low)

    by_rows(norm_two)

    def quarter(at):
        return grad_all.at[:, pl.ds(pl.multiple_of(at * cols, cols), cols)]

    g_x = remote(grad_own, quarter(tp), g_send.at[0], g_recv.at[0], across)
    g_s = remote(grad_own, quarter(tp), g_send.at[1], g_recv.at[1], sibling)
    g_x.start()
    g_s.start()
    own_cut = pl.ds(pl.multiple_of(tp * cols, cols), cols)
    grad_all[:, own_cut] = grad_own[...]
    g_x.wait_recv()
    theirs = quarter(tp + 2 - 4 * x)
    g_f = remote(theirs, theirs, g_send.at[2], g_recv.at[2], sibling)
    g_f.start()
    g_s.wait_recv()
    g_f.wait_recv()
    loads[0].wait()
    dc[...] = times_transpose(grad_all[...], wo[...]).astype(low)

    def over_y(kind, z_at):
        n = kind * 4 + z_at
        return remote(staged.at[n], from_y.at[n], y_send.at[n], y_recv.at[n], beside)

    def weight_blocks(kind, left, right):
        def other(i, carry):
            z_at = lax.rem(i * 3, 4)
            cut = pl.ds(pl.multiple_of((z_at * 2 + 1 - y) * block, block), block)
            staged[kind * 4 + z_at] = inner_rows(left[:, cut], right[...]).astype(low)
            over_y(kind, z_at).start()
            return carry

        def ours(i, carry):
            z_at = lax.rem(i * 3, 4)
            cut = pl.ds(pl.multiple_of((z_at * 2 + y) * block, block), block)
            mine[kind * 4 + z_at] = inner_rows(left[:, cut], right[...]).astype(low)
            return carry

        lax.fori_loop(0, 4, other, 0)
        lax.fori_loop(0, 4, ours, 0)

    def blocks_along_z(left, right):
        def one(i, carry):
            z_at = lax.rem(i * 3, 4)
            cut = pl.ds(pl.multiple_of((z_at * 2 + 1 - y) * block, block), block)
            staged[4 + z_at] = inner_rows(left[:, cut], right[...]).astype(low)
            cut = pl.ds(pl.multiple_of((z_at * 2 + y) * block, block), block)
            mine[4 + z_at] = inner_rows(left[:, cut], right[...]).astype(low)

            @pl.when((z == 0) & (z_at > 0))
            def _():
                up_2(z_at).start()
                up(1, z_at).start()

            @pl.when((z == 3) & (z_at < 3))
            def _():
                down_2(z_at).start()
                down(1, z_at).start()

            return carry

        lax.fori_loop(0, 4, one, 0)

    def up_2(z_at):
        return remote(
            staged.at[4 + z_at], from_below_2.at[z_at], up2_send.at[z_at], up2_recv.at[z_at], above
        )

    def down_2(z_at):
        return remote(
            staged.at[4 + z_at],
            from_above_2.at[z_at],
            down2_send.at[z_at],
            down2_recv.at[z_at],
            below,
        )

    def chain_2():
        def rise(z_at):
            up_2(z_at).wait_recv()
            add_blocks(staged.at[4 + z_at], [from_below_2.at[z_at]], block)
            up_2(z_at).start()

        def fall(z_at):
            down_2(z_at).wait_recv()
            add_blocks(staged.at[4 + z_at], [from_above_2.at[z_at]], block)
            down_2(z_at).start()

        @pl.when(z == 1)
        def _():
            rise(3)
            rise(2)
            fall(0)

        @pl.when(z == 2)
        def _():
            fall(0)
            fall(1)
            rise(3)

    def other_y_along_z():
        @pl.when(z > 0)
        def _():
            up_2(z).wait_recv()
            add_blocks(staged.at[4 + z], [from_below_2.at[z]], block)

        @pl.when(z < 3)
        def _():
            down_2(z).wait_recv()
            add_blocks(staged.at[4 + z], [from_above_2.at[z]], block)

        over_y(1, z).start()

    def own_first_along_z():
        over_y(1, z).wait_recv()
        add_blocks(mine.at[4 + z], [from_y.at[4 + z]], block)

    def up(kind, z_at):
        n = kind * 4 + z_at
        return remote(mine.at[n], from_below.at[n], up_send.at[n], up_recv.at[n], above)

    def down(kind, z_at):
        n = kind * 4 + z_at
        return remote(mine.at[n], from_above.at[n], down_send.at[n], down_recv.at[n], below)

    def y_stage(kind):
        def one(i, carry):
            z_at = lax.rem(i * 3, 4)
            n = kind * 4 + z_at
            over_y(kind, z_at).wait_recv()
            add_blocks(mine.at[n], [from_y.at[n]], block)

            @pl.when((z == 0) & (z_at > 0))
            def _():
                up(kind, z_at).start()

            @pl.when((z == 3) & (z_at < 3))
            def _():
                down(kind, z_at).start()

            return carry

        lax.fori_loop(0, 4, one, 0)

    def chain(kind):
        def rise(z_at):
            n = kind * 4 + z_at
            up(kind, z_at).wait_recv()
            add_blocks(mine.at[n], [from_below.at[n]], block)
            up(kind, z_at).start()

        def fall(z_at):
            n = kind * 4 + z_at
            down(kind, z_at).wait_recv()
            add_blocks(mine.at[n], [from_above.at[n]], block)
            down(kind, z_at).start()

        @pl.when(z == 1)
        def _():
            rise(3)
            rise(2)
            fall(0)

        @pl.when(z == 2)
        def _():
            fall(0)
            fall(1)
            rise(3)

    def final(kind):
        n = kind * 4 + z

        @pl.when(z > 0)
        def _():
            up(kind, z).wait_recv()

        @pl.when(z < 3)
        def _():
            down(kind, z).wait_recv()

        def one(i, carry):
            span = pl.ds(pl.multiple_of(i * 32, 32), 32)
            value = mine[n, span, :].astype(full)
            low_part = from_below[n, span, :].astype(full)
            high_part = from_above[n, span, :].astype(full)
            value = value + jnp.where(z > 0, low_part, 0.0) + jnp.where(z < 3, high_part, 0.0)
            weight_grads_ref[kind, span, :] = value
            return carry

        lax.fori_loop(0, block // 32, one, 0)

    weight_blocks(0, grad_all, context_ref)

    half = rows // 2

    def terms(h, qb, key_count, keys, values):
        cut = pl.ds(pl.multiple_of(h * HD, HD), HD)
        span = pl.ds(qb * half, half)
        lane = lax.broadcasted_iota(jnp.int32, (1, 128), 1)
        log_total = jnp.sum(jnp.where(lane == h, log_ref[span, :], 0.0), axis=1, keepdims=True)
        queries, grads = q_ref[span, cut], dc[span, cut]
        delta = jnp.sum(
            grads.astype(full) * context_ref[span, cut].astype(full), axis=1, keepdims=True
        )
        key_part, value_part = keys[:key_count, cut], values[:key_count, cut]
        probs = jnp.exp(times_transpose(queries, key_part) * score_scale - log_total)
        scores_grad = (probs * (times_transpose(grads, value_part) - delta)).astype(low)
        return (
            jnp.dot(scores_grad, key_part, preferred_element_type=full),
            inner_rows(scores_grad, queries),
            inner_rows(probs.astype(low), grads),
        )

    def spans(h, qb):
        return pl.ds(qb * half, half), pl.ds(pl.multiple_of(h * HD, HD), HD)

    later = (
        remote(dke, later_k, kv_send.at[0], kv_recv.at[0], beside),
        remote(dve, later_v, kv_send.at[1], kv_recv.at[1], beside),
    )

    @pl.when(y == 1)
    def _():
        def head(h, carry):
            cut = pl.ds(pl.multiple_of(h * HD, HD), HD)
            first = terms(h, 0, rows, ke_ref, ve_ref)
            dq[spans(h, 0)[0], cut] = first[0]
            dk[:, cut] = first[1]
            dv[:, cut] = first[2]
            second = terms(h, 1, rows, ke_ref, ve_ref)
            dq[spans(h, 1)[0], cut] = second[0]
            dke[:, cut] = ((dk[:, cut] + second[1]) * score_scale).astype(low)
            dve[:, cut] = (dv[:, cut] + second[2]).astype(low)
            return carry

        lax.fori_loop(0, heads, head, 0)
        for copy in later:
            copy.start()

    @pl.when(y == 0)
    def _():
        dq[...] = jnp.zeros_like(dq)

    y_stage(0)

    def head(h, carry):
        cut = pl.ds(pl.multiple_of(h * HD, HD), HD)
        second = terms(h, 1, rows, k_ref, v_ref)
        dq[half:, cut] = dq[half:, cut] + second[0]
        dk[:, cut] = second[1] * score_scale
        dv[:, cut] = second[2]
        first = terms(h, 0, half, k_ref, v_ref)
        dq[:half, cut] = dq[:half, cut] + first[0]
        dk[:half, cut] = dk[:half, cut] + first[1] * score_scale
        dv[:half, cut] = dv[:half, cut] + first[2]
        return carry

    lax.fori_loop(0, heads, head, 0)

    def rotate_back(source, target, scale):
        def one(h, carry):
            cut = pl.ds(pl.multiple_of(h * HD, HD), HD)
            value = source[:, cut] * scale
            turned = value * cos_ref[...] - pltpu.roll(value, HD // 2, 1) * sin_ref[...]
            lin_grads[target, :, cut] = turned.astype(low)
            return carry

        lax.fori_loop(0, heads, one, 0)

    rotate_back(dq, 0, score_scale)
    loads[1].wait()
    blocks_along_z(n1, lin_grads.at[0])
    chain(0)

    @pl.when(y == 0)
    def _():
        for copy in later:
            copy.wait_recv()

        def add(span):
            dk[span, :] = dk[span, :] + later_k[span, :].astype(full)
            dv[span, :] = dv[span, :] + later_v[span, :].astype(full)

        by_rows(add)

    rotate_back(dk, 1, 1.0)
    lin_grads[2] = dv[...].astype(low)
    weight_blocks(2, n1, lin_grads.at[1])
    weight_blocks(3, n1, lin_grads.at[2])
    for copy in loads[2:]:
        copy.wait()

    def dn1_part(at, target):
        cut = pl.ds(pl.multiple_of(at * cols, cols), cols)
        total = times_transpose(lin_grads[0], wq[cut, :])
        total = total + times_transpose(lin_grads[1], wk[cut, :])
        total = total + times_transpose(lin_grads[2], wv[cut, :])
        target[...] = total.astype(low)

    def to_sibling(i):
        return remote(tp_staged.at[i], tp_sib.at[i], tp_send.at[i], tp_recv.at[i], sibling)

    def part_of(i):
        x_at = 1 - x + (2 * x - 1) * i
        dn1_part(x_at * 2 + 1 - core, tp_staged.at[i])
        to_sibling(i).start()
        dn1_part(x_at * 2 + core, tp_mine.at[i])

    out_x = remote(tp_mine.at[0], tp_x, tp_send.at[2], tp_recv.at[2], across)
    part_of(0)
    to_sibling(0).wait_recv()
    add_blocks(tp_mine.at[0], [tp_sib.at[0]], rows)
    out_x.start()
    part_of(1)
    chain_2()
    to_sibling(1).wait_recv()
    out_x.wait_recv()

    def sum_parts(span):
        dn1[span, :] = (
            tp_mine[1, span, :].astype(full)
            + tp_sib[1, span, :].astype(full)
            + tp_x[span, :].astype(full)
        )

    by_rows(sum_parts)

    def unit_one(span):
        return tokens_ref[span, :].astype(full) * inv_one_ref[span, :1]

    def products(span):
        dq[span, :] = dn1[span, :] * unit_one(span)

    by_rows(products)
    gain_grad = jnp.sum(dq[...], axis=0, keepdims=True)
    dq[...] = dq[...] * first_ref[:1, :]
    total = row_exchange(1, row_of(dq[...]))
    dk[:, :128] = jnp.broadcast_to(total * (1.0 / model_dim), (rows, 128))

    def norm_one(span):
        scaled = dn1[span, :] * first_ref[:1, :]
        value = hidden_grad[span, :] + inv_one_ref[span, :1] * (
            scaled - unit_one(span) * dk[span, :1]
        )
        tokens_grad_ref[span, :] = value.astype(low)

    by_rows(norm_one)

    own = smalls.at[ep]
    own[...] = small_ref[...]
    own[0:1, :] = gain_grad
    for i in range(3):
        own[i + 1 : i + 2, :] = jnp.sum(lin_grads[i].astype(full), axis=0, keepdims=True)

    def small_to(i):
        return remote(own, own, small_send.at[i - 1], small_recv.at[i - 1], others[i - 1])

    for i in range(1, sources):
        small_to(i).start()
    other_y_along_z()
    chain(1)
    y_stage(2)
    final(0)
    chain(2)
    y_stage(3)
    chain(3)
    for i in range(1, sources):
        small_to(i).wait_recv()
    total = smalls[0]
    for i in range(1, sources):
        total = total + smalls[i]
    quarters[tp] = total
    s_x = remote(quarters.at[tp], quarters.at[tp], s_send.at[0], s_recv.at[0], across)
    s_s = remote(quarters.at[tp], quarters.at[tp], s_send.at[1], s_recv.at[1], sibling)
    s_x.start()
    s_s.start()
    final(2)
    own_first_along_z()
    s_x.wait_recv()
    other = quarters.at[tp + 2 - 4 * x]
    s_f = remote(other, other, s_send.at[2], s_recv.at[2], sibling)
    s_f.start()
    final(3)
    final(1)
    s_s.wait_recv()
    s_f.wait_recv()
    sums_ref[...] = quarters[...]

    for copy in (g_x, g_s, g_f, s_x, s_s, s_f, out_x, to_sibling(0), to_sibling(1)):
        copy.wait_send()

    @pl.when(y == 1)
    def _():
        for copy in later:
            copy.wait_send()

    for i in range(1, sources):
        small_to(i).wait_send()

    def finish(n, carry):
        z_at = lax.rem(n, 4)

        @pl.when((n < 4) | (n >= 8) | (n == 4 + z))
        def _():
            remote(staged.at[0], from_y.at[0], y_send.at[n], y_recv.at[n], beside).wait_send()


        @pl.when(z_at > z)
        def _():
            remote(mine.at[0], from_below.at[0], up_send.at[n], up_recv.at[n], above).wait_send()

        @pl.when(z_at < z)
        def _():
            remote(mine.at[0], from_above.at[0], down_send.at[n], down_recv.at[n], below).wait_send()

        return carry

    lax.fori_loop(0, 16, finish, 0)

    def finish_2(z_at, carry):
        @pl.when(z_at > z)
        def _():
            up_2(z_at).wait_send()

        @pl.when(z_at < z)
        def _():
            down_2(z_at).wait_send()

        return carry

    lax.fori_loop(0, 4, finish_2, 0)


def unwind(vmem_args, hbm_args, cid):
    rows, cols = vmem_args[0].shape
    model_dim = hbm_args[0].shape[1]
    sources = 8
    block = model_dim // sources
    low, full, dma = jnp.bfloat16, jnp.float32, pltpu.SemaphoreType.DMA
    vmem, hbm = pl.BlockSpec(memory_space=pltpu.VMEM), pl.BlockSpec(memory_space=pl.ANY)

    def buffers(*shape, dtype=low):
        return pltpu.VMEM(shape, dtype)

    return pl.pallas_call(
        unwind_kernel,
        out_shape=[
            jax.ShapeDtypeStruct((rows, cols), low),
            jax.ShapeDtypeStruct((4, block, cols), full),
            jax.ShapeDtypeStruct((4, 16, cols), full),
        ],
        in_specs=[vmem] * len(vmem_args) + [hbm] * len(hbm_args),
        out_specs=[vmem] * 3,
        scratch_shapes=[buffers(*arg.shape) for arg in hbm_args]
        + [
            buffers(rows, model_dim),
            buffers(rows, cols),
            buffers(rows, cols, dtype=full),
            buffers(rows, cols),
            buffers(rows, cols, dtype=full),
            buffers(rows, cols, dtype=full),
            buffers(rows, cols, dtype=full),
            buffers(3, rows, cols),
            buffers(rows, cols),
            buffers(rows, cols),
            buffers(rows, cols),
            buffers(rows, cols),
        ]
        + [buffers(16, block, cols)] * 5
        + [buffers(4, block, cols)] * 2
        + [
            buffers(2, rows, cols),
            buffers(2, rows, cols),
            buffers(2, rows, cols),
            buffers(rows, cols),
            buffers(rows, cols, dtype=full),
            buffers(4, 8, rows, dtype=full),
            buffers(2, 8, rows, dtype=full),
            buffers(2, 8, rows, dtype=full),
            buffers(sources, 16, cols, dtype=full),
            buffers(4, 16, cols, dtype=full),
        ]
        + [dma((5,)), dma((3,)), dma((3,)), dma((4,)), dma((4,)), dma((2,)), dma((2,))]
        + [dma((16,))] * 6
        + [dma((3,)), dma((3,)), dma((7,)), dma((7,)), dma((3,)), dma((3,))]
        + [dma((4,))] * 4,
        compiler_params=pltpu.CompilerParams(
            collective_id=cid, has_side_effects=True, vmem_limit_bytes=60 * 2**20
        ),
        name="unwind",
    )(*vmem_args, *hbm_args)


def attend_kernel(
    first_ref,
    bias_ref,
    second_ref,
    cos_ref,
    sin_ref,
    tokens_hbm,
    grad_hbm,
    wq_hbm,
    wk_hbm,
    wv_hbm,
    wo_hbm,
    hidden_ref,
    unit_ref,
    inv_ref,
    normed_ref,
    n1_ref,
    inv_one_ref,
    q_ref,
    k_ref,
    v_ref,
    ke_ref,
    ve_ref,
    context_ref,
    log_ref,
    all_ref,
    wq,
    wk,
    wv,
    wo,
    tokens,
    lin,
    total,
    most,
    weight,
    earlier_k,
    earlier_v,
    tp_staged,
    tp_mine,
    tp_sib,
    tp_x,
    row_mine,
    row_sib,
    row_x,
    load_sem,
    t_send,
    t_recv,
    kv_send,
    kv_recv,
    tp_send,
    tp_recv,
    row_send,
    row_recv,
    up_sem,
    down_sem,
    a_sem,
    b_sem,
    s_sem,
    recv_sem,
    sib_sem,
):
    ep, tp, z, y, x, core = place()
    rows, cols = hidden_ref.shape
    model_dim = n1_ref.shape[1]
    heads = cols // HD
    low, full = jnp.bfloat16, jnp.float32
    score_scale = HD ** (-0.5)
    sibling, across = (ep, tp + 1 - 2 * core), (ep, tp + 2 - 4 * x)
    beside = (ep + 1 - 2 * y, tp)
    peer_a, peer_b, _, above, below = lane_peers()

    def quarter(at):
        return tokens.at[:, pl.ds(pl.multiple_of(at * cols, cols), cols)]

    loads = [
        pltpu.make_async_copy(source, target, load_sem.at[i])
        for i, (source, target) in enumerate(
            (
                (tokens_hbm, quarter(tp)),
                (wk_hbm, wk),
                (wv_hbm, wv),
                (wq_hbm, wq),
                (wo_hbm, wo),
            )
        )
    ]
    for copy in loads:
        copy.start()
    greet([across, beside, sibling], True)

    t_x = remote(tokens_hbm, quarter(tp), t_send.at[0], t_recv.at[0], across)
    t_s = remote(tokens_hbm, quarter(tp), t_send.at[1], t_recv.at[1], sibling)
    t_x.start()
    t_s.start()

    def choose(*values):
        return jnp.where(
            z == 0, values[0], jnp.where(z == 1, values[1], jnp.where(z == 2, values[2], values[3]))
        )

    coming = (z, choose(1, 0, 3, 2), choose(2, 2, 1, 1), choose(3, 3, 0, 0))

    def spot(z_at, da, db):
        group, at_quarter = lane_spot(z_at, da, db, core)
        return all_ref.at[
            pl.ds(pl.multiple_of(group * rows, rows), rows),
            pl.ds(pl.multiple_of(at_quarter * cols, cols), cols),
        ]

    def at(z_at, da, db):
        return z_at * 4 + da * 2 + db

    def arrived(z_at, da, db):
        block, n = spot(z_at, da, db), at(z_at, da, db)
        remote(block, block, s_sem.at[n], recv_sem.at[n], sibling).wait_recv()
        return block

    def up(z_at, da, source):
        n = z_at * 2 + da
        target = recv_sem.at[at(z_at, da, 0)]
        return remote(source, spot(z_at, da, 0), up_sem.at[n], target, above)

    def down(z_at, da, source):
        n = z_at * 2 + da
        target = recv_sem.at[at(z_at, da, 0)]
        return remote(source, spot(z_at, da, 0), down_sem.at[n], target, below)

    def over_a(source):
        return remote(source, spot(z, 0, 0), a_sem, recv_sem.at[at(z, 1, 0)], peer_a)

    def over_b(z_at, da, source):
        return remote(
            source, spot(z_at, da, 0), b_sem.at[z_at * 2 + da], recv_sem.at[at(z_at, da, 1)], peer_b
        )

    def to_sibling(z_at, da, db, source):
        n = at(z_at, da, db)
        return remote(source, spot(z_at, da, db), s_sem.at[n], sib_sem.at[n], sibling)

    def along_z(da, source):
        @pl.when(z < 3)
        def _():
            up(z, da, source).start()

        @pl.when(z > 0)
        def _():
            down(z, da, source).start()

    def pass_a():
        block = arrived(z, 1, 0)
        along_z(1, block)
        over_b(z, 1, block).start()
        to_sibling(z, 1, 0, block).start()

    def pass_z(k, da):
        z_at = coming[k]
        block = arrived(z_at, da, 0)

        @pl.when((z_at > z) & (z > 0))
        def _():
            down(z_at, da, block).start()

        @pl.when((z_at < z) & (z < 3))
        def _():
            up(z_at, da, block).start()

        over_b(z_at, da, block).start()
        to_sibling(z_at, da, 0, block).start()

    def pass_b(k, da):
        block = arrived(coming[k], da, 1)
        to_sibling(coming[k], da, 1, block).start()

    own = pltpu.make_async_copy(grad_hbm, spot(z, 0, 0), load_sem.at[5])
    over_a(grad_hbm).start()
    along_z(0, grad_hbm)
    over_b(z, 0, grad_hbm).start()
    to_sibling(z, 0, 0, grad_hbm).start()
    own.start()

    t_x.wait_recv()
    theirs = quarter(tp + 2 - 4 * x)
    t_f = remote(theirs, theirs, t_send.at[2], t_recv.at[2], sibling)
    t_f.start()
    loads[0].wait()
    t_s.wait_recv()
    t_f.wait_recv()

    def by_rows(step, body):
        def one(i, carry):
            body(pl.ds(pl.multiple_of(i * step, step), step))
            return carry

        lax.fori_loop(0, rows // step, one, 0)

    def norm_one(span):
        values = tokens[span, :].astype(full)
        inv = lax.rsqrt(jnp.mean(values * values, axis=1, keepdims=True) + norm_eps)
        n1_ref[span, :] = (values * inv * first_ref[:1, :]).astype(low)
        inv_one_ref[span, :] = jnp.broadcast_to(inv, (inv.shape[0], 128))

    by_rows(32, norm_one)
    pass_a()
    pass_z(1, 0)

    def project(weights, bias_at):
        def one(i, carry):
            cut = pl.ds(pl.multiple_of(i * 256, 256), 256)
            lin[:, cut] = (
                jnp.dot(n1_ref[...], weights[:, cut], preferred_element_type=full)
                + bias_ref[bias_at : bias_at + 1, cut]
            )
            return carry

        lax.fori_loop(0, cols // 256, one, 0)

    def rotate_into(target):
        def one(h, carry):
            cut = pl.ds(pl.multiple_of(h * HD, HD), HD)
            value = lin[:, cut]
            turned = value * cos_ref[...] + pltpu.roll(value, HD // 2, 1) * sin_ref[...]
            target[:, cut] = turned.astype(low)
            return carry

        lax.fori_loop(0, heads, one, 0)

    loads[1].wait()
    project(wk, 1)
    rotate_into(k_ref)
    loads[2].wait()
    project(wv, 2)
    v_ref[...] = lin[...].astype(low)
    earlier = (
        remote(k_ref, earlier_k, kv_send.at[0], kv_recv.at[0], beside),
        remote(v_ref, earlier_v, kv_send.at[1], kv_recv.at[1], beside),
    )

    @pl.when(y == 0)
    def _():
        for copy in earlier:
            copy.start()

    pass_b(0, 0)
    pass_z(2, 0)
    pass_z(1, 1)
    loads[3].wait()
    project(wq, 0)
    rotate_into(q_ref)

    half = rows // 2
    lane = lax.broadcasted_iota(jnp.int32, (1, 128), 1)

    def pick(held, span, h):
        return jnp.sum(jnp.where(lane == h, held[span, :], 0.0), axis=1, keepdims=True)

    def put(held, span, h, value):
        held[span, :] = jnp.where(lane == h, value, held[span, :])

    most[...] = jnp.zeros_like(most)
    weight[...] = jnp.ones_like(weight)

    def local_head(h, carry):
        cut = pl.ds(pl.multiple_of(h * HD, HD), HD)
        for qb in range(2):
            span, count = pl.ds(qb * half, half), (qb + 1) * half
            scores = times_transpose(q_ref[span, cut], k_ref[:count, cut]) * score_scale
            top = jnp.max(scores, axis=1, keepdims=True)
            powers = jnp.exp(scores - top)
            put(most, span, h, top)
            put(weight, span, h, jnp.sum(powers, axis=1, keepdims=True))
            total[span, cut] = jnp.dot(
                powers.astype(low), v_ref[:count, cut], preferred_element_type=full
            )
        return carry

    lax.fori_loop(0, heads, local_head, 0)
    pass_z(2, 1)
    pass_z(3, 0)
    pass_b(0, 1)
    pass_b(1, 0)

    @pl.when(y == 0)
    def _():
        ke_ref[...] = jnp.zeros_like(ke_ref)
        ve_ref[...] = jnp.zeros_like(ve_ref)

    @pl.when(y == 1)
    def _():
        for copy in earlier:
            copy.wait_recv()
        ke_ref[...] = earlier_k[...]
        ve_ref[...] = earlier_v[...]

        def remote_head(h, carry):
            cut = pl.ds(pl.multiple_of(h * HD, HD), HD)
            for qb in range(2):
                span = pl.ds(qb * half, half)
                scores = times_transpose(q_ref[span, cut], ke_ref[:, cut]) * score_scale
                before = pick(most, span, h)
                top = jnp.maximum(before, jnp.max(scores, axis=1, keepdims=True))
                powers = jnp.exp(scores - top)
                shrink = jnp.exp(before - top)
                put(most, span, h, top)
                put(
                    weight,
                    span,
                    h,
                    pick(weight, span, h) * shrink + jnp.sum(powers, axis=1, keepdims=True),
                )
                total[span, cut] = total[span, cut] * shrink + jnp.dot(
                    powers.astype(low), ve_ref[:, cut], preferred_element_type=full
                )
            return carry

        lax.fori_loop(0, heads, remote_head, 0)

    def finish_head(h, carry):
        cut = pl.ds(pl.multiple_of(h * HD, HD), HD)
        context_ref[:, cut] = (total[:, cut] / pick(weight, slice(None), h)).astype(low)
        return carry

    lax.fori_loop(0, heads, finish_head, 0)
    log_ref[...] = most[...] + jnp.log(weight[...])

    loads[4].wait()

    def out_part(at_quarter, target):
        cut = pl.ds(pl.multiple_of(at_quarter * cols, cols), cols)
        target[...] = jnp.dot(context_ref[...], wo[:, cut], preferred_element_type=full).astype(low)

    def part_to_sibling(i):
        return remote(tp_staged.at[i], tp_sib.at[i], tp_send.at[i], tp_recv.at[i], sibling)

    def part_of(i):
        x_at = 1 - x + (2 * x - 1) * i
        out_part(x_at * 2 + 1 - core, tp_staged.at[i])
        part_to_sibling(i).start()
        out_part(x_at * 2 + core, tp_mine.at[i])

    out_x = remote(tp_mine.at[0], tp_x, tp_send.at[2], tp_recv.at[2], across)
    part_of(0)
    part_to_sibling(0).wait_recv()
    add_blocks(tp_mine.at[0], [tp_sib.at[0]], rows)
    out_x.start()
    part_of(1)
    pass_z(3, 1)
    pass_b(1, 1)
    pass_b(2, 0)
    part_to_sibling(1).wait_recv()
    out_x.wait_recv()
    own_cut = pl.ds(pl.multiple_of(tp * cols, cols), cols)

    def sum_parts(span):
        value = tokens[span, own_cut].astype(full) + (
            tp_mine[1, span, :].astype(full)
            + tp_sib[1, span, :].astype(full)
            + tp_x[span, :].astype(full)
        )
        hidden_ref[span, :] = value
        lin[span, :] = value * value

    by_rows(64, sum_parts)

    row_mine[0] = row_of(lin[...])
    first = remote(row_mine.at[0], row_sib, row_send.at[0], row_recv.at[0], sibling)
    first.start()
    first.wait_recv()
    row_mine[1] = row_mine[0] + row_sib[...]
    second = remote(row_mine.at[1], row_x, row_send.at[1], row_recv.at[1], across)
    second.start()
    second.wait_recv()
    squares = (row_mine[1] + row_x[...]).T[:, :1]
    inv_two = lax.rsqrt(squares * (1.0 / model_dim) + norm_eps)
    inv_ref[...] = jnp.broadcast_to(inv_two, (rows, 128))

    def norm_two(span):
        unit = hidden_ref[span, :] * inv_ref[span, :1]
        unit_ref[span, :] = unit
        normed_ref[span, :] = (unit * second_ref[:1, :]).astype(low)

    by_rows(64, norm_two)

    pass_b(2, 1)
    pass_b(3, 0)
    pass_b(3, 1)

    def finish_sibling(i, carry):
        block = spot(0, 0, 0)
        copy = remote(block, block, s_sem.at[i], sib_sem.at[i], sibling)
        copy.wait_recv()
        copy.wait_send()
        return carry

    lax.fori_loop(0, 16, finish_sibling, 0)

    def finish_links(i, carry):
        for da in range(2):
            over_b(i, da, grad_hbm).wait_send()

            @pl.when((z < 3) & (i <= z))
            def _(da=da):
                up(i, da, grad_hbm).wait_send()

            @pl.when((z > 0) & (i >= z))
            def _(da=da):
                down(i, da, grad_hbm).wait_send()

        return carry

    lax.fori_loop(0, 4, finish_links, 0)
    over_a(grad_hbm).wait_send()
    own.wait()
    for copy in (t_x, t_s, t_f, out_x, part_to_sibling(0), part_to_sibling(1), first, second):
        copy.wait_send()

    @pl.when(y == 0)
    def _():
        for copy in earlier:
            copy.wait_send()


def attend(vmem_args, hbm_args, cid):
    rows, cols = hbm_args[0].shape
    model_dim = vmem_args[0].shape[1]
    low, full, dma = jnp.bfloat16, jnp.float32, pltpu.SemaphoreType.DMA
    vmem, hbm = pl.BlockSpec(memory_space=pltpu.VMEM), pl.BlockSpec(memory_space=pl.ANY)

    def buffers(*shape, dtype=low):
        return pltpu.VMEM(shape, dtype)

    def result(*shape, dtype=low):
        return jax.ShapeDtypeStruct(shape, dtype)

    return pl.pallas_call(
        attend_kernel,
        out_shape=[
            result(rows, cols, dtype=full),
            result(rows, cols, dtype=full),
            result(rows, 128, dtype=full),
            result(rows, cols),
            result(rows, model_dim),
            result(rows, 128, dtype=full),
        ]
        + [result(rows, cols)] * 6
        + [result(rows, 128, dtype=full), result(8 * rows, model_dim)],
        in_specs=[vmem] * len(vmem_args) + [hbm] * len(hbm_args),
        out_specs=[vmem] * 13 + [hbm],
        scratch_shapes=[buffers(*arg.shape) for arg in hbm_args[2:]]
        + [
            buffers(rows, model_dim),
            buffers(rows, cols, dtype=full),
            buffers(rows, cols, dtype=full),
            buffers(rows, 128, dtype=full),
            buffers(rows, 128, dtype=full),
            buffers(rows, cols),
            buffers(rows, cols),
            buffers(2, rows, cols),
            buffers(2, rows, cols),
            buffers(2, rows, cols),
            buffers(rows, cols),
            buffers(2, 8, rows, dtype=full),
            buffers(8, rows, dtype=full),
            buffers(8, rows, dtype=full),
        ]
        + [dma((6,)), dma((3,)), dma((3,)), dma((2,)), dma((2,)), dma((3,)), dma((3,))]
        + [dma((2,)), dma((2,))]
        + [dma((8,)), dma((8,)), dma, dma((8,)), dma((16,)), dma((16,)), dma((16,))],
        compiler_params=pltpu.CompilerParams(
            collective_id=cid, has_side_effects=True, vmem_limit_bytes=60 * 2**20
        ),
        name="attend",
    )(*vmem_args, *hbm_args)


def kept_choice(expert_ids, pair_order, expert_total, capacity):
    tok_count, top_count = expert_ids.shape
    pair_count = tok_count * top_count
    order = pair_order.reshape(-1)
    pairs = jnp.arange(pair_count, dtype=jnp.int32)
    turn = jnp.sum(jnp.where(order[None, :] == pairs[:, None], pairs[None, :], 0), axis=1)
    turn = turn.reshape(tok_count, top_count)
    picked = expert_ids[:, :, None] == jnp.arange(expert_total, dtype=jnp.int32)[None, None, :]
    experts_apart = jnp.arange(expert_total, dtype=jnp.int32)[:, None, None]
    picked = expert_ids.T[None] == experts_apart
    named = jnp.any(picked, axis=1)
    turn_of = jnp.sum(jnp.where(picked, turn.T[None], 0), axis=1)
    turn_of = jnp.where(named, turn_of, pair_count)
    slot = jnp.sum((turn_of[:, None, :] < turn_of[:, :, None]).astype(jnp.int32), axis=2)
    return (named & (slot < capacity)).astype(jnp.float32)


def dense_plan(
    tokens,
    out_grad,
    first_gain,
    query_weight,
    key_weight,
    value_weight,
    query_bias,
    key_bias,
    value_bias,
    output_weight,
    second_gain,
    router_weight,
    shared_gate_weight,
    shared_up_weight,
    shared_down_weight,
    switch_vector,
    expert_gate_weight,
    expert_up_weight,
    expert_down_weight,
    expert_ids,
    pair_order,
):
    ep, tp = lax.axis_index("ep"), lax.axis_index("tp")
    tok_count, col_width = tokens.shape
    model_dim = query_weight.shape[0]
    sources = lax.axis_size("ep")
    place_in_seq = ep % SPAN
    expert_total = router_weight.shape[1]
    capacity = 9 * tok_count * expert_ids.shape[1] // (8 * expert_total)
    head_count = query_weight.shape[1] // HD
    expert_width = expert_gate_weight.shape[2]
    shared_width = shared_gate_weight.shape[1] // sources
    width = expert_width + shared_width

    def own_cols(vector):
        return lax.dynamic_slice_in_dim(vector, tp * col_width, col_width, vector.ndim - 1)

    kept_own = kept_choice(expert_ids, pair_order, expert_total, capacity)

    cosine, sine_part = rope_tables(tok_count, HD, place_in_seq * tok_count)
    cos_wide = jnp.concatenate([cosine[:, 0], cosine[:, 0]], axis=1)
    sin_wide = jnp.concatenate([-sine_part[:, 0], sine_part[:, 0]], axis=1)
    second_cols = own_cols(second_gain)
    biases = jnp.stack([query_bias, key_bias, value_bias])
    (
        hidden_cols,
        unit_two,
        inv_two,
        normed_cols,
        normed_one,
        inv_one,
        queries,
        keys_rot,
        values_all,
        earlier_keys,
        earlier_values,
        context,
        log_rows,
        grads_all,
    ) = attend(
        [first_gain[None], biases, second_cols[None], cos_wide, sin_wide],
        [tokens, out_grad, query_weight, key_weight, value_weight, output_weight],
        2,
    )

    extra_rows = jnp.concatenate([router_weight.T, switch_vector[None, :]], axis=0)
    extra_rows = jnp.pad(extra_rows, ((0, 16 - extra_rows.shape[0]), (0, 0)))
    kept_rows = jnp.pad(kept_own, ((0, 16 - expert_total), (0, 0))).astype(jnp.bfloat16)
    reduced, layer_out, logit_tile, down_grad, gate_grad, up_grad, shared_parts, *_ = experts(
        normed_cols,
        grads_all,
        kept_rows,
        [
            expert_gate_weight[0].T,
            shared_gate_weight,
            extra_rows,
            expert_up_weight[0].T,
            shared_up_weight,
            expert_down_weight[0],
            shared_down_weight,
        ],
        hidden_cols,
        expert_total,
        4,
    )
    shared_parts = lax.all_to_all(shared_parts, "ep", split_axis=0, concat_axis=0, tiled=True)
    shared_parts = shared_parts.transpose(1, 0, 2, 3).reshape(3, sources * shared_width, -1)
    shared_parts = shared_parts.astype(jnp.float32)
    shared_gate_grad = shared_parts[1].T
    shared_up_grad = shared_parts[2].T
    shared_down_grad = shared_parts[0]

    normed_grad = reduced[:tok_count]
    probs_grad = (reduced[tok_count : tok_count + expert_total] * kept_own).T
    switch_grad = reduced[tok_count + expert_total]
    logit_at = width % 128
    probs_own = softmax_rows(logit_tile[:, logit_at : logit_at + expert_total])
    switch = jax.nn.sigmoid(logit_tile[:, logit_at + expert_total])
    logit_grad = (
        probs_own * (probs_grad - jnp.sum(probs_own * probs_grad, axis=-1, keepdims=True))
    ).astype(jnp.bfloat16)
    router_grad = inner_rows(normed_cols, logit_grad)
    switch_lin_grad = switch_grad * switch * (1.0 - switch)
    switch_vector_grad = jnp.dot(switch_lin_grad, normed_cols, preferred_element_type=jnp.float32)
    router_cols = lax.dynamic_slice_in_dim(router_weight, tp * col_width, col_width, 0)
    normed_grad = normed_grad + times_transpose(logit_grad, router_cols)
    normed_grad = (
        normed_grad
        + switch_lin_grad[:, None] * own_cols(switch_vector).astype(jnp.float32)[None, :]
    )
    second_gain_grad = jnp.sum(normed_grad * unit_two, axis=0)

    small = jnp.concatenate(
        [second_gain_grad[None], switch_vector_grad[None], router_grad.T], axis=0
    )
    small_rows = small.shape[0]
    small = jnp.pad(small, ((4, 12 - small_rows), (0, 0)))
    tokens_grad, weight_grads, sums = unwind(
        [
            normed_grad,
            unit_two,
            inv_two,
            second_cols[None],
            out_grad,
            tokens,
            inv_one,
            own_cols(first_gain)[None],
            small,
            queries,
            keys_rot,
            values_all,
            earlier_keys,
            earlier_values,
            context,
            log_rows,
            cos_wide,
            sin_wide,
        ],
        [normed_one, query_weight, key_weight, value_weight, output_weight],
        5,
    )
    share = model_dim // sources
    bias_width = HD // sources
    bias_sums = lax.dynamic_slice_in_dim(
        lax.dynamic_index_in_dim(sums, tp, 0, keepdims=False)[1:4].reshape(3, head_count, HD),
        ep * bias_width,
        bias_width,
        2,
    )
    per_quarter = col_width // share
    spread = lax.dynamic_index_in_dim(sums, ep // per_quarter, 0, keepdims=False)
    spread = lax.dynamic_slice_in_dim(spread, ep % per_quarter * share, share, 1)
    spread = jnp.concatenate([spread[:1], spread[4 : 4 + small_rows]], axis=0)
    return (
        layer_out,
        tokens_grad,
        spread[0],
        weight_grads[1],
        weight_grads[2],
        weight_grads[3],
        bias_sums[0],
        bias_sums[1],
        bias_sums[2],
        weight_grads[0].T,
        spread[1],
        spread[3:].T,
        shared_gate_grad,
        shared_up_grad,
        shared_down_grad,
        spread[2],
        gate_grad.T[None],
        up_grad.T[None],
        down_grad[None],
    )


def solution(mesh):
    plan = dense_plan if dict(mesh.shape) == {"ep": 8, "tp": 4} else slot_plan
    return jax.shard_map(
        plan,
        mesh=mesh,
        in_specs=(
            P("ep", "tp"),
            P("ep", "tp"),
            P(),
            P(None, "tp"),
            P(None, "tp"),
            P(None, "tp"),
            P("tp"),
            P("tp"),
            P("tp"),
            P("tp", None),
            P(),
            P(),
            P(None, "tp"),
            P(None, "tp"),
            P("tp", None),
            P(),
            P("ep", None, "tp"),
            P("ep", None, "tp"),
            P("ep", "tp", None),
            P("ep", None),
            P("ep", None),
        ),
        out_specs=(
            P("ep", "tp"),
            P("ep", "tp"),
            P("ep"),
            P("ep", "tp"),
            P("ep", "tp"),
            P("ep", "tp"),
            P("tp", "ep"),
            P("tp", "ep"),
            P("tp", "ep"),
            P("tp", "ep"),
            P("ep"),
            P("ep", None),
            P("ep", "tp"),
            P("ep", "tp"),
            P("tp", "ep"),
            P("ep"),
            P("ep", None, "tp"),
            P("ep", None, "tp"),
            P("ep", "tp", None),
        ),
        check_vma=False,
    )
```
